32 devices in a mesh: seq: 8 (over z, y), head: 4 (over x, core).
Axes of the slice: x: 2, y: 2, z: 4, core: 2. Of those that a mesh axis runs over, the one named last changes fastest.
Arguments:
- inputs: bfloat16 [8192, 768], P('seq'), may hold values from -4.5 to 4.5
- cotangent: bfloat16 [8192, 768], P('seq'), may hold values from -6 to 6
- item_lengths: int32 [3], replicated, may hold values from 64 to 7168, as said below
- w_query: bfloat16 [768, 768], P('seq', 'head'), may hold values from -0.21875 to 0.21875
- w_key: bfloat16 [768, 768], P('seq', 'head'), may hold values from -0.21875 to 0.21875
- w_value: bfloat16 [768, 768], P('seq', 'head'), may hold values from -0.21875 to 0.21875
- w_out: bfloat16 [768, 768], P('seq', 'head'), may hold values from -0.21875 to 0.21875
- w_up: bfloat16 [768, 3072], P('seq', 'head'), may hold values from -0.21875 to 0.21875
- w_down: bfloat16 [768, 3072], P('seq', 'head'), may hold values from -0.109375 to 0.109375
- bias_query: float32 [768], P('head'), may hold values from -3 to 3
- bias_value: float32 [768], P('head'), may hold values from -3 to 3
- bias_out: float32 [768], replicated, may hold values from -3 to 3
- bias_up: float32 [3072], P('head'), may hold values from -3 to 3
- bias_down: float32 [768], replicated, may hold values from -3 to 3
- gain_one: float32 [768], replicated, may hold values from 0.1 to 1.9
- bias_one: float32 [768], replicated, may hold values from -3 to 3
- gain_two: float32 [768], replicated, may hold values from 0.1 to 1.9
- bias_two: float32 [768], replicated, may hold values from -3 to 3
- conv_taps: float32 [12, 33], P('head'), may hold values from -2 to 2
Outputs:
- output: bfloat16 [8192, 768], P('seq')
- grad_inputs: bfloat16 [8192, 768], P('seq')
- grad_w_query: float32 [768, 768], P('seq', 'head')
- grad_w_key: float32 [768, 768], P('seq', 'head')
- grad_w_value: float32 [768, 768], P('seq', 'head')
- grad_w_out: float32 [768, 768], P('seq', 'head')
- grad_w_up: float32 [768, 3072], P('seq', 'head')
- grad_w_down: float32 [768, 3072], P('seq', 'head')
- grad_bias_query: float32 [768], P('head')
- grad_bias_value: float32 [768], P('head')
- grad_bias_out: float32 [768], replicated
- grad_bias_up: float32 [3072], P('head')
- grad_bias_down: float32 [768], replicated
- grad_gain_one: float32 [768], replicated
- grad_bias_one: float32 [768], replicated
- grad_gain_two: float32 [768], replicated
- grad_bias_two: float32 [768], replicated
- grad_conv_taps: float32 [12, 33], P('head')
The draws below stay inside these ranges and needn't reach their ends.
Inputs may be any that keep to these rules, and one draw needn't show every extreme that they name: `item_lengths`: every length is a multiple of 64; the first and the last item are 64 and 960 tokens long, in either order, and the middle item holds the rest.
All inputs are finite; a program needn't handle non-finite values.
Results may differ from the reference program's by a relative error of at most 0.038.
Values may be sent and summed in bfloat16 or wider, within the bound.
A program may use at most 128 MiB of HBM per device.

```python
import math
import jax
import jax.numpy as jnp
from jax import lax

D = 768
HEADS = 12
HEAD_DIM = 64
FF = 3072
LAND = 64
KERNEL = 33
PINV_STEPS = 6
ITEMS = 3
TOK_DEV = 1024
TOKENS = 8192


def draw_item_lengths(key, part):
    key = jax.random.fold_in(key, 5)
    flip = jax.random.randint(key, (), 0, 2).astype(jnp.int32)
    short_rim = jnp.int32(LAND)
    long_rim = jnp.int32(TOK_DEV - LAND)
    first = jnp.where(flip == 0, short_rim, long_rim).astype(jnp.int32)
    last = jnp.where(flip == 0, long_rim, short_rim).astype(jnp.int32)
    middle = jnp.int32(TOKENS - TOK_DEV)
    return jnp.stack([first, middle, last]).astype(jnp.int32)


def draw_inputs(key, part):
    key = jax.random.fold_in(key, 11)
    key_rough, key_period, key_phase = jax.random.split(key, 3)
    position = jnp.arange(TOKENS, dtype=jnp.float32)[:, None]
    period = TOKENS / LAND * jnp.exp(jax.random.uniform(key_period, (1, D), jnp.float32, 0.0, math.log(8.0)))
    phase = jax.random.uniform(key_phase, (1, D), jnp.float32, -math.pi, math.pi)
    smooth = math.sqrt(2.0) * jnp.cos(2.0 * math.pi * position / period + phase)
    rough = jnp.clip(jax.random.normal(key_rough, (TOKENS, D), jnp.float32), -6.0, 6.0)
    return (0.5 * rough + smooth).astype(jnp.bfloat16)


def levels(key, shape, cuts, least, largest):
    def one(dim, blocks):
        heights = jax.random.uniform(jax.random.fold_in(jax.random.fold_in(key, 6), dim), (blocks,), jnp.float32, least / len(cuts), largest / len(cuts))
        return jnp.repeat(jnp.exp(heights), shape[dim] // blocks).reshape((-1,) + (1,) * (len(shape) - dim - 1))

    factor_of = one(*cuts[0])
    for cut in cuts[1:]:
        factor_of = factor_of * one(*cut)
    return factor_of


def noise(own_key, shape, deviation, most, cuts=(), held_as=jnp.bfloat16):
    array = jax.random.normal(own_key, shape, jnp.float32) * deviation
    if len(cuts) > 0:
        array = levels(own_key, shape, cuts, -0.22, 0.18) * array
    return jnp.clip(array, min=-most, max=most).astype(held_as)


def setup_inputs(seed: int = 0) -> dict:
    streams_of = jax.random.split(jax.random.key(seed), 20)
    return {
        "inputs": draw_inputs(jax.random.fold_in(streams_of[19], 71), 0),
        "cotangent": noise(streams_of[1], (TOKENS, D), 1.0, 6.0, ((0, 8),)),
        "item_lengths": draw_item_lengths(jax.random.fold_in(streams_of[19], 71), 0),
        "w_query": noise(streams_of[3], (D, D), D ** -0.5, 0.21875, ((0, 8), (1, 4))),
        "w_key": noise(streams_of[4], (D, D), D ** -0.5, 0.21875, ((0, 8), (1, 4))),
        "w_value": noise(streams_of[5], (D, D), D ** -0.5, 0.21875, ((0, 8), (1, 4))),
        "w_out": noise(streams_of[6], (D, D), D ** -0.5, 0.21875, ((0, 8), (1, 4))),
        "w_up": noise(streams_of[7], (D, FF), D ** -0.5, 0.21875, ((0, 8), (1, 4))),
        "w_down": noise(streams_of[8], (D, FF), FF ** -0.5, 0.109375, ((0, 8), (1, 4))),
        "bias_query": noise(streams_of[9], (D,), 0.5, 3.0, ((0, 4),), jnp.float32),
        "bias_value": noise(streams_of[10], (D,), 0.5, 3.0, ((0, 4),), jnp.float32),
        "bias_out": noise(streams_of[11], (D,), 0.5, 3.0, (), jnp.float32),
        "bias_up": noise(streams_of[12], (FF,), 0.5, 3.0, ((0, 4),), jnp.float32),
        "bias_down": noise(streams_of[13], (D,), 0.5, 3.0, (), jnp.float32),
        "gain_one": jnp.clip(1.0 + 0.18 * jax.random.normal(streams_of[14], (D,), jnp.float32), 0.1, 1.9),
        "bias_one": noise(streams_of[15], (D,), 0.5, 3.0, (), jnp.float32),
        "gain_two": jnp.clip(1.0 + 0.18 * jax.random.normal(streams_of[16], (D,), jnp.float32), 0.1, 1.9),
        "bias_two": noise(streams_of[17], (D,), 0.5, 3.0, (), jnp.float32),
        "conv_taps": noise(streams_of[18], (HEADS, KERNEL), (KERNEL // 4) ** -0.5, 2.0, ((0, 4),), jnp.float32),
    }


@jax.custom_vjp
def low(v):
    return lax.optimization_barrier(v.astype(jnp.bfloat16)).astype(jnp.float32)

@jax.custom_vjp
def low_back(v):
    return v

def low_keep(v):
    return (low(v), None)

def low_pass(kept, grad):
    return (grad,)

def back_keep(v):
    return (v, None)

def back_low(kept, grad):
    return (low(grad),)
low.defvjp(low_keep, low_pass)
low_back.defvjp(back_keep, back_low)
PRECISE = lax.Precision.HIGHEST
EPSILON = 1e-05
MASKED = -1e+30

def locate(item_lengths, positions):
    lengths = item_lengths.astype(jnp.int32)
    item_ends = jnp.cumsum(lengths).astype(jnp.int32)
    item_starts = (item_ends - lengths).astype(jnp.int32)
    located = lax.optimization_barrier(jnp.sum((positions[:, None] >= item_ends[None, :]).astype(jnp.int32), axis=1)).astype(jnp.int32)
    inside = (positions >= 0) & (located < ITEMS)
    picked = jnp.minimum(located, ITEMS - 1).astype(jnp.int32)
    onehot = (picked[:, None] == jnp.arange(ITEMS, dtype=jnp.int32)[None, :]).astype(jnp.int32)
    item_start = lax.optimization_barrier(jnp.sum(onehot * item_starts[None, :], axis=1)).astype(jnp.int32)
    length = lax.optimization_barrier(jnp.sum(onehot * lengths[None, :], axis=1)).astype(jnp.int32)
    segment = ((positions - item_start) * LAND // length).astype(jnp.int32)
    land_slot = (picked * LAND + jnp.clip(segment, 0, LAND - 1)).astype(jnp.int32)
    return (jnp.where(inside, picked, -1).astype(jnp.int32), land_slot)

def normalize(values):
    row_mean = lax.optimization_barrier(jnp.mean(values, axis=-1, keepdims=True))
    centered = values - row_mean
    variance = lax.optimization_barrier(jnp.mean(centered * centered, axis=-1, keepdims=True))
    return centered * lax.rsqrt(variance + EPSILON)

def pseudo_inverse(land_kernel):
    identity = jnp.eye(LAND, dtype=jnp.float32)
    frobenius = lax.optimization_barrier(jnp.sum(land_kernel * land_kernel, axis=(-2, -1), keepdims=True))
    result = jnp.swapaxes(land_kernel, -1, -2) / frobenius
    for iteration in range(PINV_STEPS):
        product = jnp.matmul(land_kernel, result, precision=PRECISE)
        nested = 7.0 * identity - product
        nested = 15.0 * identity - jnp.matmul(product, nested, precision=PRECISE)
        nested = 13.0 * identity - jnp.matmul(product, nested, precision=PRECISE)
        result = 0.25 * jnp.matmul(result, nested, precision=PRECISE)
    return result

def forward(inputs, w_query, w_key, w_value, w_out, w_up, w_down, bias_query, bias_value, bias_out, bias_up, bias_down, gain_one, bias_one, gain_two, bias_two, conv_taps, item_id, member, counts, slot_item):
    score_scale = HEAD_DIM ** (-0.5)
    reach = (KERNEL - 1) // 2
    queries = low(low_back(jnp.dot(inputs, w_query, precision=PRECISE)) + bias_query)
    key_rows = low(low_back(jnp.dot(inputs, w_key, precision=PRECISE)))
    value_rows = low(low_back(jnp.dot(inputs, w_value, precision=PRECISE)) + bias_value)
    query_land = low(jnp.dot(member.T, queries, precision=PRECISE) / counts[:, None])
    key_land = low(jnp.dot(member.T, key_rows, precision=PRECISE) / counts[:, None])
    same_b = slot_item[:, None] == item_id[None, :]

    def heads_first(values):
        return values.reshape(values.shape[0], HEADS, HEAD_DIM).transpose(1, 0, 2)

    def one_head(pieces):
        head_query, head_key, head_value, head_qland, head_kland = pieces
        scores_b = low_back(jnp.dot(head_qland, head_key.T, precision=PRECISE) * score_scale)
        scores_b = jnp.where(same_b, scores_b, MASKED)
        maxima_b = lax.optimization_barrier(jnp.max(scores_b, axis=1, keepdims=True))
        weights_b = jnp.exp(scores_b - maxima_b)
        totals_b = lax.optimization_barrier(jnp.sum(weights_b, axis=1, keepdims=True))
        numerator = low_back(jnp.dot(low(weights_b), head_value, precision=PRECISE))
        kernel_v = numerator / totals_b
        land_q = head_qland.reshape(ITEMS, LAND, HEAD_DIM)
        land_k = head_kland.reshape(ITEMS, LAND, HEAD_DIM)
        land_kernel = jax.nn.softmax(jnp.einsum('ild,imd->ilm', land_q, land_k, precision=PRECISE) * score_scale, axis=-1)
        inverse = pseudo_inverse(land_kernel)
        mixing = low(jnp.einsum('ilm,imd->ild', inverse, kernel_v.reshape(ITEMS, LAND, HEAD_DIM), precision=PRECISE))
        mixing = mixing.reshape(ITEMS * LAND, HEAD_DIM)
        scores_f = low_back(jnp.dot(head_query, head_kland.T, precision=PRECISE) * score_scale)
        weights_f = jax.nn.softmax(jnp.where(same_b.T, scores_f, MASKED), axis=-1)
        return jnp.dot(low(weights_f), mixing, precision=PRECISE)
    attended = lax.map(jax.checkpoint(one_head), (heads_first(queries), heads_first(key_rows), heads_first(value_rows), heads_first(query_land), heads_first(key_land)))
    attended = attended.transpose(1, 0, 2).reshape(TOKENS, D)

    def convolve(value_rows, conv_taps):
        padded = jnp.pad(value_rows, ((reach, reach), (0, 0)))
        rim_item = jnp.pad(item_id, (reach, reach), constant_values=-1)
        tap_cols = jnp.repeat(conv_taps, HEAD_DIM, axis=0)
        conv_sum = jnp.zeros((TOKENS, D), jnp.float32)
        for offset in range(KERNEL):
            in_item = (rim_item[offset:offset + TOKENS] == item_id)[:, None]
            conv_sum = conv_sum + jnp.where(in_item, padded[offset:offset + TOKENS] * tap_cols[:, offset][None, :], 0.0)
        return conv_sum
    conv_sum = jax.checkpoint(convolve)(value_rows, conv_taps)
    mixed_rows = low(low_back(attended + conv_sum))
    pre_one = inputs + low_back(jnp.dot(mixed_rows, w_out.T, precision=PRECISE)) + bias_out
    hidden = normalize(pre_one) * gain_one + bias_one
    lifted = low_back(jnp.dot(low(hidden), w_up, precision=PRECISE)) + bias_up
    active = jax.nn.gelu(lifted, approximate=True)
    pre_two = hidden + low_back(jnp.dot(low(active), w_down.T, precision=PRECISE)) + bias_down
    return normalize(pre_two) * gain_two + bias_two

def reference(inputs, cotangent, item_lengths, w_query, w_key, w_value, w_out, w_up, w_down, bias_query, bias_value, bias_out, bias_up, bias_down, gain_one, bias_one, gain_two, bias_two, conv_taps):
    positions = jnp.arange(TOKENS, dtype=jnp.int32)
    item_id, land_slot = locate(item_lengths, positions)
    member = (land_slot[:, None] == jnp.arange(ITEMS * LAND, dtype=jnp.int32)[None, :]).astype(jnp.float32)
    counts = jnp.repeat((item_lengths // LAND).astype(jnp.float32), LAND)
    slot_item = (jnp.arange(ITEMS * LAND, dtype=jnp.int32) // LAND).astype(jnp.int32)
    params = tuple((param.astype(jnp.float32) for param in (inputs, w_query, w_key, w_value, w_out, w_up, w_down, bias_query, bias_value, bias_out, bias_up, bias_down, gain_one, bias_one, gain_two, bias_two, conv_taps)))

    def closed(*values):
        return forward(*values, item_id, member, counts, slot_item)
    result, pullback = jax.vjp(closed, *params)
    grads = pullback(cotangent.astype(jnp.float32))
    return (result.astype(jnp.bfloat16), grads[0].astype(jnp.bfloat16), grads[1], grads[2], grads[3], grads[4], grads[5], grads[6], grads[7], grads[8], grads[9], grads[10], grads[11], grads[12], grads[13], grads[14], grads[15], grads[16])
```

```python
import functools

import jax
import jax.numpy as jnp
from jax import lax
from jax.experimental import pallas as pl
from jax.experimental.pallas import tpu as pltpu
from jax.sharding import PartitionSpec as P

HEAD_DIM = 64
LAND = 64
KERNEL = 33
PINV_STEPS = 6
ITEMS = 3


PRECISE = lax.Precision.HIGHEST
EPSILON = 1e-05
MASKED = -1e30


def extended(cells, sides, width):
    for axis, dim in sides:
        count = lax.axis_size(axis)
        ends = count - 1
        head = lax.slice_in_dim(cells, 0, width, axis=dim)
        tail = lax.slice_in_dim(cells, cells.shape[dim] - width, cells.shape[dim], axis=dim)
        cells = jnp.concatenate(
            [
                lax.ppermute(tail, axis, [(i, (i + 1) % count) for i in range(ends)]),
                cells,
                lax.ppermute(head, axis, [((i + 1) % count, i) for i in range(ends)]),
            ],
            axis=dim,
        )
    return cells


def cut_along(array, dim, length):
    lengths = array.shape
    parts = array.reshape(*lengths[:dim], length, lengths[dim] // length, *lengths[dim + 1 :])
    return jnp.moveaxis(parts, dim, 0)


def sent_and_summed(array, axis, dim):
    parts = cut_along(array, dim, lax.axis_size(axis))
    arrived = lax.all_to_all(parts, axis, split_axis=0, concat_axis=0, tiled=True)
    return arrived.astype(jnp.float32).sum(axis=0)


def side_by_side(arrays, axis, dim, along):
    both = jnp.concatenate(arrays, axis=along)
    out, at, outs = (sent_and_summed(both, axis, dim), 0, [])
    for a in arrays:
        outs.append(lax.slice_in_dim(out, at, at + a.shape[along], axis=along))
        at += a.shape[along]
    return tuple(outs)


def locate(item_lengths, positions):
    item_ends = jnp.cumsum(item_lengths)
    item_starts = item_ends - item_lengths
    located = jnp.sum((positions[:, None] >= item_ends[None, :]).astype(jnp.int32), axis=1)
    inside = (positions >= 0) & (located < ITEMS)
    picked = jnp.minimum(located, ITEMS - 1)
    onehot = (picked[:, None] == jnp.arange(ITEMS, dtype=jnp.int32)[None, :]).astype(jnp.int32)
    item_start = jnp.sum(onehot * item_starts[None, :], axis=1)
    length = jnp.sum(onehot * item_lengths[None, :], axis=1)
    segment = (positions - item_start) * LAND // length
    land_slot = picked * LAND + jnp.clip(segment, 0, LAND - 1)
    return (jnp.where(inside, picked, -1), land_slot)


def normalize(values):
    row_mean = jnp.mean(values, axis=-1, keepdims=True)
    centered = values - row_mean
    variance = jnp.mean(centered * centered, axis=-1, keepdims=True)
    inv_std = lax.rsqrt(variance + EPSILON)
    return (centered * inv_std, inv_std)


def norm_back(grad_norm, normed, inv_std):
    return inv_std * (
        grad_norm
        - jnp.mean(grad_norm, axis=-1, keepdims=True)
        - normed * jnp.mean(grad_norm * normed, axis=-1, keepdims=True)
    )


def pseudo_inverse(land_kernel):
    identity = jnp.eye(LAND, dtype=jnp.float32)
    frobenius = jnp.sum(land_kernel * land_kernel, axis=(-2, -1), keepdims=True)
    result = jnp.swapaxes(land_kernel, -1, -2) / frobenius
    for iteration in range(PINV_STEPS):
        product = jnp.matmul(land_kernel, result, precision=PRECISE)
        nested = 7.0 * identity - product
        nested = 15.0 * identity - jnp.matmul(product, nested, precision=PRECISE)
        nested = 13.0 * identity - jnp.matmul(product, nested, precision=PRECISE)
        result = 0.25 * jnp.matmul(result, nested, precision=PRECISE)
    return result


def gelu_tanh(values):
    return jax.nn.gelu(values, approximate=True)


def matmul_low(left, right):
    return jnp.dot(left, right, preferred_element_type=jnp.float32)


def against(left, right):
    return lax.dot_general(
        left, right, (((1,), (1,)), ((), ())), preferred_element_type=jnp.float32
    )


def across(left, right):
    return lax.dot_general(
        left, right, (((0,), (0,)), ((), ())), preferred_element_type=jnp.float32
    )


MESH = pl.DeviceIdType.MESH
WIDE = jnp.float32
LOW = jnp.bfloat16
CHUNKS = 4


def place():
    s, h = lax.axis_index("seq"), lax.axis_index("head")
    return s, h, s // 2, lax.rem(s, 2), h // 2, lax.rem(h, 2)


def partners(count):
    s, h, z, y, x, core = place()
    lines = count // 2
    core_peer = (s, 2 * x + 1 - core)
    x_peer = (s, 2 * (1 - x) + core)
    y_peer = (2 * z + 1 - y, h)
    z_peers = [(2 * lax.rem(z + j, lines) + y, h) for j in range(1, lines)]
    return core_peer, x_peer, y_peer, z_peers


def remote(src, dst, send, recv, device):
    return pltpu.make_async_remote_copy(
        src_ref=src, dst_ref=dst, send_sem=send, recv_sem=recv, device_id=device, device_id_type=MESH
    )


class Gather:
    def __init__(self, count, shard, full, own, zs, zr, ys, yr):
        self.count, self.shard, self.full, self.own = count, shard, full, own
        self.zs, self.zr, self.ys, self.yr = zs, zr, ys, yr
        s, h, z, y, _, _ = place()
        _, _, y_peer, z_peers = partners(count)
        lines = count // 2
        self.local = pltpu.make_async_copy(shard, full.at[s], own)
        self.z_copies = [
            remote(shard, full.at[s], zs.at[j], zr.at[j], z_peers[j]) for j in range(lines - 1)
        ]
        self.y_copies = [remote(shard, full.at[s], ys.at[0], yr.at[0], y_peer)]
        for j in range(1, lines):
            slot = 2 * lax.rem(z - j + lines, lines) + y
            self.y_copies.append(
                remote(full.at[slot], full.at[slot], ys.at[j], yr.at[j], y_peer)
            )

    def start(self):
        for copy in self.z_copies:
            copy.start()
        self.y_copies[0].start()
        self.local.start()

    def forward(self):
        for z_copy, y_copy in zip(self.z_copies, self.y_copies[1:]):
            z_copy.wait_recv()
            y_copy.start()

    def finish(self):
        self.local.wait()
        for copy in self.y_copies:
            copy.wait_recv()

    def close(self):
        for copy in self.z_copies + self.y_copies:
            copy.wait_send()


class Scatter:
    def __init__(self, count, terms, y_buf, pair, z_buf, ys, yr, zs, zr):
        self.count, self.terms, self.y_buf, self.pair, self.z_buf = count, terms, y_buf, pair, z_buf
        s, h, z, y, _, _ = place()
        _, _, y_peer, z_peers = partners(count)
        lines = count // 2
        self.lines, self.z, self.y = lines, z, y
        self.y_copies = []
        for j in range(lines):
            line = lax.rem(z + j, lines)
            self.y_copies.append(
                remote(terms.at[2 * line + 1 - y], y_buf.at[line], ys.at[j], yr.at[j], y_peer)
            )
        self.z_copies = [
            remote(pair.at[j], z_buf.at[j], zs.at[j], zr.at[j], z_peers[j])
            for j in range(lines - 1)
        ]

    def start(self):
        for j in list(range(1, self.lines)) + [0]:
            self.y_copies[j].start()

    def forward(self):
        for j in range(1, self.lines):
            line = lax.rem(self.z + j, self.lines)
            self.y_copies[j].wait_recv()
            self.pair[j - 1] = (
                self.terms[2 * line + self.y].astype(WIDE) + self.y_buf[line].astype(WIDE)
            ).astype(LOW)
            self.z_copies[j - 1].start()

    def finish(self, out):
        self.y_copies[0].wait_recv()
        total = self.terms[2 * self.z + self.y].astype(WIDE) + self.y_buf[self.z].astype(WIDE)
        for j, copy in enumerate(self.z_copies):
            copy.wait_recv()
            total = total + self.z_buf[j].astype(WIDE)
        out[...] = total

    def close(self):
        for copy in self.z_copies + self.y_copies:
            copy.wait_send()


def greet(devices):
    barrier = pltpu.get_barrier_semaphore()
    for device in devices:
        pl.semaphore_signal(barrier, inc=1, device_id=device, device_id_type=MESH)
    pl.semaphore_wait(barrier, len(devices))


def fold(rows):
    return rows.reshape(rows.shape[0] // 8, 8, rows.shape[1]).sum(axis=0)


class HeadSum:
    def __init__(self, terms, core_in, x_out, x_in, sems):
        self.terms, self.core_in, self.x_out, self.x_in, self.sems = terms, core_in, x_out, x_in, sems
        _, _, _, _, _, self.core = place()
        self.half = terms.shape[1] // 2
        self.core_peer, self.x_peer, _, _ = partners(2)

    def core_copy(self, c):
        away = pl.ds(pl.multiple_of((1 - self.core) * self.half, self.half), self.half)
        return remote(
            self.terms.at[c, away], self.core_in.at[c], self.sems.at[0, c], self.sems.at[1, c], self.core_peer
        )

    def x_copy(self, c):
        return remote(self.x_out.at[c], self.x_in.at[c], self.sems.at[2, c], self.sems.at[3, c], self.x_peer)

    def pair_up(self, c):
        self.core_copy(c).wait_recv()
        here = pl.ds(pl.multiple_of(self.core * self.half, self.half), self.half)
        self.x_out[c] = (
            self.terms[c, here].astype(WIDE) + self.core_in[c].astype(WIDE)
        ).astype(LOW)
        self.x_copy(c).start()

    def total(self, c, rows):
        return self.x_out[c, rows].astype(WIDE) + self.x_in[c, rows].astype(WIDE)


def gelu_and_slope(v):
    square = v * v
    t = jnp.tanh(0.7978845608 * (v + 0.044715 * v * square))
    half = 0.5 * (1.0 + t)
    slope = half + 0.5 * v * (1.0 - t * t) * (0.7978845608 * (1.0 + 0.134145 * square))
    return v * half, slope


def row_kernel(
    count,
    mixed_ref, inputs_ref, cot_ref, wo_ref, wu_ref, wd_ref, vec_ref,
    out_ref, one_ref, gmix_ref, gwo_ref, gwu_ref, gwd_ref, sums_ref,
    wo, wu, wd, hidden, active, slope, grad_two, grad_lift, grad_one,
    norm_one, inv_one, wide_two, tmp,
    terms1, cin1, xo1, xi1, terms2, cin2, xo2, xi2, terms3, cin3, xo3, xi3,
    go, gu, gd, yb_o, pr_o, zb_o, yb_u, pr_u, zb_u, yb_d, pr_d, zb_d, acc,
    own_sem, gz_s, gz_r, gy_s, gy_r, sy_s, sy_r, sz_s, sz_r, h1, h2, h3, share_s, share_r,
):
    s, h, z, y, x, core = place()
    core_peer, x_peer, y_peer, z_peers = partners(count)
    rows, width = inputs_ref.shape
    size = rows // CHUNKS
    half = size // 2
    step = 32
    gathers = [
        Gather(count, shard, full, own_sem.at[k], gz_s.at[k], gz_r.at[k], gy_s.at[k], gy_r.at[k])
        for k, (shard, full) in enumerate(((wo_ref, wo), (wu_ref, wu), (wd_ref, wd)))
    ]
    scatters = [
        Scatter(count, terms, yb, pr, zb, sy_s.at[k], sy_r.at[k], sz_s.at[k], sz_r.at[k])
        for k, (terms, yb, pr, zb) in enumerate(
            ((go, yb_o, pr_o, zb_o), (gu, yb_u, pr_u, zb_u), (gd, yb_d, pr_d, zb_d))
        )
    ]
    sums = [
        HeadSum(terms1, cin1, xo1, xi1, h1),
        HeadSum(terms2, cin2, xo2, xi2, h2),
        HeadSum(terms3, cin3, xo3, xi3, h3),
    ]
    greet([core_peer, x_peer, y_peer] + z_peers)
    for gather in gathers:
        gather.start()
    for gather in gathers:
        gather.forward()

    def chunk_rows(c):
        return pl.ds(pl.multiple_of(c * size, size), size)

    def my_rows(c):
        return pl.ds(pl.multiple_of(c * size + core * half, half), half)

    def share(k, ref, c):
        return remote(ref.at[my_rows(c)], ref.at[my_rows(c)], share_s.at[k, c], share_r.at[k, c], core_peer)

    def each(body):
        lax.fori_loop(0, CHUNKS, lambda c, carry: (body(c), carry)[1], 0)

    def pieces(body):
        lax.fori_loop(0, half // step, lambda i, carry: (body(pl.multiple_of(i * step, step)), carry)[1], 0)

    bias_out, bias_up, bias_down, gain_one, bias_one, gain_two, bias_two = (
        vec_ref[k : k + 1, :] for k in range(7)
    )
    acc[...] = jnp.zeros_like(acc)
    gathers[0].finish()

    def project_out(c):
        terms1[c] = against(mixed_ref[chunk_rows(c)], wo[...].reshape(width, wo.shape[2])).astype(LOW)
        sums[0].core_copy(c).start()

    each(project_out)
    each(sums[0].pair_up)
    gathers[1].finish()
    gathers[2].finish()

    def feed_forward(c):
        sums[0].x_copy(c).wait_recv()

        def norm(i):
            at = pl.ds(pl.multiple_of(c * size + core * half + i, step), step)
            kept = pl.ds(pl.multiple_of(c * half + i, step), step)
            pre = inputs_ref[at].astype(WIDE) + sums[0].total(c, pl.ds(i, step)) + bias_out
            normed, inv = normalize(pre)
            norm_one[kept] = normed
            inv_one[kept] = inv
            hidden[at] = (normed * gain_one + bias_one).astype(LOW)

        pieces(norm)
        share(0, hidden, c).start()
        share(0, hidden, c).wait_recv()
        at = chunk_rows(c)
        tmp[...] = matmul_low(hidden[at], wu[...].reshape(width, wu.shape[2]))

        def curve(i, carry):
            r = pl.ds(pl.multiple_of(i * step, step), step)
            to = pl.ds(pl.multiple_of(c * size + i * step, step), step)
            value, grade = gelu_and_slope(tmp[r] + bias_up)
            active[to] = value.astype(LOW)
            slope[to] = grade
            return carry

        lax.fori_loop(0, size // step, curve, 0)
        terms2[c] = against(active[at], wd[...].reshape(width, wd.shape[2])).astype(LOW)
        sums[1].core_copy(c).start()
        sums[1].pair_up(c)

    each(feed_forward)

    def feed_back(c):
        sums[1].x_copy(c).wait_recv()

        def norm(i):
            at = pl.ds(pl.multiple_of(c * size + core * half + i, step), step)
            kept = pl.ds(pl.multiple_of(c * half + i, step), step)
            pre = norm_one[kept] * gain_one + bias_one + sums[1].total(c, pl.ds(i, step)) + bias_down
            normed, inv = normalize(pre)
            out_ref[at] = (normed * gain_two + bias_two).astype(LOW)
            grad = cot_ref[at].astype(WIDE)
            back = norm_back(grad * gain_two, normed, inv)
            wide_two[kept] = back
            grad_two[at] = back.astype(LOW)
            acc[0] += fold(grad * normed)
            acc[1] += fold(grad)
            acc[2] += fold(back)

        pieces(norm)
        share(1, grad_two, c).start()
        share(2, out_ref, c).start()
        share(1, grad_two, c).wait_recv()
        at = chunk_rows(c)
        tmp[...] = matmul_low(grad_two[at], wd[...].reshape(width, wd.shape[2]))

        def curve(i, carry):
            r = pl.ds(pl.multiple_of(i * step, step), step)
            to = pl.ds(pl.multiple_of(c * size + i * step, step), step)
            value = tmp[r] * slope[to]
            grad_lift[to] = value.astype(LOW)
            acc[6] += fold(value)
            return carry

        lax.fori_loop(0, size // step, curve, 0)
        terms3[c] = against(grad_lift[at], wu[...].reshape(width, wu.shape[2])).astype(LOW)
        sums[2].core_copy(c).start()
        sums[2].pair_up(c)

    each(feed_back)

    def grads_of(left, right, ref):
        ref[...] = across(left, right).astype(LOW).reshape(ref.shape)

    grads_of(grad_two[...], active[...], gd)
    scatters[2].start()
    grads_of(hidden[...], grad_lift[...], gu)
    scatters[1].start()

    def mix_back(c):
        sums[2].x_copy(c).wait_recv()

        def norm(i):
            at = pl.ds(pl.multiple_of(c * size + core * half + i, step), step)
            kept = pl.ds(pl.multiple_of(c * half + i, step), step)
            normed = norm_one[kept]
            grad = wide_two[kept] + sums[2].total(c, pl.ds(i, step))
            back = norm_back(grad * gain_one, normed, inv_one[kept])
            one_ref[kept] = back
            grad_one[at] = back.astype(LOW)
            acc[3] += fold(grad * normed)
            acc[4] += fold(grad)
            acc[5] += fold(back)

        pieces(norm)
        share(3, grad_one, c).start()
        share(3, grad_one, c).wait_recv()
        at = chunk_rows(c)
        gmix_ref[at] = matmul_low(grad_one[at], wo[...].reshape(width, wo.shape[2])).astype(LOW)

    each(mix_back)
    scatters[2].forward()
    scatters[1].forward()
    grads_of(grad_one[...], mixed_ref[...], go)
    scatters[0].start()
    for k in range(7):
        sums_ref[k : k + 1, :] = jnp.sum(acc[k], axis=0, keepdims=True)
    sums_ref[7:8, :] = jnp.zeros_like(sums_ref[7:8, :])
    scatters[0].forward()
    for scatter, ref in zip(scatters, (gwo_ref, gwu_ref, gwd_ref)):
        scatter.finish(ref)

    def settle(c):
        for head_sum in sums:
            head_sum.core_copy(c).wait_send()
            head_sum.x_copy(c).wait_send()
        share(2, out_ref, c).wait_recv()
        for k, ref in enumerate((hidden, grad_two, out_ref, grad_one)):
            share(k, ref, c).wait_send()

    each(settle)
    for group in gathers + scatters:
        group.close()


def rows_forward_and_back(count, mixed, inputs, cot, w_out, w_up, w_down, vectors):
    rows, width = inputs.shape
    feed = w_up.shape[1]
    near = mixed.shape[1]
    size = rows // CHUNKS
    half = size // 2
    part = width // count
    lines = count // 2
    low, wide = (lambda *shape: pltpu.VMEM(shape, LOW)), (lambda *shape: pltpu.VMEM(shape, WIDE))
    sem = lambda *shape: pltpu.SemaphoreType.DMA(shape)
    head_sum = [low(CHUNKS, size, width)] + [low(CHUNKS, half, width)] * 3
    scatter = lambda n: [low(lines, part, n), low(lines - 1, part, n), low(lines - 1, part, n)]
    vmem = pl.BlockSpec(memory_space=pltpu.VMEM)
    shape = jax.ShapeDtypeStruct
    return pl.pallas_call(
        functools.partial(row_kernel, count),
        out_shape=(
            shape((rows, width), LOW),
            shape((rows // 2, width), WIDE),
            shape((rows, near), LOW),
            shape((part, near), WIDE),
            shape((part, feed), WIDE),
            shape((part, feed), WIDE),
            shape((8, width), WIDE),
        ),
        in_specs=[vmem] * 7,
        out_specs=[vmem] * 7,
        scratch_shapes=[
            low(count, part, near), low(count, part, feed), low(count, part, feed),
            low(rows, width), low(rows, feed), wide(rows, feed), low(rows, width), low(rows, feed), low(rows, width),
            wide(rows // 2, width), wide(rows // 2, 1), wide(rows // 2, width), wide(size, feed),
            *head_sum, *head_sum, *head_sum,
            low(count, part, near), low(count, part, feed), low(count, part, feed),
            *scatter(near), *scatter(feed), *scatter(feed),
            wide(7, 8, width),
            sem(3), sem(3, lines - 1), sem(3, lines - 1), sem(3, lines), sem(3, lines),
            sem(3, lines), sem(3, lines), sem(3, lines - 1), sem(3, lines - 1),
            sem(4, CHUNKS), sem(4, CHUNKS), sem(4, CHUNKS), sem(4, CHUNKS), sem(4, CHUNKS),
        ],
        compiler_params=pltpu.CompilerParams(
            collective_id=1, has_side_effects=True, vmem_limit_bytes=60 * 2**20
        ),
    )(mixed, inputs, cot, w_out, w_up, w_down, vectors)


def plain_body(
    inputs,
    cotangent,
    item_lengths,
    w_query,
    w_key,
    w_value,
    w_out,
    w_up,
    w_down,
    bias_query,
    bias_value,
    bias_out,
    bias_up,
    bias_down,
    gain_one,
    bias_one,
    gain_two,
    bias_two,
    conv_taps,
):
    low_type = jnp.bfloat16
    tok_rows = inputs.shape[0]
    heads_here = conv_taps.shape[0]
    width_here = heads_here * HEAD_DIM
    slots = ITEMS * LAND
    reach = (KERNEL - 1) // 2
    score_scale = HEAD_DIM ** (-0.5)
    pref = jnp.float32
    first_row = lax.axis_index("seq") * tok_rows
    positions = first_row + jnp.arange(tok_rows, dtype=jnp.int32)
    item_id, land_slot = locate(item_lengths, positions)
    rim_item = locate(
        item_lengths, first_row - reach + jnp.arange(tok_rows + 2 * reach, dtype=jnp.int32)
    )[0]
    slot_item = jnp.arange(slots, dtype=jnp.int32) // LAND
    member = land_slot[:, None] == jnp.arange(slots, dtype=jnp.int32)[None, :]
    member_low = member.astype(low_type)
    counts = jnp.repeat((item_lengths // LAND).astype(jnp.float32), LAND)
    same_f = item_id[:, None] == slot_item[None, :]
    same_b = same_f.T
    tap_cols = jnp.repeat(conv_taps, HEAD_DIM, axis=0)
    full_query, full_key, full_value, full_out, full_up, full_down = (
        lax.all_gather(w_query, "seq", axis=0, tiled=True),
        lax.all_gather(w_key, "seq", axis=0, tiled=True),
        lax.all_gather(w_value, "seq", axis=0, tiled=True),
        lax.all_gather(w_out, "seq", axis=0, tiled=True),
        lax.all_gather(w_up, "seq", axis=0, tiled=True),
        lax.all_gather(w_down, "seq", axis=0, tiled=True),
    )
    queries = (matmul_low(inputs, full_query) + bias_query).astype(low_type)
    key_rows = matmul_low(inputs, full_key).astype(low_type)
    value_rows = (matmul_low(inputs, full_value) + bias_value).astype(low_type)
    query_sums, key_sums = lax.psum(
        (across(member_low, queries), across(member_low, key_rows)), "seq"
    )
    query_land = (
        (query_sums / counts[:, None]).astype(low_type).reshape(slots, heads_here, HEAD_DIM)
    )
    key_land = (key_sums / counts[:, None]).astype(low_type).reshape(slots, heads_here, HEAD_DIM)
    query_heads = queries.reshape(tok_rows, heads_here, HEAD_DIM)
    key_heads = key_rows.reshape(tok_rows, heads_here, HEAD_DIM)
    value_heads = value_rows.reshape(tok_rows, heads_here, HEAD_DIM)
    scores_b = (
        jnp.einsum("lhd,thd->hlt", query_land, key_heads, preferred_element_type=pref) * score_scale
    )
    scores_b = jnp.where(same_b[None], scores_b, MASKED)
    maxima_b = lax.pmax(jnp.max(scores_b, axis=2), "seq")
    weights_b = jnp.exp(scores_b - maxima_b[:, :, None])
    weights_b_low = weights_b.astype(low_type)
    numer_sum, totals_b = lax.psum(
        (
            jnp.einsum("hlt,thd->lhd", weights_b_low, value_heads, preferred_element_type=pref),
            jnp.sum(weights_b, axis=2),
        ),
        "seq",
    )
    totals_cols = totals_b.T[:, :, None]
    kernel_v = numer_sum / totals_cols
    land_q = query_land.reshape(ITEMS, LAND, heads_here, HEAD_DIM)
    land_k = key_land.reshape(ITEMS, LAND, heads_here, HEAD_DIM)
    land_kernel = jax.nn.softmax(
        jnp.einsum("ilhd,imhd->ihlm", land_q, land_k, preferred_element_type=pref) * score_scale,
        axis=-1,
    )
    inverse, inverse_back = jax.vjp(pseudo_inverse, land_kernel)
    kernel_items = kernel_v.reshape(ITEMS, LAND, heads_here, HEAD_DIM)
    mixing = jnp.einsum("ihlm,imhd->ilhd", inverse, kernel_items, precision=PRECISE)
    mixing = mixing.astype(low_type).reshape(slots, heads_here, HEAD_DIM)
    scores_f = (
        jnp.einsum("thd,lhd->htl", query_heads, key_land, preferred_element_type=pref) * score_scale
    )
    weights_f = jax.nn.softmax(jnp.where(same_f[None], scores_f, MASKED), axis=-1)
    weights_f_low = weights_f.astype(low_type)
    attended = jnp.einsum("htl,lhd->thd", weights_f_low, mixing, preferred_element_type=pref)
    attended = attended.reshape(tok_rows, width_here)
    value_rim = extended(value_rows, (("seq", 0),), reach)
    conv_sum = jnp.zeros((tok_rows, width_here), jnp.float32)
    for offset in range(KERNEL):
        in_item = (rim_item[offset : offset + tok_rows] == item_id)[:, None]
        conv_sum = conv_sum + jnp.where(
            in_item,
            value_rim[offset : offset + tok_rows].astype(jnp.float32)
            * tap_cols[:, offset][None, :],
            0.0,
        )
    mixed_rows = (attended + conv_sum).astype(low_type)
    attention_sum = lax.psum(against(mixed_rows, full_out).astype(jnp.bfloat16), "head").astype(
        jnp.float32
    )
    pre_one = inputs.astype(jnp.float32) + attention_sum + bias_out
    norm_one, inv_one = normalize(pre_one)
    hidden = norm_one * gain_one + bias_one
    hidden_low = hidden.astype(low_type)
    lifted = matmul_low(hidden_low, full_up) + bias_up
    active, gelu_back = jax.vjp(gelu_tanh, lifted)
    active_low = active.astype(low_type)
    feed_terms = against(active_low, full_down)
    feed_sum = lax.psum(feed_terms.astype(jnp.bfloat16), "head").astype(jnp.float32)
    grad_output = cotangent.astype(jnp.float32)
    pre_two = hidden + feed_sum + bias_down
    norm_two, inv_two = normalize(pre_two)
    out_rows = (norm_two * gain_two + bias_two).astype(low_type)
    grad_gain_two = jnp.sum(grad_output * norm_two, axis=0)
    grad_bias_two = jnp.sum(grad_output, axis=0)
    grad_two = norm_back(grad_output * gain_two, norm_two, inv_two)
    grad_bias_down = jnp.sum(grad_two, axis=0)
    grad_two_low = grad_two.astype(low_type)
    output, grad_two_full = (out_rows, grad_two_low)
    grad_down = across(grad_two_full, active_low)
    (grad_lift,) = gelu_back(matmul_low(grad_two_full, full_down))
    grad_bias_up = jnp.sum(grad_lift, axis=0)
    grad_lift_low = grad_lift.astype(low_type)
    grad_up = across(hidden_low, grad_lift_low)
    up_terms = against(grad_lift_low, full_up)
    grad_hidden = grad_two + lax.psum(up_terms.astype(jnp.bfloat16), "head").astype(jnp.float32)
    grad_gain_one = jnp.sum(grad_hidden * norm_one, axis=0)
    grad_bias_one = jnp.sum(grad_hidden, axis=0)
    grad_one = norm_back(grad_hidden * gain_one, norm_one, inv_one)
    grad_bias_out = jnp.sum(grad_one, axis=0)
    grad_one_low = grad_one.astype(low_type)
    grad_outw = across(grad_one_low, mixed_rows)
    grad_mixed = matmul_low(grad_one_low, full_out).astype(low_type)
    grad_mixed_wide = grad_mixed.astype(jnp.float32)
    grad_heads = grad_mixed.reshape(tok_rows, heads_here, HEAD_DIM)
    grad_rim = extended(grad_mixed, (("seq", 0),), reach)
    grad_conv_v = jnp.zeros((tok_rows, width_here), jnp.float32)
    tap_terms = []
    for offset in range(KERNEL):
        in_item = (rim_item[offset : offset + tok_rows] == item_id)[:, None]
        neighbour = jnp.where(
            in_item, value_rim[offset : offset + tok_rows].astype(jnp.float32), 0.0
        )
        tap_terms.append(
            jnp.sum(
                (grad_mixed_wide * neighbour).reshape(tok_rows, heads_here, HEAD_DIM), axis=(0, 2)
            )
        )
        mirror = 2 * reach - offset
        mirror_item = (rim_item[mirror : mirror + tok_rows] == item_id)[:, None]
        grad_conv_v = grad_conv_v + jnp.where(
            mirror_item,
            grad_rim[mirror : mirror + tok_rows].astype(jnp.float32) * tap_cols[:, offset][None, :],
            0.0,
        )
    grad_taps = jnp.stack(tap_terms, axis=1)
    grad_weights_f = jnp.einsum("thd,lhd->htl", grad_heads, mixing, preferred_element_type=pref)
    grad_mix_part = jnp.einsum(
        "htl,thd->lhd", weights_f_low, grad_heads, preferred_element_type=pref
    )
    grad_scores_f = weights_f * (
        grad_weights_f - jnp.sum(weights_f * grad_weights_f, axis=2, keepdims=True)
    )
    grad_scores_f = grad_scores_f.astype(low_type)
    grad_query_f = (
        jnp.einsum("htl,lhd->thd", grad_scores_f, key_land, preferred_element_type=pref)
        * score_scale
    )
    grad_kland_part = (
        jnp.einsum("htl,thd->lhd", grad_scores_f, query_heads, preferred_element_type=pref)
        * score_scale
    )
    grad_mixing, grad_kland_f = lax.psum((grad_mix_part, grad_kland_part), "seq")
    grad_mix_items = grad_mixing.reshape(ITEMS, LAND, heads_here, HEAD_DIM)
    grad_inverse = jnp.einsum("ilhd,imhd->ihlm", grad_mix_items, kernel_items, precision=PRECISE)
    grad_kernel_v = jnp.einsum("ihlm,ilhd->imhd", inverse, grad_mix_items, precision=PRECISE)
    grad_kernel_v = grad_kernel_v.reshape(slots, heads_here, HEAD_DIM)
    (grad_land_kernel,) = inverse_back(grad_inverse)
    grad_scores_a = land_kernel * (
        grad_land_kernel - jnp.sum(land_kernel * grad_land_kernel, axis=-1, keepdims=True)
    )
    grad_scores_a = grad_scores_a * score_scale
    grad_qland_a = jnp.einsum(
        "ihlm,imhd->ilhd", grad_scores_a, land_k.astype(jnp.float32), precision=PRECISE
    )
    grad_kland_a = jnp.einsum(
        "ihlm,ilhd->imhd", grad_scores_a, land_q.astype(jnp.float32), precision=PRECISE
    )
    grad_numer = (grad_kernel_v / totals_cols).astype(low_type)
    grad_totals = -jnp.sum(grad_kernel_v * kernel_v, axis=2) / totals_b.T
    grad_weights_b = jnp.einsum(
        "lhd,thd->hlt", grad_numer, value_heads, preferred_element_type=pref
    )
    grad_weights_b = grad_weights_b + grad_totals.T[:, :, None]
    grad_scores_b = (weights_b * grad_weights_b).astype(low_type)
    grad_qland_part = (
        jnp.einsum("hlt,thd->lhd", grad_scores_b, key_heads, preferred_element_type=pref)
        * score_scale
    )
    grad_key_b = (
        jnp.einsum("hlt,lhd->thd", grad_scores_b, query_land, preferred_element_type=pref)
        * score_scale
    )
    grad_value_b = jnp.einsum(
        "hlt,lhd->thd", weights_b_low, grad_numer, preferred_element_type=pref
    )
    grad_query_rows = grad_query_f.reshape(tok_rows, width_here)
    grad_values = grad_value_b.reshape(tok_rows, width_here) + grad_conv_v
    (
        grad_qland_b,
        grad_gain_one,
        grad_bias_one,
        grad_gain_two,
        grad_bias_two,
        grad_bias_out,
        grad_bias_down,
        grad_bias_up,
        grad_taps,
        query_f_total,
        grad_bias_value,
    ) = lax.psum(
        (
            grad_qland_part,
            grad_gain_one,
            grad_bias_one,
            grad_gain_two,
            grad_bias_two,
            grad_bias_out,
            grad_bias_down,
            grad_bias_up,
            grad_taps,
            jnp.sum(grad_query_rows, axis=0),
            jnp.sum(grad_values, axis=0),
        ),
        "seq",
    )
    grad_qland = grad_qland_a.reshape(slots, width_here) + grad_qland_b.reshape(slots, width_here)
    grad_kland = grad_kland_a.reshape(slots, width_here) + grad_kland_f.reshape(slots, width_here)
    member_wide = member.astype(jnp.float32)
    grad_queries = grad_query_rows + jnp.dot(
        member_wide, grad_qland / counts[:, None], precision=PRECISE
    )
    grad_keys = grad_key_b.reshape(tok_rows, width_here) + jnp.dot(
        member_wide, grad_kland / counts[:, None], precision=PRECISE
    )
    grad_bias_query = query_f_total + jnp.sum(grad_qland, axis=0)
    queries_low = grad_queries.astype(low_type)
    keys_low = grad_keys.astype(low_type)
    values_low = grad_values.astype(low_type)
    grad_queryw = across(inputs, queries_low)
    grad_keyw = across(inputs, keys_low)
    grad_valuew = across(inputs, values_low)
    input_terms = (
        against(queries_low, full_query)
        + against(keys_low, full_key)
        + against(values_low, full_value)
    )
    grad_inputs = (
        grad_one + lax.psum(input_terms.astype(jnp.bfloat16), "head").astype(jnp.float32)
    ).astype(low_type)
    query_shard, key_shard, value_shard, out_shard, grad_up_shard, grad_down_shard = side_by_side(
        (
            grad_queryw.astype(jnp.bfloat16),
            grad_keyw.astype(jnp.bfloat16),
            grad_valuew.astype(jnp.bfloat16),
            grad_outw.astype(jnp.bfloat16),
            grad_up.astype(jnp.bfloat16),
            grad_down.astype(jnp.bfloat16),
        ),
        "seq",
        0,
        1,
    )
    return (
        output,
        grad_inputs,
        query_shard,
        key_shard,
        value_shard,
        out_shard,
        grad_up_shard,
        grad_down_shard,
        grad_bias_query,
        grad_bias_value,
        grad_bias_out,
        grad_bias_up,
        grad_bias_down,
        grad_gain_one,
        grad_bias_one,
        grad_gain_two,
        grad_bias_two,
        grad_taps,
    )


def fused_body(
    inputs,
    cotangent,
    item_lengths,
    w_query,
    w_key,
    w_value,
    w_out,
    w_up,
    w_down,
    bias_query,
    bias_value,
    bias_out,
    bias_up,
    bias_down,
    gain_one,
    bias_one,
    gain_two,
    bias_two,
    conv_taps,
):
    low_type = jnp.bfloat16
    tok_rows = inputs.shape[0]
    heads_here = conv_taps.shape[0]
    width_here = heads_here * HEAD_DIM
    slots = ITEMS * LAND
    reach = (KERNEL - 1) // 2
    score_scale = HEAD_DIM ** (-0.5)
    pref = jnp.float32
    first_row = lax.axis_index("seq") * tok_rows
    positions = first_row + jnp.arange(tok_rows, dtype=jnp.int32)
    item_id, land_slot = locate(item_lengths, positions)
    rim_item = locate(
        item_lengths, first_row - reach + jnp.arange(tok_rows + 2 * reach, dtype=jnp.int32)
    )[0]
    slot_item = jnp.arange(slots, dtype=jnp.int32) // LAND
    member = land_slot[:, None] == jnp.arange(slots, dtype=jnp.int32)[None, :]
    member_low = member.astype(low_type)
    counts = jnp.repeat((item_lengths // LAND).astype(jnp.float32), LAND)
    same_f = item_id[:, None] == slot_item[None, :]
    same_b = same_f.T
    tap_cols = jnp.repeat(conv_taps, HEAD_DIM, axis=0)
    full_query, full_key, full_value = (
        lax.all_gather(w_query, "seq", axis=0, tiled=True),
        lax.all_gather(w_key, "seq", axis=0, tiled=True),
        lax.all_gather(w_value, "seq", axis=0, tiled=True),
    )
    queries = (matmul_low(inputs, full_query) + bias_query).astype(low_type)
    key_rows = matmul_low(inputs, full_key).astype(low_type)
    value_rows = (matmul_low(inputs, full_value) + bias_value).astype(low_type)
    query_sums, key_sums = lax.psum(
        (across(member_low, queries), across(member_low, key_rows)), "seq"
    )
    query_land = (
        (query_sums / counts[:, None]).astype(low_type).reshape(slots, heads_here, HEAD_DIM)
    )
    key_land = (key_sums / counts[:, None]).astype(low_type).reshape(slots, heads_here, HEAD_DIM)
    query_heads = queries.reshape(tok_rows, heads_here, HEAD_DIM)
    key_heads = key_rows.reshape(tok_rows, heads_here, HEAD_DIM)
    value_heads = value_rows.reshape(tok_rows, heads_here, HEAD_DIM)
    scores_b = (
        jnp.einsum("lhd,thd->hlt", query_land, key_heads, preferred_element_type=pref) * score_scale
    )
    scores_b = jnp.where(same_b[None], scores_b, MASKED)
    maxima_b = lax.pmax(jnp.max(scores_b, axis=2), "seq")
    weights_b = jnp.exp(scores_b - maxima_b[:, :, None])
    weights_b_low = weights_b.astype(low_type)
    numer_sum, totals_b = lax.psum(
        (
            jnp.einsum("hlt,thd->lhd", weights_b_low, value_heads, preferred_element_type=pref),
            jnp.sum(weights_b, axis=2),
        ),
        "seq",
    )
    totals_cols = totals_b.T[:, :, None]
    kernel_v = numer_sum / totals_cols
    land_q = query_land.reshape(ITEMS, LAND, heads_here, HEAD_DIM)
    land_k = key_land.reshape(ITEMS, LAND, heads_here, HEAD_DIM)
    land_kernel = jax.nn.softmax(
        jnp.einsum("ilhd,imhd->ihlm", land_q, land_k, preferred_element_type=pref) * score_scale,
        axis=-1,
    )
    inverse, inverse_back = jax.vjp(pseudo_inverse, land_kernel)
    kernel_items = kernel_v.reshape(ITEMS, LAND, heads_here, HEAD_DIM)
    mixing = jnp.einsum("ihlm,imhd->ilhd", inverse, kernel_items, precision=PRECISE)
    mixing = mixing.astype(low_type).reshape(slots, heads_here, HEAD_DIM)
    scores_f = (
        jnp.einsum("thd,lhd->htl", query_heads, key_land, preferred_element_type=pref) * score_scale
    )
    weights_f = jax.nn.softmax(jnp.where(same_f[None], scores_f, MASKED), axis=-1)
    weights_f_low = weights_f.astype(low_type)
    attended = jnp.einsum("htl,lhd->thd", weights_f_low, mixing, preferred_element_type=pref)
    attended = attended.reshape(tok_rows, width_here)
    value_rim = extended(value_rows, (("seq", 0),), reach)
    conv_sum = jnp.zeros((tok_rows, width_here), jnp.float32)
    for offset in range(KERNEL):
        in_item = (rim_item[offset : offset + tok_rows] == item_id)[:, None]
        conv_sum = conv_sum + jnp.where(
            in_item,
            value_rim[offset : offset + tok_rows].astype(jnp.float32)
            * tap_cols[:, offset][None, :],
            0.0,
        )
    mixed_rows = (attended + conv_sum).astype(low_type)
    vectors = jnp.stack(
        [bias_out, bias_up, bias_down, gain_one, bias_one, gain_two, bias_two, bias_two]
    )
    output, grad_one_half, grad_mixed, out_shard, grad_up_shard, grad_down_shard, row_sums = (
        rows_forward_and_back(
            lax.axis_size("seq"), mixed_rows, inputs, cotangent, w_out, w_up, w_down, vectors
        )
    )
    chip_sums = lax.psum(row_sums[:6], ("seq", "head")) * 0.5
    (
        grad_gain_two,
        grad_bias_two,
        grad_bias_down,
        grad_gain_one,
        grad_bias_one,
        grad_bias_out,
    ) = (chip_sums[k] for k in range(6))
    grad_bias_up = row_sums[6]
    grad_mixed_wide = grad_mixed.astype(jnp.float32)
    grad_heads = grad_mixed.reshape(tok_rows, heads_here, HEAD_DIM)
    grad_rim = extended(grad_mixed, (("seq", 0),), reach)
    grad_conv_v = jnp.zeros((tok_rows, width_here), jnp.float32)
    tap_terms = []
    for offset in range(KERNEL):
        in_item = (rim_item[offset : offset + tok_rows] == item_id)[:, None]
        neighbour = jnp.where(
            in_item, value_rim[offset : offset + tok_rows].astype(jnp.float32), 0.0
        )
        tap_terms.append(
            jnp.sum(
                (grad_mixed_wide * neighbour).reshape(tok_rows, heads_here, HEAD_DIM), axis=(0, 2)
            )
        )
        mirror = 2 * reach - offset
        mirror_item = (rim_item[mirror : mirror + tok_rows] == item_id)[:, None]
        grad_conv_v = grad_conv_v + jnp.where(
            mirror_item,
            grad_rim[mirror : mirror + tok_rows].astype(jnp.float32) * tap_cols[:, offset][None, :],
            0.0,
        )
    grad_taps = jnp.stack(tap_terms, axis=1)
    grad_weights_f = jnp.einsum("thd,lhd->htl", grad_heads, mixing, preferred_element_type=pref)
    grad_mix_part = jnp.einsum(
        "htl,thd->lhd", weights_f_low, grad_heads, preferred_element_type=pref
    )
    grad_scores_f = weights_f * (
        grad_weights_f - jnp.sum(weights_f * grad_weights_f, axis=2, keepdims=True)
    )
    grad_scores_f = grad_scores_f.astype(low_type)
    grad_query_f = (
        jnp.einsum("htl,lhd->thd", grad_scores_f, key_land, preferred_element_type=pref)
        * score_scale
    )
    grad_kland_part = (
        jnp.einsum("htl,thd->lhd", grad_scores_f, query_heads, preferred_element_type=pref)
        * score_scale
    )
    grad_mixing, grad_kland_f = lax.psum((grad_mix_part, grad_kland_part), "seq")
    grad_mix_items = grad_mixing.reshape(ITEMS, LAND, heads_here, HEAD_DIM)
    grad_inverse = jnp.einsum("ilhd,imhd->ihlm", grad_mix_items, kernel_items, precision=PRECISE)
    grad_kernel_v = jnp.einsum("ihlm,ilhd->imhd", inverse, grad_mix_items, precision=PRECISE)
    grad_kernel_v = grad_kernel_v.reshape(slots, heads_here, HEAD_DIM)
    (grad_land_kernel,) = inverse_back(grad_inverse)
    grad_scores_a = land_kernel * (
        grad_land_kernel - jnp.sum(land_kernel * grad_land_kernel, axis=-1, keepdims=True)
    )
    grad_scores_a = grad_scores_a * score_scale
    grad_qland_a = jnp.einsum(
        "ihlm,imhd->ilhd", grad_scores_a, land_k.astype(jnp.float32), precision=PRECISE
    )
    grad_kland_a = jnp.einsum(
        "ihlm,ilhd->imhd", grad_scores_a, land_q.astype(jnp.float32), precision=PRECISE
    )
    grad_numer = (grad_kernel_v / totals_cols).astype(low_type)
    grad_totals = -jnp.sum(grad_kernel_v * kernel_v, axis=2) / totals_b.T
    grad_weights_b = jnp.einsum(
        "lhd,thd->hlt", grad_numer, value_heads, preferred_element_type=pref
    )
    grad_weights_b = grad_weights_b + grad_totals.T[:, :, None]
    grad_scores_b = (weights_b * grad_weights_b).astype(low_type)
    grad_qland_part = (
        jnp.einsum("hlt,thd->lhd", grad_scores_b, key_heads, preferred_element_type=pref)
        * score_scale
    )
    grad_key_b = (
        jnp.einsum("hlt,lhd->thd", grad_scores_b, query_land, preferred_element_type=pref)
        * score_scale
    )
    grad_value_b = jnp.einsum(
        "hlt,lhd->thd", weights_b_low, grad_numer, preferred_element_type=pref
    )
    grad_query_rows = grad_query_f.reshape(tok_rows, width_here)
    grad_values = grad_value_b.reshape(tok_rows, width_here) + grad_conv_v
    (grad_qland_b, grad_bias_up, grad_taps, query_f_total, grad_bias_value) = lax.psum(
        (
            grad_qland_part,
            grad_bias_up,
            grad_taps,
            jnp.sum(grad_query_rows, axis=0),
            jnp.sum(grad_values, axis=0),
        ),
        "seq",
    )
    grad_qland = grad_qland_a.reshape(slots, width_here) + grad_qland_b.reshape(slots, width_here)
    grad_kland = grad_kland_a.reshape(slots, width_here) + grad_kland_f.reshape(slots, width_here)
    member_wide = member.astype(jnp.float32)
    grad_queries = grad_query_rows + jnp.dot(
        member_wide, grad_qland / counts[:, None], precision=PRECISE
    )
    grad_keys = grad_key_b.reshape(tok_rows, width_here) + jnp.dot(
        member_wide, grad_kland / counts[:, None], precision=PRECISE
    )
    grad_bias_query = query_f_total + jnp.sum(grad_qland, axis=0)
    queries_low = grad_queries.astype(low_type)
    keys_low = grad_keys.astype(low_type)
    values_low = grad_values.astype(low_type)
    grad_queryw = across(inputs, queries_low)
    grad_keyw = across(inputs, keys_low)
    grad_valuew = across(inputs, values_low)
    input_terms = (
        against(queries_low, full_query)
        + against(keys_low, full_key)
        + against(values_low, full_value)
    )
    core = lax.rem(lax.axis_index("head"), 2)
    halves = lax.psum(input_terms.astype(jnp.bfloat16), "head").astype(jnp.float32)
    size = tok_rows // CHUNKS
    halves = halves.reshape(CHUNKS, 2, size // 2, -1)
    grad_one_half = grad_one_half.reshape(CHUNKS, size // 2, -1)
    mine = (
        grad_one_half + lax.dynamic_index_in_dim(halves, core, axis=1, keepdims=False)
    ).astype(low_type)
    other = lax.ppermute(mine, "head", [(0, 1), (1, 0), (2, 3), (3, 2)])
    grad_inputs = jnp.where(
        core == 0, jnp.stack([mine, other], axis=1), jnp.stack([other, mine], axis=1)
    ).reshape(tok_rows, -1)
    query_shard, key_shard, value_shard = side_by_side(
        (
            grad_queryw.astype(jnp.bfloat16),
            grad_keyw.astype(jnp.bfloat16),
            grad_valuew.astype(jnp.bfloat16),
        ),
        "seq",
        0,
        1,
    )
    return (
        output,
        grad_inputs,
        query_shard,
        key_shard,
        value_shard,
        out_shard,
        grad_up_shard,
        grad_down_shard,
        grad_bias_query,
        grad_bias_value,
        grad_bias_out,
        grad_bias_up,
        grad_bias_down,
        grad_gain_one,
        grad_bias_one,
        grad_gain_two,
        grad_bias_two,
        grad_taps,
    )


def solution(mesh):
    part = 768 // mesh.shape["seq"]
    body = fused_body if part % 16 == 0 else plain_body
    return jax.shard_map(
        body,
        mesh=mesh,
        in_specs=(
            P("seq", None),
            P("seq", None),
            P(),
            P("seq", "head"),
            P("seq", "head"),
            P("seq", "head"),
            P("seq", "head"),
            P("seq", "head"),
            P("seq", "head"),
            P("head"),
            P("head"),
            P(),
            P("head"),
            P(),
            P(),
            P(),
            P(),
            P(),
            P("head", None),
        ),
        out_specs=(
            P("seq", None),
            P("seq", None),
            P("seq", "head"),
            P("seq", "head"),
            P("seq", "head"),
            P("seq", "head"),
            P("seq", "head"),
            P("seq", "head"),
            P("head"),
            P("head"),
            P(),
            P("head"),
            P(),
            P(),
            P(),
            P(),
            P(),
            P("head", None),
        ),
        check_vma=False,
    )
```

```python
import functools
import types

import jax
import jax.numpy as jnp
from jax import lax
from jax.experimental import pallas as pl
from jax.experimental.pallas import tpu as pltpu
from jax.sharding import PartitionSpec as P

HEAD_DIM = 64
LAND = 64
KERNEL = 33
PINV_STEPS = 6
ITEMS = 3


PRECISE = lax.Precision.HIGHEST
EPSILON = 1e-05
MASKED = -1e30


def extended(cells, sides, width):
    for axis, dim in sides:
        count = lax.axis_size(axis)
        ends = count - 1
        head = lax.slice_in_dim(cells, 0, width, axis=dim)
        tail = lax.slice_in_dim(cells, cells.shape[dim] - width, cells.shape[dim], axis=dim)
        cells = jnp.concatenate(
            [
                lax.ppermute(tail, axis, [(i, (i + 1) % count) for i in range(ends)]),
                cells,
                lax.ppermute(head, axis, [((i + 1) % count, i) for i in range(ends)]),
            ],
            axis=dim,
        )
    return cells


def cut_along(array, dim, length):
    lengths = array.shape
    parts = array.reshape(*lengths[:dim], length, lengths[dim] // length, *lengths[dim + 1 :])
    return jnp.moveaxis(parts, dim, 0)


def sent_and_summed(array, axis, dim):
    parts = cut_along(array, dim, lax.axis_size(axis))
    arrived = lax.all_to_all(parts, axis, split_axis=0, concat_axis=0, tiled=True)
    return arrived.astype(jnp.float32).sum(axis=0)


def side_by_side(arrays, axis, dim, along):
    both = jnp.concatenate(arrays, axis=along)
    out, at, outs = (sent_and_summed(both, axis, dim), 0, [])
    for a in arrays:
        outs.append(lax.slice_in_dim(out, at, at + a.shape[along], axis=along))
        at += a.shape[along]
    return tuple(outs)


def locate(item_lengths, positions):
    item_ends = jnp.cumsum(item_lengths)
    item_starts = item_ends - item_lengths
    located = jnp.sum((positions[:, None] >= item_ends[None, :]).astype(jnp.int32), axis=1)
    inside = (positions >= 0) & (located < ITEMS)
    picked = jnp.minimum(located, ITEMS - 1)
    onehot = (picked[:, None] == jnp.arange(ITEMS, dtype=jnp.int32)[None, :]).astype(jnp.int32)
    item_start = jnp.sum(onehot * item_starts[None, :], axis=1)
    length = jnp.sum(onehot * item_lengths[None, :], axis=1)
    segment = (positions - item_start) * LAND // length
    land_slot = picked * LAND + jnp.clip(segment, 0, LAND - 1)
    return (jnp.where(inside, picked, -1), land_slot)


def normalize(values):
    row_mean = jnp.mean(values, axis=-1, keepdims=True)
    centered = values - row_mean
    variance = jnp.mean(centered * centered, axis=-1, keepdims=True)
    inv_std = lax.rsqrt(variance + EPSILON)
    return (centered * inv_std, inv_std)


def norm_back(grad_norm, normed, inv_std):
    return inv_std * (
        grad_norm
        - jnp.mean(grad_norm, axis=-1, keepdims=True)
        - normed * jnp.mean(grad_norm * normed, axis=-1, keepdims=True)
    )


def pseudo_inverse(land_kernel):
    identity = jnp.eye(LAND, dtype=jnp.float32)
    frobenius = jnp.sum(land_kernel * land_kernel, axis=(-2, -1), keepdims=True)
    result = jnp.swapaxes(land_kernel, -1, -2) / frobenius
    for iteration in range(PINV_STEPS):
        product = jnp.matmul(land_kernel, result, precision=PRECISE)
        nested = 7.0 * identity - product
        nested = 15.0 * identity - jnp.matmul(product, nested, precision=PRECISE)
        nested = 13.0 * identity - jnp.matmul(product, nested, precision=PRECISE)
        result = 0.25 * jnp.matmul(result, nested, precision=PRECISE)
    return result


def gelu_tanh(values):
    return jax.nn.gelu(values, approximate=True)


def matmul_low(left, right):
    return jnp.dot(left, right, preferred_element_type=jnp.float32)


def against(left, right):
    return lax.dot_general(
        left, right, (((1,), (1,)), ((), ())), preferred_element_type=jnp.float32
    )


def across(left, right):
    return lax.dot_general(
        left, right, (((0,), (0,)), ((), ())), preferred_element_type=jnp.float32
    )


MESH = pl.DeviceIdType.MESH
WIDE = jnp.float32
LOW = jnp.bfloat16
CHUNKS = 4
PAD = 256
REACH = (KERNEL - 1) // 2
BLOCK = 64
SPAN = BLOCK + 2 * REACH
BORDER = 16


def place():
    s, h = lax.axis_index("seq"), lax.axis_index("head")
    return s, h, s // 2, lax.rem(s, 2), h // 2, lax.rem(h, 2)


def core_of_chip():
    s, _, _, _, x, core = place()
    return (s, 2 * x + 1 - core)


def x_neighbour():
    s, _, _, _, x, core = place()
    return (s, 2 * (1 - x) + core)


def y_neighbour():
    _, h, z, y, _, _ = place()
    return (2 * z + 1 - y, h)


def along_z(count):
    _, h, z, y, _, _ = place()
    lines = count // 2
    return [(2 * lax.rem(z + j, lines) + y, h) for j in range(1, lines)]


def along_seq(count):
    s, h = place()[:2]
    return [(lax.rem(s + j, count), h) for j in range(1, count)]


def remote(src, dst, send, recv, device):
    return pltpu.make_async_remote_copy(
        src_ref=src, dst_ref=dst, send_sem=send, recv_sem=recv, device_id=device, device_id_type=MESH
    )


def greet(devices):
    for device in devices:
        pl.semaphore_signal(
            pltpu.get_barrier_semaphore(), inc=1, device_id=device, device_id_type=MESH
        )


def greeted(devices):
    pl.semaphore_wait(pltpu.get_barrier_semaphore(), len(devices))


class Gather:
    def __init__(self, count, shard, full, lanes, own, zs, zr, ys, yr):
        s, _, z, y, _, _ = place()
        lines = count // 2
        shard = shard.at[:, lanes]
        view = lambda slot: full.at[slot, :, lanes]
        self.local = pltpu.make_async_copy(shard, view(s), own)
        self.z_copies = [
            remote(shard, view(s), zs.at[j], zr.at[j], device)
            for j, device in enumerate(along_z(count))
        ]
        self.y_copies = [remote(shard, view(s), ys.at[0], yr.at[0], y_neighbour())]
        for j in range(1, lines):
            slot = 2 * lax.rem(z - j + lines, lines) + y
            self.y_copies.append(remote(view(slot), view(slot), ys.at[j], yr.at[j], y_neighbour()))

    def start(self):
        for copy in self.z_copies:
            copy.start()
        self.y_copies[0].start()
        self.local.start()

    def forward(self):
        for z_copy, y_copy in zip(self.z_copies, self.y_copies[1:]):
            z_copy.wait_recv()
            y_copy.start()

    def finish(self):
        self.local.wait()
        for copy in self.y_copies:
            copy.wait_recv()

    def close(self):
        for copy in self.z_copies + self.y_copies:
            copy.wait_send()


class Scatter:
    def __init__(self, count, terms, y_buf, pair, z_buf, ys, yr, zs, zr):
        self.terms, self.y_buf, self.pair, self.z_buf = terms, y_buf, pair, z_buf
        _, _, self.z, self.y, _, _ = place()
        self.lines = count // 2
        self.y_copies = []
        for j in range(self.lines):
            line = lax.rem(self.z + j, self.lines)
            self.y_copies.append(
                remote(
                    terms.at[2 * line + 1 - self.y], y_buf.at[line], ys.at[j], yr.at[j], y_neighbour()
                )
            )
        self.z_copies = [
            remote(pair.at[j], z_buf.at[j], zs.at[j], zr.at[j], device)
            for j, device in enumerate(along_z(count))
        ]

    def fill(self, left, right):
        self.terms[...] = across(left, right).astype(LOW).reshape(self.terms.shape)

    def start(self, first=0, last=None):
        order = list(range(1, self.lines)) + [0]
        for j in order[first:last]:
            self.y_copies[j].start()

    def forward(self, first=1, last=None):
        for j in range(self.lines)[first:last]:
            line = lax.rem(self.z + j, self.lines)
            self.y_copies[j].wait_recv()
            self.pair[j - 1] = (
                self.terms[2 * line + self.y].astype(WIDE) + self.y_buf[line].astype(WIDE)
            ).astype(LOW)
            self.z_copies[j - 1].start()

    def finish(self):
        self.y_copies[0].wait_recv()
        total = self.terms[2 * self.z + self.y].astype(WIDE) + self.y_buf[self.z].astype(WIDE)
        for j, copy in enumerate(self.z_copies):
            copy.wait_recv()
            total = total + self.z_buf[j].astype(WIDE)
        return total

    def close(self):
        for copy in self.z_copies + self.y_copies:
            copy.wait_send()


class Spread:
    def __init__(self, count, blocks, send, recv):
        s = place()[0]
        self.copies = [
            remote(blocks.at[s], blocks.at[s], send.at[j], recv.at[j], device)
            for j, device in enumerate(along_seq(count))
        ]

    def start(self):
        for copy in self.copies:
            copy.start()

    def finish(self):
        for copy in self.copies:
            copy.wait_recv()

    def close(self):
        for copy in self.copies:
            copy.wait_send()


class Swap(Spread):
    def __init__(self, count, out, into, send, recv):
        s = place()[0]
        self.out, self.into = out, into
        self.copies = [
            remote(out.at[device[0]], into.at[s], send.at[j], recv.at[j], device)
            for j, device in enumerate(along_seq(count))
        ]

    def start(self):
        s = place()[0]
        super().start()
        self.into[s] = self.out[s]


class HeadSum:
    def __init__(self, turn, terms, core_in, x_out, x_in, sems):
        self.turn, self.terms, self.core_in, self.x_out, self.x_in = turn, terms, core_in, x_out, x_in
        self.sems = sems
        self.core = place()[5]
        self.half = terms.shape[1] // 2

    def core_copy(self, c, turn=None):
        sems = self.sems.at[self.turn if turn is None else turn]
        away = pl.ds(pl.multiple_of((1 - self.core) * self.half, self.half), self.half)
        return remote(
            self.terms.at[c, away], self.core_in.at[c], sems.at[0, c], sems.at[1, c], core_of_chip()
        )

    def x_copy(self, c, turn=None):
        turn = self.turn if turn is None else turn
        sems = self.sems.at[turn]
        return remote(
            self.x_out.at[c], self.x_in.at[turn % 2, c], sems.at[2, c], sems.at[3, c], x_neighbour()
        )

    def offer(self, c, rows):
        if self.turn > 0:
            self.core_copy(c, self.turn - 1).wait_send()
        self.terms[c] = rows
        self.core_copy(c).start()

    def pair_up(self, c):
        self.core_copy(c).wait_recv()
        if self.turn > 0:
            self.x_copy(c, self.turn - 1).wait_send()
        here = pl.ds(pl.multiple_of(self.core * self.half, self.half), self.half)
        self.x_out[c] = (
            self.terms[c, here].astype(WIDE) + self.core_in[c].astype(WIDE)
        ).astype(LOW)
        self.x_copy(c).start()

    def arrived(self, c):
        self.x_copy(c).wait_recv()

    def total(self, c, rows):
        return self.x_out[c, rows].astype(WIDE) + self.x_in[self.turn % 2, c, rows].astype(WIDE)


def iota(shape, dim):
    return lax.broadcasted_iota(jnp.int32, shape, dim)


def fold(rows):
    return rows.reshape(rows.shape[0] // 8, 8, rows.shape[1]).sum(axis=0)


def gelu_and_slope(v):
    square = v * v
    t = jnp.tanh(0.7978845608 * (v + 0.044715 * v * square))
    half = 0.5 * (1.0 + t)
    slope = half + 0.5 * v * (1.0 - t * t) * (0.7978845608 * (1.0 + 0.134145 * square))
    return v * half, slope


def exact(left, right, dims=(1, 0)):
    return lax.dot_general(
        left,
        right,
        (((dims[0],), (dims[1],)), ((), ())),
        preferred_element_type=WIDE,
        precision=PRECISE,
    )


def dense(block):
    n = block.shape[0]
    rest = jnp.concatenate([block[0 : n // 2, 128:], block[n // 2 :, 128:]], axis=1)
    return jnp.concatenate([block[:, 0:128], rest], axis=0)


def undense(block):
    n = block.shape[0] * 2 // 3
    rest = jnp.concatenate([block[n:, 0:64], block[n:, 64:128]], axis=0)
    return jnp.concatenate([block[0:n], rest], axis=1)


def loop(count, body):
    lax.fori_loop(0, count, lambda i, carry: (body(i), carry)[1], 0)


def layer_kernel(count, names, *refs):
    r = types.SimpleNamespace(**dict(zip(names, refs)))
    s, h, z, y, x, core = place()
    rows, width = r.inputs_hbm.shape
    near = r.w_query.shape[1]
    heads = near // HEAD_DIM
    feed = r.w_up.shape[1]
    size = rows // CHUNKS
    half = size // 2
    step = 32
    lines = count // 2
    two = 2 * LAND
    scale = HEAD_DIM**-0.5
    chunk_rows = lambda c: pl.ds(pl.multiple_of(c * size, size), size)
    my_rows = lambda c: pl.ds(pl.multiple_of(c * size + core * half, half), half)
    everyone = along_seq(count)
    before, after = (lax.rem(s + count - 1, count), h), (lax.rem(s + 1, count), h)

    flat = lambda ref: ref[...].reshape(1, ref.shape[0])
    bias_query, bias_value, bias_out = flat(r.bias_query), flat(r.bias_value), flat(r.bias_out)
    bias_up, bias_down = flat(r.bias_up), flat(r.bias_down)
    gain_one, bias_one, gain_two, bias_two = (
        flat(r.gain_one), flat(r.bias_one), flat(r.gain_two), flat(r.bias_two)
    )

    def gather(k, shard, full, lo, hi):
        return Gather(
            count, shard, full, slice(lo, hi), r.g_own.at[k], r.g_zs.at[k], r.g_zr.at[k], r.g_ys.at[k], r.g_yr.at[k]
        )

    def scatter(k, terms, y_buf, pair, z_buf):
        return Scatter(
            count, terms, y_buf, pair, z_buf, r.s_ys.at[k], r.s_yr.at[k], r.s_zs.at[k], r.s_zr.at[k]
        )

    gather_qk = gather(0, r.packed, r.w_near, 0, 2 * near)
    gather_vo = gather(1, r.packed, r.w_near, 2 * near, 4 * near)
    gather_up1 = gather(2, r.w_up, r.full_up, 0, feed // 2)
    gather_up2 = gather(3, r.w_up, r.full_up, feed // 2, feed)
    gather_down1 = gather(4, r.w_down, r.full_down, 0, feed // 2)
    gather_down2 = gather(5, r.w_down, r.full_down, feed // 2, feed)
    gathers = [gather_qk, gather_vo, gather_up1, gather_up2, gather_down1, gather_down2]
    scatter_out = scatter(0, r.t_out, r.yb_out, r.pr_out, r.zb_out)
    scatter_up = scatter(1, r.t_up, r.yb_up, r.pr_up, r.zb_up)
    scatter_down = scatter(2, r.t_down, r.yb_down, r.pr_down, r.zb_down)
    scatter_qkv = scatter(3, r.t_qkv, r.yb_qkv, r.pr_qkv, r.zb_qkv)
    scatters = [scatter_out, scatter_up, scatter_down, scatter_qkv]
    sums = [HeadSum(k, r.terms, r.core_in, r.x_out, r.x_in, r.h_sems) for k in range(4)]
    landmarks = Spread(count, r.land_part, r.e_s.at[0], r.e_r.at[0])
    numer_swap = Swap(count, r.numer_out, r.numer_in, r.e_s.at[1], r.e_r.at[1])
    kernel_spread = Spread(count, r.kernel_v, r.e_s.at[2], r.e_r.at[2])
    mixing_spread = Spread(count, r.mix_part, r.e_s.at[3], r.e_r.at[3])
    kland_spread = Spread(count, r.kland_part, r.e_s.at[4], r.e_r.at[4])
    qland_spread = Spread(count, r.qland_part, r.e_s.at[5], r.e_r.at[5])
    vector_spread = Spread(count, r.vector_part, r.e_s.at[6], r.e_r.at[6])
    small_spread = Spread(count, r.small_part, r.e_s.at[7], r.e_r.at[7])
    spreads = [
        landmarks, numer_swap, kernel_spread, mixing_spread, kland_spread, qland_spread, vector_spread, small_spread,
    ]

    def rim(k, ext):
        first = remote(
            ext.at[pl.ds(REACH, REACH)], ext.at[pl.ds(REACH + rows, REACH)], r.rim_s.at[k, 0], r.rim_r.at[k, 0], before
        )
        last = remote(
            ext.at[pl.ds(rows, REACH)], ext.at[pl.ds(0, REACH)], r.rim_s.at[k, 1], r.rim_r.at[k, 1], after
        )
        return [first, last]

    rims = [rim(0, r.value_ext), rim(1, r.grad_ext)]

    def share(k, ref, c):
        return remote(
            ref.at[my_rows(c)], ref.at[my_rows(c)], r.share_s.at[k, c], r.share_r.at[k, c], core_of_chip()
        )

    load_inputs = pltpu.make_async_copy(r.inputs_hbm, r.inputs, r.io.at[0])
    load_cotangent = pltpu.make_async_copy(r.cotangent_hbm, r.cotangent, r.io.at[1])
    stores = [
        pltpu.make_async_copy(ref, out, r.io.at[2 + k])
        for k, (ref, out) in enumerate(
            (
                (r.output, r.output_hbm),
                (r.grad_inputs, r.grad_inputs_hbm),
                (r.grad_w_out, r.grad_w_out_hbm),
                (r.grad_w_up, r.grad_w_up_hbm),
                (r.grad_w_down, r.grad_w_down_hbm),
                (r.grad_near, r.grad_near_hbm),
            )
        )
    ]
    store_output, store_grad_inputs, store_out, store_up, store_down, store_near = stores
    vector_core = remote(
        r.vector_sum.at[0], r.vector_sum.at[1], r.core_s.at[0], r.core_r.at[0], core_of_chip()
    )

    met = [core_of_chip(), x_neighbour()] + everyone
    greet(met)
    load_inputs.start()
    r.packed[:, 0:near] = r.w_query[...]
    r.packed[:, near : 2 * near] = r.w_key[...]
    r.packed[:, 2 * near : 3 * near] = r.w_value[...]
    r.packed[:, 3 * near : 4 * near] = r.w_out[...]
    ends = jnp.where(s == 0, r.lengths[0], jnp.where(s == count - 1, r.lengths[2], 0))
    edge_start = jnp.where(s == 0, 0, rows - ends)
    edge_end = edge_start + ends
    edge_count = ends // LAND
    mid_count = r.lengths[1] // LAND
    mid_first = s * rows - r.lengths[0]
    first_slot = jnp.maximum(mid_first, 0) // mid_count
    item_edge = jnp.where(s == 0, ends, jnp.where(s == count - 1, rows - ends, -1))

    def members():
        token, lane = iota((rows, two), 0), iota((rows, two), 1)
        mid = lane < LAND
        at_edge = (token >= edge_start) & (token < edge_end)
        start = jnp.where(mid, (first_slot + lane) * mid_count - mid_first, (lane - LAND) * edge_count + edge_start)
        length = jnp.where(mid, mid_count, edge_count)
        inside = (token >= start) & (token < start + length)
        belongs = jnp.where(mid, jnp.where(at_edge, 0.0, 1.0), jnp.where(at_edge, 1.0, 0.0))
        r.member[...] = jnp.where(inside, belongs, 0.0).astype(LOW)

    members()
    greeted(met)
    gather_qk.start()
    gather_vo.start()
    load_cotangent.start()
    r.small_part[s] = jnp.zeros((8, PAD), WIDE)
    head_lane = iota((8, PAD), 1) // HEAD_DIM
    masks = [(head_lane == k).astype(WIDE)[0:1] for k in range(heads)]
    masks_low = [m[:, :near].astype(LOW) for m in masks]

    def spread_heads(ref, block):
        for k in range(heads):
            ref[k * two : (k + 1) * two, :] = block * masks_low[k]

    def own_heads(wide_rows, group, lanes):
        return sum(
            wide_rows[k * group : (k + 1) * group, :] * masks[k][:, :lanes] for k in range(heads)
        )

    def bands(ref, flipped):
        token, lane = iota((BLOCK, 2 * SPAN), 0), iota((BLOCK, 2 * SPAN), 1)
        upper = lane < SPAN
        offset = jnp.where(upper, lane, lane - SPAN) - token
        for k in range(heads):
            band = jnp.zeros((BLOCK, 2 * SPAN), WIDE)
            for j in range(KERNEL):
                at = KERNEL - 1 - j if flipped else j
                band = jnp.where(offset == at, r.conv_taps[k, j], band)
            high = band.astype(LOW).astype(WIDE)
            ref[k * BLOCK : (k + 1) * BLOCK, :] = jnp.where(upper, high, band - high).astype(LOW)

    bands(r.band, False)
    bands(r.band_back, True)

    def window(ext, b):
        taken = ext[pl.ds(pl.multiple_of(b * BLOCK, BLOCK), SPAN), :]
        start = b * BLOCK
        left_out = (start == item_edge) | ((s == 0) & (start == 0))
        right_out = (start + BLOCK == item_edge) | ((s == count - 1) & (start + BLOCK == rows))
        row = iota((SPAN, taken.shape[1]), 0)
        keep = jnp.where(
            row < REACH,
            jnp.where(left_out, 0.0, 1.0),
            jnp.where(row >= REACH + BLOCK, jnp.where(right_out, 0.0, 1.0), 1.0),
        )
        return taken * keep.astype(LOW)

    def convolve(band, taken):
        return own_heads(matmul_low(band[...], jnp.concatenate([taken, taken], axis=0)), BLOCK, taken.shape[1])

    gather_qk.forward()
    load_inputs.wait()
    gather_qk.finish()

    def project_qk(c):
        at = chunk_rows(c)
        both = matmul_low(r.inputs[at], r.w_near[:, :, 0 : 2 * near].reshape(width, 2 * near))
        r.queries[at] = (both[:, :near] + bias_query).astype(LOW)
        r.keys[at] = both[:, near:].astype(LOW)

    loop(CHUNKS, project_qk)
    query_sums = across(r.member[...], r.queries[...])
    key_sums = across(r.member[...], r.keys[...])
    mid_scale = 1.0 / mid_count.astype(WIDE)
    edge_scale = 1.0 / jnp.maximum(edge_count, 1).astype(WIDE)
    border = jnp.concatenate([query_sums[0:BORDER], key_sums[0:BORDER]], axis=0) * mid_scale
    r.land_part[s] = dense(border).astype(LOW)
    landmarks.start()
    gather_vo.forward()
    gather_up1.start()
    r.query_land[LAND:two] = (query_sums[LAND:two] * edge_scale).astype(LOW)
    r.key_land[LAND:two] = (key_sums[LAND:two] * edge_scale).astype(LOW)

    gather_vo.finish()

    def project_v(c):
        at = pl.ds(pl.multiple_of(REACH + c * size, REACH), size)
        values = matmul_low(r.inputs[chunk_rows(c)], r.w_near[:, :, 2 * near : 2 * near + PAD].reshape(width, PAD))
        values = values[:, :near] + bias_value
        r.value_ext[at, 0:near] = values.astype(LOW)
        r.value_ext[at, near:PAD] = jnp.zeros((size, PAD - near), LOW)

    loop(CHUNKS, project_v)
    for copy in rims[0]:
        copy.start()
    r.out_rows[...] = r.w_near[:, :, 3 * near :].reshape(width, near)

    landmarks.finish()
    lane = iota((LAND, count * BORDER), 1)
    owner = lane // BORDER
    starts = jnp.zeros((LAND, count * BORDER), jnp.int32)
    for d in range(count):
        starts = jnp.where(owner == d, jnp.maximum(d * rows - r.lengths[0], 0) // mid_count, starts)
    put = (iota((LAND, count * BORDER), 0) == starts + lane - owner * BORDER).astype(LOW)
    borders = [undense(r.land_part[d]) for d in range(count)]
    r.query_land[0:LAND] = matmul_low(put, jnp.concatenate([b[0:BORDER] for b in borders], axis=0)).astype(LOW)
    r.key_land[0:LAND] = matmul_low(put, jnp.concatenate([b[BORDER:] for b in borders], axis=0)).astype(LOW)
    spread_heads(r.query_heads, r.query_land[...])
    spread_heads(r.key_heads, r.key_land[...])

    own_values = lambda: r.value_ext[pl.ds(REACH, rows), :]

    def attend_b(g):
        at = pl.ds(pl.multiple_of(g * LAND, LAND), LAND)
        scores = against(r.query_heads[at], r.keys[...]) * scale
        token = iota((LAND, rows), 1)
        at_edge = jnp.where((token >= edge_start) & (token < edge_end), 1.0, 0.0)
        member = jnp.where(lax.rem(g, 2) == 1, at_edge, 1.0 - at_edge)
        scores = jnp.where(member > 0.5, scores, MASKED)
        largest = jnp.max(scores, axis=1, keepdims=True)
        weights = jnp.exp(scores - largest) * member
        r.weights_b[at] = weights
        r.weights_b_low[at] = weights.astype(LOW)
        r.max_b[at] = largest
        r.total_b[at] = jnp.sum(weights, axis=1, keepdims=True)

    loop(2 * heads, attend_b)
    numer = own_heads(matmul_low(r.weights_b_low[...], own_values()), two, PAD)
    lane = iota((two, PAD), 1)
    for k in range(heads):
        numer = jnp.where(lane == near + k, r.total_b[k * two : (k + 1) * two], numer)
        numer = jnp.where(lane == near + heads + k, r.max_b[k * two : (k + 1) * two], numer)
    r.numer_out[...] = numer[0:LAND].reshape(count, LAND // count, PAD)
    numer_swap.start()

    def wide_heads(stats, base):
        lane = iota(stats.shape, 1)
        out = stats
        for k in range(heads):
            out = jnp.where(lane // HEAD_DIM == k, stats[:, base + k : base + k + 1], out)
        return out

    edge = numer[LAND:two]
    edge_totals = wide_heads(edge, near)
    edge_totals = jnp.where(edge_totals > 0.0, edge_totals, 1.0)
    r.kernel_edge[...] = jnp.where(iota(edge.shape, 1) < near, edge / edge_totals, 0.0)

    pairs = [(k, g) for k in range(heads) for g in range(2)]
    identity = (iota((LAND, LAND), 0) == iota((LAND, LAND), 1)).astype(WIDE)
    group = lambda g: slice(g * LAND, (g + 1) * LAND)

    def first_inverse(k, g, i):
        lands = r.query_heads[k * two + g * LAND : k * two + (g + 1) * LAND, :]
        scores = against(lands, r.key_land[group(g), :]) * scale
        weights = jnp.exp(scores - jnp.max(scores, axis=1, keepdims=True))
        weights = weights / jnp.sum(weights, axis=1, keepdims=True)
        r.land_kernel[i] = weights
        return weights.T / jnp.sum(weights * weights)

    def invert(it, inverses):
        kernels = [r.land_kernel[i] for i in range(len(pairs))]
        products = [exact(a, b) for a, b in zip(kernels, inverses)]
        nested = [15.0 * identity - exact(p, 7.0 * identity - p) for p in products]
        for i, p in enumerate(products):
            r.history[it, 0, i] = inverses[i]
            r.history[it, 1, i] = p
            r.history[it, 2, i] = nested[i]
        nested = [13.0 * identity - exact(p, n) for p, n in zip(products, nested)]
        for i, n in enumerate(nested):
            r.history[it, 3, i] = n
        return tuple(0.25 * exact(a, n) for a, n in zip(inverses, nested))

    inverses = tuple(first_inverse(k, g, i) for i, (k, g) in enumerate(pairs))
    inverses = lax.fori_loop(0, PINV_STEPS // 2, invert, inverses)

    gather_up1.forward()

    numer_swap.finish()
    parts = [r.numer_in[d] for d in range(count)]
    largest = functools.reduce(jnp.maximum, [wide_heads(p, near + heads) for p in parts])
    lane = iota(largest.shape, 1)
    joined = jnp.zeros_like(largest)
    totals = jnp.zeros_like(largest)
    for p in parts:
        weight = jnp.exp(wide_heads(p, near + heads) - largest)
        joined = joined + jnp.where(lane < near, p * weight, 0.0)
        totals = totals + jnp.where(lane < near, wide_heads(p, near) * weight, 0.0)
    joined = jnp.where(lane < near, joined / jnp.where(lane < near, totals, 1.0), 0.0)
    for k in range(heads):
        joined = jnp.where(lane == near + k, totals[:, k * HEAD_DIM : k * HEAD_DIM + 1], joined)
        joined = jnp.where(
            lane == near + heads + k, largest[:, k * HEAD_DIM : k * HEAD_DIM + 1], joined
        )
    r.kernel_v[s] = joined
    kernel_spread.start()
    gather_up2.start()
    inverses = lax.fori_loop(PINV_STEPS // 2, PINV_STEPS, invert, inverses)
    for i, inverse in enumerate(inverses):
        r.inverse[i] = inverse
    gather_down1.start()

    def attend_f(c):
        at = pl.ds(pl.multiple_of(c * half, half), half)
        scores = against(r.queries[at], r.key_heads[...]) * scale
        token, lane = iota((half, two), 0) + c * half, iota((half, two), 1)
        at_edge = (token >= edge_start) & (token < edge_end)
        member = jnp.where(lane < LAND, jnp.where(at_edge, 0.0, 1.0), jnp.where(at_edge, 1.0, 0.0))
        for k in range(heads):
            own = jnp.where(member > 0.5, scores[:, k * two : (k + 1) * two], MASKED)
            weights = jnp.exp(own - jnp.max(own, axis=1, keepdims=True))
            r.weights_f[at, k * two : (k + 1) * two] = weights / jnp.sum(weights, axis=1, keepdims=True)

    loop(rows // half, attend_f)
    for copy in rims[0]:
        copy.wait_recv()

    def convolve_values(b):
        r.conv[pl.ds(pl.multiple_of(b * BLOCK, BLOCK), BLOCK), :] = convolve(
            r.band, window(r.value_ext, b)
        )[:, :near]

    loop(rows // BLOCK, convolve_values)
    gather_up2.forward()
    gather_down2.start()
    kernel_spread.finish()
    kernel_mid = r.kernel_v[...].reshape(LAND, PAD)
    kernel_of = lambda g: kernel_mid if g == 0 else r.kernel_edge[...]
    for g in range(2):
        mixed = jnp.zeros((LAND, PAD), WIDE)
        for i, (k, own) in enumerate(pairs):
            if own == g:
                mixed = mixed + exact(r.inverse[i], kernel_of(g)) * masks[k]
        r.mixing[group(g), :] = mixed[:, :near].astype(LOW)
    spread_heads(r.mixing_heads, r.mixing[...])

    def project_out(c):
        at = chunk_rows(c)
        attended = matmul_low(r.weights_f[at].astype(LOW), r.mixing_heads[...])
        r.mixed[at] = (attended + r.conv[at]).astype(LOW)
        sums[0].offer(c, against(r.mixed[at], r.out_rows[...]).astype(LOW))

    loop(CHUNKS, project_out)
    loop(CHUNKS, sums[0].pair_up)
    gather_down1.forward()
    r.acc[...] = jnp.zeros_like(r.acc)
    gather_up1.finish()
    gather_up2.finish()
    load_cotangent.wait()
    pieces = lambda body: loop(half // step, lambda i: body(pl.multiple_of(i * step, step)))

    def norm_first(c):
        def piece(i):
            at = pl.ds(pl.multiple_of(c * size + core * half + i, step), step)
            kept = pl.ds(pl.multiple_of(c * half + i, step), step)
            pre = r.inputs[at].astype(WIDE) + sums[0].total(c, pl.ds(i, step)) + bias_out
            normed, inv = normalize(pre)
            r.norm_one[kept] = normed
            r.inv_one[kept] = inv
            r.hidden[at] = (normed * gain_one + bias_one).astype(LOW)

        sums[0].arrived(c)
        pieces(piece)
        share(0, r.hidden, c).start()

    def lift(c):
        share(0, r.hidden, c).wait_recv()
        at = chunk_rows(c)
        r.tmp[...] = matmul_low(r.hidden[at], r.full_up[...].reshape(width, feed))

        def curve(i):
            to = pl.ds(pl.multiple_of(c * size + i * step, step), step)
            value, grade = gelu_and_slope(r.tmp[pl.ds(pl.multiple_of(i * step, step), step)] + bias_up)
            r.active[to] = value.astype(LOW)
            r.slope[to] = grade.astype(LOW)

        loop(size // step, curve)

    def lower(c):
        at = chunk_rows(c)
        sums[1].offer(c, against(r.active[at], r.full_down[...].reshape(width, feed)).astype(LOW))

    def behind(c, total):
        @pl.when(c > 0)
        def _():
            total.pair_up(c - 1)

    def feed_forward(c):
        norm_first(c)
        behind(c, sums[1])
        lift(c)

        @pl.when(c == 0)
        def _():
            gather_down2.forward()
            gather_down1.finish()
            gather_down2.finish()

        lower(c)

    loop(CHUNKS, feed_forward)
    sums[1].pair_up(CHUNKS - 1)

    def feed_back(c):
        def piece(i):
            at = pl.ds(pl.multiple_of(c * size + core * half + i, step), step)
            kept = pl.ds(pl.multiple_of(c * half + i, step), step)
            pre = r.norm_one[kept] * gain_one + bias_one + sums[1].total(c, pl.ds(i, step)) + bias_down
            normed, inv = normalize(pre)
            r.output[at] = (normed * gain_two + bias_two).astype(LOW)
            grad = r.cotangent[at].astype(WIDE)
            back = norm_back(grad * gain_two, normed, inv)
            r.wide_grad[kept] = back
            r.grad_two[at] = back.astype(LOW)
            r.acc[0] += fold(grad * normed)
            r.acc[1] += fold(grad)
            r.acc[2] += fold(back)

        sums[1].arrived(c)
        pieces(piece)
        share(1, r.grad_two, c).start()
        share(2, r.output, c).start()
        behind(c, sums[2])
        share(1, r.grad_two, c).wait_recv()
        at = chunk_rows(c)
        r.tmp[...] = matmul_low(r.grad_two[at], r.full_down[...].reshape(width, feed))

        def curve(i):
            to = pl.ds(pl.multiple_of(c * size + i * step, step), step)
            value = r.tmp[pl.ds(pl.multiple_of(i * step, step), step)] * r.slope[to].astype(WIDE)
            r.grad_lift[to] = value.astype(LOW)
            r.acc[6] += fold(value)

        loop(size // step, curve)
        sums[2].offer(c, against(r.grad_lift[at], r.full_up[...].reshape(width, feed)).astype(LOW))

    loop(CHUNKS, feed_back)
    sums[2].pair_up(CHUNKS - 1)

    scatter_down.fill(r.grad_two[...], r.active[...])
    scatter_down.start()
    scatter_up.fill(r.hidden[...], r.grad_lift[...])
    r.mix_grad[...] = jnp.zeros_like(r.mix_grad)
    r.kland_grad[...] = jnp.zeros_like(r.kland_grad)

    def mix_back(c):
        def piece(i):
            at = pl.ds(pl.multiple_of(c * size + core * half + i, step), step)
            kept = pl.ds(pl.multiple_of(c * half + i, step), step)
            normed = r.norm_one[kept]
            grad = r.wide_grad[kept] + sums[2].total(c, pl.ds(i, step))
            back = norm_back(grad * gain_one, normed, r.inv_one[kept])
            r.wide_grad[kept] = back
            r.grad_one[at] = back.astype(LOW)
            r.acc[3] += fold(grad * normed)
            r.acc[4] += fold(grad)
            r.acc[5] += fold(back)

        sums[2].arrived(c)
        pieces(piece)
        share(3, r.grad_one, c).start()
        share(3, r.grad_one, c).wait_recv()
        at = chunk_rows(c)
        grad = matmul_low(r.grad_one[at], r.out_rows[...]).astype(LOW)
        r.grad_ext[pl.ds(pl.multiple_of(REACH + c * size, REACH), size)] = grad
        weights = r.weights_f[at]
        weighted = weights * against(grad, r.mixing_heads[...])
        scores = []
        for k in range(heads):
            own = slice(k * two, (k + 1) * two)
            scores.append(weighted[:, own] - weights[:, own] * jnp.sum(weighted[:, own], axis=1, keepdims=True))
        scores = jnp.concatenate(scores, axis=1).astype(LOW)
        r.grad_query[at] = matmul_low(scores, r.key_heads[...]) * scale
        r.mix_grad[...] += across(weights.astype(LOW), grad)
        r.kland_grad[...] += across(scores, r.queries[at])

        @pl.when(c == 2)
        def _():
            scatter_down.forward(1, 2)

    loop(CHUNKS, mix_back)
    mix_grad = own_heads(r.mix_grad[...], two, near)
    kland_grad = own_heads(r.kland_grad[...], two, near) * scale
    r.mix_part[s] = dense(mix_grad[0:LAND]).astype(LOW)
    r.kland_part[s] = dense(kland_grad[0:LAND]).astype(LOW)
    mixing_spread.start()
    for copy in rims[1]:
        copy.start()
    scatter_up.start(0, 2)
    scatter_down.forward(2)

    def settle_output(c):
        share(2, r.output, c).wait_recv()

    loop(CHUNKS, settle_output)
    store_output.start()
    for k in range(7):
        r.vector_part[s, k : k + 1] = jnp.sum(r.acc[k], axis=0, keepdims=True)
    r.vector_part[s, 7:8] = jnp.zeros((1, width), WIDE)
    for copy in rims[1]:
        copy.wait_recv()

    r.tap_grad[...] = jnp.zeros_like(r.tap_grad)

    def convolve_back(b):
        at = pl.ds(pl.multiple_of(b * BLOCK, BLOCK), BLOCK)
        r.conv[at] = convolve(r.band_back, window(r.grad_ext, b))
        own = r.grad_ext[pl.ds(pl.multiple_of(b * BLOCK + REACH, REACH), BLOCK), :]
        own = jnp.concatenate([own * m for m in masks_low], axis=0)
        r.tap_grad[:, 0:SPAN] += against(own, window(r.value_ext, b)[:, :near])

    loop(rows // BLOCK, convolve_back)
    token = lax.rem(iota((heads * BLOCK, 128), 0), BLOCK)
    slanted = r.tap_grad[...]
    for bit in range(6):
        moved = pltpu.roll(slanted, 128 - (1 << bit), 1)
        slanted = jnp.where(lax.rem(token // (1 << bit), 2) == 1, moved, slanted)
    for k in range(heads):
        r.small_part[s, 2 + k : 3 + k, 0:128] = jnp.sum(
            slanted[k * BLOCK : (k + 1) * BLOCK], axis=0, keepdims=True
        )

    mixing_spread.finish()
    over_seq = lambda ref: undense(functools.reduce(jnp.add, [ref[d].astype(WIDE) for d in range(count)]))
    mix_grads = [over_seq(r.mix_part), mix_grad[LAND:two]]
    stats = r.kernel_v[...].reshape(LAND, PAD)
    mid_totals = wide_heads(stats, near)[:, :near]
    divisors = [mid_totals, edge_totals[:, :near]]
    inverse_grads = []
    for i, (k, g) in enumerate(pairs):
        inverse_grads.append(
            exact(mix_grads[g] * masks[k][:, :near], kernel_of(g)[:, :near], (1, 1))
        )
    shrink = [
        jnp.exp(r.max_b[k * two : k * two + LAND] - stats[:, near + heads + k : near + heads + k + 1])
        for k in range(heads)
    ]
    for g in range(2):
        grad = jnp.zeros((LAND, near), WIDE)
        for i, (k, own) in enumerate(pairs):
            if own == g:
                grad = grad + exact(r.inverse[i], mix_grads[g], (0, 0)) * masks[k][:, :near]
        grad = grad / divisors[g]
        lost = grad * kernel_of(g)[:, :near]
        for k in range(heads):
            at = slice(k * two + g * LAND, k * two + (g + 1) * LAND)
            factor = shrink[k] if g == 0 else 1.0
            r.numer_heads[at] = (grad * factor * masks[k][:, :near]).astype(LOW)
            r.total_grad[at] = -jnp.sum(lost * masks[k][:, :near], axis=1, keepdims=True) * factor

    def back_b(g):
        at = pl.ds(pl.multiple_of(g * LAND, LAND), LAND)
        grad = against(r.numer_heads[at], own_values()[:, :near]) + r.total_grad[at]
        r.scores_b[at] = (r.weights_b[at] * grad).astype(LOW)

    loop(2 * heads, back_b)
    qland_grad = own_heads(matmul_low(r.scores_b[...], r.keys[...]), two, near) * scale
    r.qland_part[s] = dense(qland_grad[0:LAND]).astype(LOW)
    qland_spread.start()
    kland_spread.start()
    scatter_up.start(2)
    vector_spread.start()
    scatter_out.fill(r.grad_one[...], r.mixed[...])
    scatter_out.start()

    def keys_values(c):
        at = chunk_rows(c)
        r.grad_key[at] = across(r.scores_b[:, at], r.query_heads[...]) * scale
        values = across(r.weights_b_low[:, at], r.numer_heads[...]) + r.conv[at]
        r.near_grads[at, 2 * near : 3 * near] = values.astype(LOW)
        return jnp.sum(values, axis=0, keepdims=True)

    value_bias = lax.fori_loop(
        0, CHUNKS, lambda c, total: total + keys_values(c), jnp.zeros((1, near), WIDE)
    )

    def invert_back(i, carry):
        it = PINV_STEPS - 1 - i
        grads, kernel_grads = carry
        many = range(len(pairs))
        held = [[r.history[it, part, p] for p in many] for part in range(4)]
        befores, products, nested_two, nested_three = held
        kernels = [r.land_kernel[p] for p in many]
        grad_three = [0.25 * exact(a, b, (0, 0)) for a, b in zip(befores, grads)]
        grad_two = [-exact(a, b, (0, 0)) for a, b in zip(products, grad_three)]
        grad_one = [-exact(a, b, (0, 0)) for a, b in zip(products, grad_two)]
        grad_product = [
            -exact(a, b, (1, 1)) - exact(c, 7.0 * identity - d, (1, 1)) - e
            for a, b, c, d, e in zip(grad_three, nested_two, grad_two, products, grad_one)
        ]
        kernel_grads = [k + exact(a, b, (1, 1)) for k, a, b in zip(kernel_grads, grad_product, befores)]
        grads = [
            0.25 * exact(a, b, (1, 1)) + exact(k, p, (0, 0))
            for a, b, k, p in zip(grads, nested_three, kernels, grad_product)
        ]
        return tuple(grads), tuple(kernel_grads)

    scatter_up.forward(1, 3)
    zeros = tuple(jnp.zeros((LAND, LAND), WIDE) for _ in pairs)
    grads, kernel_grads = lax.fori_loop(0, PINV_STEPS, invert_back, (tuple(inverse_grads), zeros))
    qland_a = [jnp.zeros((LAND, near), WIDE)] * 2
    kland_a = [jnp.zeros((LAND, near), WIDE)] * 2
    for i, (k, g) in enumerate(pairs):
        kernel = r.land_kernel[i]
        turned = grads[i].T
        squares = jnp.sum(kernel * kernel)
        grad = kernel_grads[i] + turned / squares - kernel * (2.0 * jnp.sum(turned * kernel) / (squares * squares))
        grad = kernel * (grad - jnp.sum(kernel * grad, axis=1, keepdims=True)) * scale
        mask = masks[k][:, :near]
        qland_a[g] = qland_a[g] + exact(grad, r.key_land[group(g)].astype(WIDE)) * mask
        kland_a[g] = kland_a[g] + exact(grad, r.query_land[group(g)].astype(WIDE), (0, 0)) * mask

    scatter_up.forward(3)

    kland_spread.finish()
    qland_spread.finish()
    pick = (iota((LAND, LAND), 1) == iota((LAND, LAND), 0) + first_slot).astype(WIDE)

    def slot_grads(mid, edge):
        mid = exact(pick, mid * mid_scale)
        both = jnp.concatenate([mid, edge * edge_scale], axis=0)
        high = both.astype(LOW)
        return jnp.concatenate([high, (both - high.astype(WIDE)).astype(LOW)], axis=0)

    r.slot_q[...] = slot_grads(qland_a[0] + over_seq(r.qland_part), qland_a[1] + qland_grad[LAND:two])
    r.slot_k[...] = slot_grads(kland_a[0] + over_seq(r.kland_part), kland_a[1] + kland_grad[LAND:two])

    def input_back(c):
        at = chunk_rows(c)
        member = jnp.concatenate([r.member[at]] * 2, axis=1)
        queries = r.grad_query[at] + matmul_low(member, r.slot_q[...])
        keys = r.grad_key[at] + matmul_low(member, r.slot_k[...])
        r.near_grads[at, 0:near] = queries.astype(LOW)
        r.near_grads[at, near : 2 * near] = keys.astype(LOW)
        terms = against(r.near_grads[at], r.w_near[:, :, 0 : 3 * near].reshape(width, 3 * near))
        sums[3].offer(c, terms.astype(LOW))
        sums[3].pair_up(c)
        return jnp.sum(queries, axis=0, keepdims=True)

    query_bias = lax.fori_loop(
        0, CHUNKS, lambda c, total: total + input_back(c), jnp.zeros((1, near), WIDE)
    )
    r.small_part[s, 0:1, 0:near] = query_bias
    r.small_part[s, 1:2, 0:near] = value_bias
    small_spread.start()
    scatter_qkv.fill(r.inputs[...], r.near_grads[...])
    scatter_qkv.start()
    scatter_out.forward()
    vector_spread.finish()
    r.vector_sum[0] = functools.reduce(jnp.add, [r.vector_part[d] for d in range(count)])
    vector_core.start()
    r.grad_w_down[...] = scatter_down.finish()
    store_down.start()
    r.grad_w_up[...] = scatter_up.finish()
    store_up.start()
    r.grad_w_out[...] = scatter_out.finish()
    store_out.start()
    scatter_qkv.forward()

    def inputs_done(c):
        def piece(i):
            at = pl.ds(pl.multiple_of(c * size + core * half + i, step), step)
            kept = pl.ds(pl.multiple_of(c * half + i, step), step)
            r.grad_inputs[at] = (r.wide_grad[kept] + sums[3].total(c, pl.ds(i, step))).astype(LOW)

        sums[3].arrived(c)
        pieces(piece)
        share(4, r.grad_inputs, c).start()

    loop(CHUNKS, inputs_done)
    near_total = scatter_qkv.finish()
    for k in range(3):
        r.grad_near[k] = near_total[:, k * near : (k + 1) * near]
    store_near.start()
    vector_core.wait_recv()
    r.vectors[0:6] = r.vector_sum[0, 0:6] + r.vector_sum[1, 0:6]
    r.vectors[6:8] = r.vector_sum[0, 6:8]
    small_spread.finish()
    r.smalls[...] = functools.reduce(jnp.add, [r.small_part[d] for d in range(count)])

    def settle_inputs(c):
        share(4, r.grad_inputs, c).wait_recv()

    loop(CHUNKS, settle_inputs)
    store_grad_inputs.start()

    def settle(c):
        sums[3].core_copy(c).wait_send()
        sums[3].x_copy(c).wait_send()
        for k, ref in enumerate((r.hidden, r.grad_two, r.output, r.grad_one, r.grad_inputs)):
            share(k, ref, c).wait_send()

    loop(CHUNKS, settle)
    vector_core.wait_send()
    for copy in stores:
        copy.wait()
    for copy in rims[0] + rims[1]:
        copy.wait_send()
    for group_of in gathers + scatters + spreads:
        group_of.close()


def hand_out(
    output, grad_inputs, grad_out, grad_up, grad_down, grad_near, vectors, smalls,
    to_output, to_inputs, to_query, to_key, to_value, to_out, to_up, to_down,
    bias_query, bias_value, bias_out, bias_up, bias_down, gain_one, bias_one, gain_two, bias_two, taps, sems,
):
    rows = output.shape[0] // 4
    copies = []
    for k, (ref, to) in enumerate(((output, to_output), (grad_inputs, to_inputs))):
        for j in range(4):
            at = pl.ds(j * rows, rows)
            copies.append(pltpu.make_async_copy(ref.at[at], to.at[at], sems.at[k, j]))
    for k, (ref, to) in enumerate(
        (
            (grad_near.at[0], to_query), (grad_near.at[1], to_key), (grad_near.at[2], to_value),
            (grad_out, to_out), (grad_up, to_up), (grad_down, to_down),
        )
    ):
        copies.append(pltpu.make_async_copy(ref, to, sems.at[2 + k, 0]))
    for copy in copies:
        copy.start()
    for k, ref in enumerate((gain_two, bias_two, bias_down, gain_one, bias_one, bias_out, bias_up)):
        ref[...] = vectors[k : k + 1].reshape(ref.shape)
    for k, ref in enumerate((bias_query, bias_value)):
        ref[...] = smalls[k : k + 1, 0 : ref.shape[0]].reshape(ref.shape)
    taps[...] = smalls[2 : 2 + taps.shape[0], 0:KERNEL]
    for copy in copies:
        copy.wait()


def fused_body(
    inputs, cotangent, item_lengths, w_query, w_key, w_value, w_out, w_up, w_down, bias_query, bias_value,
    bias_out, bias_up, bias_down, gain_one, bias_one, gain_two, bias_two, conv_taps,
):
    count = lax.axis_size("seq")
    rows, width = inputs.shape
    near, feed, heads = w_query.shape[1], w_up.shape[1], conv_taps.shape[0]
    size, part, lines = rows // CHUNKS, width // count, count // 2
    half, two = size // 2, 2 * LAND
    low = lambda *shape: pltpu.VMEM(shape, LOW)
    wide = lambda *shape: pltpu.VMEM(shape, WIDE)
    sem = lambda *shape: pltpu.SemaphoreType.DMA(shape)
    vmem, smem = pl.BlockSpec(memory_space=pltpu.VMEM), pl.BlockSpec(memory_space=pltpu.SMEM)
    operands = dict(
        lengths=item_lengths, conv_taps=conv_taps,
        inputs_hbm=inputs, cotangent_hbm=cotangent,
        w_query=w_query, w_key=w_key, w_value=w_value, w_out=w_out, w_up=w_up, w_down=w_down,
        bias_query=bias_query, bias_value=bias_value,
        bias_out=bias_out, bias_up=bias_up, bias_down=bias_down,
        gain_one=gain_one, bias_one=bias_one, gain_two=gain_two, bias_two=bias_two,
    )
    outs = dict(
        output_hbm=((rows, width), LOW), grad_inputs_hbm=((rows, width), LOW),
        grad_w_out_hbm=((part, near), WIDE), grad_w_up_hbm=((part, feed), WIDE), grad_w_down_hbm=((part, feed), WIDE),
        grad_near_hbm=((3, part, near), WIDE), vectors=((8, width), WIDE), smalls=((8, PAD), WIDE),
    )
    scratch = dict(
        inputs=low(rows, width), cotangent=low(rows, width), output=low(rows, width), grad_inputs=low(rows, width),
        grad_w_out=wide(part, near), grad_w_up=wide(part, feed), grad_w_down=wide(part, feed),
        grad_near=wide(3, part, near), io=sem(8),
        packed=low(part, 4 * near), w_near=low(count, part, 4 * near), out_rows=low(width, near),
        full_up=low(count, part, feed), full_down=low(count, part, feed),
        member=low(rows, two), band=low(heads * BLOCK, 2 * SPAN), band_back=low(heads * BLOCK, 2 * SPAN),
        queries=low(rows, near), keys=low(rows, near), value_ext=low(rows + 2 * REACH, PAD),
        land_part=low(count, 3 * BORDER, 128), query_land=low(two, near), key_land=low(two, near),
        query_heads=low(heads * two, near), key_heads=low(heads * two, near),
        weights_b=wide(heads * two, rows), weights_b_low=low(heads * two, rows),
        max_b=wide(heads * two, 1), total_b=wide(heads * two, 1),
        numer_out=wide(count, LAND // count, PAD), numer_in=wide(count, LAND // count, PAD),
        kernel_v=wide(count, LAND // count, PAD), kernel_edge=wide(LAND, PAD),
        land_kernel=wide(2 * heads, LAND, LAND), inverse=wide(2 * heads, LAND, LAND),
        history=wide(PINV_STEPS, 4, 2 * heads, LAND, LAND),
        weights_f=wide(rows, heads * two), conv=wide(rows, near),
        mixing=low(two, near), mixing_heads=low(heads * two, near), mixed=low(rows, near),
        terms=low(CHUNKS, size, width), core_in=low(CHUNKS, half, width),
        x_out=low(CHUNKS, half, width), x_in=low(2, CHUNKS, half, width),
        hidden=low(rows, width), active=low(rows, feed), slope=low(rows, feed),
        grad_two=low(rows, width), grad_lift=low(rows, feed), grad_one=low(rows, width),
        norm_one=wide(rows // 2, width), inv_one=wide(rows // 2, 1), wide_grad=wide(rows // 2, width),
        tmp=wide(size, feed), acc=wide(7, 8, width),
        grad_ext=low(rows + 2 * REACH, near), grad_query=wide(rows, near), grad_key=wide(rows, near),
        mix_grad=wide(heads * two, near), kland_grad=wide(heads * two, near),
        mix_part=low(count, 3 * LAND // 2, 128), kland_part=low(count, 3 * LAND // 2, 128),
        qland_part=low(count, 3 * LAND // 2, 128),
        tap_grad=wide(heads * BLOCK, 128), numer_heads=low(heads * two, near), total_grad=wide(heads * two, 1),
        scores_b=low(heads * two, rows), near_grads=low(rows, 3 * near),
        slot_q=low(2 * two, near), slot_k=low(2 * two, near),
        vector_part=wide(count, 8, width), vector_sum=wide(2, 8, width), small_part=wide(count, 8, PAD),
    )
    scatter = lambda lanes: (
        low(count, part, lanes), low(lines, part, lanes), low(lines - 1, part, lanes), low(lines - 1, part, lanes)
    )
    for_out, for_up, for_down, for_qkv = (scatter(lanes) for lanes in (near, feed, feed, 3 * near))
    scratch.update(
        t_out=for_out[0], yb_out=for_out[1], pr_out=for_out[2], zb_out=for_out[3],
        t_up=for_up[0], yb_up=for_up[1], pr_up=for_up[2], zb_up=for_up[3],
        t_down=for_down[0], yb_down=for_down[1], pr_down=for_down[2], zb_down=for_down[3],
        t_qkv=for_qkv[0], yb_qkv=for_qkv[1], pr_qkv=for_qkv[2], zb_qkv=for_qkv[3],
        g_own=sem(6), g_zs=sem(6, lines - 1), g_zr=sem(6, lines - 1), g_ys=sem(6, lines), g_yr=sem(6, lines),
        s_ys=sem(4, lines), s_yr=sem(4, lines), s_zs=sem(4, lines - 1), s_zr=sem(4, lines - 1),
        e_s=sem(8, count - 1), e_r=sem(8, count - 1), h_sems=sem(4, 4, CHUNKS),
        rim_s=sem(2, 2), rim_r=sem(2, 2), share_s=sem(5, CHUNKS), share_r=sem(5, CHUNKS),
        core_s=sem(1), core_r=sem(1),
    )
    any_place = pl.BlockSpec(memory_space=pltpu.HBM)
    results = pl.pallas_call(
        functools.partial(layer_kernel, count, list(operands) + list(outs) + list(scratch)),
        out_shape=tuple(jax.ShapeDtypeStruct(*out) for out in outs.values()),
        in_specs=[smem, smem, any_place, any_place] + [vmem] * (len(operands) - 4),
        out_specs=(any_place,) * 6 + (vmem, vmem),
        scratch_shapes=list(scratch.values()),
        compiler_params=pltpu.CompilerParams(
            collective_id=1, has_side_effects=True, vmem_limit_bytes=63 * 2**20
        ),
    )(*operands.values())
    vector = lambda length: jax.ShapeDtypeStruct((length,), WIDE)
    block = lambda lanes: jax.ShapeDtypeStruct((part, lanes), WIDE)
    whole = jax.ShapeDtypeStruct((rows, width), LOW)
    return pl.pallas_call(
        hand_out,
        out_shape=(
            whole, whole, block(near), block(near), block(near), block(near), block(feed), block(feed),
            vector(near), vector(near), vector(width), vector(feed), vector(width),
            vector(width), vector(width), vector(width), vector(width),
            jax.ShapeDtypeStruct((heads, KERNEL), WIDE),
        ),
        in_specs=[vmem] * 8,
        out_specs=(any_place,) * 8 + (vmem,) * 10,
        scratch_shapes=[sem(8, 4)],
    )(*results)


def plain_body(
    inputs,
    cotangent,
    item_lengths,
    w_query,
    w_key,
    w_value,
    w_out,
    w_up,
    w_down,
    bias_query,
    bias_value,
    bias_out,
    bias_up,
    bias_down,
    gain_one,
    bias_one,
    gain_two,
    bias_two,
    conv_taps,
):
    low_type = jnp.bfloat16
    tok_rows = inputs.shape[0]
    heads_here = conv_taps.shape[0]
    width_here = heads_here * HEAD_DIM
    slots = ITEMS * LAND
    reach = (KERNEL - 1) // 2
    score_scale = HEAD_DIM ** (-0.5)
    pref = jnp.float32
    first_row = lax.axis_index("seq") * tok_rows
    positions = first_row + jnp.arange(tok_rows, dtype=jnp.int32)
    item_id, land_slot = locate(item_lengths, positions)
    rim_item = locate(
        item_lengths, first_row - reach + jnp.arange(tok_rows + 2 * reach, dtype=jnp.int32)
    )[0]
    slot_item = jnp.arange(slots, dtype=jnp.int32) // LAND
    member = land_slot[:, None] == jnp.arange(slots, dtype=jnp.int32)[None, :]
    member_low = member.astype(low_type)
    counts = jnp.repeat((item_lengths // LAND).astype(jnp.float32), LAND)
    same_f = item_id[:, None] == slot_item[None, :]
    same_b = same_f.T
    tap_cols = jnp.repeat(conv_taps, HEAD_DIM, axis=0)
    full_query, full_key, full_value, full_out, full_up, full_down = (
        lax.all_gather(w_query, "seq", axis=0, tiled=True),
        lax.all_gather(w_key, "seq", axis=0, tiled=True),
        lax.all_gather(w_value, "seq", axis=0, tiled=True),
        lax.all_gather(w_out, "seq", axis=0, tiled=True),
        lax.all_gather(w_up, "seq", axis=0, tiled=True),
        lax.all_gather(w_down, "seq", axis=0, tiled=True),
    )
    queries = (matmul_low(inputs, full_query) + bias_query).astype(low_type)
    key_rows = matmul_low(inputs, full_key).astype(low_type)
    value_rows = (matmul_low(inputs, full_value) + bias_value).astype(low_type)
    query_sums, key_sums = lax.psum(
        (across(member_low, queries), across(member_low, key_rows)), "seq"
    )
    query_land = (
        (query_sums / counts[:, None]).astype(low_type).reshape(slots, heads_here, HEAD_DIM)
    )
    key_land = (key_sums / counts[:, None]).astype(low_type).reshape(slots, heads_here, HEAD_DIM)
    query_heads = queries.reshape(tok_rows, heads_here, HEAD_DIM)
    key_heads = key_rows.reshape(tok_rows, heads_here, HEAD_DIM)
    value_heads = value_rows.reshape(tok_rows, heads_here, HEAD_DIM)
    scores_b = (
        jnp.einsum("lhd,thd->hlt", query_land, key_heads, preferred_element_type=pref) * score_scale
    )
    scores_b = jnp.where(same_b[None], scores_b, MASKED)
    maxima_b = lax.pmax(jnp.max(scores_b, axis=2), "seq")
    weights_b = jnp.exp(scores_b - maxima_b[:, :, None])
    weights_b_low = weights_b.astype(low_type)
    numer_sum, totals_b = lax.psum(
        (
            jnp.einsum("hlt,thd->lhd", weights_b_low, value_heads, preferred_element_type=pref),
            jnp.sum(weights_b, axis=2),
        ),
        "seq",
    )
    totals_cols = totals_b.T[:, :, None]
    kernel_v = numer_sum / totals_cols
    land_q = query_land.reshape(ITEMS, LAND, heads_here, HEAD_DIM)
    land_k = key_land.reshape(ITEMS, LAND, heads_here, HEAD_DIM)
    land_kernel = jax.nn.softmax(
        jnp.einsum("ilhd,imhd->ihlm", land_q, land_k, preferred_element_type=pref) * score_scale,
        axis=-1,
    )
    inverse, inverse_back = jax.vjp(pseudo_inverse, land_kernel)
    kernel_items = kernel_v.reshape(ITEMS, LAND, heads_here, HEAD_DIM)
    mixing = jnp.einsum("ihlm,imhd->ilhd", inverse, kernel_items, precision=PRECISE)
    mixing = mixing.astype(low_type).reshape(slots, heads_here, HEAD_DIM)
    scores_f = (
        jnp.einsum("thd,lhd->htl", query_heads, key_land, preferred_element_type=pref) * score_scale
    )
    weights_f = jax.nn.softmax(jnp.where(same_f[None], scores_f, MASKED), axis=-1)
    weights_f_low = weights_f.astype(low_type)
    attended = jnp.einsum("htl,lhd->thd", weights_f_low, mixing, preferred_element_type=pref)
    attended = attended.reshape(tok_rows, width_here)
    value_rim = extended(value_rows, (("seq", 0),), reach)
    conv_sum = jnp.zeros((tok_rows, width_here), jnp.float32)
    for offset in range(KERNEL):
        in_item = (rim_item[offset : offset + tok_rows] == item_id)[:, None]
        conv_sum = conv_sum + jnp.where(
            in_item,
            value_rim[offset : offset + tok_rows].astype(jnp.float32)
            * tap_cols[:, offset][None, :],
            0.0,
        )
    mixed_rows = (attended + conv_sum).astype(low_type)
    attention_sum = lax.psum(against(mixed_rows, full_out).astype(jnp.bfloat16), "head").astype(
        jnp.float32
    )
    pre_one = inputs.astype(jnp.float32) + attention_sum + bias_out
    norm_one, inv_one = normalize(pre_one)
    hidden = norm_one * gain_one + bias_one
    hidden_low = hidden.astype(low_type)
    lifted = matmul_low(hidden_low, full_up) + bias_up
    active, gelu_back = jax.vjp(gelu_tanh, lifted)
    active_low = active.astype(low_type)
    feed_terms = against(active_low, full_down)
    feed_sum = lax.psum(feed_terms.astype(jnp.bfloat16), "head").astype(jnp.float32)
    grad_output = cotangent.astype(jnp.float32)
    pre_two = hidden + feed_sum + bias_down
    norm_two, inv_two = normalize(pre_two)
    out_rows = (norm_two * gain_two + bias_two).astype(low_type)
    grad_gain_two = jnp.sum(grad_output * norm_two, axis=0)
    grad_bias_two = jnp.sum(grad_output, axis=0)
    grad_two = norm_back(grad_output * gain_two, norm_two, inv_two)
    grad_bias_down = jnp.sum(grad_two, axis=0)
    grad_two_low = grad_two.astype(low_type)
    output, grad_two_full = (out_rows, grad_two_low)
    grad_down = across(grad_two_full, active_low)
    (grad_lift,) = gelu_back(matmul_low(grad_two_full, full_down))
    grad_bias_up = jnp.sum(grad_lift, axis=0)
    grad_lift_low = grad_lift.astype(low_type)
    grad_up = across(hidden_low, grad_lift_low)
    up_terms = against(grad_lift_low, full_up)
    grad_hidden = grad_two + lax.psum(up_terms.astype(jnp.bfloat16), "head").astype(jnp.float32)
    grad_gain_one = jnp.sum(grad_hidden * norm_one, axis=0)
    grad_bias_one = jnp.sum(grad_hidden, axis=0)
    grad_one = norm_back(grad_hidden * gain_one, norm_one, inv_one)
    grad_bias_out = jnp.sum(grad_one, axis=0)
    grad_one_low = grad_one.astype(low_type)
    grad_outw = across(grad_one_low, mixed_rows)
    grad_mixed = matmul_low(grad_one_low, full_out).astype(low_type)
    grad_mixed_wide = grad_mixed.astype(jnp.float32)
    grad_heads = grad_mixed.reshape(tok_rows, heads_here, HEAD_DIM)
    grad_rim = extended(grad_mixed, (("seq", 0),), reach)
    grad_conv_v = jnp.zeros((tok_rows, width_here), jnp.float32)
    tap_terms = []
    for offset in range(KERNEL):
        in_item = (rim_item[offset : offset + tok_rows] == item_id)[:, None]
        neighbour = jnp.where(
            in_item, value_rim[offset : offset + tok_rows].astype(jnp.float32), 0.0
        )
        tap_terms.append(
            jnp.sum(
                (grad_mixed_wide * neighbour).reshape(tok_rows, heads_here, HEAD_DIM), axis=(0, 2)
            )
        )
        mirror = 2 * reach - offset
        mirror_item = (rim_item[mirror : mirror + tok_rows] == item_id)[:, None]
        grad_conv_v = grad_conv_v + jnp.where(
            mirror_item,
            grad_rim[mirror : mirror + tok_rows].astype(jnp.float32) * tap_cols[:, offset][None, :],
            0.0,
        )
    grad_taps = jnp.stack(tap_terms, axis=1)
    grad_weights_f = jnp.einsum("thd,lhd->htl", grad_heads, mixing, preferred_element_type=pref)
    grad_mix_part = jnp.einsum(
        "htl,thd->lhd", weights_f_low, grad_heads, preferred_element_type=pref
    )
    grad_scores_f = weights_f * (
        grad_weights_f - jnp.sum(weights_f * grad_weights_f, axis=2, keepdims=True)
    )
    grad_scores_f = grad_scores_f.astype(low_type)
    grad_query_f = (
        jnp.einsum("htl,lhd->thd", grad_scores_f, key_land, preferred_element_type=pref)
        * score_scale
    )
    grad_kland_part = (
        jnp.einsum("htl,thd->lhd", grad_scores_f, query_heads, preferred_element_type=pref)
        * score_scale
    )
    grad_mixing, grad_kland_f = lax.psum((grad_mix_part, grad_kland_part), "seq")
    grad_mix_items = grad_mixing.reshape(ITEMS, LAND, heads_here, HEAD_DIM)
    grad_inverse = jnp.einsum("ilhd,imhd->ihlm", grad_mix_items, kernel_items, precision=PRECISE)
    grad_kernel_v = jnp.einsum("ihlm,ilhd->imhd", inverse, grad_mix_items, precision=PRECISE)
    grad_kernel_v = grad_kernel_v.reshape(slots, heads_here, HEAD_DIM)
    (grad_land_kernel,) = inverse_back(grad_inverse)
    grad_scores_a = land_kernel * (
        grad_land_kernel - jnp.sum(land_kernel * grad_land_kernel, axis=-1, keepdims=True)
    )
    grad_scores_a = grad_scores_a * score_scale
    grad_qland_a = jnp.einsum(
        "ihlm,imhd->ilhd", grad_scores_a, land_k.astype(jnp.float32), precision=PRECISE
    )
    grad_kland_a = jnp.einsum(
        "ihlm,ilhd->imhd", grad_scores_a, land_q.astype(jnp.float32), precision=PRECISE
    )
    grad_numer = (grad_kernel_v / totals_cols).astype(low_type)
    grad_totals = -jnp.sum(grad_kernel_v * kernel_v, axis=2) / totals_b.T
    grad_weights_b = jnp.einsum(
        "lhd,thd->hlt", grad_numer, value_heads, preferred_element_type=pref
    )
    grad_weights_b = grad_weights_b + grad_totals.T[:, :, None]
    grad_scores_b = (weights_b * grad_weights_b).astype(low_type)
    grad_qland_part = (
        jnp.einsum("hlt,thd->lhd", grad_scores_b, key_heads, preferred_element_type=pref)
        * score_scale
    )
    grad_key_b = (
        jnp.einsum("hlt,lhd->thd", grad_scores_b, query_land, preferred_element_type=pref)
        * score_scale
    )
    grad_value_b = jnp.einsum(
        "hlt,lhd->thd", weights_b_low, grad_numer, preferred_element_type=pref
    )
    grad_query_rows = grad_query_f.reshape(tok_rows, width_here)
    grad_values = grad_value_b.reshape(tok_rows, width_here) + grad_conv_v
    (
        grad_qland_b,
        grad_gain_one,
        grad_bias_one,
        grad_gain_two,
        grad_bias_two,
        grad_bias_out,
        grad_bias_down,
        grad_bias_up,
        grad_taps,
        query_f_total,
        grad_bias_value,
    ) = lax.psum(
        (
            grad_qland_part,
            grad_gain_one,
            grad_bias_one,
            grad_gain_two,
            grad_bias_two,
            grad_bias_out,
            grad_bias_down,
            grad_bias_up,
            grad_taps,
            jnp.sum(grad_query_rows, axis=0),
            jnp.sum(grad_values, axis=0),
        ),
        "seq",
    )
    grad_qland = grad_qland_a.reshape(slots, width_here) + grad_qland_b.reshape(slots, width_here)
    grad_kland = grad_kland_a.reshape(slots, width_here) + grad_kland_f.reshape(slots, width_here)
    member_wide = member.astype(jnp.float32)
    grad_queries = grad_query_rows + jnp.dot(
        member_wide, grad_qland / counts[:, None], precision=PRECISE
    )
    grad_keys = grad_key_b.reshape(tok_rows, width_here) + jnp.dot(
        member_wide, grad_kland / counts[:, None], precision=PRECISE
    )
    grad_bias_query = query_f_total + jnp.sum(grad_qland, axis=0)
    queries_low = grad_queries.astype(low_type)
    keys_low = grad_keys.astype(low_type)
    values_low = grad_values.astype(low_type)
    grad_queryw = across(inputs, queries_low)
    grad_keyw = across(inputs, keys_low)
    grad_valuew = across(inputs, values_low)
    input_terms = (
        against(queries_low, full_query)
        + against(keys_low, full_key)
        + against(values_low, full_value)
    )
    grad_inputs = (
        grad_one + lax.psum(input_terms.astype(jnp.bfloat16), "head").astype(jnp.float32)
    ).astype(low_type)
    query_shard, key_shard, value_shard, out_shard, grad_up_shard, grad_down_shard = side_by_side(
        (
            grad_queryw.astype(jnp.bfloat16),
            grad_keyw.astype(jnp.bfloat16),
            grad_valuew.astype(jnp.bfloat16),
            grad_outw.astype(jnp.bfloat16),
            grad_up.astype(jnp.bfloat16),
            grad_down.astype(jnp.bfloat16),
        ),
        "seq",
        0,
        1,
    )
    return (
        output,
        grad_inputs,
        query_shard,
        key_shard,
        value_shard,
        out_shard,
        grad_up_shard,
        grad_down_shard,
        grad_bias_query,
        grad_bias_value,
        grad_bias_out,
        grad_bias_up,
        grad_bias_down,
        grad_gain_one,
        grad_bias_one,
        grad_gain_two,
        grad_bias_two,
        grad_taps,
    )


def solution(mesh):
    aligned = (768 // mesh.shape["seq"]) % 16 == 0
    return jax.shard_map(
        fused_body if aligned else plain_body,
        mesh=mesh,
        in_specs=(
            P("seq", None),
            P("seq", None),
            P(),
            P("seq", "head"),
            P("seq", "head"),
            P("seq", "head"),
            P("seq", "head"),
            P("seq", "head"),
            P("seq", "head"),
            P("head"),
            P("head"),
            P(),
            P("head"),
            P(),
            P(),
            P(),
            P(),
            P(),
            P("head", None),
        ),
        out_specs=(
            P("seq", None),
            P("seq", None),
            P("seq", "head"),
            P("seq", "head"),
            P("seq", "head"),
            P("seq", "head"),
            P("seq", "head"),
            P("seq", "head"),
            P("head"),
            P("head"),
            P(),
            P("head"),
            P(),
            P(),
            P(),
            P(),
            P(),
            P("head", None),
        ),
        check_vma=False,
    )
```

```python
import functools
import types

import jax
import jax.numpy as jnp
from jax import lax
from jax.experimental import pallas as pl
from jax.experimental.pallas import tpu as pltpu
from jax.sharding import PartitionSpec as P

HEAD_DIM = 64
LAND = 64
KERNEL = 33
PINV_STEPS = 6
ITEMS = 3


PRECISE = lax.Precision.HIGHEST
EPSILON = 1e-05
MASKED = -1e30


def extended(cells, sides, width):
    for axis, dim in sides:
        count = lax.axis_size(axis)
        ends = count - 1
        head = lax.slice_in_dim(cells, 0, width, axis=dim)
        tail = lax.slice_in_dim(cells, cells.shape[dim] - width, cells.shape[dim], axis=dim)
        cells = jnp.concatenate(
            [
                lax.ppermute(tail, axis, [(i, (i + 1) % count) for i in range(ends)]),
                cells,
                lax.ppermute(head, axis, [((i + 1) % count, i) for i in range(ends)]),
            ],
            axis=dim,
        )
    return cells


def cut_along(array, dim, length):
    lengths = array.shape
    parts = array.reshape(*lengths[:dim], length, lengths[dim] // length, *lengths[dim + 1 :])
    return jnp.moveaxis(parts, dim, 0)


def sent_and_summed(array, axis, dim):
    parts = cut_along(array, dim, lax.axis_size(axis))
    arrived = lax.all_to_all(parts, axis, split_axis=0, concat_axis=0, tiled=True)
    return arrived.astype(jnp.float32).sum(axis=0)


def side_by_side(arrays, axis, dim, along):
    both = jnp.concatenate(arrays, axis=along)
    out, at, outs = (sent_and_summed(both, axis, dim), 0, [])
    for a in arrays:
        outs.append(lax.slice_in_dim(out, at, at + a.shape[along], axis=along))
        at += a.shape[along]
    return tuple(outs)


def locate(item_lengths, positions):
    item_ends = jnp.cumsum(item_lengths)
    item_starts = item_ends - item_lengths
    located = jnp.sum((positions[:, None] >= item_ends[None, :]).astype(jnp.int32), axis=1)
    inside = (positions >= 0) & (located < ITEMS)
    picked = jnp.minimum(located, ITEMS - 1)
    onehot = (picked[:, None] == jnp.arange(ITEMS, dtype=jnp.int32)[None, :]).astype(jnp.int32)
    item_start = jnp.sum(onehot * item_starts[None, :], axis=1)
    length = jnp.sum(onehot * item_lengths[None, :], axis=1)
    segment = (positions - item_start) * LAND // length
    land_slot = picked * LAND + jnp.clip(segment, 0, LAND - 1)
    return (jnp.where(inside, picked, -1), land_slot)


def normalize(values):
    row_mean = jnp.mean(values, axis=-1, keepdims=True)
    centered = values - row_mean
    variance = jnp.mean(centered * centered, axis=-1, keepdims=True)
    inv_std = lax.rsqrt(variance + EPSILON)
    return (centered * inv_std, inv_std)


def norm_back(grad_norm, normed, inv_std):
    return inv_std * (
        grad_norm
        - jnp.mean(grad_norm, axis=-1, keepdims=True)
        - normed * jnp.mean(grad_norm * normed, axis=-1, keepdims=True)
    )


def pseudo_inverse(land_kernel):
    identity = jnp.eye(LAND, dtype=jnp.float32)
    frobenius = jnp.sum(land_kernel * land_kernel, axis=(-2, -1), keepdims=True)
    result = jnp.swapaxes(land_kernel, -1, -2) / frobenius
    for iteration in range(PINV_STEPS):
        product = jnp.matmul(land_kernel, result, precision=PRECISE)
        nested = 7.0 * identity - product
        nested = 15.0 * identity - jnp.matmul(product, nested, precision=PRECISE)
        nested = 13.0 * identity - jnp.matmul(product, nested, precision=PRECISE)
        result = 0.25 * jnp.matmul(result, nested, precision=PRECISE)
    return result


def gelu_tanh(values):
    return jax.nn.gelu(values, approximate=True)


def matmul_low(left, right):
    return jnp.dot(left, right, preferred_element_type=jnp.float32)


def against(left, right):
    return lax.dot_general(
        left, right, (((1,), (1,)), ((), ())), preferred_element_type=jnp.float32
    )


def across(left, right):
    return lax.dot_general(
        left, right, (((0,), (0,)), ((), ())), preferred_element_type=jnp.float32
    )


MESH = pl.DeviceIdType.MESH
WIDE = jnp.float32
LOW = jnp.bfloat16
CHUNKS = 4
PAD = 256
REACH = (KERNEL - 1) // 2
BLOCK = 64
SPAN = BLOCK + 2 * REACH
BORDER = 16


def place():
    s, h = lax.axis_index("seq"), lax.axis_index("head")
    return s, h, s // 2, lax.rem(s, 2), h // 2, lax.rem(h, 2)


def core_of_chip():
    s, _, _, _, x, core = place()
    return (s, 2 * x + 1 - core)


def x_neighbour():
    s, _, _, _, x, core = place()
    return (s, 2 * (1 - x) + core)


def y_neighbour():
    _, h, z, y, _, _ = place()
    return (2 * z + 1 - y, h)


def along_z(count):
    _, h, z, y, _, _ = place()
    lines = count // 2
    return [(2 * lax.rem(z + j, lines) + y, h) for j in range(1, lines)]


def along_seq(count):
    s, h = place()[:2]
    return [(lax.rem(s + j, count), h) for j in range(1, count)]


def remote(src, dst, send, recv, device):
    return pltpu.make_async_remote_copy(
        src_ref=src, dst_ref=dst, send_sem=send, recv_sem=recv, device_id=device, device_id_type=MESH
    )


def greet(devices):
    for device in devices:
        pl.semaphore_signal(
            pltpu.get_barrier_semaphore(), inc=1, device_id=device, device_id_type=MESH
        )


def greeted(devices):
    pl.semaphore_wait(pltpu.get_barrier_semaphore(), len(devices))


class Gather:
    def __init__(self, count, shard, full, lanes, own, zs, zr, ys, yr):
        s, _, z, y, _, _ = place()
        lines = count // 2
        shard = shard.at[:, lanes]
        view = lambda slot: full.at[slot, :, lanes]
        self.local = pltpu.make_async_copy(shard, view(s), own)
        self.z_copies = [
            remote(shard, view(s), zs.at[j], zr.at[j], device)
            for j, device in enumerate(along_z(count))
        ]
        self.y_copies = [remote(shard, view(s), ys.at[0], yr.at[0], y_neighbour())]
        for j in range(1, lines):
            slot = 2 * lax.rem(z - j + lines, lines) + y
            self.y_copies.append(remote(view(slot), view(slot), ys.at[j], yr.at[j], y_neighbour()))

    def start(self):
        for copy in self.z_copies:
            copy.start()
        self.y_copies[0].start()
        self.local.start()

    def forward(self):
        for z_copy, y_copy in zip(self.z_copies, self.y_copies[1:]):
            z_copy.wait_recv()
            y_copy.start()

    def finish(self):
        self.local.wait()
        for copy in self.y_copies:
            copy.wait_recv()

    def close(self):
        for copy in self.z_copies + self.y_copies:
            copy.wait_send()


class Scatter:
    def __init__(self, count, terms, y_buf, pair, z_buf, ys, yr, zs, zr):
        self.terms, self.y_buf, self.pair, self.z_buf = terms, y_buf, pair, z_buf
        _, _, self.z, self.y, _, _ = place()
        self.lines = count // 2
        self.y_copies = []
        for j in range(self.lines):
            line = lax.rem(self.z + j, self.lines)
            self.y_copies.append(
                remote(
                    terms.at[2 * line + 1 - self.y], y_buf.at[line], ys.at[j], yr.at[j], y_neighbour()
                )
            )
        self.z_copies = [
            remote(pair.at[j], z_buf.at[j], zs.at[j], zr.at[j], device)
            for j, device in enumerate(along_z(count))
        ]

    def fill(self, left, right):
        self.terms[...] = across(left, right).astype(LOW).reshape(self.terms.shape)

    def fill_dense(self, left, right):
        terms = across(left, right).astype(LOW)
        part = terms.shape[0] // self.terms.shape[0]
        terms = terms.reshape(self.terms.shape[0], part, terms.shape[1])
        self.terms[:, 0:part] = terms[:, :, 0:128]
        self.terms[:, part:] = jnp.concatenate(
            [terms[:, 0 : part // 2, 128:], terms[:, part // 2 :, 128:]], axis=2
        )

    def start(self, first=0, last=None):
        order = list(range(1, self.lines)) + [0]
        for j in order[first:last]:
            self.y_copies[j].start()

    def forward(self, first=1, last=None):
        for j in range(self.lines)[first:last]:
            line = lax.rem(self.z + j, self.lines)
            self.y_copies[j].wait_recv()
            self.pair[j - 1] = (
                self.terms[2 * line + self.y].astype(WIDE) + self.y_buf[line].astype(WIDE)
            ).astype(LOW)
            self.z_copies[j - 1].start()

    def finish(self):
        self.y_copies[0].wait_recv()
        total = self.terms[2 * self.z + self.y].astype(WIDE) + self.y_buf[self.z].astype(WIDE)
        for j, copy in enumerate(self.z_copies):
            copy.wait_recv()
            total = total + self.z_buf[j].astype(WIDE)
        return total

    def close(self):
        for copy in self.z_copies + self.y_copies:
            copy.wait_send()


class Spread:
    def __init__(self, count, blocks, send, recv):
        s = place()[0]
        self.copies = [
            remote(blocks.at[s], blocks.at[s], send.at[j], recv.at[j], device)
            for j, device in enumerate(along_seq(count))
        ]

    def start(self):
        for copy in self.copies:
            copy.start()

    def finish(self):
        for copy in self.copies:
            copy.wait_recv()

    def close(self):
        for copy in self.copies:
            copy.wait_send()


class Swap(Spread):
    def __init__(self, count, out, into, send, recv):
        s = place()[0]
        self.out, self.into = out, into
        self.copies = [
            remote(out.at[device[0]], into.at[s], send.at[j], recv.at[j], device)
            for j, device in enumerate(along_seq(count))
        ]

    def start(self):
        s = place()[0]
        super().start()
        self.into[s] = self.out[s]


class HeadSum:
    def __init__(self, turn, terms, core_in, x_out, x_in, sems):
        self.turn, self.terms, self.core_in, self.x_out, self.x_in = turn, terms, core_in, x_out, x_in
        self.sems = sems
        self.core = place()[5]
        self.half = terms.shape[1] // 2

    def core_copy(self, c, turn=None):
        sems = self.sems.at[self.turn if turn is None else turn]
        away = pl.ds(pl.multiple_of((1 - self.core) * self.half, self.half), self.half)
        return remote(
            self.terms.at[c, away], self.core_in.at[c], sems.at[0, c], sems.at[1, c], core_of_chip()
        )

    def x_copy(self, c, turn=None):
        turn = self.turn if turn is None else turn
        sems = self.sems.at[turn]
        return remote(
            self.x_out.at[c], self.x_in.at[turn % 2, c], sems.at[2, c], sems.at[3, c], x_neighbour()
        )

    def offer(self, c, rows):
        if self.turn > 0:
            self.core_copy(c, self.turn - 1).wait_send()
        self.terms[c] = rows
        self.core_copy(c).start()

    def pair_up(self, c):
        self.core_copy(c).wait_recv()
        if self.turn > 0:
            self.x_copy(c, self.turn - 1).wait_send()
        here = pl.ds(pl.multiple_of(self.core * self.half, self.half), self.half)
        self.x_out[c] = (
            self.terms[c, here].astype(WIDE) + self.core_in[c].astype(WIDE)
        ).astype(LOW)
        self.x_copy(c).start()

    def arrived(self, c):
        self.x_copy(c).wait_recv()

    def total(self, c, rows):
        return self.x_out[c, rows].astype(WIDE) + self.x_in[self.turn % 2, c, rows].astype(WIDE)


def iota(shape, dim):
    return lax.broadcasted_iota(jnp.int32, shape, dim)


def fold(rows):
    return rows.reshape(rows.shape[0] // 8, 8, rows.shape[1]).sum(axis=0)


def gelu_and_slope(v):
    square = v * v
    t = jnp.tanh(0.7978845608 * (v + 0.044715 * v * square))
    half = 0.5 * (1.0 + t)
    slope = half + 0.5 * v * (1.0 - t * t) * (0.7978845608 * (1.0 + 0.134145 * square))
    return v * half, slope


def exact(left, right, dims=(1, 0)):
    return lax.dot_general(
        left,
        right,
        (((dims[0],), (dims[1],)), ((), ())),
        preferred_element_type=WIDE,
        precision=PRECISE,
    )


def dense(block):
    n = block.shape[0]
    rest = jnp.concatenate([block[0 : n // 2, 128:], block[n // 2 :, 128:]], axis=1)
    return jnp.concatenate([block[:, 0:128], rest], axis=0)


def undense(block):
    n = block.shape[0] * 2 // 3
    rest = jnp.concatenate([block[n:, 0:64], block[n:, 64:128]], axis=0)
    return jnp.concatenate([block[0:n], rest], axis=1)


def loop(count, body):
    lax.fori_loop(0, count, lambda i, carry: (body(i), carry)[1], 0)


def layer_kernel(count, names, *refs):
    r = types.SimpleNamespace(**dict(zip(names, refs)))
    s, h, z, y, x, core = place()
    rows, width = r.inputs_hbm.shape
    near = r.w_query.shape[1]
    heads = near // HEAD_DIM
    feed = r.w_up.shape[1]
    size = rows // CHUNKS
    half = size // 2
    step = 32
    lines = count // 2
    two = 2 * LAND
    scale = HEAD_DIM**-0.5
    chunk_rows = lambda c: pl.ds(pl.multiple_of(c * size, size), size)
    my_rows = lambda c: pl.ds(pl.multiple_of(c * size + core * half, half), half)
    everyone = along_seq(count)
    before, after = (lax.rem(s + count - 1, count), h), (lax.rem(s + 1, count), h)

    flat = lambda ref: ref[...].reshape(1, ref.shape[0])
    bias_query, bias_value, bias_out = flat(r.bias_query), flat(r.bias_value), flat(r.bias_out)
    bias_up, bias_down = flat(r.bias_up), flat(r.bias_down)
    gain_one, bias_one, gain_two, bias_two = (
        flat(r.gain_one), flat(r.bias_one), flat(r.gain_two), flat(r.bias_two)
    )

    def gather(k, shard, full, lo, hi):
        return Gather(
            count, shard, full, slice(lo, hi), r.g_own.at[k], r.g_zs.at[k], r.g_zr.at[k], r.g_ys.at[k], r.g_yr.at[k]
        )

    def scatter(k, terms, y_buf, pair, z_buf):
        return Scatter(
            count, terms, y_buf, pair, z_buf, r.s_ys.at[k], r.s_yr.at[k], r.s_zs.at[k], r.s_zr.at[k]
        )

    gather_qk = gather(0, r.packed, r.w_near, 0, 2 * near)
    gather_vo = gather(1, r.packed, r.w_near, 2 * near, 4 * near)
    third = feed // 3
    ups = [gather(2 + k, r.w_up, r.full_up, k * third, (k + 1) * third) for k in range(3)]
    downs = [gather(5 + k, r.w_down, r.full_down, k * third, (k + 1) * third) for k in range(3)]
    gathers = [gather_qk, gather_vo] + ups + downs
    scatter_out = scatter(0, r.t_out, r.yb_out, r.pr_out, r.zb_out)
    scatter_up = scatter(1, r.t_up, r.yb_up, r.pr_up, r.zb_up)
    scatter_down = scatter(2, r.t_down, r.yb_down, r.pr_down, r.zb_down)
    scatter_qk = scatter(3, r.t_qk, r.yb_qk, r.pr_qk, r.zb_qk)
    scatter_v = scatter(4, r.t_v, r.yb_v, r.pr_v, r.zb_v)
    scatters = [scatter_out, scatter_up, scatter_down, scatter_qk, scatter_v]
    correction = HeadSum(0, r.corr_terms, r.corr_core, r.corr_out, r.corr_in, r.corr_sems)
    sums = [HeadSum(k, r.terms, r.core_in, r.x_out, r.x_in, r.h_sems) for k in range(4)]
    landmarks = Spread(count, r.land_part, r.e_s.at[0], r.e_r.at[0])
    numer_swap = Swap(count, r.numer_out, r.numer_in, r.e_s.at[1], r.e_r.at[1])
    kernel_spread = Spread(count, r.kernel_v, r.e_s.at[2], r.e_r.at[2])
    mixing_spread = Spread(count, r.mix_part, r.e_s.at[3], r.e_r.at[3])
    kland_spread = Spread(count, r.kland_part, r.e_s.at[4], r.e_r.at[4])
    qland_spread = Spread(count, r.qland_part, r.e_s.at[5], r.e_r.at[5])
    vector_spread = Spread(count, r.vector_part, r.e_s.at[6], r.e_r.at[6])
    small_spread = Spread(count, r.small_part, r.e_s.at[7], r.e_r.at[7])
    spreads = [
        landmarks, numer_swap, kernel_spread, mixing_spread, kland_spread, qland_spread, vector_spread, small_spread,
    ]

    def rim(k, ext):
        first = remote(
            ext.at[pl.ds(REACH, REACH)], ext.at[pl.ds(REACH + rows, REACH)], r.rim_s.at[k, 0], r.rim_r.at[k, 0], before
        )
        last = remote(
            ext.at[pl.ds(rows, REACH)], ext.at[pl.ds(0, REACH)], r.rim_s.at[k, 1], r.rim_r.at[k, 1], after
        )
        return [first, last]

    rims = [rim(0, r.value_ext), rim(1, r.grad_ext)]

    def share(k, ref, c):
        return remote(
            ref.at[my_rows(c)], ref.at[my_rows(c)], r.share_s.at[k, c], r.share_r.at[k, c], core_of_chip()
        )

    load_inputs = pltpu.make_async_copy(r.inputs_hbm, r.inputs, r.io.at[0])
    load_cotangent = pltpu.make_async_copy(r.cotangent_hbm, r.cotangent, r.io.at[1])
    stores = [
        pltpu.make_async_copy(ref, out, r.io.at[2 + k])
        for k, (ref, out) in enumerate(
            (
                (r.output, r.output_hbm),
                (r.cotangent, r.grad_inputs_hbm),
                (r.grad_w_out, r.grad_w_out_hbm),
                (r.grad_w_up, r.grad_w_up_hbm),
                (r.grad_w_down, r.grad_w_down_hbm),
                (r.grad_near, r.grad_near_hbm),
            )
        )
    ]
    store_output, store_grad_inputs, store_out, store_up, store_down, store_near = stores
    vector_core = remote(
        r.vector_sum.at[0], r.vector_sum.at[1], r.core_s.at[0], r.core_r.at[0], core_of_chip()
    )

    met = [core_of_chip(), x_neighbour()] + everyone
    greet(met)
    load_inputs.start()
    r.packed[:, 0:near] = r.w_query[...]
    r.packed[:, near : 2 * near] = r.w_key[...]
    r.packed[:, 2 * near : 3 * near] = r.w_value[...]
    r.packed[:, 3 * near : 4 * near] = r.w_out[...]
    ends = jnp.where(s == 0, r.lengths[0], jnp.where(s == count - 1, r.lengths[2], 0))
    edge_start = jnp.where(s == 0, 0, rows - ends)
    edge_end = edge_start + ends
    edge_count = ends // LAND
    mid_count = r.lengths[1] // LAND
    mid_first = s * rows - r.lengths[0]
    first_slot = jnp.maximum(mid_first, 0) // mid_count
    item_edge = jnp.where(s == 0, ends, jnp.where(s == count - 1, rows - ends, -1))

    def members():
        token, lane = iota((rows, two), 0), iota((rows, two), 1)
        mid = lane < LAND
        at_edge = (token >= edge_start) & (token < edge_end)
        start = jnp.where(mid, (first_slot + lane) * mid_count - mid_first, (lane - LAND) * edge_count + edge_start)
        length = jnp.where(mid, mid_count, edge_count)
        inside = (token >= start) & (token < start + length)
        belongs = jnp.where(mid, jnp.where(at_edge, 0.0, 1.0), jnp.where(at_edge, 1.0, 0.0))
        r.member[...] = jnp.where(inside, belongs, 0.0).astype(LOW)

    members()
    greeted(met)
    gather_qk.start()
    gather_vo.start()
    load_cotangent.start()
    r.small_part[s] = jnp.zeros((8, PAD), WIDE)
    head_lane = iota((8, PAD), 1) // HEAD_DIM
    masks = [(head_lane == k).astype(WIDE)[0:1] for k in range(heads)]
    masks_low = [m[:, :near].astype(LOW) for m in masks]

    def spread_heads(ref, block):
        for k in range(heads):
            ref[k * two : (k + 1) * two, :] = block * masks_low[k]

    def own_heads(wide_rows, group, lanes):
        return sum(
            wide_rows[k * group : (k + 1) * group, :] * masks[k][:, :lanes] for k in range(heads)
        )

    def bands(ref, flipped):
        token, lane = iota((BLOCK, 2 * SPAN), 0), iota((BLOCK, 2 * SPAN), 1)
        upper = lane < SPAN
        offset = jnp.where(upper, lane, lane - SPAN) - token
        for k in range(heads):
            band = jnp.zeros((BLOCK, 2 * SPAN), WIDE)
            for j in range(KERNEL):
                at = KERNEL - 1 - j if flipped else j
                band = jnp.where(offset == at, r.conv_taps[k, j], band)
            high = band.astype(LOW).astype(WIDE)
            ref[k * BLOCK : (k + 1) * BLOCK, :] = jnp.where(upper, high, band - high).astype(LOW)

    bands(r.band, False)
    bands(r.band_back, True)

    def window(ext, b):
        taken = ext[pl.ds(pl.multiple_of(b * BLOCK, BLOCK), SPAN), :]
        start = b * BLOCK
        left_out = (start == item_edge) | ((s == 0) & (start == 0))
        right_out = (start + BLOCK == item_edge) | ((s == count - 1) & (start + BLOCK == rows))
        row = iota((SPAN, taken.shape[1]), 0)
        keep = jnp.where(
            row < REACH,
            jnp.where(left_out, 0.0, 1.0),
            jnp.where(row >= REACH + BLOCK, jnp.where(right_out, 0.0, 1.0), 1.0),
        )
        return taken * keep.astype(LOW)

    def convolve(band, taken):
        return own_heads(matmul_low(band[...], jnp.concatenate([taken, taken], axis=0)), BLOCK, taken.shape[1])

    gather_qk.forward()
    gather_vo.forward()
    load_inputs.wait()
    gather_qk.finish()

    def project_qk(c):
        at = chunk_rows(c)
        both = matmul_low(r.inputs[at], r.w_near[:, :, 0 : 2 * near].reshape(width, 2 * near))
        r.queries[at] = (both[:, :near] + bias_query).astype(LOW)
        r.keys[at] = both[:, near:].astype(LOW)

    loop(CHUNKS, project_qk)
    query_sums = across(r.member[...], r.queries[...])
    key_sums = across(r.member[...], r.keys[...])
    mid_scale = 1.0 / mid_count.astype(WIDE)
    edge_scale = 1.0 / jnp.maximum(edge_count, 1).astype(WIDE)
    border = jnp.concatenate([query_sums[0:BORDER], key_sums[0:BORDER]], axis=0) * mid_scale
    r.land_part[s] = dense(border).astype(LOW)
    landmarks.start()
    ups[0].start()
    ups[1].start()
    r.query_land[LAND:two] = (query_sums[LAND:two] * edge_scale).astype(LOW)
    r.key_land[LAND:two] = (key_sums[LAND:two] * edge_scale).astype(LOW)

    gather_vo.finish()

    def project_v(c):
        at = pl.ds(pl.multiple_of(REACH + c * size, REACH), size)
        values = matmul_low(r.inputs[chunk_rows(c)], r.w_near[:, :, 2 * near : 2 * near + PAD].reshape(width, PAD))
        values = values[:, :near] + bias_value
        r.value_ext[at, 0:near] = values.astype(LOW)
        r.value_ext[at, near:PAD] = jnp.zeros((size, PAD - near), LOW)

    loop(CHUNKS, project_v)
    for copy in rims[0]:
        copy.start()
    r.out_rows[...] = r.w_near[:, :, 3 * near :].reshape(width, near)

    def convolve_values(b):
        r.conv[pl.ds(pl.multiple_of(b * BLOCK, BLOCK), BLOCK), :] = convolve(
            r.band, window(r.value_ext, b)
        )[:, :near]

    blocks = rows // BLOCK
    loop(blocks - 2, lambda b: convolve_values(b + 1))

    landmarks.finish()
    lane = iota((LAND, count * BORDER), 1)
    owner = lane // BORDER
    starts = jnp.zeros((LAND, count * BORDER), jnp.int32)
    for d in range(count):
        starts = jnp.where(owner == d, jnp.maximum(d * rows - r.lengths[0], 0) // mid_count, starts)
    put = (iota((LAND, count * BORDER), 0) == starts + lane - owner * BORDER).astype(LOW)
    borders = [undense(r.land_part[d]) for d in range(count)]
    r.query_land[0:LAND] = matmul_low(put, jnp.concatenate([b[0:BORDER] for b in borders], axis=0)).astype(LOW)
    r.key_land[0:LAND] = matmul_low(put, jnp.concatenate([b[BORDER:] for b in borders], axis=0)).astype(LOW)
    spread_heads(r.query_heads, r.query_land[...])
    spread_heads(r.key_heads, r.key_land[...])

    own_values = lambda: r.value_ext[pl.ds(REACH, rows), :]

    def score_b(c):
        at = chunk_rows(c)
        r.weights_b[:, at] = against(r.query_heads[...], r.keys[at]) * scale

    def attend_b(g):
        at = pl.ds(pl.multiple_of(g * LAND, LAND), LAND)
        token = iota((LAND, rows), 1)
        at_edge = jnp.where((token >= edge_start) & (token < edge_end), 1.0, 0.0)
        member = jnp.where(lax.rem(g, 2) == 1, at_edge, 1.0 - at_edge)
        scores = jnp.where(member > 0.5, r.weights_b[at], MASKED)
        largest = jnp.max(scores, axis=1, keepdims=True)
        weights = jnp.exp(scores - largest) * member
        r.weights_b[at] = weights
        r.weights_b_low[at] = weights.astype(LOW)
        r.max_b[at] = largest
        r.total_b[at] = jnp.sum(weights, axis=1, keepdims=True)

    loop(CHUNKS, score_b)
    loop(2 * heads, attend_b)
    numer = own_heads(matmul_low(r.weights_b_low[...], own_values()), two, PAD)
    lane = iota((two, PAD), 1)
    for k in range(heads):
        numer = jnp.where(lane == near + k, r.total_b[k * two : (k + 1) * two], numer)
        numer = jnp.where(lane == near + heads + k, r.max_b[k * two : (k + 1) * two], numer)
    r.numer_out[...] = numer[0:LAND].reshape(count, LAND // count, PAD)
    numer_swap.start()
    ups[2].start()
    for copy in rims[0]:
        copy.wait_recv()
    loop(2, lambda b: convolve_values(b * (blocks - 1)))

    def wide_heads(stats, base):
        lane = iota(stats.shape, 1)
        out = stats
        for k in range(heads):
            out = jnp.where(lane // HEAD_DIM == k, stats[:, base + k : base + k + 1], out)
        return out

    edge = numer[LAND:two]
    edge_totals = wide_heads(edge, near)
    edge_totals = jnp.where(edge_totals > 0.0, edge_totals, 1.0)
    r.kernel_edge[...] = jnp.where(iota(edge.shape, 1) < near, edge / edge_totals, 0.0)

    pairs = [(k, g) for k in range(heads) for g in range(2)]
    identity = (iota((LAND, LAND), 0) == iota((LAND, LAND), 1)).astype(WIDE)
    group = lambda g: slice(g * LAND, (g + 1) * LAND)

    def first_inverse(k, g, i):
        lands = r.query_heads[k * two + g * LAND : k * two + (g + 1) * LAND, :]
        scores = against(lands, r.key_land[group(g), :]) * scale
        weights = jnp.exp(scores - jnp.max(scores, axis=1, keepdims=True))
        weights = weights / jnp.sum(weights, axis=1, keepdims=True)
        r.land_kernel[i] = weights
        return weights.T / jnp.sum(weights * weights)

    def invert(it, inverses):
        kernels = [r.land_kernel[i] for i in range(len(pairs))]
        products = [exact(a, b) for a, b in zip(kernels, inverses)]
        for i, (a, p) in enumerate(zip(inverses, products)):
            r.befores[it, i] = a
            r.products[it, i] = p
        nested = [15.0 * identity - exact(p, 7.0 * identity - p) for p in products]
        nested = [13.0 * identity - exact(p, n) for p, n in zip(products, nested)]
        return tuple(0.25 * exact(a, n) for a, n in zip(inverses, nested))

    inverses = tuple(first_inverse(k, g, i) for i, (k, g) in enumerate(pairs))
    inverses = lax.fori_loop(0, PINV_STEPS // 2, invert, inverses)

    ups[0].forward()
    ups[1].forward()

    numer_swap.finish()
    parts = [r.numer_in[d] for d in range(count)]
    largest = functools.reduce(jnp.maximum, [wide_heads(p, near + heads) for p in parts])
    lane = iota(largest.shape, 1)
    joined = jnp.zeros_like(largest)
    totals = jnp.zeros_like(largest)
    for p in parts:
        weight = jnp.exp(wide_heads(p, near + heads) - largest)
        joined = joined + jnp.where(lane < near, p * weight, 0.0)
        totals = totals + jnp.where(lane < near, wide_heads(p, near) * weight, 0.0)
    joined = jnp.where(lane < near, joined / jnp.where(lane < near, totals, 1.0), 0.0)
    for k in range(heads):
        joined = jnp.where(lane == near + k, totals[:, k * HEAD_DIM : k * HEAD_DIM + 1], joined)
        joined = jnp.where(
            lane == near + heads + k, largest[:, k * HEAD_DIM : k * HEAD_DIM + 1], joined
        )
    r.kernel_v[s] = joined
    kernel_spread.start()
    for piece in downs:
        piece.start()
    inverses = lax.fori_loop(PINV_STEPS // 2, PINV_STEPS, invert, inverses)
    for i, inverse in enumerate(inverses):
        r.inverse[i] = inverse

    def attend_f(c):
        at = pl.ds(pl.multiple_of(c * half, half), half)
        scores = against(r.queries[at], r.key_heads[...]) * scale
        token, lane = iota((half, two), 0) + c * half, iota((half, two), 1)
        at_edge = (token >= edge_start) & (token < edge_end)
        member = jnp.where(lane < LAND, jnp.where(at_edge, 0.0, 1.0), jnp.where(at_edge, 1.0, 0.0))
        for k in range(heads):
            own = jnp.where(member > 0.5, scores[:, k * two : (k + 1) * two], MASKED)
            weights = jnp.exp(own - jnp.max(own, axis=1, keepdims=True))
            r.weights_f[at, k * two : (k + 1) * two] = weights / jnp.sum(weights, axis=1, keepdims=True)

    loop(rows // half, attend_f)
    kernel_spread.finish()
    kernel_mid = r.kernel_v[...].reshape(LAND, PAD)
    kernel_of = lambda g: kernel_mid if g == 0 else r.kernel_edge[...]
    for g in range(2):
        mixed = jnp.zeros((LAND, PAD), WIDE)
        for i, (k, own) in enumerate(pairs):
            if own == g:
                mixed = mixed + exact(r.inverse[i], kernel_of(g)) * masks[k]
        r.mixing[group(g), :] = mixed[:, :near].astype(LOW)
    spread_heads(r.mixing_heads, r.mixing[...])
    ups[2].forward()

    def project_out(c):
        at = chunk_rows(c)
        attended = matmul_low(r.weights_f[at].astype(LOW), r.mixing_heads[...])
        r.mixed[at] = (attended + r.conv[at]).astype(LOW)
        sums[0].offer(c, against(r.mixed[at], r.out_rows[...]).astype(LOW))

    loop(CHUNKS, project_out)
    loop(CHUNKS, sums[0].pair_up)
    downs[0].forward()

    def prepare(it):
        many = range(len(pairs))
        befores = [r.befores[it, i] for i in many]
        products = [r.products[it, i] for i in many]
        squares = [exact(p, p) for p in products]
        firsts = [exact(a, p) for a, p in zip(befores, products)]
        cubes = [exact(p, q) for p, q in zip(products, squares)]
        seconds = [exact(t, p) for t, p in zip(firsts, products)]
        for i in many:
            p, q, c = products[i].T, squares[i].T, cubes[i].T
            r.uppers[it, i, :, 0:LAND] = 3.25 * identity - 3.75 * p + 1.75 * q - 0.25 * c
            r.uppers[it, i, :, LAND:two] = 1.75 * p - 3.75 * identity - 0.25 * q
            r.uppers[it, i, :, two:] = 1.75 * identity - 0.25 * p
            r.lowers[it, i, :, 0:LAND] = befores[i].T
            r.lowers[it, i, :, LAND:two] = firsts[i].T
            r.lowers[it, i, :, two:] = -0.25 * seconds[i].T

    loop(PINV_STEPS, prepare)
    for i in range(len(pairs)):
        r.turned_kernel[i] = r.land_kernel[i].T
    r.acc[...] = jnp.zeros_like(r.acc)
    for piece in ups:
        piece.finish()
    load_cotangent.wait()
    pieces = lambda body: loop(half // step, lambda i: body(pl.multiple_of(i * step, step)))

    def norm_first(c):
        def piece(i):
            at = pl.ds(pl.multiple_of(c * size + core * half + i, step), step)
            kept = pl.ds(pl.multiple_of(c * half + i, step), step)
            pre = r.inputs[at].astype(WIDE) + sums[0].total(c, pl.ds(i, step)) + bias_out
            normed, inv = normalize(pre)
            r.norm_one[kept] = normed
            r.inv_one[kept] = inv
            r.hidden[at] = (normed * gain_one + bias_one).astype(LOW)

        sums[0].arrived(c)
        pieces(piece)
        share(0, r.hidden, c).start()

    def lift(c):
        share(0, r.hidden, c).wait_recv()
        at = chunk_rows(c)
        r.tmp[...] = matmul_low(r.hidden[at], r.full_up[...].reshape(width, feed))

        def curve(i):
            to = pl.ds(pl.multiple_of(c * size + i * step, step), step)
            value, grade = gelu_and_slope(r.tmp[pl.ds(pl.multiple_of(i * step, step), step)] + bias_up)
            r.active[to] = value.astype(LOW)
            r.slope[to] = grade.astype(LOW)

        loop(size // step, curve)

    def lower(c):
        at = chunk_rows(c)
        sums[1].offer(c, against(r.active[at], r.full_down[...].reshape(width, feed)).astype(LOW))

    def behind(c, total):
        @pl.when(c > 0)
        def _():
            total.pair_up(c - 1)

    def feed_forward(c):
        norm_first(c)
        behind(c, sums[1])
        lift(c)

        @pl.when(c == 0)
        def _():
            for piece in downs[1:]:
                piece.forward()
            for piece in downs:
                piece.finish()

        lower(c)

    loop(CHUNKS, feed_forward)
    sums[1].pair_up(CHUNKS - 1)

    def feed_back(c):
        def piece(i):
            at = pl.ds(pl.multiple_of(c * size + core * half + i, step), step)
            kept = pl.ds(pl.multiple_of(c * half + i, step), step)
            pre = r.norm_one[kept] * gain_one + bias_one + sums[1].total(c, pl.ds(i, step)) + bias_down
            normed, inv = normalize(pre)
            r.output[at] = (normed * gain_two + bias_two).astype(LOW)
            grad = r.cotangent[at].astype(WIDE)
            back = norm_back(grad * gain_two, normed, inv)
            r.wide_grad[kept] = back
            r.grad_two[at] = back.astype(LOW)
            r.acc[0] += fold(grad * normed)
            r.acc[1] += fold(grad)
            r.acc[2] += fold(back)

        sums[1].arrived(c)
        pieces(piece)
        share(1, r.grad_two, c).start()
        share(2, r.output, c).start()
        behind(c, sums[2])
        share(1, r.grad_two, c).wait_recv()
        at = chunk_rows(c)
        r.tmp[...] = matmul_low(r.grad_two[at], r.full_down[...].reshape(width, feed))

        def curve(i):
            to = pl.ds(pl.multiple_of(c * size + i * step, step), step)
            value = r.tmp[pl.ds(pl.multiple_of(i * step, step), step)] * r.slope[to].astype(WIDE)
            r.grad_lift[to] = value.astype(LOW)
            r.acc[6] += fold(value)

        loop(size // step, curve)
        sums[2].offer(c, against(r.grad_lift[at], r.full_up[...].reshape(width, feed)).astype(LOW))

    loop(CHUNKS, feed_back)
    sums[2].pair_up(CHUNKS - 1)

    scatter_down.fill(r.grad_two[...], r.active[...])
    scatter_down.start()
    r.mix_grad[...] = jnp.zeros_like(r.mix_grad)
    r.kland_grad[...] = jnp.zeros_like(r.kland_grad)

    def mix_back(c):
        def piece(i):
            at = pl.ds(pl.multiple_of(c * size + core * half + i, step), step)
            kept = pl.ds(pl.multiple_of(c * half + i, step), step)
            normed = r.norm_one[kept]
            grad = r.wide_grad[kept] + sums[2].total(c, pl.ds(i, step))
            back = norm_back(grad * gain_one, normed, r.inv_one[kept])
            r.wide_grad[kept] = back
            r.grad_one[at] = back.astype(LOW)
            r.acc[3] += fold(grad * normed)
            r.acc[4] += fold(grad)
            r.acc[5] += fold(back)

        sums[2].arrived(c)
        pieces(piece)
        share(3, r.grad_one, c).start()
        share(3, r.grad_one, c).wait_recv()
        at = chunk_rows(c)
        grad = matmul_low(r.grad_one[at], r.out_rows[...]).astype(LOW)
        r.grad_ext[pl.ds(pl.multiple_of(REACH + c * size, REACH), size)] = grad
        weights = r.weights_f[at]
        weighted = weights * against(grad, r.mixing_heads[...])
        scores = []
        for k in range(heads):
            own = slice(k * two, (k + 1) * two)
            scores.append(weighted[:, own] - weights[:, own] * jnp.sum(weighted[:, own], axis=1, keepdims=True))
        scores = jnp.concatenate(scores, axis=1).astype(LOW)
        r.grad_query[at] = matmul_low(scores, r.key_heads[...]) * scale
        r.mix_grad[...] += across(weights.astype(LOW), grad)
        r.kland_grad[...] += across(scores, r.queries[at])

        @pl.when(c == 1)
        def _():
            scatter_up.fill(r.hidden[...], r.grad_lift[...])

        @pl.when(c == 2)
        def _():
            scatter_down.forward(1, 2)

    loop(CHUNKS, mix_back)
    mix_grad = own_heads(r.mix_grad[...], two, near)
    kland_grad = own_heads(r.kland_grad[...], two, near) * scale
    r.mix_part[s] = dense(mix_grad[0:LAND]).astype(LOW)
    r.kland_part[s] = dense(kland_grad[0:LAND]).astype(LOW)
    mixing_spread.start()
    for copy in rims[1]:
        copy.start()

    def convolve_back(b):
        at = pl.ds(pl.multiple_of(b * BLOCK, BLOCK), BLOCK)
        r.conv[at] = convolve(r.band_back, window(r.grad_ext, b))

    scatter_out.fill_dense(r.grad_one[...], r.mixed[...])
    scatter_out.start()
    scatter_up.start(0, 1)
    loop(blocks - 2, lambda b: convolve_back(b + 1))
    for copy in rims[1]:
        copy.wait_recv()
    loop(2, lambda b: convolve_back(b * (blocks - 1)))
    scatter_down.forward(2)

    mixing_spread.finish()
    over_seq = lambda ref: undense(functools.reduce(jnp.add, [ref[d].astype(WIDE) for d in range(count)]))
    mix_grads = [over_seq(r.mix_part), mix_grad[LAND:two]]
    stats = r.kernel_v[...].reshape(LAND, PAD)
    mid_totals = wide_heads(stats, near)[:, :near]
    divisors = [mid_totals, edge_totals[:, :near]]
    inverse_grads = []
    for i, (k, g) in enumerate(pairs):
        inverse_grads.append(
            exact(mix_grads[g] * masks[k][:, :near], kernel_of(g)[:, :near], (1, 1))
        )
    shrink = [
        jnp.exp(r.max_b[k * two : k * two + LAND] - stats[:, near + heads + k : near + heads + k + 1])
        for k in range(heads)
    ]
    for g in range(2):
        grad = jnp.zeros((LAND, near), WIDE)
        for i, (k, own) in enumerate(pairs):
            if own == g:
                grad = grad + exact(r.inverse[i], mix_grads[g], (0, 0)) * masks[k][:, :near]
        grad = grad / divisors[g]
        lost = grad * kernel_of(g)[:, :near]
        for k in range(heads):
            at = slice(k * two + g * LAND, k * two + (g + 1) * LAND)
            factor = shrink[k] if g == 0 else 1.0
            r.numer_heads[at] = (grad * factor * masks[k][:, :near]).astype(LOW)
            r.total_grad[at] = -jnp.sum(lost * masks[k][:, :near], axis=1, keepdims=True) * factor

    def back_b(c):
        at = chunk_rows(c)
        values = r.value_ext[pl.ds(pl.multiple_of(REACH + c * size, REACH), size), 0:near]
        grad = against(r.numer_heads[...], values) + r.total_grad[...]
        r.scores_b[:, at] = (r.weights_b[:, at] * grad).astype(LOW)

    loop(CHUNKS, back_b)
    qland_grad = own_heads(matmul_low(r.scores_b[...], r.keys[...]), two, near) * scale
    r.qland_part[s] = dense(qland_grad[0:LAND]).astype(LOW)
    qland_spread.start()
    kland_spread.start()
    scatter_up.start(1)

    def keys_values(c):
        at = chunk_rows(c)
        r.grad_key[at] = across(r.scores_b[:, at], r.query_heads[...]) * scale
        values = across(r.weights_b_low[:, at], r.numer_heads[...]) + r.conv[at]
        r.near_grads[at, 0:near] = r.grad_query[at].astype(LOW)
        r.near_grads[at, near : 2 * near] = r.grad_key[at].astype(LOW)
        r.near_grads[at, 2 * near : 3 * near] = values.astype(LOW)
        terms = against(r.near_grads[at], r.w_near[:, :, 0 : 3 * near].reshape(width, 3 * near))
        behind(c, sums[3])
        sums[3].offer(c, terms.astype(LOW))
        return jnp.sum(values, axis=0, keepdims=True)

    value_bias = lax.fori_loop(
        0, CHUNKS, lambda c, total: total + keys_values(c), jnp.zeros((1, near), WIDE)
    )
    sums[3].pair_up(CHUNKS - 1)
    scatter_v.fill_dense(r.inputs[...], r.near_grads[:, 2 * near : 3 * near])
    scatter_v.start()

    def invert_back(i, carry):
        it = PINV_STEPS - 1 - i
        grads, kernel_grads = carry
        many = range(len(pairs))
        wides = [exact(grads[p], r.uppers[it, p]) for p in many]
        product_grads = [
            exact(r.lowers[it, p], jnp.concatenate([w[:, LAND:two], w[:, two:], grads[p]], axis=0))
            for p, w in enumerate(wides)
        ]
        kernel_grads = [
            old + exact(grad, r.lowers[it, p, :, 0:LAND])
            for p, (old, grad) in enumerate(zip(kernel_grads, product_grads))
        ]
        grads = [wides[p][:, 0:LAND] + exact(r.turned_kernel[p], product_grads[p]) for p in many]
        return tuple(grads), tuple(kernel_grads)

    scatter_up.forward(1, 2)
    scatter_out.forward()
    zeros = tuple(jnp.zeros((LAND, LAND), WIDE) for _ in pairs)
    grads, kernel_grads = lax.fori_loop(0, PINV_STEPS, invert_back, (tuple(inverse_grads), zeros))
    qland_a = [jnp.zeros((LAND, near), WIDE)] * 2
    kland_a = [jnp.zeros((LAND, near), WIDE)] * 2
    for i, (k, g) in enumerate(pairs):
        kernel = r.land_kernel[i]
        turned = grads[i].T
        squares = jnp.sum(kernel * kernel)
        grad = kernel_grads[i] + turned / squares - kernel * (2.0 * jnp.sum(turned * kernel) / (squares * squares))
        grad = kernel * (grad - jnp.sum(kernel * grad, axis=1, keepdims=True)) * scale
        mask = masks[k][:, :near]
        qland_a[g] = qland_a[g] + exact(grad, r.key_land[group(g)].astype(WIDE)) * mask
        kland_a[g] = kland_a[g] + exact(grad, r.query_land[group(g)].astype(WIDE), (0, 0)) * mask

    scatter_up.forward(2)

    kland_spread.finish()
    qland_spread.finish()
    pick = (iota((LAND, LAND), 1) == iota((LAND, LAND), 0) + first_slot).astype(WIDE)

    def slot_grads(mid, edge):
        return jnp.concatenate([exact(pick, mid * mid_scale), edge * edge_scale], axis=0)

    def parted(both):
        high = both.astype(LOW)
        return jnp.concatenate([high, (both - high.astype(WIDE)).astype(LOW)], axis=0)

    slot_q = slot_grads(qland_a[0] + over_seq(r.qland_part), qland_a[1] + qland_grad[LAND:two])
    slot_k = slot_grads(kland_a[0] + over_seq(r.kland_part), kland_a[1] + kland_grad[LAND:two])
    r.slot_q[...] = parted(slot_q)
    r.slot_k[...] = parted(slot_k)
    r.slot_both[:, 0:near] = r.slot_q[0:two]
    r.slot_both[:, near:] = r.slot_k[0:two]
    slot_terms = against(r.slot_both[...], r.w_near[:, :, 0 : 2 * near].reshape(width, 2 * near))
    correction.offer(0, slot_terms.astype(LOW))

    def add_slots(c):
        at = chunk_rows(c)
        member = jnp.concatenate([r.member[at]] * 2, axis=1)
        queries = r.grad_query[at] + matmul_low(member, r.slot_q[...])
        keys = r.grad_key[at] + matmul_low(member, r.slot_k[...])
        r.near_grads[at, 0:near] = queries.astype(LOW)
        r.near_grads[at, near : 2 * near] = keys.astype(LOW)
        return jnp.sum(queries, axis=0, keepdims=True)

    query_bias = lax.fori_loop(
        0, CHUNKS, lambda c, total: total + add_slots(c), jnp.zeros((1, near), WIDE)
    )
    correction.pair_up(0)
    scatter_qk.fill(r.inputs[...], r.near_grads[:, 0 : 2 * near])
    scatter_qk.start()
    scatter_v.forward()

    r.tap_grad[...] = jnp.zeros_like(r.tap_grad)

    def tap_products(b):
        own = r.grad_ext[pl.ds(pl.multiple_of(b * BLOCK + REACH, REACH), BLOCK), :]
        own = jnp.concatenate([own * m for m in masks_low], axis=0)
        r.tap_grad[:, 0:SPAN] += against(own, window(r.value_ext, b)[:, :near])

    loop(blocks, tap_products)
    token = lax.rem(iota((heads * BLOCK, 128), 0), BLOCK)
    slanted = r.tap_grad[...]
    for bit in range(6):
        moved = pltpu.roll(slanted, 128 - (1 << bit), 1)
        slanted = jnp.where(lax.rem(token // (1 << bit), 2) == 1, moved, slanted)
    for k in range(heads):
        r.small_part[s, 2 + k : 3 + k, 0:128] = jnp.sum(
            slanted[k * BLOCK : (k + 1) * BLOCK], axis=0, keepdims=True
        )
    r.small_part[s, 0:1, 0:near] = query_bias
    r.small_part[s, 1:2, 0:near] = value_bias
    for k in range(7):
        r.vector_part[s, k : k + 1] = jnp.sum(r.acc[k], axis=0, keepdims=True)
    r.vector_part[s, 7:8] = jnp.zeros((1, width), WIDE)
    small_spread.start()
    vector_spread.start()

    def settle_output(c):
        share(2, r.output, c).wait_recv()

    loop(CHUNKS, settle_output)
    store_output.start()
    r.grad_w_down[...] = scatter_down.finish()
    store_down.start()
    r.grad_w_up[...] = scatter_up.finish()
    store_up.start()
    r.grad_w_out[...] = undense(scatter_out.finish())
    store_out.start()
    r.grad_near[2] = undense(scatter_v.finish())
    scatter_qk.forward()
    vector_spread.finish()
    r.vector_sum[0] = functools.reduce(jnp.add, [r.vector_part[d] for d in range(count)])
    vector_core.start()

    def total_inputs(c):
        def piece(i):
            kept = pl.ds(pl.multiple_of(c * half + i, step), step)
            r.wide_grad[kept] = r.wide_grad[kept] + sums[3].total(c, pl.ds(i, step))

        sums[3].arrived(c)
        pieces(piece)

    loop(CHUNKS, total_inputs)
    here = pl.ds(pl.multiple_of(core * LAND, LAND), LAND)
    share_slots = remote(
        r.corr_all.at[here], r.corr_all.at[here], r.corr_s.at[0], r.corr_r.at[0], core_of_chip()
    )
    correction.arrived(0)
    r.corr_all[here] = correction.total(0, pl.ds(0, LAND)).astype(LOW)
    share_slots.start()
    share_slots.wait_recv()

    def inputs_done(c):
        slots = matmul_low(r.member[my_rows(c)], r.corr_all[...])
        r.cotangent[my_rows(c)] = (r.wide_grad[pl.ds(pl.multiple_of(c * half, half), half)] + slots).astype(LOW)
        share(4, r.cotangent, c).start()

    loop(CHUNKS, inputs_done)
    near_total = scatter_qk.finish()
    for k in range(2):
        r.grad_near[k] = near_total[:, k * near : (k + 1) * near]
    store_near.start()
    vector_core.wait_recv()
    r.vectors[0:6] = r.vector_sum[0, 0:6] + r.vector_sum[1, 0:6]
    r.vectors[6:8] = r.vector_sum[0, 6:8]
    small_spread.finish()
    r.smalls[...] = functools.reduce(jnp.add, [r.small_part[d] for d in range(count)])

    def settle_inputs(c):
        share(4, r.cotangent, c).wait_recv()

    loop(CHUNKS, settle_inputs)
    store_grad_inputs.start()

    def settle(c):
        sums[3].core_copy(c).wait_send()
        sums[3].x_copy(c).wait_send()
        for k, ref in enumerate((r.hidden, r.grad_two, r.output, r.grad_one, r.cotangent)):
            share(k, ref, c).wait_send()

    loop(CHUNKS, settle)
    vector_core.wait_send()
    correction.core_copy(0).wait_send()
    correction.x_copy(0).wait_send()
    share_slots.wait_send()
    for copy in stores:
        copy.wait()
    for copy in rims[0] + rims[1]:
        copy.wait_send()
    for group_of in gathers + scatters + spreads:
        group_of.close()


def hand_out(
    output, grad_inputs, grad_out, grad_up, grad_down, grad_near, vectors, smalls,
    to_output, to_inputs, to_query, to_key, to_value, to_out, to_up, to_down,
    bias_query, bias_value, bias_out, bias_up, bias_down, gain_one, bias_one, gain_two, bias_two, taps, sems,
):
    rows = output.shape[0] // 4
    copies = []
    for k, (ref, to) in enumerate(((output, to_output), (grad_inputs, to_inputs))):
        for j in range(4):
            at = pl.ds(j * rows, rows)
            copies.append(pltpu.make_async_copy(ref.at[at], to.at[at], sems.at[k, j]))
    for k, (ref, to) in enumerate(
        (
            (grad_near.at[0], to_query), (grad_near.at[1], to_key), (grad_near.at[2], to_value),
            (grad_out, to_out), (grad_up, to_up), (grad_down, to_down),
        )
    ):
        copies.append(pltpu.make_async_copy(ref, to, sems.at[2 + k, 0]))
    for copy in copies:
        copy.start()
    for k, ref in enumerate((gain_two, bias_two, bias_down, gain_one, bias_one, bias_out, bias_up)):
        ref[...] = vectors[k : k + 1].reshape(ref.shape)
    for k, ref in enumerate((bias_query, bias_value)):
        ref[...] = smalls[k : k + 1, 0 : ref.shape[0]].reshape(ref.shape)
    taps[...] = smalls[2 : 2 + taps.shape[0], 0:KERNEL]
    for copy in copies:
        copy.wait()


def fused_body(
    inputs, cotangent, item_lengths, w_query, w_key, w_value, w_out, w_up, w_down, bias_query, bias_value,
    bias_out, bias_up, bias_down, gain_one, bias_one, gain_two, bias_two, conv_taps,
):
    count = lax.axis_size("seq")
    rows, width = inputs.shape
    near, feed, heads = w_query.shape[1], w_up.shape[1], conv_taps.shape[0]
    size, part, lines = rows // CHUNKS, width // count, count // 2
    half, two = size // 2, 2 * LAND
    low = lambda *shape: pltpu.VMEM(shape, LOW)
    wide = lambda *shape: pltpu.VMEM(shape, WIDE)
    sem = lambda *shape: pltpu.SemaphoreType.DMA(shape)
    vmem, smem = pl.BlockSpec(memory_space=pltpu.VMEM), pl.BlockSpec(memory_space=pltpu.SMEM)
    operands = dict(
        lengths=item_lengths, conv_taps=conv_taps,
        inputs_hbm=inputs, cotangent_hbm=cotangent,
        w_query=w_query, w_key=w_key, w_value=w_value, w_out=w_out, w_up=w_up, w_down=w_down,
        bias_query=bias_query, bias_value=bias_value,
        bias_out=bias_out, bias_up=bias_up, bias_down=bias_down,
        gain_one=gain_one, bias_one=bias_one, gain_two=gain_two, bias_two=bias_two,
    )
    outs = dict(
        output_hbm=((rows, width), LOW), grad_inputs_hbm=((rows, width), LOW),
        grad_w_out_hbm=((part, near), WIDE), grad_w_up_hbm=((part, feed), WIDE), grad_w_down_hbm=((part, feed), WIDE),
        grad_near_hbm=((3, part, near), WIDE), vectors=((8, width), WIDE), smalls=((8, PAD), WIDE),
    )
    scratch = dict(
        inputs=low(rows, width), cotangent=low(rows, width), output=low(rows, width),
        grad_w_out=wide(part, near), grad_w_up=wide(part, feed), grad_w_down=wide(part, feed),
        grad_near=wide(3, part, near), io=sem(8),
        packed=low(part, 4 * near), w_near=low(count, part, 4 * near), out_rows=low(width, near),
        full_up=low(count, part, feed), full_down=low(count, part, feed),
        member=low(rows, two), band=low(heads * BLOCK, 2 * SPAN), band_back=low(heads * BLOCK, 2 * SPAN),
        queries=low(rows, near), keys=low(rows, near), value_ext=low(rows + 2 * REACH, PAD),
        land_part=low(count, 3 * BORDER, 128), query_land=low(two, near), key_land=low(two, near),
        query_heads=low(heads * two, near), key_heads=low(heads * two, near),
        weights_b=wide(heads * two, rows), weights_b_low=low(heads * two, rows),
        max_b=wide(heads * two, 1), total_b=wide(heads * two, 1),
        numer_out=wide(count, LAND // count, PAD), numer_in=wide(count, LAND // count, PAD),
        kernel_v=wide(count, LAND // count, PAD), kernel_edge=wide(LAND, PAD),
        land_kernel=wide(2 * heads, LAND, LAND), inverse=wide(2 * heads, LAND, LAND),
        befores=wide(PINV_STEPS, 2 * heads, LAND, LAND), products=wide(PINV_STEPS, 2 * heads, LAND, LAND),
        uppers=wide(PINV_STEPS, 2 * heads, LAND, 3 * LAND), lowers=wide(PINV_STEPS, 2 * heads, LAND, 3 * LAND),
        turned_kernel=wide(2 * heads, LAND, LAND),
        weights_f=wide(rows, heads * two), conv=wide(rows, near),
        mixing=low(two, near), mixing_heads=low(heads * two, near), mixed=low(rows, near),
        terms=low(CHUNKS, size, width), core_in=low(CHUNKS, half, width),
        x_out=low(CHUNKS, half, width), x_in=low(2, CHUNKS, half, width),
        hidden=low(rows, width), active=low(rows, feed), slope=low(rows, feed),
        grad_two=low(rows, width), grad_lift=low(rows, feed), grad_one=low(rows, width),
        norm_one=wide(rows // 2, width), inv_one=wide(rows // 2, 1), wide_grad=wide(rows // 2, width),
        tmp=wide(size, feed), acc=wide(7, 8, width),
        grad_ext=low(rows + 2 * REACH, near), grad_query=wide(rows, near), grad_key=wide(rows, near),
        mix_grad=wide(heads * two, near), kland_grad=wide(heads * two, near),
        mix_part=low(count, 3 * LAND // 2, 128), kland_part=low(count, 3 * LAND // 2, 128),
        qland_part=low(count, 3 * LAND // 2, 128),
        tap_grad=wide(heads * BLOCK, 128), numer_heads=low(heads * two, near), total_grad=wide(heads * two, 1),
        scores_b=low(heads * two, rows), near_grads=low(rows, 3 * near),
        slot_q=low(2 * two, near), slot_k=low(2 * two, near), slot_both=low(two, 2 * near),
        vector_part=wide(count, 8, width), vector_sum=wide(2, 8, width), small_part=wide(count, 8, PAD),
    )
    tall = 3 * part // 2
    for_out, for_up, for_down, for_qk, for_v = (
        (low(count, *of), low(lines, *of), low(lines - 1, *of), low(lines - 1, *of))
        for of in ((tall, 128), (part, feed), (part, feed), (part, 2 * near), (tall, 128))
    )
    scratch.update(
        t_out=for_out[0], yb_out=for_out[1], pr_out=for_out[2], zb_out=for_out[3],
        t_up=for_up[0], yb_up=for_up[1], pr_up=for_up[2], zb_up=for_up[3],
        t_down=for_down[0], yb_down=for_down[1], pr_down=for_down[2], zb_down=for_down[3],
        t_qk=for_qk[0], yb_qk=for_qk[1], pr_qk=for_qk[2], zb_qk=for_qk[3],
        t_v=for_v[0], yb_v=for_v[1], pr_v=for_v[2], zb_v=for_v[3],
        corr_terms=low(1, two, width), corr_core=low(1, LAND, width), corr_out=low(1, LAND, width),
        corr_in=low(2, 1, LAND, width), corr_sems=sem(1, 4, 1), corr_all=low(two, width),
        corr_s=sem(1), corr_r=sem(1),
        g_own=sem(8), g_zs=sem(8, lines - 1), g_zr=sem(8, lines - 1), g_ys=sem(8, lines), g_yr=sem(8, lines),
        s_ys=sem(5, lines), s_yr=sem(5, lines), s_zs=sem(5, lines - 1), s_zr=sem(5, lines - 1),
        e_s=sem(8, count - 1), e_r=sem(8, count - 1), h_sems=sem(4, 4, CHUNKS),
        rim_s=sem(2, 2), rim_r=sem(2, 2), share_s=sem(5, CHUNKS), share_r=sem(5, CHUNKS),
        core_s=sem(1), core_r=sem(1),
    )
    any_place = pl.BlockSpec(memory_space=pltpu.HBM)
    results = pl.pallas_call(
        functools.partial(layer_kernel, count, list(operands) + list(outs) + list(scratch)),
        out_shape=tuple(jax.ShapeDtypeStruct(*out) for out in outs.values()),
        in_specs=[smem, smem, any_place, any_place] + [vmem] * (len(operands) - 4),
        out_specs=(any_place,) * 6 + (vmem, vmem),
        scratch_shapes=list(scratch.values()),
        compiler_params=pltpu.CompilerParams(
            collective_id=1, has_side_effects=True, vmem_limit_bytes=63 * 2**20
        ),
    )(*operands.values())
    vector = lambda length: jax.ShapeDtypeStruct((length,), WIDE)
    block = lambda lanes: jax.ShapeDtypeStruct((part, lanes), WIDE)
    whole = jax.ShapeDtypeStruct((rows, width), LOW)
    return pl.pallas_call(
        hand_out,
        out_shape=(
            whole, whole, block(near), block(near), block(near), block(near), block(feed), block(feed),
            vector(near), vector(near), vector(width), vector(feed), vector(width),
            vector(width), vector(width), vector(width), vector(width),
            jax.ShapeDtypeStruct((heads, KERNEL), WIDE),
        ),
        in_specs=[vmem] * 8,
        out_specs=(any_place,) * 8 + (vmem,) * 10,
        scratch_shapes=[sem(8, 4)],
    )(*results)


def plain_body(
    inputs,
    cotangent,
    item_lengths,
    w_query,
    w_key,
    w_value,
    w_out,
    w_up,
    w_down,
    bias_query,
    bias_value,
    bias_out,
    bias_up,
    bias_down,
    gain_one,
    bias_one,
    gain_two,
    bias_two,
    conv_taps,
):
    low_type = jnp.bfloat16
    tok_rows = inputs.shape[0]
    heads_here = conv_taps.shape[0]
    width_here = heads_here * HEAD_DIM
    slots = ITEMS * LAND
    reach = (KERNEL - 1) // 2
    score_scale = HEAD_DIM ** (-0.5)
    pref = jnp.float32
    first_row = lax.axis_index("seq") * tok_rows
    positions = first_row + jnp.arange(tok_rows, dtype=jnp.int32)
    item_id, land_slot = locate(item_lengths, positions)
    rim_item = locate(
        item_lengths, first_row - reach + jnp.arange(tok_rows + 2 * reach, dtype=jnp.int32)
    )[0]
    slot_item = jnp.arange(slots, dtype=jnp.int32) // LAND
    member = land_slot[:, None] == jnp.arange(slots, dtype=jnp.int32)[None, :]
    member_low = member.astype(low_type)
    counts = jnp.repeat((item_lengths // LAND).astype(jnp.float32), LAND)
    same_f = item_id[:, None] == slot_item[None, :]
    same_b = same_f.T
    tap_cols = jnp.repeat(conv_taps, HEAD_DIM, axis=0)
    full_query, full_key, full_value, full_out, full_up, full_down = (
        lax.all_gather(w_query, "seq", axis=0, tiled=True),
        lax.all_gather(w_key, "seq", axis=0, tiled=True),
        lax.all_gather(w_value, "seq", axis=0, tiled=True),
        lax.all_gather(w_out, "seq", axis=0, tiled=True),
        lax.all_gather(w_up, "seq", axis=0, tiled=True),
        lax.all_gather(w_down, "seq", axis=0, tiled=True),
    )
    queries = (matmul_low(inputs, full_query) + bias_query).astype(low_type)
    key_rows = matmul_low(inputs, full_key).astype(low_type)
    value_rows = (matmul_low(inputs, full_value) + bias_value).astype(low_type)
    query_sums, key_sums = lax.psum(
        (across(member_low, queries), across(member_low, key_rows)), "seq"
    )
    query_land = (
        (query_sums / counts[:, None]).astype(low_type).reshape(slots, heads_here, HEAD_DIM)
    )
    key_land = (key_sums / counts[:, None]).astype(low_type).reshape(slots, heads_here, HEAD_DIM)
    query_heads = queries.reshape(tok_rows, heads_here, HEAD_DIM)
    key_heads = key_rows.reshape(tok_rows, heads_here, HEAD_DIM)
    value_heads = value_rows.reshape(tok_rows, heads_here, HEAD_DIM)
    scores_b = (
        jnp.einsum("lhd,thd->hlt", query_land, key_heads, preferred_element_type=pref) * score_scale
    )
    scores_b = jnp.where(same_b[None], scores_b, MASKED)
    maxima_b = lax.pmax(jnp.max(scores_b, axis=2), "seq")
    weights_b = jnp.exp(scores_b - maxima_b[:, :, None])
    weights_b_low = weights_b.astype(low_type)
    numer_sum, totals_b = lax.psum(
        (
            jnp.einsum("hlt,thd->lhd", weights_b_low, value_heads, preferred_element_type=pref),
            jnp.sum(weights_b, axis=2),
        ),
        "seq",
    )
    totals_cols = totals_b.T[:, :, None]
    kernel_v = numer_sum / totals_cols
    land_q = query_land.reshape(ITEMS, LAND, heads_here, HEAD_DIM)
    land_k = key_land.reshape(ITEMS, LAND, heads_here, HEAD_DIM)
    land_kernel = jax.nn.softmax(
        jnp.einsum("ilhd,imhd->ihlm", land_q, land_k, preferred_element_type=pref) * score_scale,
        axis=-1,
    )
    inverse, inverse_back = jax.vjp(pseudo_inverse, land_kernel)
    kernel_items = kernel_v.reshape(ITEMS, LAND, heads_here, HEAD_DIM)
    mixing = jnp.einsum("ihlm,imhd->ilhd", inverse, kernel_items, precision=PRECISE)
    mixing = mixing.astype(low_type).reshape(slots, heads_here, HEAD_DIM)
    scores_f = (
        jnp.einsum("thd,lhd->htl", query_heads, key_land, preferred_element_type=pref) * score_scale
    )
    weights_f = jax.nn.softmax(jnp.where(same_f[None], scores_f, MASKED), axis=-1)
    weights_f_low = weights_f.astype(low_type)
    attended = jnp.einsum("htl,lhd->thd", weights_f_low, mixing, preferred_element_type=pref)
    attended = attended.reshape(tok_rows, width_here)
    value_rim = extended(value_rows, (("seq", 0),), reach)
    conv_sum = jnp.zeros((tok_rows, width_here), jnp.float32)
    for offset in range(KERNEL):
        in_item = (rim_item[offset : offset + tok_rows] == item_id)[:, None]
        conv_sum = conv_sum + jnp.where(
            in_item,
            value_rim[offset : offset + tok_rows].astype(jnp.float32)
            * tap_cols[:, offset][None, :],
            0.0,
        )
    mixed_rows = (attended + conv_sum).astype(low_type)
    attention_sum = lax.psum(against(mixed_rows, full_out).astype(jnp.bfloat16), "head").astype(
        jnp.float32
    )
    pre_one = inputs.astype(jnp.float32) + attention_sum + bias_out
    norm_one, inv_one = normalize(pre_one)
    hidden = norm_one * gain_one + bias_one
    hidden_low = hidden.astype(low_type)
    lifted = matmul_low(hidden_low, full_up) + bias_up
    active, gelu_back = jax.vjp(gelu_tanh, lifted)
    active_low = active.astype(low_type)
    feed_terms = against(active_low, full_down)
    feed_sum = lax.psum(feed_terms.astype(jnp.bfloat16), "head").astype(jnp.float32)
    grad_output = cotangent.astype(jnp.float32)
    pre_two = hidden + feed_sum + bias_down
    norm_two, inv_two = normalize(pre_two)
    out_rows = (norm_two * gain_two + bias_two).astype(low_type)
    grad_gain_two = jnp.sum(grad_output * norm_two, axis=0)
    grad_bias_two = jnp.sum(grad_output, axis=0)
    grad_two = norm_back(grad_output * gain_two, norm_two, inv_two)
    grad_bias_down = jnp.sum(grad_two, axis=0)
    grad_two_low = grad_two.astype(low_type)
    output, grad_two_full = (out_rows, grad_two_low)
    grad_down = across(grad_two_full, active_low)
    (grad_lift,) = gelu_back(matmul_low(grad_two_full, full_down))
    grad_bias_up = jnp.sum(grad_lift, axis=0)
    grad_lift_low = grad_lift.astype(low_type)
    grad_up = across(hidden_low, grad_lift_low)
    up_terms = against(grad_lift_low, full_up)
    grad_hidden = grad_two + lax.psum(up_terms.astype(jnp.bfloat16), "head").astype(jnp.float32)
    grad_gain_one = jnp.sum(grad_hidden * norm_one, axis=0)
    grad_bias_one = jnp.sum(grad_hidden, axis=0)
    grad_one = norm_back(grad_hidden * gain_one, norm_one, inv_one)
    grad_bias_out = jnp.sum(grad_one, axis=0)
    grad_one_low = grad_one.astype(low_type)
    grad_outw = across(grad_one_low, mixed_rows)
    grad_mixed = matmul_low(grad_one_low, full_out).astype(low_type)
    grad_mixed_wide = grad_mixed.astype(jnp.float32)
    grad_heads = grad_mixed.reshape(tok_rows, heads_here, HEAD_DIM)
    grad_rim = extended(grad_mixed, (("seq", 0),), reach)
    grad_conv_v = jnp.zeros((tok_rows, width_here), jnp.float32)
    tap_terms = []
    for offset in range(KERNEL):
        in_item = (rim_item[offset : offset + tok_rows] == item_id)[:, None]
        neighbour = jnp.where(
            in_item, value_rim[offset : offset + tok_rows].astype(jnp.float32), 0.0
        )
        tap_terms.append(
            jnp.sum(
                (grad_mixed_wide * neighbour).reshape(tok_rows, heads_here, HEAD_DIM), axis=(0, 2)
            )
        )
        mirror = 2 * reach - offset
        mirror_item = (rim_item[mirror : mirror + tok_rows] == item_id)[:, None]
        grad_conv_v = grad_conv_v + jnp.where(
            mirror_item,
            grad_rim[mirror : mirror + tok_rows].astype(jnp.float32) * tap_cols[:, offset][None, :],
            0.0,
        )
    grad_taps = jnp.stack(tap_terms, axis=1)
    grad_weights_f = jnp.einsum("thd,lhd->htl", grad_heads, mixing, preferred_element_type=pref)
    grad_mix_part = jnp.einsum(
        "htl,thd->lhd", weights_f_low, grad_heads, preferred_element_type=pref
    )
    grad_scores_f = weights_f * (
        grad_weights_f - jnp.sum(weights_f * grad_weights_f, axis=2, keepdims=True)
    )
    grad_scores_f = grad_scores_f.astype(low_type)
    grad_query_f = (
        jnp.einsum("htl,lhd->thd", grad_scores_f, key_land, preferred_element_type=pref)
        * score_scale
    )
    grad_kland_part = (
        jnp.einsum("htl,thd->lhd", grad_scores_f, query_heads, preferred_element_type=pref)
        * score_scale
    )
    grad_mixing, grad_kland_f = lax.psum((grad_mix_part, grad_kland_part), "seq")
    grad_mix_items = grad_mixing.reshape(ITEMS, LAND, heads_here, HEAD_DIM)
    grad_inverse = jnp.einsum("ilhd,imhd->ihlm", grad_mix_items, kernel_items, precision=PRECISE)
    grad_kernel_v = jnp.einsum("ihlm,ilhd->imhd", inverse, grad_mix_items, precision=PRECISE)
    grad_kernel_v = grad_kernel_v.reshape(slots, heads_here, HEAD_DIM)
    (grad_land_kernel,) = inverse_back(grad_inverse)
    grad_scores_a = land_kernel * (
        grad_land_kernel - jnp.sum(land_kernel * grad_land_kernel, axis=-1, keepdims=True)
    )
    grad_scores_a = grad_scores_a * score_scale
    grad_qland_a = jnp.einsum(
        "ihlm,imhd->ilhd", grad_scores_a, land_k.astype(jnp.float32), precision=PRECISE
    )
    grad_kland_a = jnp.einsum(
        "ihlm,ilhd->imhd", grad_scores_a, land_q.astype(jnp.float32), precision=PRECISE
    )
    grad_numer = (grad_kernel_v / totals_cols).astype(low_type)
    grad_totals = -jnp.sum(grad_kernel_v * kernel_v, axis=2) / totals_b.T
    grad_weights_b = jnp.einsum(
        "lhd,thd->hlt", grad_numer, value_heads, preferred_element_type=pref
    )
    grad_weights_b = grad_weights_b + grad_totals.T[:, :, None]
    grad_scores_b = (weights_b * grad_weights_b).astype(low_type)
    grad_qland_part = (
        jnp.einsum("hlt,thd->lhd", grad_scores_b, key_heads, preferred_element_type=pref)
        * score_scale
    )
    grad_key_b = (
        jnp.einsum("hlt,lhd->thd", grad_scores_b, query_land, preferred_element_type=pref)
        * score_scale
    )
    grad_value_b = jnp.einsum(
        "hlt,lhd->thd", weights_b_low, grad_numer, preferred_element_type=pref
    )
    grad_query_rows = grad_query_f.reshape(tok_rows, width_here)
    grad_values = grad_value_b.reshape(tok_rows, width_here) + grad_conv_v
    (
        grad_qland_b,
        grad_gain_one,
        grad_bias_one,
        grad_gain_two,
        grad_bias_two,
        grad_bias_out,
        grad_bias_down,
        grad_bias_up,
        grad_taps,
        query_f_total,
        grad_bias_value,
    ) = lax.psum(
        (
            grad_qland_part,
            grad_gain_one,
            grad_bias_one,
            grad_gain_two,
            grad_bias_two,
            grad_bias_out,
            grad_bias_down,
            grad_bias_up,
            grad_taps,
            jnp.sum(grad_query_rows, axis=0),
            jnp.sum(grad_values, axis=0),
        ),
        "seq",
    )
    grad_qland = grad_qland_a.reshape(slots, width_here) + grad_qland_b.reshape(slots, width_here)
    grad_kland = grad_kland_a.reshape(slots, width_here) + grad_kland_f.reshape(slots, width_here)
    member_wide = member.astype(jnp.float32)
    grad_queries = grad_query_rows + jnp.dot(
        member_wide, grad_qland / counts[:, None], precision=PRECISE
    )
    grad_keys = grad_key_b.reshape(tok_rows, width_here) + jnp.dot(
        member_wide, grad_kland / counts[:, None], precision=PRECISE
    )
    grad_bias_query = query_f_total + jnp.sum(grad_qland, axis=0)
    queries_low = grad_queries.astype(low_type)
    keys_low = grad_keys.astype(low_type)
    values_low = grad_values.astype(low_type)
    grad_queryw = across(inputs, queries_low)
    grad_keyw = across(inputs, keys_low)
    grad_valuew = across(inputs, values_low)
    input_terms = (
        against(queries_low, full_query)
        + against(keys_low, full_key)
        + against(values_low, full_value)
    )
    grad_inputs = (
        grad_one + lax.psum(input_terms.astype(jnp.bfloat16), "head").astype(jnp.float32)
    ).astype(low_type)
    query_shard, key_shard, value_shard, out_shard, grad_up_shard, grad_down_shard = side_by_side(
        (
            grad_queryw.astype(jnp.bfloat16),
            grad_keyw.astype(jnp.bfloat16),
            grad_valuew.astype(jnp.bfloat16),
            grad_outw.astype(jnp.bfloat16),
            grad_up.astype(jnp.bfloat16),
            grad_down.astype(jnp.bfloat16),
        ),
        "seq",
        0,
        1,
    )
    return (
        output,
        grad_inputs,
        query_shard,
        key_shard,
        value_shard,
        out_shard,
        grad_up_shard,
        grad_down_shard,
        grad_bias_query,
        grad_bias_value,
        grad_bias_out,
        grad_bias_up,
        grad_bias_down,
        grad_gain_one,
        grad_bias_one,
        grad_gain_two,
        grad_bias_two,
        grad_taps,
    )


def solution(mesh):
    aligned = (768 // mesh.shape["seq"]) % 16 == 0
    return jax.shard_map(
        fused_body if aligned else plain_body,
        mesh=mesh,
        in_specs=(
            P("seq", None),
            P("seq", None),
            P(),
            P("seq", "head"),
            P("seq", "head"),
            P("seq", "head"),
            P("seq", "head"),
            P("seq", "head"),
            P("seq", "head"),
            P("head"),
            P("head"),
            P(),
            P("head"),
            P(),
            P(),
            P(),
            P(),
            P(),
            P("head", None),
        ),
        out_specs=(
            P("seq", None),
            P("seq", None),
            P("seq", "head"),
            P("seq", "head"),
            P("seq", "head"),
            P("seq", "head"),
            P("seq", "head"),
            P("seq", "head"),
            P("head"),
            P("head"),
            P(),
            P("head"),
            P(),
            P(),
            P(),
            P(),
            P(),
            P("head", None),
        ),
        check_vma=False,
    )
```

```python
import functools
import types

import jax
import jax.numpy as jnp
from jax import lax
from jax.experimental import pallas as pl
from jax.experimental.pallas import tpu as pltpu
from jax.sharding import PartitionSpec as P

HEAD_DIM = 64
LAND = 64
KERNEL = 33
PINV_STEPS = 6
ITEMS = 3


PRECISE = lax.Precision.HIGHEST
EPSILON = 1e-05
MASKED = -1e30


def extended(cells, sides, width):
    for axis, dim in sides:
        count = lax.axis_size(axis)
        ends = count - 1
        head = lax.slice_in_dim(cells, 0, width, axis=dim)
        tail = lax.slice_in_dim(cells, cells.shape[dim] - width, cells.shape[dim], axis=dim)
        cells = jnp.concatenate(
            [
                lax.ppermute(tail, axis, [(i, (i + 1) % count) for i in range(ends)]),
                cells,
                lax.ppermute(head, axis, [((i + 1) % count, i) for i in range(ends)]),
            ],
            axis=dim,
        )
    return cells


def cut_along(array, dim, length):
    lengths = array.shape
    parts = array.reshape(*lengths[:dim], length, lengths[dim] // length, *lengths[dim + 1 :])
    return jnp.moveaxis(parts, dim, 0)


def sent_and_summed(array, axis, dim):
    parts = cut_along(array, dim, lax.axis_size(axis))
    arrived = lax.all_to_all(parts, axis, split_axis=0, concat_axis=0, tiled=True)
    return arrived.astype(jnp.float32).sum(axis=0)


def side_by_side(arrays, axis, dim, along):
    both = jnp.concatenate(arrays, axis=along)
    out, at, outs = (sent_and_summed(both, axis, dim), 0, [])
    for a in arrays:
        outs.append(lax.slice_in_dim(out, at, at + a.shape[along], axis=along))
        at += a.shape[along]
    return tuple(outs)


def locate(item_lengths, positions):
    item_ends = jnp.cumsum(item_lengths)
    item_starts = item_ends - item_lengths
    located = jnp.sum((positions[:, None] >= item_ends[None, :]).astype(jnp.int32), axis=1)
    inside = (positions >= 0) & (located < ITEMS)
    picked = jnp.minimum(located, ITEMS - 1)
    onehot = (picked[:, None] == jnp.arange(ITEMS, dtype=jnp.int32)[None, :]).astype(jnp.int32)
    item_start = jnp.sum(onehot * item_starts[None, :], axis=1)
    length = jnp.sum(onehot * item_lengths[None, :], axis=1)
    segment = (positions - item_start) * LAND // length
    land_slot = picked * LAND + jnp.clip(segment, 0, LAND - 1)
    return (jnp.where(inside, picked, -1), land_slot)


def normalize(values):
    row_mean = jnp.mean(values, axis=-1, keepdims=True)
    centered = values - row_mean
    variance = jnp.mean(centered * centered, axis=-1, keepdims=True)
    inv_std = lax.rsqrt(variance + EPSILON)
    return (centered * inv_std, inv_std)


def norm_back(grad_norm, normed, inv_std):
    return inv_std * (
        grad_norm
        - jnp.mean(grad_norm, axis=-1, keepdims=True)
        - normed * jnp.mean(grad_norm * normed, axis=-1, keepdims=True)
    )


def pseudo_inverse(land_kernel):
    identity = jnp.eye(LAND, dtype=jnp.float32)
    frobenius = jnp.sum(land_kernel * land_kernel, axis=(-2, -1), keepdims=True)
    result = jnp.swapaxes(land_kernel, -1, -2) / frobenius
    for iteration in range(PINV_STEPS):
        product = jnp.matmul(land_kernel, result, precision=PRECISE)
        nested = 7.0 * identity - product
        nested = 15.0 * identity - jnp.matmul(product, nested, precision=PRECISE)
        nested = 13.0 * identity - jnp.matmul(product, nested, precision=PRECISE)
        result = 0.25 * jnp.matmul(result, nested, precision=PRECISE)
    return result


def gelu_tanh(values):
    return jax.nn.gelu(values, approximate=True)


def matmul_low(left, right):
    return jnp.dot(left, right, preferred_element_type=jnp.float32)


def against(left, right):
    return lax.dot_general(
        left, right, (((1,), (1,)), ((), ())), preferred_element_type=jnp.float32
    )


def across(left, right):
    return lax.dot_general(
        left, right, (((0,), (0,)), ((), ())), preferred_element_type=jnp.float32
    )


MESH = pl.DeviceIdType.MESH
WIDE = jnp.float32
LOW = jnp.bfloat16
CHUNKS = 4
PAD = 256
REACH = (KERNEL - 1) // 2
BLOCK = 64
SPAN = BLOCK + 2 * REACH
BORDER = 16


def place():
    s, h = lax.axis_index("seq"), lax.axis_index("head")
    return s, h, s // 2, lax.rem(s, 2), h // 2, lax.rem(h, 2)


def core_of_chip():
    s, _, _, _, x, core = place()
    return (s, 2 * x + 1 - core)


def x_neighbour():
    s, _, _, _, x, core = place()
    return (s, 2 * (1 - x) + core)


def y_neighbour():
    _, h, z, y, _, _ = place()
    return (2 * z + 1 - y, h)


def along_z(count):
    _, h, z, y, _, _ = place()
    lines = count // 2
    return [(2 * lax.rem(z + j, lines) + y, h) for j in range(1, lines)]


def along_seq(count):
    s, h = place()[:2]
    return [(lax.rem(s + j, count), h) for j in range(1, count)]


def remote(src, dst, send, recv, device):
    return pltpu.make_async_remote_copy(
        src_ref=src, dst_ref=dst, send_sem=send, recv_sem=recv, device_id=device, device_id_type=MESH
    )


def greet(devices):
    for device in devices:
        pl.semaphore_signal(
            pltpu.get_barrier_semaphore(), inc=1, device_id=device, device_id_type=MESH
        )


def greeted(devices):
    pl.semaphore_wait(pltpu.get_barrier_semaphore(), len(devices))


class Gather:
    def __init__(self, count, shard, full, lanes, own, zs, zr, ys, yr):
        s, _, z, y, _, _ = place()
        lines = count // 2
        shard = shard.at[:, lanes]
        view = lambda slot: full.at[slot, :, lanes]
        self.local = pltpu.make_async_copy(shard, view(s), own)
        self.z_copies = [
            remote(shard, view(s), zs.at[j], zr.at[j], device)
            for j, device in enumerate(along_z(count))
        ]
        self.y_copies = [remote(shard, view(s), ys.at[0], yr.at[0], y_neighbour())]
        for j in range(1, lines):
            slot = 2 * lax.rem(z - j + lines, lines) + y
            self.y_copies.append(remote(view(slot), view(slot), ys.at[j], yr.at[j], y_neighbour()))

    def start(self):
        for copy in self.z_copies:
            copy.start()
        self.y_copies[0].start()
        self.local.start()

    def forward(self):
        for z_copy, y_copy in zip(self.z_copies, self.y_copies[1:]):
            z_copy.wait_recv()
            y_copy.start()

    def finish(self):
        self.local.wait()
        for copy in self.y_copies:
            copy.wait_recv()

    def close(self):
        for copy in self.z_copies + self.y_copies:
            copy.wait_send()


class Scatter:
    def __init__(self, count, terms, y_buf, pair, z_buf, ys, yr, zs, zr):
        self.terms, self.y_buf, self.pair, self.z_buf = terms, y_buf, pair, z_buf
        _, _, self.z, self.y, _, _ = place()
        self.lines = count // 2
        self.y_copies = []
        for j in range(self.lines):
            line = lax.rem(self.z + j, self.lines)
            self.y_copies.append(
                remote(
                    terms.at[2 * line + 1 - self.y], y_buf.at[line], ys.at[j], yr.at[j], y_neighbour()
                )
            )
        self.z_copies = [
            remote(pair.at[j], z_buf.at[j], zs.at[j], zr.at[j], device)
            for j, device in enumerate(along_z(count))
        ]

    def fill(self, left, right):
        self.terms[...] = across(left, right).astype(LOW).reshape(self.terms.shape)

    def fill_dense(self, left, right):
        terms = across(left, right).astype(LOW)
        part = terms.shape[0] // self.terms.shape[0]
        terms = terms.reshape(self.terms.shape[0], part, terms.shape[1])
        self.terms[:, 0:part] = terms[:, :, 0:128]
        self.terms[:, part:] = jnp.concatenate(
            [terms[:, 0 : part // 2, 128:], terms[:, part // 2 :, 128:]], axis=2
        )

    def start(self, *away):
        for j in away or list(range(1, self.lines)) + [0]:
            self.y_copies[j].start()

    def forward(self, *away):
        for j in away or range(1, self.lines):
            line = lax.rem(self.z + j, self.lines)
            self.y_copies[j].wait_recv()
            self.pair[j - 1] = (
                self.terms[2 * line + self.y].astype(WIDE) + self.y_buf[line].astype(WIDE)
            ).astype(LOW)
            self.z_copies[j - 1].start()

    def finish(self):
        self.y_copies[0].wait_recv()
        total = self.terms[2 * self.z + self.y].astype(WIDE) + self.y_buf[self.z].astype(WIDE)
        for j, copy in enumerate(self.z_copies):
            copy.wait_recv()
            total = total + self.z_buf[j].astype(WIDE)
        return total

    def close(self):
        for copy in self.z_copies + self.y_copies:
            copy.wait_send()


class Spread:
    def __init__(self, count, blocks, send, recv):
        s = place()[0]
        self.copies = [
            remote(blocks.at[s], blocks.at[s], send.at[j], recv.at[j], device)
            for j, device in enumerate(along_seq(count))
        ]

    def start(self):
        for copy in self.copies:
            copy.start()

    def finish(self):
        for copy in self.copies:
            copy.wait_recv()

    def close(self):
        for copy in self.copies:
            copy.wait_send()


class Swap(Spread):
    def __init__(self, count, out, into, send, recv):
        s = place()[0]
        self.out, self.into = out, into
        self.copies = [
            remote(out.at[device[0]], into.at[s], send.at[j], recv.at[j], device)
            for j, device in enumerate(along_seq(count))
        ]

    def start(self):
        s = place()[0]
        super().start()
        self.into[s] = self.out[s]


class SeqSum:
    def __init__(self, count, out, into, sums, send, recv):
        self.count, self.into, self.sums = count, into, sums
        self.swap = Swap(count, out, into, send.at[0], recv.at[0])
        self.spread = Spread(count, sums, send.at[1], recv.at[1])

    def start(self):
        self.swap.start()

    def add(self):
        self.swap.finish()
        self.sums[place()[0]] = functools.reduce(jnp.add, [self.into[d] for d in range(self.count)])
        self.spread.start()

    def finish(self):
        self.spread.finish()

    def close(self):
        self.swap.close()
        self.spread.close()


class HeadSum:
    def __init__(self, turn, terms, core_in, x_out, x_in, sems):
        self.turn, self.terms, self.core_in, self.x_out, self.x_in = turn, terms, core_in, x_out, x_in
        self.sems = sems
        self.core = place()[5]
        self.half = terms.shape[1] // 2

    def core_copy(self, c, turn=None):
        sems = self.sems.at[self.turn if turn is None else turn]
        away = pl.ds(pl.multiple_of((1 - self.core) * self.half, self.half), self.half)
        return remote(
            self.terms.at[c, away], self.core_in.at[c], sems.at[0, c], sems.at[1, c], core_of_chip()
        )

    def x_copy(self, c, turn=None):
        turn = self.turn if turn is None else turn
        sems = self.sems.at[turn]
        return remote(
            self.x_out.at[c], self.x_in.at[turn % 2, c], sems.at[2, c], sems.at[3, c], x_neighbour()
        )

    def offer(self, c, rows):
        if self.turn > 0:
            self.core_copy(c, self.turn - 1).wait_send()
        self.terms[c] = rows
        self.core_copy(c).start()

    def pair_up(self, c):
        self.core_copy(c).wait_recv()
        if self.turn > 0:
            self.x_copy(c, self.turn - 1).wait_send()
        here = pl.ds(pl.multiple_of(self.core * self.half, self.half), self.half)
        self.x_out[c] = (
            self.terms[c, here].astype(WIDE) + self.core_in[c].astype(WIDE)
        ).astype(LOW)
        self.x_copy(c).start()

    def arrived(self, c):
        self.x_copy(c).wait_recv()

    def total(self, c, rows):
        return self.x_out[c, rows].astype(WIDE) + self.x_in[self.turn % 2, c, rows].astype(WIDE)


def iota(shape, dim):
    return lax.broadcasted_iota(jnp.int32, shape, dim)


def fold(rows):
    return rows.reshape(rows.shape[0] // 8, 8, rows.shape[1]).sum(axis=0)


def gelu_and_slope(v):
    square = v * v
    t = jnp.tanh(0.7978845608 * (v + 0.044715 * v * square))
    half = 0.5 * (1.0 + t)
    slope = half + 0.5 * v * (1.0 - t * t) * (0.7978845608 * (1.0 + 0.134145 * square))
    return v * half, slope


def exact(left, right, dims=(1, 0)):
    return lax.dot_general(
        left,
        right,
        (((dims[0],), (dims[1],)), ((), ())),
        preferred_element_type=WIDE,
        precision=PRECISE,
    )


def dense(block):
    n = block.shape[0]
    rest = jnp.concatenate([block[0 : n // 2, 128:], block[n // 2 :, 128:]], axis=1)
    return jnp.concatenate([block[:, 0:128], rest], axis=0)


def undense(block):
    n = block.shape[0] * 2 // 3
    rest = jnp.concatenate([block[n:, 0:64], block[n:, 64:128]], axis=0)
    return jnp.concatenate([block[0:n], rest], axis=1)


def loop(count, body):
    lax.fori_loop(0, count, lambda i, carry: (body(i), carry)[1], 0)


def layer_kernel(count, names, *refs):
    r = types.SimpleNamespace(**dict(zip(names, refs)))
    s, h, z, y, x, core = place()
    rows, width = r.inputs_hbm.shape
    near = r.w_query.shape[1]
    heads = near // HEAD_DIM
    feed = r.w_up.shape[1]
    size = rows // CHUNKS
    half = size // 2
    step = 32
    lines = count // 2
    two = 2 * LAND
    scale = HEAD_DIM**-0.5
    chunk_rows = lambda c: pl.ds(pl.multiple_of(c * size, size), size)
    my_rows = lambda c: pl.ds(pl.multiple_of(c * size + core * half, half), half)
    everyone = along_seq(count)
    before, after = (lax.rem(s + count - 1, count), h), (lax.rem(s + 1, count), h)

    flat = lambda ref: ref[...].reshape(1, ref.shape[0])
    bias_query, bias_value, bias_out = flat(r.bias_query), flat(r.bias_value), flat(r.bias_out)
    bias_up, bias_down = flat(r.bias_up), flat(r.bias_down)
    gain_one, bias_one, gain_two, bias_two = (
        flat(r.gain_one), flat(r.bias_one), flat(r.gain_two), flat(r.bias_two)
    )

    def gather(k, shard, full, lo, hi):
        return Gather(
            count, shard, full, slice(lo, hi), r.g_own.at[k], r.g_zs.at[k], r.g_zr.at[k], r.g_ys.at[k], r.g_yr.at[k]
        )

    def scatter(k, terms, y_buf, pair, z_buf):
        return Scatter(
            count, terms, y_buf, pair, z_buf, r.s_ys.at[k], r.s_yr.at[k], r.s_zs.at[k], r.s_zr.at[k]
        )

    gather_qk = gather(0, r.packed, r.w_near, 0, 2 * near)
    gather_vo = gather(1, r.packed, r.w_near, 2 * near, 4 * near)
    third = feed // 3
    ups = [gather(2 + k, r.w_up, r.full_up, k * third, (k + 1) * third) for k in range(3)]
    downs = [gather(5 + k, r.w_down, r.full_down, k * third, (k + 1) * third) for k in range(3)]
    gathers = [gather_qk, gather_vo] + ups + downs
    scatter_out = scatter(0, r.t_out, r.yb_out, r.pr_out, r.zb_out)
    scatter_up = scatter(1, r.t_up, r.yb_up, r.pr_up, r.zb_up)
    scatter_down = scatter(2, r.t_down, r.yb_down, r.pr_down, r.zb_down)
    scatter_qk = scatter(3, r.t_qk, r.yb_qk, r.pr_qk, r.zb_qk)
    scatter_v = scatter(4, r.t_v, r.yb_v, r.pr_v, r.zb_v)
    scatters = [scatter_out, scatter_up, scatter_down, scatter_qk, scatter_v]
    correction = HeadSum(0, r.corr_terms, r.corr_core, r.corr_out, r.corr_in, r.corr_sems)
    sums = [HeadSum(k, r.terms, r.core_in, r.x_out, r.x_in, r.h_sems) for k in range(4)]
    landmarks = Spread(count, r.land_part, r.e_s.at[0], r.e_r.at[0])
    numer_swap = Swap(count, r.numer_out, r.numer_in, r.e_s.at[1], r.e_r.at[1])
    kernel_spread = Spread(count, r.kernel_v, r.e_s.at[2], r.e_r.at[2])
    small_spread = Spread(count, r.small_part, r.e_s.at[3], r.e_r.at[3])
    mix_sum, land_sum, vector_total = (
        SeqSum(count, out, into, total, r.e_s.at[pl.ds(4 + 2 * k, 2)], r.e_r.at[pl.ds(4 + 2 * k, 2)])
        for k, (out, into, total) in enumerate(
            (
                (r.mix_out, r.mix_in, r.mix_sums),
                (r.land_out, r.land_in, r.land_sums),
                (r.vector_out, r.vector_in, r.vector_sums),
            )
        )
    )
    spreads = [landmarks, numer_swap, kernel_spread, small_spread, mix_sum, land_sum, vector_total]

    def rim(k, ext):
        first = remote(
            ext.at[pl.ds(REACH, REACH)], ext.at[pl.ds(REACH + rows, REACH)], r.rim_s.at[k, 0], r.rim_r.at[k, 0], before
        )
        last = remote(
            ext.at[pl.ds(rows, REACH)], ext.at[pl.ds(0, REACH)], r.rim_s.at[k, 1], r.rim_r.at[k, 1], after
        )
        return [first, last]

    rims = [rim(0, r.value_ext), rim(1, r.grad_ext)]

    def share(k, ref, c):
        return remote(
            ref.at[my_rows(c)], ref.at[my_rows(c)], r.share_s.at[k, c], r.share_r.at[k, c], core_of_chip()
        )

    load_inputs = pltpu.make_async_copy(r.inputs_hbm, r.inputs, r.io.at[0])
    load_cotangent = pltpu.make_async_copy(r.cotangent_hbm, r.cotangent, r.io.at[1])
    stores = [
        pltpu.make_async_copy(ref, out, r.io.at[2 + k])
        for k, (ref, out) in enumerate(
            (
                (r.output, r.output_hbm),
                (r.cotangent, r.grad_inputs_hbm),
                (r.grad_w_out, r.grad_w_out_hbm),
                (r.grad_w_up, r.grad_w_up_hbm),
                (r.grad_w_down, r.grad_w_down_hbm),
                (r.grad_near, r.grad_near_hbm),
            )
        )
    ]
    store_output, store_grad_inputs, store_out, store_up, store_down, store_near = stores
    vector_core = remote(
        r.vector_sum.at[0], r.vector_sum.at[1], r.core_s.at[0], r.core_r.at[0], core_of_chip()
    )

    met = [core_of_chip(), x_neighbour()] + everyone
    greet(met)
    load_inputs.start()
    r.packed[:, 0:near] = r.w_query[...]
    r.packed[:, near : 2 * near] = r.w_key[...]
    r.packed[:, 2 * near : 3 * near] = r.w_value[...]
    r.packed[:, 3 * near : 4 * near] = r.w_out[...]
    ends = jnp.where(s == 0, r.lengths[0], jnp.where(s == count - 1, r.lengths[2], 0))
    edge_start = jnp.where(s == 0, 0, rows - ends)
    edge_end = edge_start + ends
    edge_count = ends // LAND
    mid_count = r.lengths[1] // LAND
    mid_first = s * rows - r.lengths[0]
    first_slot = jnp.maximum(mid_first, 0) // mid_count
    item_edge = jnp.where(s == 0, ends, jnp.where(s == count - 1, rows - ends, -1))

    def members():
        token, lane = iota((rows, two), 0), iota((rows, two), 1)
        mid = lane < LAND
        at_edge = (token >= edge_start) & (token < edge_end)
        start = jnp.where(mid, (first_slot + lane) * mid_count - mid_first, (lane - LAND) * edge_count + edge_start)
        length = jnp.where(mid, mid_count, edge_count)
        inside = (token >= start) & (token < start + length)
        belongs = jnp.where(mid, jnp.where(at_edge, 0.0, 1.0), jnp.where(at_edge, 1.0, 0.0))
        r.member[...] = jnp.where(inside, belongs, 0.0).astype(LOW)

    members()
    greeted(met)
    gather_qk.start()
    gather_vo.start()
    load_cotangent.start()
    r.small_part[s] = jnp.zeros((8, PAD), WIDE)
    r.vectors[...] = jnp.zeros_like(r.vectors)
    head_lane = iota((8, PAD), 1) // HEAD_DIM
    masks = [(head_lane == k).astype(WIDE)[0:1] for k in range(heads)]
    masks_low = [m[:, :near].astype(LOW) for m in masks]

    def spread_heads(ref, block):
        for k in range(heads):
            ref[k * two : (k + 1) * two, :] = block * masks_low[k]

    def own_heads(wide_rows, group, lanes):
        return sum(
            wide_rows[k * group : (k + 1) * group, :] * masks[k][:, :lanes] for k in range(heads)
        )

    def bands(ref, flipped):
        token, lane = iota((BLOCK, 2 * SPAN), 0), iota((BLOCK, 2 * SPAN), 1)
        upper = lane < SPAN
        offset = jnp.where(upper, lane, lane - SPAN) - token
        for k in range(heads):
            band = jnp.zeros((BLOCK, 2 * SPAN), WIDE)
            for j in range(KERNEL):
                at = KERNEL - 1 - j if flipped else j
                band = jnp.where(offset == at, r.conv_taps[k, j], band)
            high = band.astype(LOW).astype(WIDE)
            ref[k * BLOCK : (k + 1) * BLOCK, :] = jnp.where(upper, high, band - high).astype(LOW)

    bands(r.band, False)
    bands(r.band_back, True)

    def window(ext, b):
        taken = ext[pl.ds(pl.multiple_of(b * BLOCK, BLOCK), SPAN), :]
        start = b * BLOCK
        left_out = (start == item_edge) | ((s == 0) & (start == 0))
        right_out = (start + BLOCK == item_edge) | ((s == count - 1) & (start + BLOCK == rows))
        row = iota((SPAN, taken.shape[1]), 0)
        keep = jnp.where(
            row < REACH,
            jnp.where(left_out, 0.0, 1.0),
            jnp.where(row >= REACH + BLOCK, jnp.where(right_out, 0.0, 1.0), 1.0),
        )
        return taken * keep.astype(LOW)

    def convolve(band, taken):
        return own_heads(matmul_low(band[...], jnp.concatenate([taken, taken], axis=0)), BLOCK, taken.shape[1])

    gather_qk.forward()
    gather_vo.forward()
    load_inputs.wait()
    gather_qk.finish()

    def project_qk(c):
        at = chunk_rows(c)
        both = matmul_low(r.inputs[at], r.w_near[:, :, 0 : 2 * near].reshape(width, 2 * near))
        r.queries[at] = (both[:, :near] + bias_query).astype(LOW)
        r.keys[at] = both[:, near:].astype(LOW)

    loop(CHUNKS, project_qk)
    query_sums = across(r.member[...], r.queries[...])
    key_sums = across(r.member[...], r.keys[...])
    mid_scale = 1.0 / mid_count.astype(WIDE)
    edge_scale = 1.0 / jnp.maximum(edge_count, 1).astype(WIDE)
    border = jnp.concatenate([query_sums[0:BORDER], key_sums[0:BORDER]], axis=0) * mid_scale
    r.land_part[s] = dense(border).astype(LOW)
    landmarks.start()
    ups[0].start()
    ups[1].start()
    r.query_land[LAND:two] = (query_sums[LAND:two] * edge_scale).astype(LOW)
    r.key_land[LAND:two] = (key_sums[LAND:two] * edge_scale).astype(LOW)

    gather_vo.finish()

    def project_v(c):
        at = pl.ds(pl.multiple_of(REACH + c * size, REACH), size)
        values = matmul_low(r.inputs[chunk_rows(c)], r.w_near[:, :, 2 * near : 2 * near + PAD].reshape(width, PAD))
        values = values[:, :near] + bias_value
        r.value_ext[at, 0:near] = values.astype(LOW)
        r.value_ext[at, near:PAD] = jnp.zeros((size, PAD - near), LOW)

    loop(CHUNKS, project_v)
    for copy in rims[0]:
        copy.start()
    r.out_rows[...] = r.w_near[:, :, 3 * near :].reshape(width, near)

    def convolve_values(b):
        r.conv[pl.ds(pl.multiple_of(b * BLOCK, BLOCK), BLOCK), :] = convolve(
            r.band, window(r.value_ext, b)
        )[:, :near]

    blocks = rows // BLOCK
    loop(blocks - 2, lambda b: convolve_values(b + 1))

    landmarks.finish()
    lane = iota((LAND, count * BORDER), 1)
    owner = lane // BORDER
    starts = jnp.zeros((LAND, count * BORDER), jnp.int32)
    for d in range(count):
        starts = jnp.where(owner == d, jnp.maximum(d * rows - r.lengths[0], 0) // mid_count, starts)
    put = (iota((LAND, count * BORDER), 0) == starts + lane - owner * BORDER).astype(LOW)
    borders = [undense(r.land_part[d]) for d in range(count)]
    r.query_land[0:LAND] = matmul_low(put, jnp.concatenate([b[0:BORDER] for b in borders], axis=0)).astype(LOW)
    r.key_land[0:LAND] = matmul_low(put, jnp.concatenate([b[BORDER:] for b in borders], axis=0)).astype(LOW)
    spread_heads(r.query_heads, r.query_land[...])
    spread_heads(r.key_heads, r.key_land[...])

    own_values = lambda: r.value_ext[pl.ds(REACH, rows), :]

    def score_b(c):
        at = chunk_rows(c)
        r.weights_b[:, at] = against(r.query_heads[...], r.keys[at]) * scale

    def attend_b(g):
        at = pl.ds(pl.multiple_of(g * LAND, LAND), LAND)
        token = iota((LAND, rows), 1)
        at_edge = jnp.where((token >= edge_start) & (token < edge_end), 1.0, 0.0)
        member = jnp.where(lax.rem(g, 2) == 1, at_edge, 1.0 - at_edge)
        scores = jnp.where(member > 0.5, r.weights_b[at], MASKED)
        largest = jnp.max(scores, axis=1, keepdims=True)
        weights = jnp.exp(scores - largest) * member
        r.weights_b[at] = weights
        r.weights_b_low[at] = weights.astype(LOW)
        r.max_b[at] = largest
        r.total_b[at] = jnp.sum(weights, axis=1, keepdims=True)

    loop(CHUNKS, score_b)
    loop(2 * heads, attend_b)
    numer = own_heads(matmul_low(r.weights_b_low[...], own_values()), two, PAD)
    lane = iota((two, PAD), 1)
    for k in range(heads):
        numer = jnp.where(lane == near + k, r.total_b[k * two : (k + 1) * two], numer)
        numer = jnp.where(lane == near + heads + k, r.max_b[k * two : (k + 1) * two], numer)
    r.numer_out[...] = numer[0:LAND].reshape(count, LAND // count, PAD)
    numer_swap.start()
    ups[2].start()
    for copy in rims[0]:
        copy.wait_recv()
    loop(2, lambda b: convolve_values(b * (blocks - 1)))

    def wide_heads(stats, base):
        lane = iota(stats.shape, 1)
        out = stats
        for k in range(heads):
            out = jnp.where(lane // HEAD_DIM == k, stats[:, base + k : base + k + 1], out)
        return out

    edge = numer[LAND:two]
    edge_totals = wide_heads(edge, near)
    edge_totals = jnp.where(edge_totals > 0.0, edge_totals, 1.0)
    r.kernel_edge[...] = jnp.where(iota(edge.shape, 1) < near, edge / edge_totals, 0.0)

    pairs = [(k, g) for k in range(heads) for g in range(2)]
    identity = (iota((LAND, LAND), 0) == iota((LAND, LAND), 1)).astype(WIDE)
    group = lambda g: slice(g * LAND, (g + 1) * LAND)

    def first_inverse(k, g, i):
        lands = r.query_heads[k * two + g * LAND : k * two + (g + 1) * LAND, :]
        scores = against(lands, r.key_land[group(g), :]) * scale
        weights = jnp.exp(scores - jnp.max(scores, axis=1, keepdims=True))
        weights = weights / jnp.sum(weights, axis=1, keepdims=True)
        r.land_kernel[i] = weights
        return weights.T / jnp.sum(weights * weights)

    def invert(it, inverses):
        kernels = [r.land_kernel[i] for i in range(len(pairs))]
        products = [exact(a, b) for a, b in zip(kernels, inverses)]
        for i, (a, p) in enumerate(zip(inverses, products)):
            r.befores[it, i] = a
            r.products[it, i] = p
        nested = [15.0 * identity - exact(p, 7.0 * identity - p) for p in products]
        nested = [13.0 * identity - exact(p, n) for p, n in zip(products, nested)]
        return tuple(0.25 * exact(a, n) for a, n in zip(inverses, nested))

    inverses = tuple(first_inverse(k, g, i) for i, (k, g) in enumerate(pairs))
    inverses = lax.fori_loop(0, PINV_STEPS // 2, invert, inverses)


    numer_swap.finish()
    parts = [r.numer_in[d] for d in range(count)]
    largest = functools.reduce(jnp.maximum, [wide_heads(p, near + heads) for p in parts])
    lane = iota(largest.shape, 1)
    joined = jnp.zeros_like(largest)
    totals = jnp.zeros_like(largest)
    for p in parts:
        weight = jnp.exp(wide_heads(p, near + heads) - largest)
        joined = joined + jnp.where(lane < near, p * weight, 0.0)
        totals = totals + jnp.where(lane < near, wide_heads(p, near) * weight, 0.0)
    joined = jnp.where(lane < near, joined / jnp.where(lane < near, totals, 1.0), 0.0)
    for k in range(heads):
        joined = jnp.where(lane == near + k, totals[:, k * HEAD_DIM : k * HEAD_DIM + 1], joined)
        joined = jnp.where(
            lane == near + heads + k, largest[:, k * HEAD_DIM : k * HEAD_DIM + 1], joined
        )
    r.kernel_v[s] = joined
    kernel_spread.start()
    ups[0].forward()
    ups[1].forward()
    downs[0].start()
    inverses = lax.fori_loop(PINV_STEPS // 2, PINV_STEPS, invert, inverses)
    for i, inverse in enumerate(inverses):
        r.inverse[i] = inverse

    def attend_f(c):
        at = pl.ds(pl.multiple_of(c * half, half), half)
        scores = against(r.queries[at], r.key_heads[...]) * scale
        token, lane = iota((half, two), 0) + c * half, iota((half, two), 1)
        at_edge = (token >= edge_start) & (token < edge_end)
        member = jnp.where(lane < LAND, jnp.where(at_edge, 0.0, 1.0), jnp.where(at_edge, 1.0, 0.0))
        for k in range(heads):
            own = jnp.where(member > 0.5, scores[:, k * two : (k + 1) * two], MASKED)
            weights = jnp.exp(own - jnp.max(own, axis=1, keepdims=True))
            r.weights_f[at, k * two : (k + 1) * two] = weights / jnp.sum(weights, axis=1, keepdims=True)

    loop(rows // half, attend_f)
    kernel_spread.finish()
    kernel_mid = r.kernel_v[...].reshape(LAND, PAD)
    kernel_of = lambda g: kernel_mid if g == 0 else r.kernel_edge[...]
    for g in range(2):
        mixed = jnp.zeros((LAND, PAD), WIDE)
        for i, (k, own) in enumerate(pairs):
            if own == g:
                mixed = mixed + exact(r.inverse[i], kernel_of(g)) * masks[k]
        r.mixing[group(g), :] = mixed[:, :near].astype(LOW)
    spread_heads(r.mixing_heads, r.mixing[...])
    ups[2].forward()
    downs[1].start()
    downs[2].start()

    def project_out(c):
        at = chunk_rows(c)
        attended = matmul_low(r.weights_f[at].astype(LOW), r.mixing_heads[...])
        r.mixed[at] = (attended + r.conv[at]).astype(LOW)
        sums[0].offer(c, against(r.mixed[at], r.out_rows[...]).astype(LOW))

    loop(CHUNKS, project_out)
    loop(CHUNKS, sums[0].pair_up)
    downs[0].forward()

    def prepare(it):
        many = range(len(pairs))
        befores = [r.befores[it, i] for i in many]
        products = [r.products[it, i] for i in many]
        squares = [exact(p, p) for p in products]
        firsts = [exact(a, p) for a, p in zip(befores, products)]
        cubes = [exact(p, q) for p, q in zip(products, squares)]
        seconds = [exact(t, p) for t, p in zip(firsts, products)]
        for i in many:
            p, q, c = products[i].T, squares[i].T, cubes[i].T
            r.uppers[it, i, :, 0:LAND] = 3.25 * identity - 3.75 * p + 1.75 * q - 0.25 * c
            r.uppers[it, i, :, LAND:two] = 1.75 * p - 3.75 * identity - 0.25 * q
            r.uppers[it, i, :, two:] = 1.75 * identity - 0.25 * p
            r.lowers[it, i, :, 0:LAND] = befores[i].T
            r.lowers[it, i, :, LAND:two] = firsts[i].T
            r.lowers[it, i, :, two:] = -0.25 * seconds[i].T

    loop(PINV_STEPS, prepare)
    for i in range(len(pairs)):
        r.turned_kernel[i] = r.land_kernel[i].T
    r.acc[...] = jnp.zeros_like(r.acc)
    for piece in ups:
        piece.finish()
    load_cotangent.wait()
    pieces = lambda body: loop(half // step, lambda i: body(pl.multiple_of(i * step, step)))

    def norm_first(c):
        def piece(i):
            at = pl.ds(pl.multiple_of(c * size + core * half + i, step), step)
            kept = pl.ds(pl.multiple_of(c * half + i, step), step)
            pre = r.inputs[at].astype(WIDE) + sums[0].total(c, pl.ds(i, step)) + bias_out
            normed, inv = normalize(pre)
            r.norm_one[kept] = normed
            r.inv_one[kept] = inv
            r.hidden[at] = (normed * gain_one + bias_one).astype(LOW)

        sums[0].arrived(c)
        pieces(piece)
        share(0, r.hidden, c).start()

    def lift(c):
        share(0, r.hidden, c).wait_recv()
        at = chunk_rows(c)
        r.tmp[...] = matmul_low(r.hidden[at], r.full_up[...].reshape(width, feed))

        def curve(i):
            to = pl.ds(pl.multiple_of(c * size + i * step, step), step)
            value, grade = gelu_and_slope(r.tmp[pl.ds(pl.multiple_of(i * step, step), step)] + bias_up)
            r.active[to] = value.astype(LOW)
            r.slope[to] = grade.astype(LOW)

        loop(size // step, curve)

    def lower(c):
        at = chunk_rows(c)
        sums[1].offer(c, against(r.active[at], r.full_down[...].reshape(width, feed)).astype(LOW))

    def behind(c, total):
        @pl.when(c > 0)
        def _():
            total.pair_up(c - 1)

    def feed_forward(c):
        norm_first(c)
        behind(c, sums[1])
        lift(c)

        @pl.when(c == 0)
        def _():
            for piece in downs[1:]:
                piece.forward()
            for piece in downs:
                piece.finish()

        lower(c)

    loop(CHUNKS, feed_forward)
    sums[1].pair_up(CHUNKS - 1)

    order = [2, 1] + list(range(3, lines)) + [0] if lines > 2 else [1, 0]

    def feed_back(c):
        def piece(i):
            at = pl.ds(pl.multiple_of(c * size + core * half + i, step), step)
            kept = pl.ds(pl.multiple_of(c * half + i, step), step)
            pre = r.norm_one[kept] * gain_one + bias_one + sums[1].total(c, pl.ds(i, step)) + bias_down
            normed, inv = normalize(pre)
            r.output[at] = (normed * gain_two + bias_two).astype(LOW)
            grad = r.cotangent[at].astype(WIDE)
            back = norm_back(grad * gain_two, normed, inv)
            r.wide_grad[kept] = back
            r.grad_two[at] = back.astype(LOW)
            r.acc[0] += fold(grad * normed)
            r.acc[1] += fold(grad)
            r.acc[2] += fold(back)

        sums[1].arrived(c)
        pieces(piece)
        share(1, r.grad_two, c).start()
        share(2, r.output, c).start()
        behind(c, sums[2])
        share(1, r.grad_two, c).wait_recv()

        @pl.when(c == CHUNKS - 1)
        def _():
            scatter_down.fill(r.grad_two[...], r.active[...])
            scatter_down.start(*order)

        at = chunk_rows(c)
        r.tmp[...] = matmul_low(r.grad_two[at], r.full_down[...].reshape(width, feed))

        def curve(i):
            to = pl.ds(pl.multiple_of(c * size + i * step, step), step)
            value = r.tmp[pl.ds(pl.multiple_of(i * step, step), step)] * r.slope[to].astype(WIDE)
            r.grad_lift[to] = value.astype(LOW)
            r.acc[6] += fold(value)

        loop(size // step, curve)
        sums[2].offer(c, against(r.grad_lift[at], r.full_up[...].reshape(width, feed)).astype(LOW))

    loop(CHUNKS, feed_back)
    sums[2].pair_up(CHUNKS - 1)

    ups_next = list(range(2, lines)) + [0]
    r.mix_grad[...] = jnp.zeros_like(r.mix_grad)
    r.kland_grad[...] = jnp.zeros_like(r.kland_grad)

    def mix_back(c):
        def piece(i):
            at = pl.ds(pl.multiple_of(c * size + core * half + i, step), step)
            kept = pl.ds(pl.multiple_of(c * half + i, step), step)
            normed = r.norm_one[kept]
            grad = r.wide_grad[kept] + sums[2].total(c, pl.ds(i, step))
            back = norm_back(grad * gain_one, normed, r.inv_one[kept])
            r.wide_grad[kept] = back
            r.grad_one[at] = back.astype(LOW)
            r.acc[3] += fold(grad * normed)
            r.acc[4] += fold(grad)
            r.acc[5] += fold(back)

        @pl.when(c == 1)
        def _():
            scatter_down.forward(order[0])
            scatter_up.fill(r.hidden[...], r.grad_lift[...])

        if lines > 2:

            @pl.when(c == 2)
            def _():
                scatter_down.forward(order[1])

        @pl.when(c == CHUNKS - 1)
        def _():
            scatter_up.start(1)

        sums[2].arrived(c)
        pieces(piece)
        share(3, r.grad_one, c).start()
        share(3, r.grad_one, c).wait_recv()
        at = chunk_rows(c)
        grad = matmul_low(r.grad_one[at], r.out_rows[...]).astype(LOW)
        r.grad_ext[pl.ds(pl.multiple_of(REACH + c * size, REACH), size)] = grad
        weights = r.weights_f[at]
        weighted = weights * against(grad, r.mixing_heads[...])
        scores = []
        for k in range(heads):
            own = slice(k * two, (k + 1) * two)
            scores.append(weighted[:, own] - weights[:, own] * jnp.sum(weighted[:, own], axis=1, keepdims=True))
        scores = jnp.concatenate(scores, axis=1).astype(LOW)
        r.grad_query[at] = matmul_low(scores, r.key_heads[...]) * scale
        r.mix_grad[...] += across(weights.astype(LOW), grad)
        r.kland_grad[...] += across(scores, r.queries[at])

    loop(CHUNKS, mix_back)
    mix_grad = own_heads(r.mix_grad[...], two, near)
    kland_grad = own_heads(r.kland_grad[...], two, near) * scale
    each = LAND // count
    r.mix_out[...] = mix_grad[0:LAND].reshape(count, each, near)
    mix_sum.start()
    for copy in rims[1]:
        copy.start()

    def convolve_back(b):
        at = pl.ds(pl.multiple_of(b * BLOCK, BLOCK), BLOCK)
        r.conv[at] = convolve(r.band_back, window(r.grad_ext, b))

    scatter_out.fill_dense(r.grad_one[...], r.mixed[...])
    scatter_out.start()
    loop(blocks // 2 - 1, lambda b: convolve_back(b + 1))
    mix_sum.add()
    if order[2:-1]:
        scatter_down.forward(*order[2:-1])
    scatter_up.start(*ups_next[:1])
    loop(blocks // 2 - 1, lambda b: convolve_back(b + blocks // 2))
    for copy in rims[1]:
        copy.wait_recv()
    loop(2, lambda b: convolve_back(b * (blocks - 1)))

    mix_sum.finish()
    mix_grads = [r.mix_sums[...].reshape(LAND, near), mix_grad[LAND:two]]
    stats = r.kernel_v[...].reshape(LAND, PAD)
    mid_totals = wide_heads(stats, near)[:, :near]
    divisors = [mid_totals, edge_totals[:, :near]]
    inverse_grads = []
    for i, (k, g) in enumerate(pairs):
        inverse_grads.append(
            exact(mix_grads[g] * masks[k][:, :near], kernel_of(g)[:, :near], (1, 1))
        )
    shrink = [
        jnp.exp(r.max_b[k * two : k * two + LAND] - stats[:, near + heads + k : near + heads + k + 1])
        for k in range(heads)
    ]
    for g in range(2):
        grad = jnp.zeros((LAND, near), WIDE)
        for i, (k, own) in enumerate(pairs):
            if own == g:
                grad = grad + exact(r.inverse[i], mix_grads[g], (0, 0)) * masks[k][:, :near]
        grad = grad / divisors[g]
        lost = grad * kernel_of(g)[:, :near]
        for k in range(heads):
            at = slice(k * two + g * LAND, k * two + (g + 1) * LAND)
            factor = shrink[k] if g == 0 else 1.0
            r.numer_heads[at] = (grad * factor * masks[k][:, :near]).astype(LOW)
            r.total_grad[at] = -jnp.sum(lost * masks[k][:, :near], axis=1, keepdims=True) * factor

    def back_b(c):
        at = chunk_rows(c)
        values = r.value_ext[pl.ds(pl.multiple_of(REACH + c * size, REACH), size), 0:near]
        grad = against(r.numer_heads[...], values) + r.total_grad[...]
        r.scores_b[:, at] = (r.weights_b[:, at] * grad).astype(LOW)

    loop(CHUNKS, back_b)
    qland_grad = own_heads(matmul_low(r.scores_b[...], r.keys[...]), two, near) * scale
    r.land_out[:, :, 0:near] = qland_grad[0:LAND].reshape(count, each, near)
    r.land_out[:, :, near:] = kland_grad[0:LAND].reshape(count, each, near)
    land_sum.start()
    if ups_next[1:]:
        scatter_up.start(*ups_next[1:])
    scatter_up.forward(1)

    def values_back(c):
        at = chunk_rows(c)
        values = across(r.weights_b_low[:, at], r.numer_heads[...]) + r.conv[at]
        r.near_grads[at, 2 * near : 3 * near] = values.astype(LOW)
        return jnp.sum(values, axis=0, keepdims=True)

    value_bias = lax.fori_loop(
        0, CHUNKS, lambda c, total: total + values_back(c), jnp.zeros((1, near), WIDE)
    )
    scatter_v.fill_dense(r.inputs[...], r.near_grads[:, 2 * near : 3 * near])
    scatter_v.start()

    def input_terms(c):
        at = chunk_rows(c)
        r.grad_key[at] = across(r.scores_b[:, at], r.query_heads[...]) * scale
        r.near_grads[at, 0:near] = r.grad_query[at].astype(LOW)
        r.near_grads[at, near : 2 * near] = r.grad_key[at].astype(LOW)
        terms = against(r.near_grads[at], r.w_near[:, :, 0 : 3 * near].reshape(width, 3 * near))
        behind(c, sums[3])
        sums[3].offer(c, terms.astype(LOW))

    loop(CHUNKS // 2, input_terms)
    land_sum.add()
    if lines > 2:
        scatter_up.forward(2)

    def invert_back(i, carry):
        it = PINV_STEPS - 1 - i
        grads, kernel_grads = carry
        many = range(len(pairs))
        wides = [exact(grads[p], r.uppers[it, p]) for p in many]
        product_grads = [
            exact(r.lowers[it, p], jnp.concatenate([w[:, LAND:two], w[:, two:], grads[p]], axis=0))
            for p, w in enumerate(wides)
        ]
        kernel_grads = [
            old + exact(grad, r.lowers[it, p, :, 0:LAND])
            for p, (old, grad) in enumerate(zip(kernel_grads, product_grads))
        ]
        grads = [wides[p][:, 0:LAND] + exact(r.turned_kernel[p], product_grads[p]) for p in many]
        return tuple(grads), tuple(kernel_grads)

    zeros = tuple(jnp.zeros((LAND, LAND), WIDE) for _ in pairs)
    grads, kernel_grads = lax.fori_loop(0, PINV_STEPS, invert_back, (tuple(inverse_grads), zeros))
    scatter_out.forward()
    loop(CHUNKS // 2, lambda c: input_terms(c + CHUNKS // 2))
    sums[3].pair_up(CHUNKS - 1)
    for k in range(7):
        r.vectors[k : k + 1] = jnp.sum(r.acc[k], axis=0, keepdims=True)
    lanes = r.vector_out.shape[2]
    for d in range(count):
        r.vector_out[d] = r.vectors[:, d * lanes : (d + 1) * lanes] if d * lanes < width else jnp.zeros((8, lanes), WIDE)
    vector_total.start()
    if lines > 3:
        scatter_up.forward(*range(3, lines))
    qland_a = [jnp.zeros((LAND, near), WIDE)] * 2
    kland_a = [jnp.zeros((LAND, near), WIDE)] * 2
    for i, (k, g) in enumerate(pairs):
        kernel = r.land_kernel[i]
        turned = grads[i].T
        squares = jnp.sum(kernel * kernel)
        grad = kernel_grads[i] + turned / squares - kernel * (2.0 * jnp.sum(turned * kernel) / (squares * squares))
        grad = kernel * (grad - jnp.sum(kernel * grad, axis=1, keepdims=True)) * scale
        mask = masks[k][:, :near]
        qland_a[g] = qland_a[g] + exact(grad, r.key_land[group(g)].astype(WIDE)) * mask
        kland_a[g] = kland_a[g] + exact(grad, r.query_land[group(g)].astype(WIDE), (0, 0)) * mask


    land_sum.finish()
    land_total = r.land_sums[...].reshape(LAND, 2 * near)
    pick = (iota((LAND, LAND), 1) == iota((LAND, LAND), 0) + first_slot).astype(WIDE)

    def slot_grads(mid, edge):
        return jnp.concatenate([exact(pick, mid * mid_scale), edge * edge_scale], axis=0)

    def parted(both):
        high = both.astype(LOW)
        return jnp.concatenate([high, (both - high.astype(WIDE)).astype(LOW)], axis=0)

    slot_q = slot_grads(qland_a[0] + land_total[:, 0:near], qland_a[1] + qland_grad[LAND:two])
    slot_k = slot_grads(kland_a[0] + land_total[:, near:], kland_a[1] + kland_grad[LAND:two])
    r.slot_q[...] = parted(slot_q)
    r.slot_k[...] = parted(slot_k)
    r.slot_both[:, 0:near] = r.slot_q[0:two]
    r.slot_both[:, near:] = r.slot_k[0:two]
    slot_terms = against(r.slot_both[...], r.w_near[:, :, 0 : 2 * near].reshape(width, 2 * near))
    correction.offer(0, slot_terms.astype(LOW))

    def add_slots(c):
        at = chunk_rows(c)
        member = jnp.concatenate([r.member[at]] * 2, axis=1)
        queries = r.grad_query[at] + matmul_low(member, r.slot_q[...])
        keys = r.grad_key[at] + matmul_low(member, r.slot_k[...])
        r.near_grads[at, 0:near] = queries.astype(LOW)
        r.near_grads[at, near : 2 * near] = keys.astype(LOW)
        return jnp.sum(queries, axis=0, keepdims=True)

    query_bias = lax.fori_loop(
        0, CHUNKS, lambda c, total: total + add_slots(c), jnp.zeros((1, near), WIDE)
    )
    correction.pair_up(0)
    scatter_qk.fill(r.inputs[...], r.near_grads[:, 0 : 2 * near])
    scatter_qk.start()
    vector_total.add()
    scatter_v.forward()

    r.tap_grad[...] = jnp.zeros_like(r.tap_grad)

    def tap_products(b):
        own = r.grad_ext[pl.ds(pl.multiple_of(b * BLOCK + REACH, REACH), BLOCK), :]
        own = jnp.concatenate([own * m for m in masks_low], axis=0)
        r.tap_grad[:, 0:SPAN] += against(own, window(r.value_ext, b)[:, :near])

    loop(blocks, tap_products)
    token = lax.rem(iota((heads * BLOCK, 128), 0), BLOCK)
    slanted = r.tap_grad[...]
    for bit in range(6):
        moved = pltpu.roll(slanted, 128 - (1 << bit), 1)
        slanted = jnp.where(lax.rem(token // (1 << bit), 2) == 1, moved, slanted)
    for k in range(heads):
        r.small_part[s, 2 + k : 3 + k, 0:128] = jnp.sum(
            slanted[k * BLOCK : (k + 1) * BLOCK], axis=0, keepdims=True
        )
    r.small_part[s, 0:1, 0:near] = query_bias
    r.small_part[s, 1:2, 0:near] = value_bias
    small_spread.start()

    def settle_output(c):
        share(2, r.output, c).wait_recv()

    loop(CHUNKS, settle_output)
    store_output.start()
    r.grad_w_down[...] = scatter_down.finish()
    store_down.start()
    r.grad_w_up[...] = scatter_up.finish()
    store_up.start()
    r.grad_w_out[...] = undense(scatter_out.finish())
    store_out.start()
    r.grad_near[2] = undense(scatter_v.finish())
    scatter_qk.forward()
    vector_total.finish()
    for d in range(width // lanes):
        r.vector_sum[0, :, d * lanes : (d + 1) * lanes] = r.vector_sums[d]
    vector_core.start()

    def total_inputs(c):
        def piece(i):
            kept = pl.ds(pl.multiple_of(c * half + i, step), step)
            r.wide_grad[kept] = r.wide_grad[kept] + sums[3].total(c, pl.ds(i, step))

        sums[3].arrived(c)
        pieces(piece)

    loop(CHUNKS, total_inputs)
    here = pl.ds(pl.multiple_of(core * LAND, LAND), LAND)
    share_slots = remote(
        r.corr_all.at[here], r.corr_all.at[here], r.corr_s.at[0], r.corr_r.at[0], core_of_chip()
    )
    correction.arrived(0)
    r.corr_all[here] = correction.total(0, pl.ds(0, LAND)).astype(LOW)
    share_slots.start()
    share_slots.wait_recv()

    def inputs_done(c):
        slots = matmul_low(r.member[my_rows(c)], r.corr_all[...])
        r.cotangent[my_rows(c)] = (r.wide_grad[pl.ds(pl.multiple_of(c * half, half), half)] + slots).astype(LOW)
        share(4, r.cotangent, c).start()

    loop(CHUNKS, inputs_done)
    near_total = scatter_qk.finish()
    for k in range(2):
        r.grad_near[k] = near_total[:, k * near : (k + 1) * near]
    store_near.start()
    vector_core.wait_recv()
    r.vectors[0:6] = r.vector_sum[0, 0:6] + r.vector_sum[1, 0:6]
    r.vectors[6:8] = r.vector_sum[0, 6:8]
    small_spread.finish()
    r.smalls[...] = functools.reduce(jnp.add, [r.small_part[d] for d in range(count)])

    def settle_inputs(c):
        share(4, r.cotangent, c).wait_recv()

    loop(CHUNKS, settle_inputs)
    store_grad_inputs.start()

    def settle(c):
        sums[3].core_copy(c).wait_send()
        sums[3].x_copy(c).wait_send()
        for k, ref in enumerate((r.hidden, r.grad_two, r.output, r.grad_one, r.cotangent)):
            share(k, ref, c).wait_send()

    loop(CHUNKS, settle)
    vector_core.wait_send()
    correction.core_copy(0).wait_send()
    correction.x_copy(0).wait_send()
    share_slots.wait_send()
    for copy in stores:
        copy.wait()
    for copy in rims[0] + rims[1]:
        copy.wait_send()
    for group_of in gathers + scatters + spreads:
        group_of.close()


def hand_out(
    output, grad_inputs, grad_out, grad_up, grad_down, grad_near, vectors, smalls,
    to_output, to_inputs, to_query, to_key, to_value, to_out, to_up, to_down,
    bias_query, bias_value, bias_out, bias_up, bias_down, gain_one, bias_one, gain_two, bias_two, taps, sems,
):
    rows = output.shape[0] // 4
    copies = []
    for k, (ref, to) in enumerate(((output, to_output), (grad_inputs, to_inputs))):
        for j in range(4):
            at = pl.ds(j * rows, rows)
            copies.append(pltpu.make_async_copy(ref.at[at], to.at[at], sems.at[k, j]))
    for k, (ref, to) in enumerate(
        (
            (grad_near.at[0], to_query), (grad_near.at[1], to_key), (grad_near.at[2], to_value),
            (grad_out, to_out), (grad_up, to_up), (grad_down, to_down),
        )
    ):
        copies.append(pltpu.make_async_copy(ref, to, sems.at[2 + k, 0]))
    for copy in copies:
        copy.start()
    for k, ref in enumerate((gain_two, bias_two, bias_down, gain_one, bias_one, bias_out, bias_up)):
        ref[...] = vectors[k : k + 1].reshape(ref.shape)
    for k, ref in enumerate((bias_query, bias_value)):
        ref[...] = smalls[k : k + 1, 0 : ref.shape[0]].reshape(ref.shape)
    taps[...] = smalls[2 : 2 + taps.shape[0], 0:KERNEL]
    for copy in copies:
        copy.wait()


def fused_body(
    inputs, cotangent, item_lengths, w_query, w_key, w_value, w_out, w_up, w_down, bias_query, bias_value,
    bias_out, bias_up, bias_down, gain_one, bias_one, gain_two, bias_two, conv_taps,
):
    count = lax.axis_size("seq")
    rows, width = inputs.shape
    near, feed, heads = w_query.shape[1], w_up.shape[1], conv_taps.shape[0]
    size, part, lines = rows // CHUNKS, width // count, count // 2
    half, two = size // 2, 2 * LAND
    share = 128 * -(-width // 128 // count)
    low = lambda *shape: pltpu.VMEM(shape, LOW)
    wide = lambda *shape: pltpu.VMEM(shape, WIDE)
    sem = lambda *shape: pltpu.SemaphoreType.DMA(shape)
    vmem, smem = pl.BlockSpec(memory_space=pltpu.VMEM), pl.BlockSpec(memory_space=pltpu.SMEM)
    operands = dict(
        lengths=item_lengths, conv_taps=conv_taps,
        inputs_hbm=inputs, cotangent_hbm=cotangent,
        w_query=w_query, w_key=w_key, w_value=w_value, w_out=w_out, w_up=w_up, w_down=w_down,
        bias_query=bias_query, bias_value=bias_value,
        bias_out=bias_out, bias_up=bias_up, bias_down=bias_down,
        gain_one=gain_one, bias_one=bias_one, gain_two=gain_two, bias_two=bias_two,
    )
    outs = dict(
        output_hbm=((rows, width), LOW), grad_inputs_hbm=((rows, width), LOW),
        grad_w_out_hbm=((part, near), WIDE), grad_w_up_hbm=((part, feed), WIDE), grad_w_down_hbm=((part, feed), WIDE),
        grad_near_hbm=((3, part, near), WIDE), vectors=((8, width), WIDE), smalls=((8, PAD), WIDE),
    )
    scratch = dict(
        inputs=low(rows, width), cotangent=low(rows, width), output=low(rows, width),
        grad_w_out=wide(part, near), grad_w_up=wide(part, feed), grad_w_down=wide(part, feed),
        grad_near=wide(3, part, near), io=sem(8),
        packed=low(part, 4 * near), w_near=low(count, part, 4 * near), out_rows=low(width, near),
        full_up=low(count, part, feed), full_down=low(count, part, feed),
        member=low(rows, two), band=low(heads * BLOCK, 2 * SPAN), band_back=low(heads * BLOCK, 2 * SPAN),
        queries=low(rows, near), keys=low(rows, near), value_ext=low(rows + 2 * REACH, PAD),
        land_part=low(count, 3 * BORDER, 128), query_land=low(two, near), key_land=low(two, near),
        query_heads=low(heads * two, near), key_heads=low(heads * two, near),
        weights_b=wide(heads * two, rows), weights_b_low=low(heads * two, rows),
        max_b=wide(heads * two, 1), total_b=wide(heads * two, 1),
        numer_out=wide(count, LAND // count, PAD), numer_in=wide(count, LAND // count, PAD),
        kernel_v=wide(count, LAND // count, PAD), kernel_edge=wide(LAND, PAD),
        land_kernel=wide(2 * heads, LAND, LAND), inverse=wide(2 * heads, LAND, LAND),
        befores=wide(PINV_STEPS, 2 * heads, LAND, LAND), products=wide(PINV_STEPS, 2 * heads, LAND, LAND),
        uppers=wide(PINV_STEPS, 2 * heads, LAND, 3 * LAND), lowers=wide(PINV_STEPS, 2 * heads, LAND, 3 * LAND),
        turned_kernel=wide(2 * heads, LAND, LAND),
        weights_f=wide(rows, heads * two), conv=wide(rows, near),
        mixing=low(two, near), mixing_heads=low(heads * two, near), mixed=low(rows, near),
        terms=low(CHUNKS, size, width), core_in=low(CHUNKS, half, width),
        x_out=low(CHUNKS, half, width), x_in=low(2, CHUNKS, half, width),
        hidden=low(rows, width), active=low(rows, feed), slope=low(rows, feed),
        grad_two=low(rows, width), grad_lift=low(rows, feed), grad_one=low(rows, width),
        norm_one=wide(rows // 2, width), inv_one=wide(rows // 2, 1), wide_grad=wide(rows // 2, width),
        tmp=wide(size, feed), acc=wide(7, 8, width),
        grad_ext=low(rows + 2 * REACH, near), grad_query=wide(rows, near), grad_key=wide(rows, near),
        mix_grad=wide(heads * two, near), kland_grad=wide(heads * two, near),
        mix_out=wide(count, LAND // count, near), mix_in=wide(count, LAND // count, near),
        mix_sums=wide(count, LAND // count, near), land_out=wide(count, LAND // count, 2 * near),
        land_in=wide(count, LAND // count, 2 * near), land_sums=wide(count, LAND // count, 2 * near),
        vector_out=wide(count, 8, share), vector_in=wide(count, 8, share), vector_sums=wide(count, 8, share),
        tap_grad=wide(heads * BLOCK, 128), numer_heads=low(heads * two, near), total_grad=wide(heads * two, 1),
        scores_b=low(heads * two, rows), near_grads=low(rows, 3 * near),
        slot_q=low(2 * two, near), slot_k=low(2 * two, near), slot_both=low(two, 2 * near),
        vector_sum=wide(2, 8, width), small_part=wide(count, 8, PAD),
    )
    tall = 3 * part // 2
    for_out, for_up, for_down, for_qk, for_v = (
        (low(count, *of), low(lines, *of), low(lines - 1, *of), low(lines - 1, *of))
        for of in ((tall, 128), (part, feed), (part, feed), (part, 2 * near), (tall, 128))
    )
    scratch.update(
        t_out=for_out[0], yb_out=for_out[1], pr_out=for_out[2], zb_out=for_out[3],
        t_up=for_up[0], yb_up=for_up[1], pr_up=for_up[2], zb_up=for_up[3],
        t_down=for_down[0], yb_down=for_down[1], pr_down=for_down[2], zb_down=for_down[3],
        t_qk=for_qk[0], yb_qk=for_qk[1], pr_qk=for_qk[2], zb_qk=for_qk[3],
        t_v=for_v[0], yb_v=for_v[1], pr_v=for_v[2], zb_v=for_v[3],
        corr_terms=low(1, two, width), corr_core=low(1, LAND, width), corr_out=low(1, LAND, width),
        corr_in=low(2, 1, LAND, width), corr_sems=sem(1, 4, 1), corr_all=low(two, width),
        corr_s=sem(1), corr_r=sem(1),
        g_own=sem(8), g_zs=sem(8, lines - 1), g_zr=sem(8, lines - 1), g_ys=sem(8, lines), g_yr=sem(8, lines),
        s_ys=sem(5, lines), s_yr=sem(5, lines), s_zs=sem(5, lines - 1), s_zr=sem(5, lines - 1),
        e_s=sem(10, count - 1), e_r=sem(10, count - 1), h_sems=sem(4, 4, CHUNKS),
        rim_s=sem(2, 2), rim_r=sem(2, 2), share_s=sem(5, CHUNKS), share_r=sem(5, CHUNKS),
        core_s=sem(1), core_r=sem(1),
    )
    any_place = pl.BlockSpec(memory_space=pltpu.HBM)
    results = pl.pallas_call(
        functools.partial(layer_kernel, count, list(operands) + list(outs) + list(scratch)),
        out_shape=tuple(jax.ShapeDtypeStruct(*out) for out in outs.values()),
        in_specs=[smem, smem, any_place, any_place] + [vmem] * (len(operands) - 4),
        out_specs=(any_place,) * 6 + (vmem, vmem),
        scratch_shapes=list(scratch.values()),
        compiler_params=pltpu.CompilerParams(
            collective_id=1, has_side_effects=True, vmem_limit_bytes=63 * 2**20
        ),
    )(*operands.values())
    vector = lambda length: jax.ShapeDtypeStruct((length,), WIDE)
    block = lambda lanes: jax.ShapeDtypeStruct((part, lanes), WIDE)
    whole = jax.ShapeDtypeStruct((rows, width), LOW)
    return pl.pallas_call(
        hand_out,
        out_shape=(
            whole, whole, block(near), block(near), block(near), block(near), block(feed), block(feed),
            vector(near), vector(near), vector(width), vector(feed), vector(width),
            vector(width), vector(width), vector(width), vector(width),
            jax.ShapeDtypeStruct((heads, KERNEL), WIDE),
        ),
        in_specs=[vmem] * 8,
        out_specs=(any_place,) * 8 + (vmem,) * 10,
        scratch_shapes=[sem(8, 4)],
    )(*results)


def plain_body(
    inputs,
    cotangent,
    item_lengths,
    w_query,
    w_key,
    w_value,
    w_out,
    w_up,
    w_down,
    bias_query,
    bias_value,
    bias_out,
    bias_up,
    bias_down,
    gain_one,
    bias_one,
    gain_two,
    bias_two,
    conv_taps,
):
    low_type = jnp.bfloat16
    tok_rows = inputs.shape[0]
    heads_here = conv_taps.shape[0]
    width_here = heads_here * HEAD_DIM
    slots = ITEMS * LAND
    reach = (KERNEL - 1) // 2
    score_scale = HEAD_DIM ** (-0.5)
    pref = jnp.float32
    first_row = lax.axis_index("seq") * tok_rows
    positions = first_row + jnp.arange(tok_rows, dtype=jnp.int32)
    item_id, land_slot = locate(item_lengths, positions)
    rim_item = locate(
        item_lengths, first_row - reach + jnp.arange(tok_rows + 2 * reach, dtype=jnp.int32)
    )[0]
    slot_item = jnp.arange(slots, dtype=jnp.int32) // LAND
    member = land_slot[:, None] == jnp.arange(slots, dtype=jnp.int32)[None, :]
    member_low = member.astype(low_type)
    counts = jnp.repeat((item_lengths // LAND).astype(jnp.float32), LAND)
    same_f = item_id[:, None] == slot_item[None, :]
    same_b = same_f.T
    tap_cols = jnp.repeat(conv_taps, HEAD_DIM, axis=0)
    full_query, full_key, full_value, full_out, full_up, full_down = (
        lax.all_gather(w_query, "seq", axis=0, tiled=True),
        lax.all_gather(w_key, "seq", axis=0, tiled=True),
        lax.all_gather(w_value, "seq", axis=0, tiled=True),
        lax.all_gather(w_out, "seq", axis=0, tiled=True),
        lax.all_gather(w_up, "seq", axis=0, tiled=True),
        lax.all_gather(w_down, "seq", axis=0, tiled=True),
    )
    queries = (matmul_low(inputs, full_query) + bias_query).astype(low_type)
    key_rows = matmul_low(inputs, full_key).astype(low_type)
    value_rows = (matmul_low(inputs, full_value) + bias_value).astype(low_type)
    query_sums, key_sums = lax.psum(
        (across(member_low, queries), across(member_low, key_rows)), "seq"
    )
    query_land = (
        (query_sums / counts[:, None]).astype(low_type).reshape(slots, heads_here, HEAD_DIM)
    )
    key_land = (key_sums / counts[:, None]).astype(low_type).reshape(slots, heads_here, HEAD_DIM)
    query_heads = queries.reshape(tok_rows, heads_here, HEAD_DIM)
    key_heads = key_rows.reshape(tok_rows, heads_here, HEAD_DIM)
    value_heads = value_rows.reshape(tok_rows, heads_here, HEAD_DIM)
    scores_b = (
        jnp.einsum("lhd,thd->hlt", query_land, key_heads, preferred_element_type=pref) * score_scale
    )
    scores_b = jnp.where(same_b[None], scores_b, MASKED)
    maxima_b = lax.pmax(jnp.max(scores_b, axis=2), "seq")
    weights_b = jnp.exp(scores_b - maxima_b[:, :, None])
    weights_b_low = weights_b.astype(low_type)
    numer_sum, totals_b = lax.psum(
        (
            jnp.einsum("hlt,thd->lhd", weights_b_low, value_heads, preferred_element_type=pref),
            jnp.sum(weights_b, axis=2),
        ),
        "seq",
    )
    totals_cols = totals_b.T[:, :, None]
    kernel_v = numer_sum / totals_cols
    land_q = query_land.reshape(ITEMS, LAND, heads_here, HEAD_DIM)
    land_k = key_land.reshape(ITEMS, LAND, heads_here, HEAD_DIM)
    land_kernel = jax.nn.softmax(
        jnp.einsum("ilhd,imhd->ihlm", land_q, land_k, preferred_element_type=pref) * score_scale,
        axis=-1,
    )
    inverse, inverse_back = jax.vjp(pseudo_inverse, land_kernel)
    kernel_items = kernel_v.reshape(ITEMS, LAND, heads_here, HEAD_DIM)
    mixing = jnp.einsum("ihlm,imhd->ilhd", inverse, kernel_items, precision=PRECISE)
    mixing = mixing.astype(low_type).reshape(slots, heads_here, HEAD_DIM)
    scores_f = (
        jnp.einsum("thd,lhd->htl", query_heads, key_land, preferred_element_type=pref) * score_scale
    )
    weights_f = jax.nn.softmax(jnp.where(same_f[None], scores_f, MASKED), axis=-1)
    weights_f_low = weights_f.astype(low_type)
    attended = jnp.einsum("htl,lhd->thd", weights_f_low, mixing, preferred_element_type=pref)
    attended = attended.reshape(tok_rows, width_here)
    value_rim = extended(value_rows, (("seq", 0),), reach)
    conv_sum = jnp.zeros((tok_rows, width_here), jnp.float32)
    for offset in range(KERNEL):
        in_item = (rim_item[offset : offset + tok_rows] == item_id)[:, None]
        conv_sum = conv_sum + jnp.where(
            in_item,
            value_rim[offset : offset + tok_rows].astype(jnp.float32)
            * tap_cols[:, offset][None, :],
            0.0,
        )
    mixed_rows = (attended + conv_sum).astype(low_type)
    attention_sum = lax.psum(against(mixed_rows, full_out).astype(jnp.bfloat16), "head").astype(
        jnp.float32
    )
    pre_one = inputs.astype(jnp.float32) + attention_sum + bias_out
    norm_one, inv_one = normalize(pre_one)
    hidden = norm_one * gain_one + bias_one
    hidden_low = hidden.astype(low_type)
    lifted = matmul_low(hidden_low, full_up) + bias_up
    active, gelu_back = jax.vjp(gelu_tanh, lifted)
    active_low = active.astype(low_type)
    feed_terms = against(active_low, full_down)
    feed_sum = lax.psum(feed_terms.astype(jnp.bfloat16), "head").astype(jnp.float32)
    grad_output = cotangent.astype(jnp.float32)
    pre_two = hidden + feed_sum + bias_down
    norm_two, inv_two = normalize(pre_two)
    out_rows = (norm_two * gain_two + bias_two).astype(low_type)
    grad_gain_two = jnp.sum(grad_output * norm_two, axis=0)
    grad_bias_two = jnp.sum(grad_output, axis=0)
    grad_two = norm_back(grad_output * gain_two, norm_two, inv_two)
    grad_bias_down = jnp.sum(grad_two, axis=0)
    grad_two_low = grad_two.astype(low_type)
    output, grad_two_full = (out_rows, grad_two_low)
    grad_down = across(grad_two_full, active_low)
    (grad_lift,) = gelu_back(matmul_low(grad_two_full, full_down))
    grad_bias_up = jnp.sum(grad_lift, axis=0)
    grad_lift_low = grad_lift.astype(low_type)
    grad_up = across(hidden_low, grad_lift_low)
    up_terms = against(grad_lift_low, full_up)
    grad_hidden = grad_two + lax.psum(up_terms.astype(jnp.bfloat16), "head").astype(jnp.float32)
    grad_gain_one = jnp.sum(grad_hidden * norm_one, axis=0)
    grad_bias_one = jnp.sum(grad_hidden, axis=0)
    grad_one = norm_back(grad_hidden * gain_one, norm_one, inv_one)
    grad_bias_out = jnp.sum(grad_one, axis=0)
    grad_one_low = grad_one.astype(low_type)
    grad_outw = across(grad_one_low, mixed_rows)
    grad_mixed = matmul_low(grad_one_low, full_out).astype(low_type)
    grad_mixed_wide = grad_mixed.astype(jnp.float32)
    grad_heads = grad_mixed.reshape(tok_rows, heads_here, HEAD_DIM)
    grad_rim = extended(grad_mixed, (("seq", 0),), reach)
    grad_conv_v = jnp.zeros((tok_rows, width_here), jnp.float32)
    tap_terms = []
    for offset in range(KERNEL):
        in_item = (rim_item[offset : offset + tok_rows] == item_id)[:, None]
        neighbour = jnp.where(
            in_item, value_rim[offset : offset + tok_rows].astype(jnp.float32), 0.0
        )
        tap_terms.append(
            jnp.sum(
                (grad_mixed_wide * neighbour).reshape(tok_rows, heads_here, HEAD_DIM), axis=(0, 2)
            )
        )
        mirror = 2 * reach - offset
        mirror_item = (rim_item[mirror : mirror + tok_rows] == item_id)[:, None]
        grad_conv_v = grad_conv_v + jnp.where(
            mirror_item,
            grad_rim[mirror : mirror + tok_rows].astype(jnp.float32) * tap_cols[:, offset][None, :],
            0.0,
        )
    grad_taps = jnp.stack(tap_terms, axis=1)
    grad_weights_f = jnp.einsum("thd,lhd->htl", grad_heads, mixing, preferred_element_type=pref)
    grad_mix_part = jnp.einsum(
        "htl,thd->lhd", weights_f_low, grad_heads, preferred_element_type=pref
    )
    grad_scores_f = weights_f * (
        grad_weights_f - jnp.sum(weights_f * grad_weights_f, axis=2, keepdims=True)
    )
    grad_scores_f = grad_scores_f.astype(low_type)
    grad_query_f = (
        jnp.einsum("htl,lhd->thd", grad_scores_f, key_land, preferred_element_type=pref)
        * score_scale
    )
    grad_kland_part = (
        jnp.einsum("htl,thd->lhd", grad_scores_f, query_heads, preferred_element_type=pref)
        * score_scale
    )
    grad_mixing, grad_kland_f = lax.psum((grad_mix_part, grad_kland_part), "seq")
    grad_mix_items = grad_mixing.reshape(ITEMS, LAND, heads_here, HEAD_DIM)
    grad_inverse = jnp.einsum("ilhd,imhd->ihlm", grad_mix_items, kernel_items, precision=PRECISE)
    grad_kernel_v = jnp.einsum("ihlm,ilhd->imhd", inverse, grad_mix_items, precision=PRECISE)
    grad_kernel_v = grad_kernel_v.reshape(slots, heads_here, HEAD_DIM)
    (grad_land_kernel,) = inverse_back(grad_inverse)
    grad_scores_a = land_kernel * (
        grad_land_kernel - jnp.sum(land_kernel * grad_land_kernel, axis=-1, keepdims=True)
    )
    grad_scores_a = grad_scores_a * score_scale
    grad_qland_a = jnp.einsum(
        "ihlm,imhd->ilhd", grad_scores_a, land_k.astype(jnp.float32), precision=PRECISE
    )
    grad_kland_a = jnp.einsum(
        "ihlm,ilhd->imhd", grad_scores_a, land_q.astype(jnp.float32), precision=PRECISE
    )
    grad_numer = (grad_kernel_v / totals_cols).astype(low_type)
    grad_totals = -jnp.sum(grad_kernel_v * kernel_v, axis=2) / totals_b.T
    grad_weights_b = jnp.einsum(
        "lhd,thd->hlt", grad_numer, value_heads, preferred_element_type=pref
    )
    grad_weights_b = grad_weights_b + grad_totals.T[:, :, None]
    grad_scores_b = (weights_b * grad_weights_b).astype(low_type)
    grad_qland_part = (
        jnp.einsum("hlt,thd->lhd", grad_scores_b, key_heads, preferred_element_type=pref)
        * score_scale
    )
    grad_key_b = (
        jnp.einsum("hlt,lhd->thd", grad_scores_b, query_land, preferred_element_type=pref)
        * score_scale
    )
    grad_value_b = jnp.einsum(
        "hlt,lhd->thd", weights_b_low, grad_numer, preferred_element_type=pref
    )
    grad_query_rows = grad_query_f.reshape(tok_rows, width_here)
    grad_values = grad_value_b.reshape(tok_rows, width_here) + grad_conv_v
    (
        grad_qland_b,
        grad_gain_one,
        grad_bias_one,
        grad_gain_two,
        grad_bias_two,
        grad_bias_out,
        grad_bias_down,
        grad_bias_up,
        grad_taps,
        query_f_total,
        grad_bias_value,
    ) = lax.psum(
        (
            grad_qland_part,
            grad_gain_one,
            grad_bias_one,
            grad_gain_two,
            grad_bias_two,
            grad_bias_out,
            grad_bias_down,
            grad_bias_up,
            grad_taps,
            jnp.sum(grad_query_rows, axis=0),
            jnp.sum(grad_values, axis=0),
        ),
        "seq",
    )
    grad_qland = grad_qland_a.reshape(slots, width_here) + grad_qland_b.reshape(slots, width_here)
    grad_kland = grad_kland_a.reshape(slots, width_here) + grad_kland_f.reshape(slots, width_here)
    member_wide = member.astype(jnp.float32)
    grad_queries = grad_query_rows + jnp.dot(
        member_wide, grad_qland / counts[:, None], precision=PRECISE
    )
    grad_keys = grad_key_b.reshape(tok_rows, width_here) + jnp.dot(
        member_wide, grad_kland / counts[:, None], precision=PRECISE
    )
    grad_bias_query = query_f_total + jnp.sum(grad_qland, axis=0)
    queries_low = grad_queries.astype(low_type)
    keys_low = grad_keys.astype(low_type)
    values_low = grad_values.astype(low_type)
    grad_queryw = across(inputs, queries_low)
    grad_keyw = across(inputs, keys_low)
    grad_valuew = across(inputs, values_low)
    input_terms = (
        against(queries_low, full_query)
        + against(keys_low, full_key)
        + against(values_low, full_value)
    )
    grad_inputs = (
        grad_one + lax.psum(input_terms.astype(jnp.bfloat16), "head").astype(jnp.float32)
    ).astype(low_type)
    query_shard, key_shard, value_shard, out_shard, grad_up_shard, grad_down_shard = side_by_side(
        (
            grad_queryw.astype(jnp.bfloat16),
            grad_keyw.astype(jnp.bfloat16),
            grad_valuew.astype(jnp.bfloat16),
            grad_outw.astype(jnp.bfloat16),
            grad_up.astype(jnp.bfloat16),
            grad_down.astype(jnp.bfloat16),
        ),
        "seq",
        0,
        1,
    )
    return (
        output,
        grad_inputs,
        query_shard,
        key_shard,
        value_shard,
        out_shard,
        grad_up_shard,
        grad_down_shard,
        grad_bias_query,
        grad_bias_value,
        grad_bias_out,
        grad_bias_up,
        grad_bias_down,
        grad_gain_one,
        grad_bias_one,
        grad_gain_two,
        grad_bias_two,
        grad_taps,
    )


def solution(mesh):
    seq, head = mesh.shape["seq"], mesh.shape["head"]
    fits = head == 4 and seq >= 4 and LAND % (8 * seq) == 0
    return jax.shard_map(
        fused_body if fits else plain_body,
        mesh=mesh,
        in_specs=(
            P("seq", None),
            P("seq", None),
            P(),
            P("seq", "head"),
            P("seq", "head"),
            P("seq", "head"),
            P("seq", "head"),
            P("seq", "head"),
            P("seq", "head"),
            P("head"),
            P("head"),
            P(),
            P("head"),
            P(),
            P(),
            P(),
            P(),
            P(),
            P("head", None),
        ),
        out_specs=(
            P("seq", None),
            P("seq", None),
            P("seq", "head"),
            P("seq", "head"),
            P("seq", "head"),
            P("seq", "head"),
            P("seq", "head"),
            P("seq", "head"),
            P("head"),
            P("head"),
            P(),
            P("head"),
            P(),
            P(),
            P(),
            P(),
            P(),
            P("head", None),
        ),
        check_vma=False,
    )
```

```python
import functools
import types

import jax
import jax.numpy as jnp
from jax import lax
from jax.experimental import pallas as pl
from jax.experimental.pallas import tpu as pltpu
from jax.sharding import PartitionSpec as P

HEAD_DIM = 64
LAND = 64
KERNEL = 33
PINV_STEPS = 6
ITEMS = 3


PRECISE = lax.Precision.HIGHEST
EPSILON = 1e-05
MASKED = -1e30


def extended(cells, sides, width):
    for axis, dim in sides:
        count = lax.axis_size(axis)
        ends = count - 1
        head = lax.slice_in_dim(cells, 0, width, axis=dim)
        tail = lax.slice_in_dim(cells, cells.shape[dim] - width, cells.shape[dim], axis=dim)
        cells = jnp.concatenate(
            [
                lax.ppermute(tail, axis, [(i, (i + 1) % count) for i in range(ends)]),
                cells,
                lax.ppermute(head, axis, [((i + 1) % count, i) for i in range(ends)]),
            ],
            axis=dim,
        )
    return cells


def cut_along(array, dim, length):
    lengths = array.shape
    parts = array.reshape(*lengths[:dim], length, lengths[dim] // length, *lengths[dim + 1 :])
    return jnp.moveaxis(parts, dim, 0)


def sent_and_summed(array, axis, dim):
    parts = cut_along(array, dim, lax.axis_size(axis))
    arrived = lax.all_to_all(parts, axis, split_axis=0, concat_axis=0, tiled=True)
    return arrived.astype(jnp.float32).sum(axis=0)


def side_by_side(arrays, axis, dim, along):
    both = jnp.concatenate(arrays, axis=along)
    out, at, outs = (sent_and_summed(both, axis, dim), 0, [])
    for a in arrays:
        outs.append(lax.slice_in_dim(out, at, at + a.shape[along], axis=along))
        at += a.shape[along]
    return tuple(outs)


def locate(item_lengths, positions):
    item_ends = jnp.cumsum(item_lengths)
    item_starts = item_ends - item_lengths
    located = jnp.sum((positions[:, None] >= item_ends[None, :]).astype(jnp.int32), axis=1)
    inside = (positions >= 0) & (located < ITEMS)
    picked = jnp.minimum(located, ITEMS - 1)
    onehot = (picked[:, None] == jnp.arange(ITEMS, dtype=jnp.int32)[None, :]).astype(jnp.int32)
    item_start = jnp.sum(onehot * item_starts[None, :], axis=1)
    length = jnp.sum(onehot * item_lengths[None, :], axis=1)
    segment = (positions - item_start) * LAND // length
    land_slot = picked * LAND + jnp.clip(segment, 0, LAND - 1)
    return (jnp.where(inside, picked, -1), land_slot)


def normalize(values):
    row_mean = jnp.mean(values, axis=-1, keepdims=True)
    centered = values - row_mean
    variance = jnp.mean(centered * centered, axis=-1, keepdims=True)
    inv_std = lax.rsqrt(variance + EPSILON)
    return (centered * inv_std, inv_std)


def norm_back(grad_norm, normed, inv_std):
    return inv_std * (
        grad_norm
        - jnp.mean(grad_norm, axis=-1, keepdims=True)
        - normed * jnp.mean(grad_norm * normed, axis=-1, keepdims=True)
    )


def pseudo_inverse(land_kernel):
    identity = jnp.eye(LAND, dtype=jnp.float32)
    frobenius = jnp.sum(land_kernel * land_kernel, axis=(-2, -1), keepdims=True)
    result = jnp.swapaxes(land_kernel, -1, -2) / frobenius
    for iteration in range(PINV_STEPS):
        product = jnp.matmul(land_kernel, result, precision=PRECISE)
        nested = 7.0 * identity - product
        nested = 15.0 * identity - jnp.matmul(product, nested, precision=PRECISE)
        nested = 13.0 * identity - jnp.matmul(product, nested, precision=PRECISE)
        result = 0.25 * jnp.matmul(result, nested, precision=PRECISE)
    return result


def gelu_tanh(values):
    return jax.nn.gelu(values, approximate=True)


def matmul_low(left, right):
    return jnp.dot(left, right, preferred_element_type=jnp.float32)


def against(left, right):
    return lax.dot_general(
        left, right, (((1,), (1,)), ((), ())), preferred_element_type=jnp.float32
    )


def across(left, right):
    return lax.dot_general(
        left, right, (((0,), (0,)), ((), ())), preferred_element_type=jnp.float32
    )


MESH = pl.DeviceIdType.MESH
WIDE = jnp.float32
LOW = jnp.bfloat16
CHUNKS = 4
PAD = 256
REACH = (KERNEL - 1) // 2
BLOCK = 64
SPAN = BLOCK + 2 * REACH
BORDER = 16


def place():
    s, h = lax.axis_index("seq"), lax.axis_index("head")
    return s, h, s // 2, lax.rem(s, 2), h // 2, lax.rem(h, 2)


def core_of_chip():
    s, _, _, _, x, core = place()
    return (s, 2 * x + 1 - core)


def x_neighbour():
    s, _, _, _, x, core = place()
    return (s, 2 * (1 - x) + core)


def across_x():
    s, _, _, _, x, core = place()
    return (s, 2 * (1 - x) + 1 - core)


def y_neighbour():
    _, h, z, y, _, _ = place()
    return (2 * z + 1 - y, h)


def along_z(count):
    _, h, z, y, _, _ = place()
    lines = count // 2
    return [(2 * lax.rem(z + j, lines) + y, h) for j in range(1, lines)]


def along_seq(count):
    s, h = place()[:2]
    return [(lax.rem(s + j, count), h) for j in range(1, count)]


def remote(src, dst, send, recv, device):
    return pltpu.make_async_remote_copy(
        src_ref=src, dst_ref=dst, send_sem=send, recv_sem=recv, device_id=device, device_id_type=MESH
    )


def greet(devices):
    for device in devices:
        pl.semaphore_signal(
            pltpu.get_barrier_semaphore(), inc=1, device_id=device, device_id_type=MESH
        )


def greeted(devices):
    pl.semaphore_wait(pltpu.get_barrier_semaphore(), len(devices))


class Gather:
    def __init__(self, count, shard, full, lanes, own, zs, zr, ys, yr):
        s, _, z, y, _, _ = place()
        lines = count // 2
        shard = shard.at[:, lanes]
        view = lambda slot: full.at[slot, :, lanes]
        self.local = pltpu.make_async_copy(shard, view(s), own)
        self.z_copies = [
            remote(shard, view(s), zs.at[j], zr.at[j], device)
            for j, device in enumerate(along_z(count))
        ]
        self.y_copies = [remote(shard, view(s), ys.at[0], yr.at[0], y_neighbour())]
        for j in range(1, lines):
            slot = 2 * lax.rem(z - j + lines, lines) + y
            self.y_copies.append(remote(view(slot), view(slot), ys.at[j], yr.at[j], y_neighbour()))

    def start(self):
        for copy in self.z_copies:
            copy.start()
        self.y_copies[0].start()
        self.local.start()

    def forward(self):
        for z_copy, y_copy in zip(self.z_copies, self.y_copies[1:]):
            z_copy.wait_recv()
            y_copy.start()

    def finish(self):
        self.local.wait()
        for copy in self.y_copies:
            copy.wait_recv()

    def close(self):
        for copy in self.z_copies + self.y_copies:
            copy.wait_send()


class Scatter:
    def __init__(self, count, terms, y_buf, pair, z_buf, ys, yr, zs, zr):
        self.terms, self.y_buf, self.pair, self.z_buf = terms, y_buf, pair, z_buf
        _, _, self.z, self.y, _, _ = place()
        self.lines = count // 2
        self.y_copies = []
        for j in range(self.lines):
            line = lax.rem(self.z + j, self.lines)
            self.y_copies.append(
                remote(
                    terms.at[2 * line + 1 - self.y], y_buf.at[line], ys.at[j], yr.at[j], y_neighbour()
                )
            )
        self.z_copies = [
            remote(pair.at[j], z_buf.at[j], zs.at[j], zr.at[j], device)
            for j, device in enumerate(along_z(count))
        ]

    def fill(self, left, right):
        self.terms[...] = across(left, right).astype(LOW).reshape(self.terms.shape)

    def fill_dense(self, left, right):
        terms = across(left, right).astype(LOW)
        part = terms.shape[0] // self.terms.shape[0]
        terms = terms.reshape(self.terms.shape[0], part, terms.shape[1])
        self.terms[:, 0:part] = terms[:, :, 0:128]
        self.terms[:, part:] = jnp.concatenate(
            [terms[:, 0 : part // 2, 128:], terms[:, part // 2 :, 128:]], axis=2
        )

    def start(self, *away):
        for j in away or list(range(1, self.lines)) + [0]:
            self.y_copies[j].start()

    def forward(self, *away):
        for j in away or range(1, self.lines):
            line = lax.rem(self.z + j, self.lines)
            self.y_copies[j].wait_recv()
            self.pair[j - 1] = (
                self.terms[2 * line + self.y].astype(WIDE) + self.y_buf[line].astype(WIDE)
            ).astype(LOW)
            self.z_copies[j - 1].start()

    def finish(self):
        self.y_copies[0].wait_recv()
        total = self.terms[2 * self.z + self.y].astype(WIDE) + self.y_buf[self.z].astype(WIDE)
        for j, copy in enumerate(self.z_copies):
            copy.wait_recv()
            total = total + self.z_buf[j].astype(WIDE)
        return total

    def close(self):
        for copy in self.z_copies + self.y_copies:
            copy.wait_send()


class Spread:
    def __init__(self, count, blocks, send, recv):
        s = place()[0]
        self.copies = [
            remote(blocks.at[s], blocks.at[s], send.at[j], recv.at[j], device)
            for j, device in enumerate(along_seq(count))
        ]

    def start(self):
        for copy in self.copies:
            copy.start()

    def finish(self):
        for copy in self.copies:
            copy.wait_recv()

    def close(self):
        for copy in self.copies:
            copy.wait_send()


class Swap(Spread):
    def __init__(self, count, out, into, send, recv):
        s = place()[0]
        self.out, self.into = out, into
        self.copies = [
            remote(out.at[device[0]], into.at[s], send.at[j], recv.at[j], device)
            for j, device in enumerate(along_seq(count))
        ]

    def start(self):
        s = place()[0]
        super().start()
        self.into[s] = self.out[s]


class SeqSum:
    def __init__(self, count, out, into, sums, send, recv):
        self.count, self.into, self.sums = count, into, sums
        self.swap = Swap(count, out, into, send.at[0], recv.at[0])
        self.spread = Spread(count, sums, send.at[1], recv.at[1])

    def start(self):
        self.swap.start()

    def add(self):
        self.swap.finish()
        self.sums[place()[0]] = functools.reduce(jnp.add, [self.into[d] for d in range(self.count)])
        self.spread.start()

    def finish(self):
        self.spread.finish()

    def close(self):
        self.swap.close()
        self.spread.close()


class HeadSum:
    def __init__(self, turn, terms, core_in, x_out, x_in, sems):
        self.turn, self.terms, self.core_in, self.x_out, self.x_in = turn, terms, core_in, x_out, x_in
        self.sems = sems
        self.core = place()[5]
        self.half = terms.shape[1] // 2

    def core_copy(self, c, turn=None):
        sems = self.sems.at[self.turn if turn is None else turn]
        away = pl.ds(pl.multiple_of((1 - self.core) * self.half, self.half), self.half)
        return remote(
            self.terms.at[c, away], self.core_in.at[c], sems.at[0, c], sems.at[1, c], core_of_chip()
        )

    def x_copy(self, c, turn=None):
        turn = self.turn if turn is None else turn
        sems = self.sems.at[turn]
        return remote(
            self.x_out.at[c], self.x_in.at[turn % 2, c], sems.at[2, c], sems.at[3, c], x_neighbour()
        )

    def offer(self, c, rows):
        if self.turn > 0:
            self.core_copy(c, self.turn - 1).wait_send()
        self.terms[c] = rows
        self.core_copy(c).start()

    def pair_up(self, c):
        self.core_copy(c).wait_recv()
        if self.turn > 0:
            self.x_copy(c, self.turn - 1).wait_send()
        here = pl.ds(pl.multiple_of(self.core * self.half, self.half), self.half)
        self.x_out[c] = (
            self.terms[c, here].astype(WIDE) + self.core_in[c].astype(WIDE)
        ).astype(LOW)
        self.x_copy(c).start()

    def arrived(self, c):
        self.x_copy(c).wait_recv()

    def total(self, c, rows):
        return self.x_out[c, rows].astype(WIDE) + self.x_in[self.turn % 2, c, rows].astype(WIDE)


def iota(shape, dim):
    return lax.broadcasted_iota(jnp.int32, shape, dim)


def fold(rows):
    return rows.reshape(rows.shape[0] // 8, 8, rows.shape[1]).sum(axis=0)


def gelu_and_slope(v):
    square = v * v
    t = jnp.tanh(0.7978845608 * (v + 0.044715 * v * square))
    half = 0.5 * (1.0 + t)
    slope = half + 0.5 * v * (1.0 - t * t) * (0.7978845608 * (1.0 + 0.134145 * square))
    return v * half, slope


def exact(left, right, dims=(1, 0)):
    return lax.dot_general(
        left,
        right,
        (((dims[0],), (dims[1],)), ((), ())),
        preferred_element_type=WIDE,
        precision=PRECISE,
    )


def dense(block):
    n = block.shape[0]
    rest = jnp.concatenate([block[0 : n // 2, 128:], block[n // 2 :, 128:]], axis=1)
    return jnp.concatenate([block[:, 0:128], rest], axis=0)


def undense(block):
    n = block.shape[0] * 2 // 3
    rest = jnp.concatenate([block[n:, 0:64], block[n:, 64:128]], axis=0)
    return jnp.concatenate([block[0:n], rest], axis=1)


def halves(wide_block):
    high = wide_block.astype(LOW)
    return high, (wide_block - high.astype(WIDE)).astype(LOW)


def thrice(left, right):
    return matmul_low(left[0], right[0]) + (matmul_low(left[0], right[1]) + matmul_low(left[1], right[0]))


def loop(count, body):
    lax.fori_loop(0, count, lambda i, carry: (body(i), carry)[1], 0)


def layer_kernel(count, names, *refs):
    r = types.SimpleNamespace(**dict(zip(names, refs)))
    s, h, z, y, x, core = place()
    rows, width = r.inputs_hbm.shape
    near = r.w_query.shape[1]
    heads = near // HEAD_DIM
    feed = r.w_up.shape[1]
    size = rows // CHUNKS
    half = size // 2
    step = 32
    lines = count // 2
    two = 2 * LAND
    scale = HEAD_DIM**-0.5
    chunk_rows = lambda c: pl.ds(pl.multiple_of(c * size, size), size)
    my_rows = lambda c: pl.ds(pl.multiple_of(c * size + core * half, half), half)
    everyone = along_seq(count)
    before, after = (lax.rem(s + count - 1, count), h), (lax.rem(s + 1, count), h)

    load_shards, load_vectors = (
        [pltpu.make_async_copy(ref, held, sems.at[k]) for k, (ref, held) in enumerate(pairs_of)]
        for pairs_of, sems in (
            (
                (
                    (r.w_query_hbm, r.w_query), (r.w_key_hbm, r.w_key),
                    (r.w_value_hbm, r.w_value), (r.w_out_hbm, r.w_out),
                ),
                r.shard_sems,
            ),
            (
                (
                    (r.bias_query_hbm, r.bias_query), (r.bias_value_hbm, r.bias_value), (r.bias_out_hbm, r.bias_out),
                    (r.bias_up_hbm, r.bias_up), (r.bias_down_hbm, r.bias_down), (r.gain_one_hbm, r.gain_one),
                    (r.bias_one_hbm, r.bias_one), (r.gain_two_hbm, r.gain_two), (r.bias_two_hbm, r.bias_two),
                ),
                r.vector_sems,
            ),
        )
    )

    def gather(k, shard, full, lo, hi):
        return Gather(
            count, shard, full, slice(lo, hi), r.g_own.at[k], r.g_zs.at[k], r.g_zr.at[k], r.g_ys.at[k], r.g_yr.at[k]
        )

    def scatter(k, terms, y_buf, pair, z_buf):
        return Scatter(
            count, terms, y_buf, pair, z_buf, r.s_ys.at[k], r.s_yr.at[k], r.s_zs.at[k], r.s_zr.at[k]
        )

    gather_qk = gather(0, r.packed, r.w_near, 0, 2 * near)
    gather_vo = gather(1, r.packed, r.w_near, 2 * near, 4 * near)
    third = feed // 3
    ups = [gather(2 + k, r.w_up, r.full_up, k * third, (k + 1) * third) for k in range(3)]
    downs = [gather(5 + k, r.w_down, r.full_down, k * third, (k + 1) * third) for k in range(3)]
    gathers = [gather_qk, gather_vo] + ups + downs
    scatter_out = scatter(0, r.t_out, r.yb_out, r.pr_out, r.zb_out)
    scatter_up = scatter(1, r.t_up, r.yb_up, r.pr_up, r.zb_up)
    scatter_down = scatter(2, r.t_down, r.yb_down, r.pr_down, r.zb_down)
    scatter_qk = scatter(3, r.t_qk, r.yb_qk, r.pr_qk, r.zb_qk)
    scatter_v = scatter(4, r.t_v, r.yb_v, r.pr_v, r.zb_v)
    scatters = [scatter_out, scatter_up, scatter_down, scatter_qk, scatter_v]
    correction = HeadSum(0, r.corr_terms, r.corr_core, r.corr_out, r.corr_in, r.corr_sems)
    sums = [HeadSum(k, r.terms, r.core_in, r.x_out, r.x_in, r.h_sems) for k in range(3)]

    out_copies = [
        remote(r.out_turned.at[0], r.out_turned.at[1], r.w_s.at[0], r.w_r.at[0], core_of_chip()),
        remote(r.out_turned.at[0], r.out_turned.at[2], r.w_s.at[1], r.w_r.at[1], x_neighbour()),
        remote(r.out_turned.at[2], r.out_turned.at[3], r.w_s.at[2], r.w_r.at[2], core_of_chip()),
    ]

    def mixed_copies(c):
        return [
            remote(r.mixed_out.at[c, part], r.mixed_in.at[k, c], r.m_s.at[k, c], r.m_r.at[k, c], device)
            for k, (part, device) in enumerate(
                ((1 - core, core_of_chip()), (core, x_neighbour()), (1 - core, across_x()))
            )
        ]

    landmarks = Spread(count, r.land_part, r.e_s.at[0], r.e_r.at[0])
    numer_swap = Swap(count, r.numer_out, r.numer_in, r.e_s.at[1], r.e_r.at[1])
    kernel_spread = Spread(count, r.kernel_v, r.e_s.at[2], r.e_r.at[2])
    small_spread = Spread(count, r.small_part, r.e_s.at[3], r.e_r.at[3])
    mix_sum, land_sum, vector_total = (
        SeqSum(count, out, into, total, r.e_s.at[pl.ds(4 + 2 * k, 2)], r.e_r.at[pl.ds(4 + 2 * k, 2)])
        for k, (out, into, total) in enumerate(
            (
                (r.mix_out, r.mix_in, r.mix_sums),
                (r.land_out, r.land_in, r.land_sums),
                (r.vector_out, r.vector_in, r.vector_sums),
            )
        )
    )
    spreads = [landmarks, numer_swap, kernel_spread, small_spread, mix_sum, land_sum, vector_total]

    def rim(k, ext):
        first = remote(
            ext.at[pl.ds(REACH, REACH)], ext.at[pl.ds(REACH + rows, REACH)], r.rim_s.at[k, 0], r.rim_r.at[k, 0], before
        )
        last = remote(
            ext.at[pl.ds(rows, REACH)], ext.at[pl.ds(0, REACH)], r.rim_s.at[k, 1], r.rim_r.at[k, 1], after
        )
        return [first, last]

    rims = [rim(0, r.value_ext), rim(1, r.grad_ext)]

    def share(k, ref, c):
        return remote(
            ref.at[my_rows(c)], ref.at[my_rows(c)], r.share_s.at[k, c], r.share_r.at[k, c], core_of_chip()
        )

    load_inputs = pltpu.make_async_copy(r.inputs_hbm, r.inputs, r.io.at[0])
    load_cotangent = pltpu.make_async_copy(r.cotangent_hbm, r.cotangent, r.io.at[1])
    stores = [
        pltpu.make_async_copy(ref, out, r.io.at[2 + k])
        for k, (ref, out) in enumerate(
            (
                (r.output, r.output_hbm),
                (r.grad_w_out, r.grad_w_out_hbm),
                (r.grad_w_up, r.grad_w_up_hbm),
                (r.grad_w_down, r.grad_w_down_hbm),
                (r.grad_near, r.grad_near_hbm),
            )
        )
    ]
    store_output, store_out, store_up, store_down, store_near = stores
    vector_core = remote(
        r.vector_sum.at[0], r.vector_sum.at[1], r.core_s.at[0], r.core_r.at[0], core_of_chip()
    )

    met = [core_of_chip(), x_neighbour(), across_x()] + everyone
    greet(met)
    for copy in load_shards + [load_inputs] + load_vectors:
        copy.start()
    for copy in load_shards:
        copy.wait()
    r.packed[:, 0:near] = r.w_query[...]
    r.packed[:, near : 2 * near] = r.w_key[...]
    r.packed[:, 2 * near : 3 * near] = r.w_value[...]
    r.packed[:, 3 * near : 4 * near] = r.w_out[...]
    ends = jnp.where(s == 0, r.lengths[0], jnp.where(s == count - 1, r.lengths[2], 0))
    edge_start = jnp.where(s == 0, 0, rows - ends)
    edge_end = edge_start + ends
    edge_count = ends // LAND
    mid_count = r.lengths[1] // LAND
    mid_first = s * rows - r.lengths[0]
    first_slot = jnp.maximum(mid_first, 0) // mid_count
    item_edge = jnp.where(s == 0, ends, jnp.where(s == count - 1, rows - ends, -1))

    def members():
        token, lane = iota((rows, two), 0), iota((rows, two), 1)
        mid = lane < LAND
        at_edge = (token >= edge_start) & (token < edge_end)
        start = jnp.where(mid, (first_slot + lane) * mid_count - mid_first, (lane - LAND) * edge_count + edge_start)
        length = jnp.where(mid, mid_count, edge_count)
        inside = (token >= start) & (token < start + length)
        belongs = jnp.where(mid, jnp.where(at_edge, 0.0, 1.0), jnp.where(at_edge, 1.0, 0.0))
        r.member[...] = jnp.where(inside, belongs, 0.0).astype(LOW)

    members()
    greeted(met)
    gather_qk.start()
    gather_vo.start()
    load_cotangent.start()
    r.small_part[s] = jnp.zeros((8, PAD), WIDE)
    r.vectors[...] = jnp.zeros_like(r.vectors)
    head_lane = iota((8, PAD), 1) // HEAD_DIM
    masks = [(head_lane == k).astype(WIDE)[0:1] for k in range(heads)]
    masks_low = [m[:, :near].astype(LOW) for m in masks]

    def spread_heads(ref, block):
        for k in range(heads):
            ref[k * two : (k + 1) * two, :] = block * masks_low[k]

    def own_heads(wide_rows, group, lanes):
        return sum(
            wide_rows[k * group : (k + 1) * group, :] * masks[k][:, :lanes] for k in range(heads)
        )

    def bands(ref, flipped):
        token, lane = iota((BLOCK, 2 * SPAN), 0), iota((BLOCK, 2 * SPAN), 1)
        upper = lane < SPAN
        offset = jnp.where(upper, lane, lane - SPAN) - token
        for k in range(heads):
            band = jnp.zeros((BLOCK, 2 * SPAN), WIDE)
            for j in range(KERNEL):
                at = KERNEL - 1 - j if flipped else j
                band = jnp.where(offset == at, r.conv_taps[k, j], band)
            high = band.astype(LOW).astype(WIDE)
            ref[k * BLOCK : (k + 1) * BLOCK, :] = jnp.where(upper, high, band - high).astype(LOW)

    bands(r.band, False)
    bands(r.band_back, True)

    def window(ext, b):
        taken = ext[pl.ds(pl.multiple_of(b * BLOCK, BLOCK), SPAN), :]
        start = b * BLOCK
        left_out = (start == item_edge) | ((s == 0) & (start == 0))
        right_out = (start + BLOCK == item_edge) | ((s == count - 1) & (start + BLOCK == rows))
        row = iota((SPAN, taken.shape[1]), 0)
        keep = jnp.where(
            row < REACH,
            jnp.where(left_out, 0.0, 1.0),
            jnp.where(row >= REACH + BLOCK, jnp.where(right_out, 0.0, 1.0), 1.0),
        )
        return taken * keep.astype(LOW)

    def convolve(band, taken):
        return own_heads(matmul_low(band[...], jnp.concatenate([taken, taken], axis=0)), BLOCK, taken.shape[1])

    gather_qk.forward()
    gather_vo.forward()
    load_inputs.wait()
    for copy in load_vectors:
        copy.wait()
    flat = lambda ref: ref[...].reshape(1, ref.shape[0])
    bias_query, bias_value, bias_out = flat(r.bias_query), flat(r.bias_value), flat(r.bias_out)
    bias_up, bias_down = flat(r.bias_up), flat(r.bias_down)
    gain_one, bias_one, gain_two, bias_two = (
        flat(r.gain_one), flat(r.bias_one), flat(r.gain_two), flat(r.bias_two)
    )
    gather_qk.finish()

    def project_qk(c):
        at = chunk_rows(c)
        both = matmul_low(r.inputs[at], r.w_near[:, :, 0 : 2 * near].reshape(width, 2 * near))
        r.queries[at] = (both[:, :near] + bias_query).astype(LOW)
        r.keys[at] = both[:, near:].astype(LOW)

    loop(CHUNKS, project_qk)
    query_sums = across(r.member[...], r.queries[...])
    key_sums = across(r.member[...], r.keys[...])
    mid_scale = 1.0 / mid_count.astype(WIDE)
    edge_scale = 1.0 / jnp.maximum(edge_count, 1).astype(WIDE)
    border = jnp.concatenate([query_sums[0:BORDER], key_sums[0:BORDER]], axis=0) * mid_scale
    r.land_part[s] = dense(border).astype(LOW)
    landmarks.start()
    ups[0].start()
    ups[1].start()
    r.query_land[LAND:two] = (query_sums[LAND:two] * edge_scale).astype(LOW)
    r.key_land[LAND:two] = (key_sums[LAND:two] * edge_scale).astype(LOW)

    gather_vo.finish()

    def project_v(c):
        at = pl.ds(pl.multiple_of(REACH + c * size, REACH), size)
        values = matmul_low(r.inputs[chunk_rows(c)], r.w_near[:, :, 2 * near : 2 * near + PAD].reshape(width, PAD))
        values = values[:, :near] + bias_value
        r.value_ext[at, 0:near] = values.astype(LOW)
        r.value_ext[at, near:PAD] = jnp.zeros((size, PAD - near), LOW)

    loop(CHUNKS, project_v)
    for copy in rims[0]:
        copy.start()
    r.out_turned[0] = r.w_near[:, :, 3 * near :].reshape(width, near).T
    for copy in out_copies[0:2]:
        copy.start()

    def convolve_values(b):
        r.conv[pl.ds(pl.multiple_of(b * BLOCK, BLOCK), BLOCK), :] = convolve(
            r.band, window(r.value_ext, b)
        )[:, :near]

    blocks = rows // BLOCK
    loop(blocks - 2, lambda b: convolve_values(b + 1))

    landmarks.finish()
    lane = iota((LAND, count * BORDER), 1)
    owner = lane // BORDER
    starts = jnp.zeros((LAND, count * BORDER), jnp.int32)
    for d in range(count):
        starts = jnp.where(owner == d, jnp.maximum(d * rows - r.lengths[0], 0) // mid_count, starts)
    put = (iota((LAND, count * BORDER), 0) == starts + lane - owner * BORDER).astype(LOW)
    borders = [undense(r.land_part[d]) for d in range(count)]
    r.query_land[0:LAND] = matmul_low(put, jnp.concatenate([b[0:BORDER] for b in borders], axis=0)).astype(LOW)
    r.key_land[0:LAND] = matmul_low(put, jnp.concatenate([b[BORDER:] for b in borders], axis=0)).astype(LOW)
    spread_heads(r.query_heads, r.query_land[...])
    spread_heads(r.key_heads, r.key_land[...])

    own_values = lambda: r.value_ext[pl.ds(REACH, rows), :]

    def score_b(c):
        at = chunk_rows(c)
        r.weights_b[:, at] = against(r.query_heads[...], r.keys[at]) * scale

    def attend_b(g):
        at = pl.ds(pl.multiple_of(g * LAND, LAND), LAND)
        token = iota((LAND, rows), 1)
        at_edge = jnp.where((token >= edge_start) & (token < edge_end), 1.0, 0.0)
        member = jnp.where(lax.rem(g, 2) == 1, at_edge, 1.0 - at_edge)
        scores = jnp.where(member > 0.5, r.weights_b[at], MASKED)
        largest = jnp.max(scores, axis=1, keepdims=True)
        weights = jnp.exp(scores - largest) * member
        r.weights_b[at] = weights
        r.max_b[at] = largest
        r.total_b[at] = jnp.sum(weights, axis=1, keepdims=True)

    loop(CHUNKS, score_b)
    loop(2 * heads, attend_b)
    numer = own_heads(matmul_low(r.weights_b[...].astype(LOW), own_values()), two, PAD)
    lane = iota((two, PAD), 1)
    for k in range(heads):
        numer = jnp.where(lane == near + k, r.total_b[k * two : (k + 1) * two], numer)
        numer = jnp.where(lane == near + heads + k, r.max_b[k * two : (k + 1) * two], numer)
    r.numer_out[...] = numer[0:LAND].reshape(count, LAND // count, PAD)
    numer_swap.start()
    ups[2].start()
    for copy in rims[0]:
        copy.wait_recv()
    loop(2, lambda b: convolve_values(b * (blocks - 1)))

    def wide_heads(stats, base):
        lane = iota(stats.shape, 1)
        out = stats
        for k in range(heads):
            out = jnp.where(lane // HEAD_DIM == k, stats[:, base + k : base + k + 1], out)
        return out

    edge = numer[LAND:two]
    edge_totals = wide_heads(edge, near)
    edge_totals = jnp.where(edge_totals > 0.0, edge_totals, 1.0)
    r.kernel_edge[...] = jnp.where(iota(edge.shape, 1) < near, edge / edge_totals, 0.0)

    pairs = [(k, g) for k in range(heads) for g in range(2)]
    identity = (iota((LAND, LAND), 0) == iota((LAND, LAND), 1)).astype(WIDE)
    group = lambda g: slice(g * LAND, (g + 1) * LAND)

    def first_inverse(k, g, i):
        lands = r.query_heads[k * two + g * LAND : k * two + (g + 1) * LAND, :]
        scores = against(lands, r.key_land[group(g), :]) * scale
        weights = jnp.exp(scores - jnp.max(scores, axis=1, keepdims=True))
        weights = weights / jnp.sum(weights, axis=1, keepdims=True)
        r.land_kernel[i] = weights
        return weights.T / jnp.sum(weights * weights)

    def invert(it, inverses):
        kernels = [r.land_kernel[i] for i in range(len(pairs))]
        products = [exact(a, b) for a, b in zip(kernels, inverses)]
        for i, (a, p) in enumerate(zip(inverses, products)):
            r.befores[it, i] = a
            r.products[it, i] = p
        nested = [15.0 * identity - exact(p, 7.0 * identity - p) for p in products]
        nested = [13.0 * identity - exact(p, n) for p, n in zip(products, nested)]
        return tuple(0.25 * exact(a, n) for a, n in zip(inverses, nested))

    inverses = tuple(first_inverse(k, g, i) for i, (k, g) in enumerate(pairs))
    inverses = lax.fori_loop(0, PINV_STEPS // 2, invert, inverses)


    numer_swap.finish()
    parts = [r.numer_in[d] for d in range(count)]
    largest = functools.reduce(jnp.maximum, [wide_heads(p, near + heads) for p in parts])
    lane = iota(largest.shape, 1)
    joined = jnp.zeros_like(largest)
    totals = jnp.zeros_like(largest)
    for p in parts:
        weight = jnp.exp(wide_heads(p, near + heads) - largest)
        joined = joined + jnp.where(lane < near, p * weight, 0.0)
        totals = totals + jnp.where(lane < near, wide_heads(p, near) * weight, 0.0)
    joined = jnp.where(lane < near, joined / jnp.where(lane < near, totals, 1.0), 0.0)
    for k in range(heads):
        joined = jnp.where(lane == near + k, totals[:, k * HEAD_DIM : k * HEAD_DIM + 1], joined)
        joined = jnp.where(
            lane == near + heads + k, largest[:, k * HEAD_DIM : k * HEAD_DIM + 1], joined
        )
    r.kernel_v[s] = joined
    kernel_spread.start()
    ups[0].forward()
    ups[1].forward()
    downs[0].start()
    inverses = lax.fori_loop(PINV_STEPS // 2, PINV_STEPS, invert, inverses)
    for i, inverse in enumerate(inverses):
        r.inverse[i] = inverse

    def attend_f(c):
        at = pl.ds(pl.multiple_of(c * half, half), half)
        scores = against(r.queries[at], r.key_heads[...]) * scale
        token, lane = iota((half, two), 0) + c * half, iota((half, two), 1)
        at_edge = (token >= edge_start) & (token < edge_end)
        member = jnp.where(lane < LAND, jnp.where(at_edge, 0.0, 1.0), jnp.where(at_edge, 1.0, 0.0))
        for k in range(heads):
            own = jnp.where(member > 0.5, scores[:, k * two : (k + 1) * two], MASKED)
            weights = jnp.exp(own - jnp.max(own, axis=1, keepdims=True))
            r.weights_f[at, k * two : (k + 1) * two] = weights / jnp.sum(weights, axis=1, keepdims=True)

    loop(rows // half, attend_f)
    kernel_spread.finish()
    kernel_mid = r.kernel_v[...].reshape(LAND, PAD)
    kernel_of = lambda g: kernel_mid if g == 0 else r.kernel_edge[...]
    for g in range(2):
        mixed = jnp.zeros((LAND, PAD), WIDE)
        for i, (k, own) in enumerate(pairs):
            if own == g:
                mixed = mixed + exact(r.inverse[i], kernel_of(g)) * masks[k]
        r.mixing[group(g), :] = mixed[:, :near].astype(LOW)
    spread_heads(r.mixing_heads, r.mixing[...])
    ups[2].forward()
    downs[1].start()
    downs[2].start()

    def project_out(c):
        at = chunk_rows(c)
        attended = matmul_low(r.weights_f[at].astype(LOW), r.mixing_heads[...])
        r.mixed[at] = (attended + r.conv[at]).astype(LOW)
        for part in range(2):
            at = pl.ds(pl.multiple_of(c * size + part * half, half), half)
            r.mixed_out[c, part] = dense(r.mixed[at])
        for copy in mixed_copies(c):
            copy.start()

    out_copies[1].wait_recv()
    out_copies[2].start()
    loop(CHUNKS, project_out)
    out_copies[0].wait_recv()
    out_copies[2].wait_recv()
    downs[0].forward()

    def prepare(it):
        many = range(len(pairs))
        befores = [r.befores[it, i] for i in many]
        products = [r.products[it, i] for i in many]
        squares = [exact(p, p) for p in products]
        firsts = [exact(a, p) for a, p in zip(befores, products)]
        cubes = [exact(p, q) for p, q in zip(products, squares)]
        seconds = [exact(t, p) for t, p in zip(firsts, products)]
        for i in many:
            p, q, c = products[i].T, squares[i].T, cubes[i].T
            uppers = (
                3.25 * identity - 3.75 * p + 1.75 * q - 0.25 * c,
                1.75 * p - 3.75 * identity - 0.25 * q,
                1.75 * identity - 0.25 * p,
            )
            for k, (upper, lower) in enumerate(zip(uppers, (befores[i].T, firsts[i].T, -0.25 * seconds[i].T))):
                for half_of, (a, b) in enumerate(zip(halves(upper), halves(lower))):
                    r.uppers[it, i, half_of, :, group(k)] = a
                    r.lowers[it, i, half_of, :, group(k)] = b

    loop(PINV_STEPS, prepare)
    for i in range(len(pairs)):
        r.turned_kernel[i, 0], r.turned_kernel[i, 1] = halves(r.land_kernel[i].T)
    r.acc[...] = jnp.zeros_like(r.acc)
    for piece in ups:
        piece.finish()
    load_cotangent.wait()
    pieces = lambda body: loop(half // step, lambda i: body(pl.multiple_of(i * step, step)))

    def norm_first(c):
        for copy in mixed_copies(c):
            copy.wait_recv()
        theirs = [undense(r.mixed_in[k, c]) for k in range(3)]
        r.tmp[0:half] = matmul_low(r.mixed[my_rows(c)], r.out_turned[0]) + matmul_low(theirs[0], r.out_turned[1])
        r.tmp[half:size] = matmul_low(theirs[1], r.out_turned[2]) + matmul_low(theirs[2], r.out_turned[3])

        def piece(i):
            at = pl.ds(pl.multiple_of(c * size + core * half + i, step), step)
            kept = pl.ds(pl.multiple_of(c * half + i, step), step)
            attended = r.tmp[pl.ds(i, step)] + r.tmp[pl.ds(pl.multiple_of(half + i, step), step)]
            pre = r.inputs[at].astype(WIDE) + attended + bias_out
            normed, inv = normalize(pre)
            r.norm_one[kept] = normed
            r.inv_one[kept] = inv
            r.hidden[at] = (normed * gain_one + bias_one).astype(LOW)

        pieces(piece)
        share(0, r.hidden, c).start()

    def lift(c):
        share(0, r.hidden, c).wait_recv()
        at = chunk_rows(c)
        r.tmp[...] = matmul_low(r.hidden[at], r.full_up[...].reshape(width, feed))

        def curve(i):
            to = pl.ds(pl.multiple_of(c * size + i * step, step), step)
            value, grade = gelu_and_slope(r.tmp[pl.ds(pl.multiple_of(i * step, step), step)] + bias_up)
            r.active[to] = value.astype(LOW)
            r.slope[to] = grade.astype(LOW)

        loop(size // step, curve)

    def lower(c):
        at = chunk_rows(c)
        sums[0].offer(c, against(r.active[at], r.full_down[...].reshape(width, feed)).astype(LOW))

    def behind(c, total):
        @pl.when(c > 0)
        def _():
            total.pair_up(c - 1)

    def feed_forward(c):
        norm_first(c)
        behind(c, sums[0])
        lift(c)

        @pl.when(c == 0)
        def _():
            for piece in downs[1:]:
                piece.forward()
            for piece in downs:
                piece.finish()

        lower(c)

    loop(CHUNKS, feed_forward)
    sums[0].pair_up(CHUNKS - 1)

    order = [2, 1] + list(range(3, lines)) + [0] if lines > 2 else [1, 0]

    def feed_back(c):
        def piece(i):
            at = pl.ds(pl.multiple_of(c * size + core * half + i, step), step)
            kept = pl.ds(pl.multiple_of(c * half + i, step), step)
            pre = r.norm_one[kept] * gain_one + bias_one + sums[0].total(c, pl.ds(i, step)) + bias_down
            normed, inv = normalize(pre)
            r.output[at] = (normed * gain_two + bias_two).astype(LOW)
            grad = r.cotangent[at].astype(WIDE)
            back = norm_back(grad * gain_two, normed, inv)
            r.wide_grad[kept] = back
            r.grad_two[at] = back.astype(LOW)
            r.acc[0] += fold(grad * normed)
            r.acc[1] += fold(grad)
            r.acc[2] += fold(back)

        sums[0].arrived(c)
        pieces(piece)
        share(1, r.grad_two, c).start()
        share(2, r.output, c).start()
        behind(c, sums[1])
        share(1, r.grad_two, c).wait_recv()

        @pl.when(c == CHUNKS - 1)
        def _():
            scatter_down.fill(r.grad_two[...], r.active[...])
            scatter_down.start(*order)

        at = chunk_rows(c)
        r.tmp[...] = matmul_low(r.grad_two[at], r.full_down[...].reshape(width, feed))

        def curve(i):
            to = pl.ds(pl.multiple_of(c * size + i * step, step), step)
            value = r.tmp[pl.ds(pl.multiple_of(i * step, step), step)] * r.slope[to].astype(WIDE)
            r.grad_lift[to] = value.astype(LOW)
            r.acc[6] += fold(value)

        loop(size // step, curve)
        sums[1].offer(c, against(r.grad_lift[at], r.full_up[...].reshape(width, feed)).astype(LOW))

    loop(CHUNKS, feed_back)
    sums[1].pair_up(CHUNKS - 1)

    ups_next = list(range(2, lines)) + [0]
    r.mix_grad[...] = jnp.zeros_like(r.mix_grad)
    r.kland_grad[...] = jnp.zeros_like(r.kland_grad)

    def mix_back(c):
        def piece(i):
            at = pl.ds(pl.multiple_of(c * size + core * half + i, step), step)
            kept = pl.ds(pl.multiple_of(c * half + i, step), step)
            normed = r.norm_one[kept]
            grad = r.wide_grad[kept] + sums[1].total(c, pl.ds(i, step))
            back = norm_back(grad * gain_one, normed, r.inv_one[kept])
            r.wide_grad[kept] = back
            r.grad_one[at] = back.astype(LOW)
            r.acc[3] += fold(grad * normed)
            r.acc[4] += fold(grad)
            r.acc[5] += fold(back)

        @pl.when(c == 1)
        def _():
            scatter_down.forward(order[0])
            scatter_up.fill(r.hidden[...], r.grad_lift[...])

        if lines > 2:

            @pl.when(c == 2)
            def _():
                scatter_down.forward(order[1])

        @pl.when(c == CHUNKS - 1)
        def _():
            scatter_up.start(1)

        sums[1].arrived(c)
        pieces(piece)
        share(3, r.grad_one, c).start()
        share(3, r.grad_one, c).wait_recv()
        at = chunk_rows(c)
        grad = against(r.grad_one[at], r.out_turned[0]).astype(LOW)
        r.grad_ext[pl.ds(pl.multiple_of(REACH + c * size, REACH), size)] = grad
        weights = r.weights_f[at]
        weighted = weights * against(grad, r.mixing_heads[...])
        scores = []
        for k in range(heads):
            own = slice(k * two, (k + 1) * two)
            scores.append(weighted[:, own] - weights[:, own] * jnp.sum(weighted[:, own], axis=1, keepdims=True))
        scores = jnp.concatenate(scores, axis=1).astype(LOW)
        r.grad_query[at] = matmul_low(scores, r.key_heads[...]) * scale
        r.mix_grad[...] += across(weights.astype(LOW), grad)
        r.kland_grad[...] += across(scores, r.queries[at])

    loop(CHUNKS, mix_back)
    mix_grad = own_heads(r.mix_grad[...], two, near)
    kland_grad = own_heads(r.kland_grad[...], two, near) * scale
    each = LAND // count
    r.mix_out[...] = mix_grad[0:LAND].reshape(count, each, near)
    mix_sum.start()
    for copy in rims[1]:
        copy.start()

    def convolve_back(b):
        at = pl.ds(pl.multiple_of(b * BLOCK, BLOCK), BLOCK)
        r.conv[at] = convolve(r.band_back, window(r.grad_ext, b))

    scatter_out.fill_dense(r.grad_one[...], r.mixed[...])
    scatter_out.start()
    loop(blocks // 2 - 1, lambda b: convolve_back(b + 1))
    mix_sum.add()
    if order[2:-1]:
        scatter_down.forward(*order[2:-1])
    scatter_up.start(*ups_next[:1])
    loop(blocks // 2 - 1, lambda b: convolve_back(b + blocks // 2))
    for copy in rims[1]:
        copy.wait_recv()
    loop(2, lambda b: convolve_back(b * (blocks - 1)))

    mix_sum.finish()
    mix_grads = [r.mix_sums[...].reshape(LAND, near), mix_grad[LAND:two]]
    stats = r.kernel_v[...].reshape(LAND, PAD)
    mid_totals = wide_heads(stats, near)[:, :near]
    divisors = [mid_totals, edge_totals[:, :near]]
    inverse_grads = []
    for i, (k, g) in enumerate(pairs):
        inverse_grads.append(
            exact(mix_grads[g] * masks[k][:, :near], kernel_of(g)[:, :near], (1, 1))
        )
    shrink = [
        jnp.exp(r.max_b[k * two : k * two + LAND] - stats[:, near + heads + k : near + heads + k + 1])
        for k in range(heads)
    ]
    for g in range(2):
        grad = jnp.zeros((LAND, near), WIDE)
        for i, (k, own) in enumerate(pairs):
            if own == g:
                grad = grad + exact(r.inverse[i], mix_grads[g], (0, 0)) * masks[k][:, :near]
        grad = grad / divisors[g]
        lost = grad * kernel_of(g)[:, :near]
        for k in range(heads):
            at = slice(k * two + g * LAND, k * two + (g + 1) * LAND)
            factor = shrink[k] if g == 0 else 1.0
            r.numer_heads[at] = (grad * factor * masks[k][:, :near]).astype(LOW)
            r.total_grad[at] = -jnp.sum(lost * masks[k][:, :near], axis=1, keepdims=True) * factor

    def back_b(c):
        at = chunk_rows(c)
        values = r.value_ext[pl.ds(pl.multiple_of(REACH + c * size, REACH), size), 0:near]
        grad = against(r.numer_heads[...], values) + r.total_grad[...]
        r.scores_b[:, at] = (r.weights_b[:, at] * grad).astype(LOW)

    loop(CHUNKS, back_b)
    qland_grad = own_heads(matmul_low(r.scores_b[...], r.keys[...]), two, near) * scale
    r.land_out[:, :, 0:near] = qland_grad[0:LAND].reshape(count, each, near)
    r.land_out[:, :, near:] = kland_grad[0:LAND].reshape(count, each, near)
    land_sum.start()
    for k in range(7):
        r.vectors[k : k + 1] = jnp.sum(r.acc[k], axis=0, keepdims=True)
    lanes = r.vector_out.shape[2]
    for d in range(count):
        r.vector_out[d] = r.vectors[:, d * lanes : (d + 1) * lanes] if d * lanes < width else jnp.zeros((8, lanes), WIDE)
    vector_total.start()
    if ups_next[1:]:
        scatter_up.start(*ups_next[1:])
    scatter_up.forward(1)

    def values_back(c):
        at = chunk_rows(c)
        values = across(r.weights_b[:, at].astype(LOW), r.numer_heads[...]) + r.conv[at]
        r.near_grads[at, 2 * near : 3 * near] = values.astype(LOW)
        return jnp.sum(values, axis=0, keepdims=True)

    value_bias = lax.fori_loop(
        0, CHUNKS, lambda c, total: total + values_back(c), jnp.zeros((1, near), WIDE)
    )
    scatter_v.fill_dense(r.inputs[...], r.near_grads[:, 2 * near : 3 * near])
    scatter_v.start()

    def input_terms(c):
        at = chunk_rows(c)
        r.grad_key[at] = across(r.scores_b[:, at], r.query_heads[...]) * scale
        r.near_grads[at, 0:near] = r.grad_query[at].astype(LOW)
        r.near_grads[at, near : 2 * near] = r.grad_key[at].astype(LOW)
        terms = against(r.near_grads[at], r.w_near[:, :, 0 : 3 * near].reshape(width, 3 * near))
        sums[2].offer(c, terms.astype(LOW))

    input_terms(0)
    input_terms(1)
    sums[2].pair_up(0)
    land_sum.add()
    vector_total.add()
    sums[2].pair_up(1)
    if lines > 2:
        scatter_up.forward(2)

    def invert_back(i, carry):
        it = PINV_STEPS - 1 - i
        grads, kernel_grads = carry
        many = range(len(pairs))
        both = lambda ref: (ref[0], ref[1])
        wides = [thrice(halves(grads[p]), both(r.uppers[it, p])) for p in many]
        product_grads = [
            thrice(
                both(r.lowers[it, p]),
                halves(jnp.concatenate([w[:, LAND:two], w[:, two:], grads[p]], axis=0)),
            )
            for p, w in enumerate(wides)
        ]
        parts = [halves(grad) for grad in product_grads]
        kernel_grads = [
            old + thrice(part, both(r.lowers[it, p, :, :, 0:LAND]))
            for p, (old, part) in enumerate(zip(kernel_grads, parts))
        ]
        grads = [wides[p][:, 0:LAND] + thrice(both(r.turned_kernel[p]), parts[p]) for p in many]
        return tuple(grads), tuple(kernel_grads)

    zeros = tuple(jnp.zeros((LAND, LAND), WIDE) for _ in pairs)
    grads, kernel_grads = lax.fori_loop(0, PINV_STEPS, invert_back, (tuple(inverse_grads), zeros))
    scatter_out.forward()
    input_terms(2)
    vector_total.finish()
    for d in range(width // lanes):
        r.vector_sum[0, :, d * lanes : (d + 1) * lanes] = r.vector_sums[d]
    vector_core.start()

    qland_a = [jnp.zeros((LAND, near), WIDE)] * 2
    kland_a = [jnp.zeros((LAND, near), WIDE)] * 2
    for i, (k, g) in enumerate(pairs):
        kernel = r.land_kernel[i]
        turned = grads[i].T
        squares = jnp.sum(kernel * kernel)
        grad = kernel_grads[i] + turned / squares - kernel * (2.0 * jnp.sum(turned * kernel) / (squares * squares))
        grad = kernel * (grad - jnp.sum(kernel * grad, axis=1, keepdims=True)) * scale
        mask = masks[k][:, :near]
        qland_a[g] = qland_a[g] + exact(grad, r.key_land[group(g)].astype(WIDE)) * mask
        kland_a[g] = kland_a[g] + exact(grad, r.query_land[group(g)].astype(WIDE), (0, 0)) * mask


    sums[2].pair_up(2)
    if lines > 3:
        scatter_up.forward(*range(3, lines))
    land_sum.finish()
    land_total = r.land_sums[...].reshape(LAND, 2 * near)
    pick = (iota((LAND, LAND), 1) == iota((LAND, LAND), 0) + first_slot).astype(WIDE)

    def slot_grads(mid, edge):
        return jnp.concatenate([exact(pick, mid * mid_scale), edge * edge_scale], axis=0)

    def parted(both):
        high = both.astype(LOW)
        return jnp.concatenate([high, (both - high.astype(WIDE)).astype(LOW)], axis=0)

    slot_q = slot_grads(qland_a[0] + land_total[:, 0:near], qland_a[1] + qland_grad[LAND:two])
    slot_k = slot_grads(kland_a[0] + land_total[:, near:], kland_a[1] + kland_grad[LAND:two])
    r.slot_q[...] = parted(slot_q)
    r.slot_k[...] = parted(slot_k)
    r.slot_both[:, 0:near] = r.slot_q[0:two]
    r.slot_both[:, near:] = r.slot_k[0:two]
    slot_terms = against(r.slot_both[...], r.w_near[:, :, 0 : 2 * near].reshape(width, 2 * near))
    correction.offer(0, slot_terms.astype(LOW))
    input_terms(3)
    correction.pair_up(0)

    def add_slots(c):
        at = chunk_rows(c)
        member = jnp.concatenate([r.member[at]] * 2, axis=1)
        queries = r.grad_query[at] + matmul_low(member, r.slot_q[...])
        keys = r.grad_key[at] + matmul_low(member, r.slot_k[...])
        r.near_grads[at, 0:near] = queries.astype(LOW)
        r.near_grads[at, near : 2 * near] = keys.astype(LOW)
        return jnp.sum(queries, axis=0, keepdims=True)

    query_bias = lax.fori_loop(
        0, CHUNKS, lambda c, total: total + add_slots(c), jnp.zeros((1, near), WIDE)
    )
    sums[2].pair_up(3)
    scatter_qk.fill(r.inputs[...], r.near_grads[:, 0 : 2 * near])
    scatter_qk.start()
    scatter_v.forward()

    r.tap_grad[...] = jnp.zeros_like(r.tap_grad)

    def tap_products(b):
        own = r.grad_ext[pl.ds(pl.multiple_of(b * BLOCK + REACH, REACH), BLOCK), :]
        own = jnp.concatenate([own * m for m in masks_low], axis=0)
        r.tap_grad[:, 0:SPAN] += against(own, window(r.value_ext, b)[:, :near])

    loop(blocks, tap_products)
    token = lax.rem(iota((heads * BLOCK, 128), 0), BLOCK)
    slanted = r.tap_grad[...]
    for bit in range(6):
        moved = pltpu.roll(slanted, 128 - (1 << bit), 1)
        slanted = jnp.where(lax.rem(token // (1 << bit), 2) == 1, moved, slanted)
    for k in range(heads):
        r.small_part[s, 2 + k : 3 + k, 0:128] = jnp.sum(
            slanted[k * BLOCK : (k + 1) * BLOCK], axis=0, keepdims=True
        )
    r.small_part[s, 0:1, 0:near] = query_bias
    r.small_part[s, 1:2, 0:near] = value_bias
    small_spread.start()

    def settle_output(c):
        share(2, r.output, c).wait_recv()

    loop(CHUNKS, settle_output)
    store_output.start()
    r.grad_w_down[...] = scatter_down.finish()
    store_down.start()
    r.grad_w_up[...] = scatter_up.finish()
    store_up.start()
    r.grad_w_out[...] = undense(scatter_out.finish())
    store_out.start()
    r.grad_near[2] = undense(scatter_v.finish())
    scatter_qk.forward()
    here = pl.ds(pl.multiple_of(core * LAND, LAND), LAND)
    share_slots = remote(
        r.corr_all.at[here], r.corr_all.at[here], r.corr_s.at[0], r.corr_r.at[0], core_of_chip()
    )
    correction.arrived(0)
    r.corr_all[here] = correction.total(0, pl.ds(0, LAND)).astype(LOW)
    share_slots.start()
    share_slots.wait_recv()

    def store_inputs(c):
        at = chunk_rows(c)
        return pltpu.make_async_copy(r.cotangent.at[at], r.grad_inputs_hbm.at[at], r.chunk_sems.at[c])

    def inputs_done(c):
        sums[2].arrived(c)
        slots = matmul_low(r.member[my_rows(c)], r.corr_all[...])
        kept = r.wide_grad[pl.ds(pl.multiple_of(c * half, half), half)]
        r.cotangent[my_rows(c)] = (kept + sums[2].total(c, pl.ds(0, half)) + slots).astype(LOW)
        share(4, r.cotangent, c).start()

        @pl.when(c > 0)
        def _():
            share(4, r.cotangent, c - 1).wait_recv()
            store_inputs(c - 1).start()

    loop(CHUNKS, inputs_done)
    near_total = scatter_qk.finish()
    for k in range(2):
        r.grad_near[k] = near_total[:, k * near : (k + 1) * near]
    store_near.start()
    vector_core.wait_recv()
    r.vectors[0:6] = r.vector_sum[0, 0:6] + r.vector_sum[1, 0:6]
    r.vectors[6:8] = r.vector_sum[0, 6:8]
    small_spread.finish()
    r.smalls[...] = functools.reduce(jnp.add, [r.small_part[d] for d in range(count)])

    share(4, r.cotangent, CHUNKS - 1).wait_recv()
    store_inputs(CHUNKS - 1).start()

    def settle(c):
        sums[2].core_copy(c).wait_send()
        sums[2].x_copy(c).wait_send()
        store_inputs(c).wait()
        for copy in mixed_copies(c):
            copy.wait_send()
        for k, ref in enumerate((r.hidden, r.grad_two, r.output, r.grad_one, r.cotangent)):
            share(k, ref, c).wait_send()

    loop(CHUNKS, settle)
    vector_core.wait_send()
    correction.core_copy(0).wait_send()
    correction.x_copy(0).wait_send()
    share_slots.wait_send()
    for copy in stores:
        copy.wait()
    for copy in rims[0] + rims[1] + out_copies:
        copy.wait_send()
    for group_of in gathers + scatters + spreads:
        group_of.close()


def hand_out(
    output, grad_inputs, grad_out, grad_up, grad_down, grad_near, vectors, smalls,
    to_output, to_inputs, to_query, to_key, to_value, to_out, to_up, to_down,
    bias_query, bias_value, bias_out, bias_up, bias_down, gain_one, bias_one, gain_two, bias_two, taps,
    hold, hold_near, hold_feed, hold_vectors, hold_smalls, sems, more, few_sems,
):
    parts = hold.shape[1]
    rows = output.shape[0] // parts
    copy = pltpu.make_async_copy
    first, second = [], []
    for j in range(parts):
        for k, (ref, to) in enumerate(((output, to_output), (grad_inputs, to_inputs))):
            at = pl.ds(j * rows, rows)
            first.append(copy(ref.at[at], hold.at[k, j], sems.at[k, j, 0]))
            second.append(copy(hold.at[k, j], to.at[at], sems.at[k, j, 1]))
    for k, (ref, held, to) in enumerate(
        (
            (grad_near.at[0], hold_near.at[0], to_query),
            (grad_near.at[1], hold_near.at[1], to_key),
            (grad_near.at[2], hold_near.at[2], to_value),
            (grad_out, hold_near.at[3], to_out),
            (grad_up, hold_feed.at[0], to_up),
            (grad_down, hold_feed.at[1], to_down),
        )
    ):
        first.append(copy(ref, held, more.at[k, 0]))
        second.append(copy(held, to, more.at[k, 1]))
    few = [copy(vectors, hold_vectors, few_sems.at[0]), copy(smalls, hold_smalls, few_sems.at[1])]
    for one in few + first:
        one.start()
    for one in few:
        one.wait()
    for k, ref in enumerate((gain_two, bias_two, bias_down, gain_one, bias_one, bias_out, bias_up)):
        ref[...] = hold_vectors[k : k + 1].reshape(ref.shape)
    for k, ref in enumerate((bias_query, bias_value)):
        ref[...] = hold_smalls[k : k + 1, 0 : ref.shape[0]].reshape(ref.shape)
    taps[...] = hold_smalls[2 : 2 + taps.shape[0], 0:KERNEL]
    for arriving, leaving in zip(first, second):
        arriving.wait()
        leaving.start()
    for one in second:
        one.wait()


def fused_body(
    inputs, cotangent, item_lengths, w_query, w_key, w_value, w_out, w_up, w_down, bias_query, bias_value,
    bias_out, bias_up, bias_down, gain_one, bias_one, gain_two, bias_two, conv_taps,
):
    count = lax.axis_size("seq")
    rows, width = inputs.shape
    near, feed, heads = w_query.shape[1], w_up.shape[1], conv_taps.shape[0]
    size, part, lines = rows // CHUNKS, width // count, count // 2
    half, two = size // 2, 2 * LAND
    share = 128 * -(-width // 128 // count)
    low = lambda *shape: pltpu.VMEM(shape, LOW)
    wide = lambda *shape: pltpu.VMEM(shape, WIDE)
    sem = lambda *shape: pltpu.SemaphoreType.DMA(shape)
    vmem, smem = pl.BlockSpec(memory_space=pltpu.VMEM), pl.BlockSpec(memory_space=pltpu.SMEM)
    operands = dict(
        lengths=item_lengths, conv_taps=conv_taps,
        inputs_hbm=inputs, cotangent_hbm=cotangent,
        w_up=w_up, w_down=w_down,
        w_query_hbm=w_query, w_key_hbm=w_key, w_value_hbm=w_value, w_out_hbm=w_out,
        bias_query_hbm=bias_query, bias_value_hbm=bias_value,
        bias_out_hbm=bias_out, bias_up_hbm=bias_up, bias_down_hbm=bias_down,
        gain_one_hbm=gain_one, bias_one_hbm=bias_one, gain_two_hbm=gain_two, bias_two_hbm=bias_two,
    )
    outs = dict(
        output_hbm=((rows, width), LOW), grad_inputs_hbm=((rows, width), LOW),
        grad_w_out_hbm=((part, near), WIDE), grad_w_up_hbm=((part, feed), WIDE), grad_w_down_hbm=((part, feed), WIDE),
        grad_near_hbm=((3, part, near), WIDE), vectors=((8, width), WIDE), smalls=((8, PAD), WIDE),
    )
    line = lambda length: pltpu.VMEM((length,), WIDE)
    scratch = dict(
        w_query=low(part, near), w_key=low(part, near), w_value=low(part, near), w_out=low(part, near),
        bias_query=line(near), bias_value=line(near), bias_out=line(width), bias_up=line(feed), bias_down=line(width),
        gain_one=line(width), bias_one=line(width), gain_two=line(width), bias_two=line(width),
        shard_sems=sem(4), vector_sems=sem(9),
        inputs=low(rows, width), cotangent=low(rows, width), output=low(rows, width),
        grad_w_out=wide(part, near), grad_w_up=wide(part, feed), grad_w_down=wide(part, feed),
        grad_near=wide(3, part, near), io=sem(8),
        packed=low(part, 4 * near), w_near=low(count, part, 4 * near), out_turned=low(4, near, width),
        mixed_out=low(CHUNKS, 2, 3 * half // 2, 128), mixed_in=low(3, CHUNKS, 3 * half // 2, 128),
        full_up=low(count, part, feed), full_down=low(count, part, feed),
        member=low(rows, two), band=low(heads * BLOCK, 2 * SPAN), band_back=low(heads * BLOCK, 2 * SPAN),
        queries=low(rows, near), keys=low(rows, near), value_ext=low(rows + 2 * REACH, PAD),
        land_part=low(count, 3 * BORDER, 128), query_land=low(two, near), key_land=low(two, near),
        query_heads=low(heads * two, near), key_heads=low(heads * two, near),
        weights_b=wide(heads * two, rows),
        max_b=wide(heads * two, 1), total_b=wide(heads * two, 1),
        numer_out=wide(count, LAND // count, PAD), numer_in=wide(count, LAND // count, PAD),
        kernel_v=wide(count, LAND // count, PAD), kernel_edge=wide(LAND, PAD),
        land_kernel=wide(2 * heads, LAND, LAND), inverse=wide(2 * heads, LAND, LAND),
        befores=wide(PINV_STEPS, 2 * heads, LAND, LAND), products=wide(PINV_STEPS, 2 * heads, LAND, LAND),
        uppers=low(PINV_STEPS, 2 * heads, 2, LAND, 3 * LAND), lowers=low(PINV_STEPS, 2 * heads, 2, LAND, 3 * LAND),
        turned_kernel=low(2 * heads, 2, LAND, LAND),
        weights_f=wide(rows, heads * two), conv=wide(rows, near),
        mixing=low(two, near), mixing_heads=low(heads * two, near), mixed=low(rows, near),
        terms=low(CHUNKS, size, width), core_in=low(CHUNKS, half, width),
        x_out=low(CHUNKS, half, width), x_in=low(2, CHUNKS, half, width),
        hidden=low(rows, width), active=low(rows, feed), slope=low(rows, feed),
        grad_two=low(rows, width), grad_lift=low(rows, feed), grad_one=low(rows, width),
        norm_one=wide(rows // 2, width), inv_one=wide(rows // 2, 1), wide_grad=wide(rows // 2, width),
        tmp=wide(size, feed), acc=wide(7, 8, width),
        grad_ext=low(rows + 2 * REACH, near), grad_query=wide(rows, near), grad_key=wide(rows, near),
        mix_grad=wide(heads * two, near), kland_grad=wide(heads * two, near),
        mix_out=wide(count, LAND // count, near), mix_in=wide(count, LAND // count, near),
        mix_sums=wide(count, LAND // count, near), land_out=wide(count, LAND // count, 2 * near),
        land_in=wide(count, LAND // count, 2 * near), land_sums=wide(count, LAND // count, 2 * near),
        vector_out=wide(count, 8, share), vector_in=wide(count, 8, share), vector_sums=wide(count, 8, share),
        tap_grad=wide(heads * BLOCK, 128), numer_heads=low(heads * two, near), total_grad=wide(heads * two, 1),
        scores_b=low(heads * two, rows), near_grads=low(rows, 3 * near),
        slot_q=low(2 * two, near), slot_k=low(2 * two, near), slot_both=low(two, 2 * near),
        vector_sum=wide(2, 8, width), small_part=wide(count, 8, PAD),
    )
    tall = 3 * part // 2
    for_out, for_up, for_down, for_qk, for_v = (
        (low(count, *of), low(lines, *of), low(lines - 1, *of), low(lines - 1, *of))
        for of in ((tall, 128), (part, feed), (part, feed), (part, 2 * near), (tall, 128))
    )
    scratch.update(
        t_out=for_out[0], yb_out=for_out[1], pr_out=for_out[2], zb_out=for_out[3],
        t_up=for_up[0], yb_up=for_up[1], pr_up=for_up[2], zb_up=for_up[3],
        t_down=for_down[0], yb_down=for_down[1], pr_down=for_down[2], zb_down=for_down[3],
        t_qk=for_qk[0], yb_qk=for_qk[1], pr_qk=for_qk[2], zb_qk=for_qk[3],
        t_v=for_v[0], yb_v=for_v[1], pr_v=for_v[2], zb_v=for_v[3],
        corr_terms=low(1, two, width), corr_core=low(1, LAND, width), corr_out=low(1, LAND, width),
        corr_in=low(2, 1, LAND, width), corr_sems=sem(1, 4, 1), corr_all=low(two, width),
        corr_s=sem(1), corr_r=sem(1),
        g_own=sem(8), g_zs=sem(8, lines - 1), g_zr=sem(8, lines - 1), g_ys=sem(8, lines), g_yr=sem(8, lines),
        s_ys=sem(5, lines), s_yr=sem(5, lines), s_zs=sem(5, lines - 1), s_zr=sem(5, lines - 1),
        e_s=sem(10, count - 1), e_r=sem(10, count - 1), h_sems=sem(3, 4, CHUNKS), w_s=sem(3), w_r=sem(3), m_s=sem(3, CHUNKS), m_r=sem(3, CHUNKS),
        rim_s=sem(2, 2), rim_r=sem(2, 2), share_s=sem(5, CHUNKS), share_r=sem(5, CHUNKS),
        core_s=sem(1), core_r=sem(1), chunk_sems=sem(CHUNKS),
    )
    any_place = pl.BlockSpec(memory_space=pltpu.HBM)
    results = pl.pallas_call(
        functools.partial(layer_kernel, count, list(operands) + list(outs) + list(scratch)),
        out_shape=tuple(jax.ShapeDtypeStruct(*out) for out in outs.values()),
        in_specs=[smem, smem] + [any_place] * (len(operands) - 2),
        out_specs=(any_place,) * 6 + (vmem, vmem),
        scratch_shapes=list(scratch.values()),
        compiler_params=pltpu.CompilerParams(
            collective_id=1, has_side_effects=True, vmem_limit_bytes=63 * 2**20
        ),
    )(*operands.values())
    vector = lambda length: jax.ShapeDtypeStruct((length,), WIDE)
    block = lambda lanes: jax.ShapeDtypeStruct((part, lanes), WIDE)
    whole = jax.ShapeDtypeStruct((rows, width), LOW)
    return pl.pallas_call(
        hand_out,
        out_shape=(
            whole, whole, block(near), block(near), block(near), block(near), block(feed), block(feed),
            vector(near), vector(near), vector(width), vector(feed), vector(width),
            vector(width), vector(width), vector(width), vector(width),
            jax.ShapeDtypeStruct((heads, KERNEL), WIDE),
        ),
        in_specs=[any_place] * 8,
        out_specs=(any_place,) * 8 + (vmem,) * 10,
        scratch_shapes=[
            low(2, CHUNKS, size, width), wide(4, part, near), wide(2, part, feed), wide(8, width), wide(8, PAD),
            sem(2, CHUNKS, 2), sem(6, 2), sem(2),
        ],
    )(*results)


def plain_body(
    inputs,
    cotangent,
    item_lengths,
    w_query,
    w_key,
    w_value,
    w_out,
    w_up,
    w_down,
    bias_query,
    bias_value,
    bias_out,
    bias_up,
    bias_down,
    gain_one,
    bias_one,
    gain_two,
    bias_two,
    conv_taps,
):
    low_type = jnp.bfloat16
    tok_rows = inputs.shape[0]
    heads_here = conv_taps.shape[0]
    width_here = heads_here * HEAD_DIM
    slots = ITEMS * LAND
    reach = (KERNEL - 1) // 2
    score_scale = HEAD_DIM ** (-0.5)
    pref = jnp.float32
    first_row = lax.axis_index("seq") * tok_rows
    positions = first_row + jnp.arange(tok_rows, dtype=jnp.int32)
    item_id, land_slot = locate(item_lengths, positions)
    rim_item = locate(
        item_lengths, first_row - reach + jnp.arange(tok_rows + 2 * reach, dtype=jnp.int32)
    )[0]
    slot_item = jnp.arange(slots, dtype=jnp.int32) // LAND
    member = land_slot[:, None] == jnp.arange(slots, dtype=jnp.int32)[None, :]
    member_low = member.astype(low_type)
    counts = jnp.repeat((item_lengths // LAND).astype(jnp.float32), LAND)
    same_f = item_id[:, None] == slot_item[None, :]
    same_b = same_f.T
    tap_cols = jnp.repeat(conv_taps, HEAD_DIM, axis=0)
    full_query, full_key, full_value, full_out, full_up, full_down = (
        lax.all_gather(w_query, "seq", axis=0, tiled=True),
        lax.all_gather(w_key, "seq", axis=0, tiled=True),
        lax.all_gather(w_value, "seq", axis=0, tiled=True),
        lax.all_gather(w_out, "seq", axis=0, tiled=True),
        lax.all_gather(w_up, "seq", axis=0, tiled=True),
        lax.all_gather(w_down, "seq", axis=0, tiled=True),
    )
    queries = (matmul_low(inputs, full_query) + bias_query).astype(low_type)
    key_rows = matmul_low(inputs, full_key).astype(low_type)
    value_rows = (matmul_low(inputs, full_value) + bias_value).astype(low_type)
    query_sums, key_sums = lax.psum(
        (across(member_low, queries), across(member_low, key_rows)), "seq"
    )
    query_land = (
        (query_sums / counts[:, None]).astype(low_type).reshape(slots, heads_here, HEAD_DIM)
    )
    key_land = (key_sums / counts[:, None]).astype(low_type).reshape(slots, heads_here, HEAD_DIM)
    query_heads = queries.reshape(tok_rows, heads_here, HEAD_DIM)
    key_heads = key_rows.reshape(tok_rows, heads_here, HEAD_DIM)
    value_heads = value_rows.reshape(tok_rows, heads_here, HEAD_DIM)
    scores_b = (
        jnp.einsum("lhd,thd->hlt", query_land, key_heads, preferred_element_type=pref) * score_scale
    )
    scores_b = jnp.where(same_b[None], scores_b, MASKED)
    maxima_b = lax.pmax(jnp.max(scores_b, axis=2), "seq")
    weights_b = jnp.exp(scores_b - maxima_b[:, :, None])
    weights_b_low = weights_b.astype(low_type)
    numer_sum, totals_b = lax.psum(
        (
            jnp.einsum("hlt,thd->lhd", weights_b_low, value_heads, preferred_element_type=pref),
            jnp.sum(weights_b, axis=2),
        ),
        "seq",
    )
    totals_cols = totals_b.T[:, :, None]
    kernel_v = numer_sum / totals_cols
    land_q = query_land.reshape(ITEMS, LAND, heads_here, HEAD_DIM)
    land_k = key_land.reshape(ITEMS, LAND, heads_here, HEAD_DIM)
    land_kernel = jax.nn.softmax(
        jnp.einsum("ilhd,imhd->ihlm", land_q, land_k, preferred_element_type=pref) * score_scale,
        axis=-1,
    )
    inverse, inverse_back = jax.vjp(pseudo_inverse, land_kernel)
    kernel_items = kernel_v.reshape(ITEMS, LAND, heads_here, HEAD_DIM)
    mixing = jnp.einsum("ihlm,imhd->ilhd", inverse, kernel_items, precision=PRECISE)
    mixing = mixing.astype(low_type).reshape(slots, heads_here, HEAD_DIM)
    scores_f = (
        jnp.einsum("thd,lhd->htl", query_heads, key_land, preferred_element_type=pref) * score_scale
    )
    weights_f = jax.nn.softmax(jnp.where(same_f[None], scores_f, MASKED), axis=-1)
    weights_f_low = weights_f.astype(low_type)
    attended = jnp.einsum("htl,lhd->thd", weights_f_low, mixing, preferred_element_type=pref)
    attended = attended.reshape(tok_rows, width_here)
    value_rim = extended(value_rows, (("seq", 0),), reach)
    conv_sum = jnp.zeros((tok_rows, width_here), jnp.float32)
    for offset in range(KERNEL):
        in_item = (rim_item[offset : offset + tok_rows] == item_id)[:, None]
        conv_sum = conv_sum + jnp.where(
            in_item,
            value_rim[offset : offset + tok_rows].astype(jnp.float32)
            * tap_cols[:, offset][None, :],
            0.0,
        )
    mixed_rows = (attended + conv_sum).astype(low_type)
    attention_sum = lax.psum(against(mixed_rows, full_out).astype(jnp.bfloat16), "head").astype(
        jnp.float32
    )
    pre_one = inputs.astype(jnp.float32) + attention_sum + bias_out
    norm_one, inv_one = normalize(pre_one)
    hidden = norm_one * gain_one + bias_one
    hidden_low = hidden.astype(low_type)
    lifted = matmul_low(hidden_low, full_up) + bias_up
    active, gelu_back = jax.vjp(gelu_tanh, lifted)
    active_low = active.astype(low_type)
    feed_terms = against(active_low, full_down)
    feed_sum = lax.psum(feed_terms.astype(jnp.bfloat16), "head").astype(jnp.float32)
    grad_output = cotangent.astype(jnp.float32)
    pre_two = hidden + feed_sum + bias_down
    norm_two, inv_two = normalize(pre_two)
    out_rows = (norm_two * gain_two + bias_two).astype(low_type)
    grad_gain_two = jnp.sum(grad_output * norm_two, axis=0)
    grad_bias_two = jnp.sum(grad_output, axis=0)
    grad_two = norm_back(grad_output * gain_two, norm_two, inv_two)
    grad_bias_down = jnp.sum(grad_two, axis=0)
    grad_two_low = grad_two.astype(low_type)
    output, grad_two_full = (out_rows, grad_two_low)
    grad_down = across(grad_two_full, active_low)
    (grad_lift,) = gelu_back(matmul_low(grad_two_full, full_down))
    grad_bias_up = jnp.sum(grad_lift, axis=0)
    grad_lift_low = grad_lift.astype(low_type)
    grad_up = across(hidden_low, grad_lift_low)
    up_terms = against(grad_lift_low, full_up)
    grad_hidden = grad_two + lax.psum(up_terms.astype(jnp.bfloat16), "head").astype(jnp.float32)
    grad_gain_one = jnp.sum(grad_hidden * norm_one, axis=0)
    grad_bias_one = jnp.sum(grad_hidden, axis=0)
    grad_one = norm_back(grad_hidden * gain_one, norm_one, inv_one)
    grad_bias_out = jnp.sum(grad_one, axis=0)
    grad_one_low = grad_one.astype(low_type)
    grad_outw = across(grad_one_low, mixed_rows)
    grad_mixed = matmul_low(grad_one_low, full_out).astype(low_type)
    grad_mixed_wide = grad_mixed.astype(jnp.float32)
    grad_heads = grad_mixed.reshape(tok_rows, heads_here, HEAD_DIM)
    grad_rim = extended(grad_mixed, (("seq", 0),), reach)
    grad_conv_v = jnp.zeros((tok_rows, width_here), jnp.float32)
    tap_terms = []
    for offset in range(KERNEL):
        in_item = (rim_item[offset : offset + tok_rows] == item_id)[:, None]
        neighbour = jnp.where(
            in_item, value_rim[offset : offset + tok_rows].astype(jnp.float32), 0.0
        )
        tap_terms.append(
            jnp.sum(
                (grad_mixed_wide * neighbour).reshape(tok_rows, heads_here, HEAD_DIM), axis=(0, 2)
            )
        )
        mirror = 2 * reach - offset
        mirror_item = (rim_item[mirror : mirror + tok_rows] == item_id)[:, None]
        grad_conv_v = grad_conv_v + jnp.where(
            mirror_item,
            grad_rim[mirror : mirror + tok_rows].astype(jnp.float32) * tap_cols[:, offset][None, :],
            0.0,
        )
    grad_taps = jnp.stack(tap_terms, axis=1)
    grad_weights_f = jnp.einsum("thd,lhd->htl", grad_heads, mixing, preferred_element_type=pref)
    grad_mix_part = jnp.einsum(
        "htl,thd->lhd", weights_f_low, grad_heads, preferred_element_type=pref
    )
    grad_scores_f = weights_f * (
        grad_weights_f - jnp.sum(weights_f * grad_weights_f, axis=2, keepdims=True)
    )
    grad_scores_f = grad_scores_f.astype(low_type)
    grad_query_f = (
        jnp.einsum("htl,lhd->thd", grad_scores_f, key_land, preferred_element_type=pref)
        * score_scale
    )
    grad_kland_part = (
        jnp.einsum("htl,thd->lhd", grad_scores_f, query_heads, preferred_element_type=pref)
        * score_scale
    )
    grad_mixing, grad_kland_f = lax.psum((grad_mix_part, grad_kland_part), "seq")
    grad_mix_items = grad_mixing.reshape(ITEMS, LAND, heads_here, HEAD_DIM)
    grad_inverse = jnp.einsum("ilhd,imhd->ihlm", grad_mix_items, kernel_items, precision=PRECISE)
    grad_kernel_v = jnp.einsum("ihlm,ilhd->imhd", inverse, grad_mix_items, precision=PRECISE)
    grad_kernel_v = grad_kernel_v.reshape(slots, heads_here, HEAD_DIM)
    (grad_land_kernel,) = inverse_back(grad_inverse)
    grad_scores_a = land_kernel * (
        grad_land_kernel - jnp.sum(land_kernel * grad_land_kernel, axis=-1, keepdims=True)
    )
    grad_scores_a = grad_scores_a * score_scale
    grad_qland_a = jnp.einsum(
        "ihlm,imhd->ilhd", grad_scores_a, land_k.astype(jnp.float32), precision=PRECISE
    )
    grad_kland_a = jnp.einsum(
        "ihlm,ilhd->imhd", grad_scores_a, land_q.astype(jnp.float32), precision=PRECISE
    )
    grad_numer = (grad_kernel_v / totals_cols).astype(low_type)
    grad_totals = -jnp.sum(grad_kernel_v * kernel_v, axis=2) / totals_b.T
    grad_weights_b = jnp.einsum(
        "lhd,thd->hlt", grad_numer, value_heads, preferred_element_type=pref
    )
    grad_weights_b = grad_weights_b + grad_totals.T[:, :, None]
    grad_scores_b = (weights_b * grad_weights_b).astype(low_type)
    grad_qland_part = (
        jnp.einsum("hlt,thd->lhd", grad_scores_b, key_heads, preferred_element_type=pref)
        * score_scale
    )
    grad_key_b = (
        jnp.einsum("hlt,lhd->thd", grad_scores_b, query_land, preferred_element_type=pref)
        * score_scale
    )
    grad_value_b = jnp.einsum(
        "hlt,lhd->thd", weights_b_low, grad_numer, preferred_element_type=pref
    )
    grad_query_rows = grad_query_f.reshape(tok_rows, width_here)
    grad_values = grad_value_b.reshape(tok_rows, width_here) + grad_conv_v
    (
        grad_qland_b,
        grad_gain_one,
        grad_bias_one,
        grad_gain_two,
        grad_bias_two,
        grad_bias_out,
        grad_bias_down,
        grad_bias_up,
        grad_taps,
        query_f_total,
        grad_bias_value,
    ) = lax.psum(
        (
            grad_qland_part,
            grad_gain_one,
            grad_bias_one,
            grad_gain_two,
            grad_bias_two,
            grad_bias_out,
            grad_bias_down,
            grad_bias_up,
            grad_taps,
            jnp.sum(grad_query_rows, axis=0),
            jnp.sum(grad_values, axis=0),
        ),
        "seq",
    )
    grad_qland = grad_qland_a.reshape(slots, width_here) + grad_qland_b.reshape(slots, width_here)
    grad_kland = grad_kland_a.reshape(slots, width_here) + grad_kland_f.reshape(slots, width_here)
    member_wide = member.astype(jnp.float32)
    grad_queries = grad_query_rows + jnp.dot(
        member_wide, grad_qland / counts[:, None], precision=PRECISE
    )
    grad_keys = grad_key_b.reshape(tok_rows, width_here) + jnp.dot(
        member_wide, grad_kland / counts[:, None], precision=PRECISE
    )
    grad_bias_query = query_f_total + jnp.sum(grad_qland, axis=0)
    queries_low = grad_queries.astype(low_type)
    keys_low = grad_keys.astype(low_type)
    values_low = grad_values.astype(low_type)
    grad_queryw = across(inputs, queries_low)
    grad_keyw = across(inputs, keys_low)
    grad_valuew = across(inputs, values_low)
    input_terms = (
        against(queries_low, full_query)
        + against(keys_low, full_key)
        + against(values_low, full_value)
    )
    grad_inputs = (
        grad_one + lax.psum(input_terms.astype(jnp.bfloat16), "head").astype(jnp.float32)
    ).astype(low_type)
    query_shard, key_shard, value_shard, out_shard, grad_up_shard, grad_down_shard = side_by_side(
        (
            grad_queryw.astype(jnp.bfloat16),
            grad_keyw.astype(jnp.bfloat16),
            grad_valuew.astype(jnp.bfloat16),
            grad_outw.astype(jnp.bfloat16),
            grad_up.astype(jnp.bfloat16),
            grad_down.astype(jnp.bfloat16),
        ),
        "seq",
        0,
        1,
    )
    return (
        output,
        grad_inputs,
        query_shard,
        key_shard,
        value_shard,
        out_shard,
        grad_up_shard,
        grad_down_shard,
        grad_bias_query,
        grad_bias_value,
        grad_bias_out,
        grad_bias_up,
        grad_bias_down,
        grad_gain_one,
        grad_bias_one,
        grad_gain_two,
        grad_bias_two,
        grad_taps,
    )


def solution(mesh):
    seq, head = mesh.shape["seq"], mesh.shape["head"]
    fits = head == 4 and seq == 8
    return jax.shard_map(
        fused_body if fits else plain_body,
        mesh=mesh,
        in_specs=(
            P("seq", None),
            P("seq", None),
            P(),
            P("seq", "head"),
            P("seq", "head"),
            P("seq", "head"),
            P("seq", "head"),
            P("seq", "head"),
            P("seq", "head"),
            P("head"),
            P("head"),
            P(),
            P("head"),
            P(),
            P(),
            P(),
            P(),
            P(),
            P("head", None),
        ),
        out_specs=(
            P("seq", None),
            P("seq", None),
            P("seq", "head"),
            P("seq", "head"),
            P("seq", "head"),
            P("seq", "head"),
            P("seq", "head"),
            P("seq", "head"),
            P("head"),
            P("head"),
            P(),
            P("head"),
            P(),
            P(),
            P(),
            P(),
            P(),
            P("head", None),
        ),
        check_vma=False,
    )
```

```python
import functools
import types

import jax
import jax.numpy as jnp
from jax import lax
from jax.experimental import pallas as pl
from jax.experimental.pallas import tpu as pltpu
from jax.sharding import PartitionSpec as P

HEAD_DIM = 64
LAND = 64
KERNEL = 33
PINV_STEPS = 6
ITEMS = 3


PRECISE = lax.Precision.HIGHEST
EPSILON = 1e-05
MASKED = -1e30


def extended(cells, sides, width):
    for axis, dim in sides:
        count = lax.axis_size(axis)
        ends = count - 1
        head = lax.slice_in_dim(cells, 0, width, axis=dim)
        tail = lax.slice_in_dim(cells, cells.shape[dim] - width, cells.shape[dim], axis=dim)
        cells = jnp.concatenate(
            [
                lax.ppermute(tail, axis, [(i, (i + 1) % count) for i in range(ends)]),
                cells,
                lax.ppermute(head, axis, [((i + 1) % count, i) for i in range(ends)]),
            ],
            axis=dim,
        )
    return cells


def cut_along(array, dim, length):
    lengths = array.shape
    parts = array.reshape(*lengths[:dim], length, lengths[dim] // length, *lengths[dim + 1 :])
    return jnp.moveaxis(parts, dim, 0)


def sent_and_summed(array, axis, dim):
    parts = cut_along(array, dim, lax.axis_size(axis))
    arrived = lax.all_to_all(parts, axis, split_axis=0, concat_axis=0, tiled=True)
    return arrived.astype(jnp.float32).sum(axis=0)


def side_by_side(arrays, axis, dim, along):
    both = jnp.concatenate(arrays, axis=along)
    out, at, outs = (sent_and_summed(both, axis, dim), 0, [])
    for a in arrays:
        outs.append(lax.slice_in_dim(out, at, at + a.shape[along], axis=along))
        at += a.shape[along]
    return tuple(outs)


def locate(item_lengths, positions):
    item_ends = jnp.cumsum(item_lengths)
    item_starts = item_ends - item_lengths
    located = jnp.sum((positions[:, None] >= item_ends[None, :]).astype(jnp.int32), axis=1)
    inside = (positions >= 0) & (located < ITEMS)
    picked = jnp.minimum(located, ITEMS - 1)
    onehot = (picked[:, None] == jnp.arange(ITEMS, dtype=jnp.int32)[None, :]).astype(jnp.int32)
    item_start = jnp.sum(onehot * item_starts[None, :], axis=1)
    length = jnp.sum(onehot * item_lengths[None, :], axis=1)
    segment = (positions - item_start) * LAND // length
    land_slot = picked * LAND + jnp.clip(segment, 0, LAND - 1)
    return (jnp.where(inside, picked, -1), land_slot)


def normalize(values):
    row_mean = jnp.mean(values, axis=-1, keepdims=True)
    centered = values - row_mean
    variance = jnp.mean(centered * centered, axis=-1, keepdims=True)
    inv_std = lax.rsqrt(variance + EPSILON)
    return (centered * inv_std, inv_std)


def norm_back(grad_norm, normed, inv_std):
    return inv_std * (
        grad_norm
        - jnp.mean(grad_norm, axis=-1, keepdims=True)
        - normed * jnp.mean(grad_norm * normed, axis=-1, keepdims=True)
    )


def pseudo_inverse(land_kernel):
    identity = jnp.eye(LAND, dtype=jnp.float32)
    frobenius = jnp.sum(land_kernel * land_kernel, axis=(-2, -1), keepdims=True)
    result = jnp.swapaxes(land_kernel, -1, -2) / frobenius
    for iteration in range(PINV_STEPS):
        product = jnp.matmul(land_kernel, result, precision=PRECISE)
        nested = 7.0 * identity - product
        nested = 15.0 * identity - jnp.matmul(product, nested, precision=PRECISE)
        nested = 13.0 * identity - jnp.matmul(product, nested, precision=PRECISE)
        result = 0.25 * jnp.matmul(result, nested, precision=PRECISE)
    return result


def gelu_tanh(values):
    return jax.nn.gelu(values, approximate=True)


def matmul_low(left, right):
    return jnp.dot(left, right, preferred_element_type=jnp.float32)


def against(left, right):
    return lax.dot_general(
        left, right, (((1,), (1,)), ((), ())), preferred_element_type=jnp.float32
    )


def across(left, right):
    return lax.dot_general(
        left, right, (((0,), (0,)), ((), ())), preferred_element_type=jnp.float32
    )


MESH = pl.DeviceIdType.MESH
WIDE = jnp.float32
LOW = jnp.bfloat16
CHUNKS = 4
PAD = 256
REACH = (KERNEL - 1) // 2
BLOCK = 64
SPAN = BLOCK + 2 * REACH
BORDER = 16


def place():
    s, h = lax.axis_index("seq"), lax.axis_index("head")
    return s, h, s // 2, lax.rem(s, 2), h // 2, lax.rem(h, 2)


def core_of_chip():
    s, _, _, _, x, core = place()
    return (s, 2 * x + 1 - core)


def x_neighbour():
    s, _, _, _, x, core = place()
    return (s, 2 * (1 - x) + core)


def across_x():
    s, _, _, _, x, core = place()
    return (s, 2 * (1 - x) + 1 - core)


def y_neighbour():
    _, h, z, y, _, _ = place()
    return (2 * z + 1 - y, h)


def along_z(count):
    _, h, z, y, _, _ = place()
    lines = count // 2
    return [(2 * lax.rem(z + j, lines) + y, h) for j in range(1, lines)]


def along_seq(count):
    s, h = place()[:2]
    return [(lax.rem(s + j, count), h) for j in range(1, count)]


def remote(src, dst, send, recv, device):
    return pltpu.make_async_remote_copy(
        src_ref=src, dst_ref=dst, send_sem=send, recv_sem=recv, device_id=device, device_id_type=MESH
    )


def greet(devices):
    for device in devices:
        pl.semaphore_signal(
            pltpu.get_barrier_semaphore(), inc=1, device_id=device, device_id_type=MESH
        )


def greeted(devices):
    pl.semaphore_wait(pltpu.get_barrier_semaphore(), len(devices))


class Gather:
    def __init__(self, count, shard, full, lanes, own, zs, zr, ys, yr):
        s, _, z, y, _, _ = place()
        lines = count // 2
        shard = shard.at[:, lanes]
        view = lambda slot: full.at[slot, :, lanes]
        self.local = pltpu.make_async_copy(shard, view(s), own)
        self.z_copies = [
            remote(shard, view(s), zs.at[j], zr.at[j], device)
            for j, device in enumerate(along_z(count))
        ]
        self.y_copies = [remote(shard, view(s), ys.at[0], yr.at[0], y_neighbour())]
        for j in range(1, lines):
            slot = 2 * lax.rem(z - j + lines, lines) + y
            self.y_copies.append(remote(view(slot), view(slot), ys.at[j], yr.at[j], y_neighbour()))

    def start(self):
        for copy in self.z_copies:
            copy.start()
        self.y_copies[0].start()
        self.local.start()

    def forward(self):
        for z_copy, y_copy in zip(self.z_copies, self.y_copies[1:]):
            z_copy.wait_recv()
            y_copy.start()

    def finish(self):
        self.local.wait()
        for copy in self.y_copies:
            copy.wait_recv()

    def close(self):
        for copy in self.z_copies + self.y_copies:
            copy.wait_send()


class Scatter:
    def __init__(self, count, terms, y_buf, pair, z_buf, ys, yr, zs, zr):
        self.terms, self.y_buf, self.pair, self.z_buf = terms, y_buf, pair, z_buf
        _, _, self.z, self.y, _, _ = place()
        self.lines = count // 2
        self.y_copies = []
        for j in range(self.lines):
            line = lax.rem(self.z + j, self.lines)
            self.y_copies.append(
                remote(
                    terms.at[2 * line + 1 - self.y], y_buf.at[line], ys.at[j], yr.at[j], y_neighbour()
                )
            )
        self.z_copies = [
            remote(pair.at[j], z_buf.at[j], zs.at[j], zr.at[j], device)
            for j, device in enumerate(along_z(count))
        ]

    def fill(self, left, right):
        self.terms[...] = across(left, right).astype(LOW).reshape(self.terms.shape)

    def fill_dense(self, left, right):
        terms = across(left, right).astype(LOW)
        part = terms.shape[0] // self.terms.shape[0]
        terms = terms.reshape(self.terms.shape[0], part, terms.shape[1])
        self.terms[:, 0:part] = terms[:, :, 0:128]
        self.terms[:, part:] = jnp.concatenate(
            [terms[:, 0 : part // 2, 128:], terms[:, part // 2 :, 128:]], axis=2
        )

    def start(self, *away):
        for j in away or list(range(1, self.lines)) + [0]:
            self.y_copies[j].start()

    def forward(self, *away):
        for j in away or range(1, self.lines):
            line = lax.rem(self.z + j, self.lines)
            self.y_copies[j].wait_recv()
            self.pair[j - 1] = (
                self.terms[2 * line + self.y].astype(WIDE) + self.y_buf[line].astype(WIDE)
            ).astype(LOW)
            self.z_copies[j - 1].start()

    def finish(self):
        self.y_copies[0].wait_recv()
        total = self.terms[2 * self.z + self.y].astype(WIDE) + self.y_buf[self.z].astype(WIDE)
        for j, copy in enumerate(self.z_copies):
            copy.wait_recv()
            total = total + self.z_buf[j].astype(WIDE)
        return total

    def close(self):
        for copy in self.z_copies + self.y_copies:
            copy.wait_send()


class Spread:
    def __init__(self, count, blocks, send, recv):
        s = place()[0]
        self.copies = [
            remote(blocks.at[s], blocks.at[s], send.at[j], recv.at[j], device)
            for j, device in enumerate(along_seq(count))
        ]

    def start(self):
        for copy in self.copies:
            copy.start()

    def finish(self):
        for copy in self.copies:
            copy.wait_recv()

    def close(self):
        for copy in self.copies:
            copy.wait_send()


class Swap(Spread):
    def __init__(self, count, out, into, send, recv):
        s = place()[0]
        self.out, self.into = out, into
        self.copies = [
            remote(out.at[device[0]], into.at[s], send.at[j], recv.at[j], device)
            for j, device in enumerate(along_seq(count))
        ]

    def start(self):
        s = place()[0]
        super().start()
        self.into[s] = self.out[s]


class SeqSum:
    def __init__(self, count, out, into, sums, send, recv):
        self.count, self.into, self.sums = count, into, sums
        self.swap = Swap(count, out, into, send.at[0], recv.at[0])
        self.spread = Spread(count, sums, send.at[1], recv.at[1])

    def start(self):
        self.swap.start()

    def add(self):
        self.swap.finish()
        self.sums[place()[0]] = functools.reduce(jnp.add, [self.into[d] for d in range(self.count)])
        self.spread.start()

    def finish(self):
        self.spread.finish()

    def close(self):
        self.swap.close()
        self.spread.close()


class HeadSum:
    def __init__(self, turn, terms, core_in, x_out, x_in, sems):
        self.turn, self.terms, self.core_in, self.x_out, self.x_in = turn, terms, core_in, x_out, x_in
        self.sems = sems
        self.core = place()[5]
        self.half = terms.shape[1] // 2

    def core_copy(self, c, turn=None):
        sems = self.sems.at[self.turn if turn is None else turn]
        away = pl.ds(pl.multiple_of((1 - self.core) * self.half, self.half), self.half)
        return remote(
            self.terms.at[c, away], self.core_in.at[c], sems.at[0, c], sems.at[1, c], core_of_chip()
        )

    def x_copy(self, c, turn=None):
        turn = self.turn if turn is None else turn
        sems = self.sems.at[turn]
        return remote(
            self.x_out.at[c], self.x_in.at[turn % 2, c], sems.at[2, c], sems.at[3, c], x_neighbour()
        )

    def offer(self, c, rows):
        if self.turn > 0:
            self.core_copy(c, self.turn - 1).wait_send()
        self.terms[c] = rows
        self.core_copy(c).start()

    def pair_up(self, c):
        self.core_copy(c).wait_recv()
        if self.turn > 0:
            self.x_copy(c, self.turn - 1).wait_send()
        here = pl.ds(pl.multiple_of(self.core * self.half, self.half), self.half)
        self.x_out[c] = (
            self.terms[c, here].astype(WIDE) + self.core_in[c].astype(WIDE)
        ).astype(LOW)
        self.x_copy(c).start()

    def arrived(self, c):
        self.x_copy(c).wait_recv()

    def total(self, c, rows):
        return self.x_out[c, rows].astype(WIDE) + self.x_in[self.turn % 2, c, rows].astype(WIDE)


def iota(shape, dim):
    return lax.broadcasted_iota(jnp.int32, shape, dim)


def fold(rows):
    return rows.reshape(rows.shape[0] // 8, 8, rows.shape[1]).sum(axis=0)


def gelu_and_slope(v):
    square = v * v
    t = jnp.tanh(0.7978845608 * (v + 0.044715 * v * square))
    half = 0.5 * (1.0 + t)
    slope = half + 0.5 * v * (1.0 - t * t) * (0.7978845608 * (1.0 + 0.134145 * square))
    return v * half, slope


def exact(left, right, dims=(1, 0)):
    return lax.dot_general(
        left,
        right,
        (((dims[0],), (dims[1],)), ((), ())),
        preferred_element_type=WIDE,
        precision=PRECISE,
    )


def dense(block):
    n = block.shape[0]
    rest = jnp.concatenate([block[0 : n // 2, 128:], block[n // 2 :, 128:]], axis=1)
    return jnp.concatenate([block[:, 0:128], rest], axis=0)


def undense(block):
    n = block.shape[0] * 2 // 3
    rest = jnp.concatenate([block[n:, 0:64], block[n:, 64:128]], axis=0)
    return jnp.concatenate([block[0:n], rest], axis=1)


def halves(wide_block):
    high = wide_block.astype(LOW)
    return high, (wide_block - high.astype(WIDE)).astype(LOW)


def thrice(left, right):
    return matmul_low(left[0], right[0]) + (matmul_low(left[0], right[1]) + matmul_low(left[1], right[0]))


def loop(count, body):
    lax.fori_loop(0, count, lambda i, carry: (body(i), carry)[1], 0)


def layer_kernel(count, names, *refs):
    r = types.SimpleNamespace(**dict(zip(names, refs)))
    s, h, z, y, x, core = place()
    rows, width = r.inputs_hbm.shape
    near = r.w_query.shape[1]
    heads = near // HEAD_DIM
    feed = r.w_up.shape[1]
    size = rows // CHUNKS
    half = size // 2
    step = 128
    lines = count // 2
    two = 2 * LAND
    scale = HEAD_DIM**-0.5
    chunk_rows = lambda c: pl.ds(pl.multiple_of(c * size, size), size)
    my_rows = lambda c: pl.ds(pl.multiple_of(c * size + core * half, half), half)
    everyone = along_seq(count)
    before, after = (lax.rem(s + count - 1, count), h), (lax.rem(s + 1, count), h)

    load_shards, load_vectors = (
        [pltpu.make_async_copy(ref, held, sems.at[k]) for k, (ref, held) in enumerate(pairs_of)]
        for pairs_of, sems in (
            (
                (
                    (r.w_query_hbm, r.w_query), (r.w_key_hbm, r.w_key),
                    (r.w_value_hbm, r.w_value), (r.w_out_hbm, r.w_out),
                ),
                r.shard_sems,
            ),
            (
                (
                    (r.bias_query_hbm, r.bias_query), (r.bias_value_hbm, r.bias_value), (r.bias_out_hbm, r.bias_out),
                    (r.bias_up_hbm, r.bias_up), (r.bias_down_hbm, r.bias_down), (r.gain_one_hbm, r.gain_one),
                    (r.bias_one_hbm, r.bias_one), (r.gain_two_hbm, r.gain_two), (r.bias_two_hbm, r.bias_two),
                ),
                r.vector_sems,
            ),
        )
    )

    def gather(k, shard, full, lo, hi):
        return Gather(
            count, shard, full, slice(lo, hi), r.g_own.at[k], r.g_zs.at[k], r.g_zr.at[k], r.g_ys.at[k], r.g_yr.at[k]
        )

    def scatter(k, terms, y_buf, pair, z_buf):
        return Scatter(
            count, terms, y_buf, pair, z_buf, r.s_ys.at[k], r.s_yr.at[k], r.s_zs.at[k], r.s_zr.at[k]
        )

    gather_qk = gather(0, r.packed, r.w_near, 0, 2 * near)
    gather_vo = gather(1, r.packed, r.w_near, 2 * near, 4 * near)
    third = feed // 3
    ups = [gather(2 + k, r.w_up, r.full_up, k * third, (k + 1) * third) for k in range(3)]
    downs = [gather(5 + k, r.w_down, r.full_down, k * third, (k + 1) * third) for k in range(3)]
    gathers = [gather_qk, gather_vo] + ups + downs
    scatter_out = scatter(0, r.t_out, r.yb_out, r.pr_out, r.zb_out)
    scatter_up = scatter(1, r.t_up, r.yb_up, r.pr_up, r.zb_up)
    scatter_down = scatter(2, r.t_down, r.yb_down, r.pr_down, r.zb_down)
    scatter_qk = scatter(3, r.t_qk, r.yb_qk, r.pr_qk, r.zb_qk)
    scatter_v = scatter(4, r.t_v, r.yb_v, r.pr_v, r.zb_v)
    scatters = [scatter_out, scatter_up, scatter_down, scatter_qk, scatter_v]
    correction = HeadSum(0, r.corr_terms, r.corr_core, r.corr_out, r.corr_in, r.corr_sems)
    sums = [HeadSum(k, r.terms, r.core_in, r.x_out, r.x_in, r.h_sems) for k in range(3)]

    out_copies = [
        remote(r.out_turned.at[0], r.out_turned.at[1], r.w_s.at[0], r.w_r.at[0], core_of_chip()),
        remote(r.out_turned.at[0], r.out_turned.at[2], r.w_s.at[1], r.w_r.at[1], x_neighbour()),
        remote(r.out_turned.at[2], r.out_turned.at[3], r.w_s.at[2], r.w_r.at[2], core_of_chip()),
    ]

    def mixed_copies(c):
        return [
            remote(r.mixed_out.at[c, part], r.mixed_in.at[k, c], r.m_s.at[k, c], r.m_r.at[k, c], device)
            for k, (part, device) in enumerate(
                ((1 - core, core_of_chip()), (core, x_neighbour()), (1 - core, across_x()))
            )
        ]

    landmarks = Spread(count, r.land_part, r.e_s.at[0], r.e_r.at[0])
    numer_swap = Swap(count, r.numer_out, r.numer_in, r.e_s.at[1], r.e_r.at[1])
    kernel_spread = Spread(count, r.kernel_v, r.e_s.at[2], r.e_r.at[2])
    small_spread = Spread(count, r.small_part, r.e_s.at[3], r.e_r.at[3])
    mix_sum, land_sum, vector_total = (
        SeqSum(count, out, into, total, r.e_s.at[pl.ds(4 + 2 * k, 2)], r.e_r.at[pl.ds(4 + 2 * k, 2)])
        for k, (out, into, total) in enumerate(
            (
                (r.mix_out, r.mix_in, r.mix_sums),
                (r.land_out, r.land_in, r.land_sums),
                (r.vector_out, r.vector_in, r.vector_sums),
            )
        )
    )
    spreads = [landmarks, numer_swap, kernel_spread, small_spread, mix_sum, land_sum, vector_total]

    def rim(k, ext):
        first = remote(
            ext.at[pl.ds(REACH, REACH)], ext.at[pl.ds(REACH + rows, REACH)], r.rim_s.at[k, 0], r.rim_r.at[k, 0], before
        )
        last = remote(
            ext.at[pl.ds(rows, REACH)], ext.at[pl.ds(0, REACH)], r.rim_s.at[k, 1], r.rim_r.at[k, 1], after
        )
        return [first, last]

    rims = [rim(0, r.value_ext), rim(1, r.grad_ext)]

    def share(k, ref, c):
        return remote(
            ref.at[my_rows(c)], ref.at[my_rows(c)], r.share_s.at[k, c], r.share_r.at[k, c], core_of_chip()
        )

    load_inputs = pltpu.make_async_copy(r.inputs_hbm, r.inputs, r.io.at[0])
    load_cotangent = pltpu.make_async_copy(r.cotangent_hbm, r.cotangent, r.io.at[1])
    stores = [
        pltpu.make_async_copy(ref, out, r.io.at[2 + k])
        for k, (ref, out) in enumerate(
            (
                (r.output, r.output_hbm),
                (r.grad_w_out, r.grad_w_out_hbm),
                (r.grad_w_up, r.grad_w_up_hbm),
                (r.grad_w_down, r.grad_w_down_hbm),
                (r.grad_near, r.grad_near_hbm),
            )
        )
    ]
    store_output, store_out, store_up, store_down, store_near = stores
    vector_core = remote(
        r.vector_sum.at[0], r.vector_sum.at[1], r.core_s.at[0], r.core_r.at[0], core_of_chip()
    )

    met = [core_of_chip(), x_neighbour(), across_x()] + everyone
    greet(met)
    for copy in load_shards + [load_inputs] + load_vectors:
        copy.start()
    for copy in load_shards:
        copy.wait()
    r.packed[:, 0:near] = r.w_query[...]
    r.packed[:, near : 2 * near] = r.w_key[...]
    r.packed[:, 2 * near : 3 * near] = r.w_value[...]
    r.packed[:, 3 * near : 4 * near] = r.w_out[...]
    ends = jnp.where(s == 0, r.lengths[0], jnp.where(s == count - 1, r.lengths[2], 0))
    edge_start = jnp.where(s == 0, 0, rows - ends)
    edge_end = edge_start + ends
    edge_count = ends // LAND
    mid_count = r.lengths[1] // LAND
    mid_first = s * rows - r.lengths[0]
    first_slot = jnp.maximum(mid_first, 0) // mid_count
    item_edge = jnp.where(s == 0, ends, jnp.where(s == count - 1, rows - ends, -1))

    def members():
        token, lane = iota((rows, two), 0), iota((rows, two), 1)
        mid = lane < LAND
        at_edge = (token >= edge_start) & (token < edge_end)
        start = jnp.where(mid, (first_slot + lane) * mid_count - mid_first, (lane - LAND) * edge_count + edge_start)
        length = jnp.where(mid, mid_count, edge_count)
        inside = (token >= start) & (token < start + length)
        belongs = jnp.where(mid, jnp.where(at_edge, 0.0, 1.0), jnp.where(at_edge, 1.0, 0.0))
        r.member[...] = jnp.where(inside, belongs, 0.0).astype(LOW)

    members()
    greeted(met)
    gather_qk.start()
    gather_vo.start()
    load_cotangent.start()
    r.small_part[s] = jnp.zeros((8, PAD), WIDE)
    r.vectors[...] = jnp.zeros_like(r.vectors)
    head_lane = iota((8, PAD), 1) // HEAD_DIM
    masks = [(head_lane == k).astype(WIDE)[0:1] for k in range(heads)]
    masks_low = [m[:, :near].astype(LOW) for m in masks]

    def spread_heads(ref, block):
        for k in range(heads):
            ref[k * two : (k + 1) * two, :] = block * masks_low[k]

    def own_heads(wide_rows, group, lanes):
        return sum(
            wide_rows[k * group : (k + 1) * group, :] * masks[k][:, :lanes] for k in range(heads)
        )

    def bands(ref, flipped):
        token, lane = iota((BLOCK, 2 * SPAN), 0), iota((BLOCK, 2 * SPAN), 1)
        upper = lane < SPAN
        offset = jnp.where(upper, lane, lane - SPAN) - token
        for k in range(heads):
            band = jnp.zeros((BLOCK, 2 * SPAN), WIDE)
            for j in range(KERNEL):
                at = KERNEL - 1 - j if flipped else j
                band = jnp.where(offset == at, r.conv_taps[k, j], band)
            high = band.astype(LOW).astype(WIDE)
            ref[k * BLOCK : (k + 1) * BLOCK, :] = jnp.where(upper, high, band - high).astype(LOW)

    bands(r.band, False)
    bands(r.band_back, True)

    def window(ext, b):
        taken = ext[pl.ds(pl.multiple_of(b * BLOCK, BLOCK), SPAN), :]
        start = b * BLOCK
        left_out = (start == item_edge) | ((s == 0) & (start == 0))
        right_out = (start + BLOCK == item_edge) | ((s == count - 1) & (start + BLOCK == rows))
        row = iota((SPAN, taken.shape[1]), 0)
        keep = jnp.where(
            row < REACH,
            jnp.where(left_out, 0.0, 1.0),
            jnp.where(row >= REACH + BLOCK, jnp.where(right_out, 0.0, 1.0), 1.0),
        )
        return taken * keep.astype(LOW)

    def convolve(band, taken):
        return own_heads(matmul_low(band[...], jnp.concatenate([taken, taken], axis=0)), BLOCK, taken.shape[1])

    gather_qk.forward()
    gather_vo.forward()
    load_inputs.wait()
    for copy in load_vectors:
        copy.wait()
    flat = lambda ref: ref[...].reshape(1, ref.shape[0])
    bias_query, bias_value, bias_out = flat(r.bias_query), flat(r.bias_value), flat(r.bias_out)
    bias_up, bias_down = flat(r.bias_up), flat(r.bias_down)
    gain_one, bias_one, gain_two, bias_two = (
        flat(r.gain_one), flat(r.bias_one), flat(r.gain_two), flat(r.bias_two)
    )
    gather_qk.finish()

    def project_qk(c):
        at = chunk_rows(c)
        both = matmul_low(r.inputs[at], r.w_near[:, :, 0 : 2 * near].reshape(width, 2 * near))
        r.queries[at] = (both[:, :near] + bias_query).astype(LOW)
        r.keys[at] = both[:, near:].astype(LOW)

    loop(CHUNKS, project_qk)
    query_sums = across(r.member[...], r.queries[...])
    key_sums = across(r.member[...], r.keys[...])
    mid_scale = 1.0 / mid_count.astype(WIDE)
    edge_scale = 1.0 / jnp.maximum(edge_count, 1).astype(WIDE)
    border = jnp.concatenate([query_sums[0:BORDER], key_sums[0:BORDER]], axis=0) * mid_scale
    r.land_part[s] = dense(border).astype(LOW)
    landmarks.start()
    ups[0].start()
    ups[1].start()
    r.query_land[LAND:two] = (query_sums[LAND:two] * edge_scale).astype(LOW)
    r.key_land[LAND:two] = (key_sums[LAND:two] * edge_scale).astype(LOW)

    gather_vo.finish()

    def project_v(c):
        at = pl.ds(pl.multiple_of(REACH + c * size, REACH), size)
        values = matmul_low(r.inputs[chunk_rows(c)], r.w_near[:, :, 2 * near : 2 * near + PAD].reshape(width, PAD))
        values = values[:, :near] + bias_value
        r.value_ext[at, 0:near] = values.astype(LOW)
        r.value_ext[at, near:PAD] = jnp.zeros((size, PAD - near), LOW)

    loop(CHUNKS, project_v)
    for copy in rims[0]:
        copy.start()
    r.out_turned[0] = r.w_near[:, :, 3 * near :].reshape(width, near).T
    for copy in out_copies[0:2]:
        copy.start()

    def convolve_values(b):
        r.conv[pl.ds(pl.multiple_of(b * BLOCK, BLOCK), BLOCK), :] = convolve(
            r.band, window(r.value_ext, b)
        )[:, :near]

    blocks = rows // BLOCK
    loop(blocks - 2, lambda b: convolve_values(b + 1))

    landmarks.finish()
    lane = iota((LAND, count * BORDER), 1)
    owner = lane // BORDER
    starts = jnp.zeros((LAND, count * BORDER), jnp.int32)
    for d in range(count):
        starts = jnp.where(owner == d, jnp.maximum(d * rows - r.lengths[0], 0) // mid_count, starts)
    put = (iota((LAND, count * BORDER), 0) == starts + lane - owner * BORDER).astype(LOW)
    borders = [undense(r.land_part[d]) for d in range(count)]
    r.query_land[0:LAND] = matmul_low(put, jnp.concatenate([b[0:BORDER] for b in borders], axis=0)).astype(LOW)
    r.key_land[0:LAND] = matmul_low(put, jnp.concatenate([b[BORDER:] for b in borders], axis=0)).astype(LOW)
    spread_heads(r.query_heads, r.query_land[...])
    spread_heads(r.key_heads, r.key_land[...])

    own_values = lambda: r.value_ext[pl.ds(REACH, rows), :]

    def score_b(c):
        at = chunk_rows(c)
        r.weights_b[:, at] = against(r.query_heads[...], r.keys[at]) * scale

    def attend_b(g):
        at = pl.ds(pl.multiple_of(g * LAND, LAND), LAND)
        token = iota((LAND, rows), 1)
        at_edge = jnp.where((token >= edge_start) & (token < edge_end), 1.0, 0.0)
        member = jnp.where(lax.rem(g, 2) == 1, at_edge, 1.0 - at_edge)
        scores = jnp.where(member > 0.5, r.weights_b[at], MASKED)
        largest = jnp.max(scores, axis=1, keepdims=True)
        weights = jnp.exp(scores - largest) * member
        r.weights_b[at] = weights
        r.max_b[at] = largest
        r.total_b[at] = jnp.sum(weights, axis=1, keepdims=True)

    loop(CHUNKS, score_b)
    loop(2 * heads, attend_b)
    numer = own_heads(matmul_low(r.weights_b[...].astype(LOW), own_values()), two, PAD)
    lane = iota((two, PAD), 1)
    for k in range(heads):
        numer = jnp.where(lane == near + k, r.total_b[k * two : (k + 1) * two], numer)
        numer = jnp.where(lane == near + heads + k, r.max_b[k * two : (k + 1) * two], numer)
    r.numer_out[...] = numer[0:LAND].reshape(count, LAND // count, PAD)
    numer_swap.start()
    ups[2].start()
    for copy in rims[0]:
        copy.wait_recv()
    loop(2, lambda b: convolve_values(b * (blocks - 1)))

    def wide_heads(stats, base):
        lane = iota(stats.shape, 1)
        out = stats
        for k in range(heads):
            out = jnp.where(lane // HEAD_DIM == k, stats[:, base + k : base + k + 1], out)
        return out

    edge = numer[LAND:two]
    edge_totals = wide_heads(edge, near)
    edge_totals = jnp.where(edge_totals > 0.0, edge_totals, 1.0)
    r.kernel_edge[...] = jnp.where(iota(edge.shape, 1) < near, edge / edge_totals, 0.0)

    pairs = [(k, g) for k in range(heads) for g in range(2)]
    identity = (iota((LAND, LAND), 0) == iota((LAND, LAND), 1)).astype(WIDE)
    group = lambda g: slice(g * LAND, (g + 1) * LAND)

    def first_inverse(k, g, i):
        lands = r.query_heads[k * two + g * LAND : k * two + (g + 1) * LAND, :]
        scores = against(lands, r.key_land[group(g), :]) * scale
        weights = jnp.exp(scores - jnp.max(scores, axis=1, keepdims=True))
        weights = weights / jnp.sum(weights, axis=1, keepdims=True)
        r.land_kernel[i] = weights
        return weights.T / jnp.sum(weights * weights)

    def invert(it, inverses):
        kernels = [r.land_kernel[i] for i in range(len(pairs))]
        products = [exact(a, b) for a, b in zip(kernels, inverses)]
        for i, (a, p) in enumerate(zip(inverses, products)):
            r.befores[it, i] = a
            r.products[it, i] = p
        nested = [15.0 * identity - exact(p, 7.0 * identity - p) for p in products]
        nested = [13.0 * identity - exact(p, n) for p, n in zip(products, nested)]
        return tuple(0.25 * exact(a, n) for a, n in zip(inverses, nested))

    inverses = tuple(first_inverse(k, g, i) for i, (k, g) in enumerate(pairs))
    inverses = lax.fori_loop(0, PINV_STEPS // 2, invert, inverses)


    numer_swap.finish()
    parts = [r.numer_in[d] for d in range(count)]
    largest = functools.reduce(jnp.maximum, [wide_heads(p, near + heads) for p in parts])
    lane = iota(largest.shape, 1)
    joined = jnp.zeros_like(largest)
    totals = jnp.zeros_like(largest)
    for p in parts:
        weight = jnp.exp(wide_heads(p, near + heads) - largest)
        joined = joined + jnp.where(lane < near, p * weight, 0.0)
        totals = totals + jnp.where(lane < near, wide_heads(p, near) * weight, 0.0)
    joined = jnp.where(lane < near, joined / jnp.where(lane < near, totals, 1.0), 0.0)
    for k in range(heads):
        joined = jnp.where(lane == near + k, totals[:, k * HEAD_DIM : k * HEAD_DIM + 1], joined)
        joined = jnp.where(
            lane == near + heads + k, largest[:, k * HEAD_DIM : k * HEAD_DIM + 1], joined
        )
    r.kernel_v[s] = joined
    kernel_spread.start()
    ups[0].forward()
    ups[1].forward()
    downs[0].start()
    inverses = lax.fori_loop(PINV_STEPS // 2, PINV_STEPS, invert, inverses)
    for i, inverse in enumerate(inverses):
        r.inverse[i] = inverse

    def attend_f(c):
        at = pl.ds(pl.multiple_of(c * size, size), size)
        scores = against(r.queries[at], r.key_heads[...]) * scale
        token, lane = iota((size, two), 0) + c * size, iota((size, two), 1)
        at_edge = (token >= edge_start) & (token < edge_end)
        member = jnp.where(lane < LAND, jnp.where(at_edge, 0.0, 1.0), jnp.where(at_edge, 1.0, 0.0))
        for k in range(heads):
            own = jnp.where(member > 0.5, scores[:, k * two : (k + 1) * two], MASKED)
            weights = jnp.exp(own - jnp.max(own, axis=1, keepdims=True))
            r.weights_f[at, k * two : (k + 1) * two] = weights / jnp.sum(weights, axis=1, keepdims=True)

    loop(rows // size, attend_f)
    kernel_spread.finish()
    kernel_mid = r.kernel_v[...].reshape(LAND, PAD)
    kernel_of = lambda g: kernel_mid if g == 0 else r.kernel_edge[...]
    for g in range(2):
        mixed = jnp.zeros((LAND, PAD), WIDE)
        for i, (k, own) in enumerate(pairs):
            if own == g:
                mixed = mixed + exact(r.inverse[i], kernel_of(g)) * masks[k]
        r.mixing[group(g), :] = mixed[:, :near].astype(LOW)
    spread_heads(r.mixing_heads, r.mixing[...])
    ups[2].forward()
    downs[1].start()
    downs[2].start()

    def project_out(c):
        at = chunk_rows(c)
        attended = matmul_low(r.weights_f[at].astype(LOW), r.mixing_heads[...])
        r.mixed[at] = (attended + r.conv[at]).astype(LOW)
        for part in range(2):
            at = pl.ds(pl.multiple_of(c * size + part * half, half), half)
            r.mixed_out[c, part] = dense(r.mixed[at])
        for copy in mixed_copies(c):
            copy.start()

    out_copies[1].wait_recv()
    out_copies[2].start()
    loop(CHUNKS, project_out)
    out_copies[0].wait_recv()
    out_copies[2].wait_recv()
    downs[0].forward()

    def prepare(it):
        many = range(len(pairs))
        befores = [r.befores[it, i] for i in many]
        products = [r.products[it, i] for i in many]
        squares = [exact(p, p) for p in products]
        firsts = [exact(a, p) for a, p in zip(befores, products)]
        cubes = [exact(p, q) for p, q in zip(products, squares)]
        seconds = [exact(t, p) for t, p in zip(firsts, products)]
        for i in many:
            p, q, c = products[i].T, squares[i].T, cubes[i].T
            uppers = (
                3.25 * identity - 3.75 * p + 1.75 * q - 0.25 * c,
                1.75 * p - 3.75 * identity - 0.25 * q,
                1.75 * identity - 0.25 * p,
            )
            for k, (upper, lower) in enumerate(zip(uppers, (befores[i].T, firsts[i].T, -0.25 * seconds[i].T))):
                for half_of, (a, b) in enumerate(zip(halves(upper), halves(lower))):
                    r.uppers[it, i, half_of, :, group(k)] = a
                    r.lowers[it, i, half_of, :, group(k)] = b

    loop(PINV_STEPS, prepare)
    for i in range(len(pairs)):
        r.turned_kernel[i, 0], r.turned_kernel[i, 1] = halves(r.land_kernel[i].T)
    r.acc[...] = jnp.zeros_like(r.acc)
    for piece in ups:
        piece.finish()
    load_cotangent.wait()
    pieces = lambda body: loop(half // step, lambda i: body(pl.multiple_of(i * step, step)))

    def norm_first(c):
        for copy in mixed_copies(c):
            copy.wait_recv()
        theirs = [undense(r.mixed_in[k, c]) for k in range(3)]
        r.tmp[0:half] = matmul_low(r.mixed[my_rows(c)], r.out_turned[0]) + matmul_low(theirs[0], r.out_turned[1])
        r.tmp[half:size] = matmul_low(theirs[1], r.out_turned[2]) + matmul_low(theirs[2], r.out_turned[3])

        def piece(i):
            at = pl.ds(pl.multiple_of(c * size + core * half + i, step), step)
            kept = pl.ds(pl.multiple_of(c * half + i, step), step)
            attended = r.tmp[pl.ds(i, step)] + r.tmp[pl.ds(pl.multiple_of(half + i, step), step)]
            pre = r.inputs[at].astype(WIDE) + attended + bias_out
            normed, inv = normalize(pre)
            r.norm_one[kept] = normed
            r.inv_one[kept] = inv
            r.hidden[at] = (normed * gain_one + bias_one).astype(LOW)

        pieces(piece)
        share(0, r.hidden, c).start()

    def lift(c):
        share(0, r.hidden, c).wait_recv()
        at = chunk_rows(c)
        r.tmp[...] = matmul_low(r.hidden[at], r.full_up[...].reshape(width, feed))

        def curve(i):
            to = pl.ds(pl.multiple_of(c * size + i * step, step), step)
            value, grade = gelu_and_slope(r.tmp[pl.ds(pl.multiple_of(i * step, step), step)] + bias_up)
            r.active[to] = value.astype(LOW)
            r.slope[to] = grade.astype(LOW)

        loop(size // step, curve)

    def lower(c):
        at = chunk_rows(c)
        sums[0].offer(c, against(r.active[at], r.full_down[...].reshape(width, feed)).astype(LOW))

    def behind(c, total):
        @pl.when(c > 0)
        def _():
            total.pair_up(c - 1)

    def feed_forward(c):
        norm_first(c)
        behind(c, sums[0])
        lift(c)

        @pl.when(c == 0)
        def _():
            for piece in downs[1:]:
                piece.forward()
            for piece in downs:
                piece.finish()

        lower(c)

    loop(CHUNKS, feed_forward)
    sums[0].pair_up(CHUNKS - 1)

    order = [2, 1] + list(range(3, lines)) + [0] if lines > 2 else [1, 0]

    def feed_back(c):
        def piece(i):
            at = pl.ds(pl.multiple_of(c * size + core * half + i, step), step)
            kept = pl.ds(pl.multiple_of(c * half + i, step), step)
            pre = r.norm_one[kept] * gain_one + bias_one + sums[0].total(c, pl.ds(i, step)) + bias_down
            normed, inv = normalize(pre)
            r.output[at] = (normed * gain_two + bias_two).astype(LOW)
            grad = r.cotangent[at].astype(WIDE)
            back = norm_back(grad * gain_two, normed, inv)
            r.wide_grad[kept] = back
            r.grad_two[at] = back.astype(LOW)
            r.acc[0] += fold(grad * normed)
            r.acc[1] += fold(grad)
            r.acc[2] += fold(back)

        sums[0].arrived(c)
        pieces(piece)
        share(1, r.grad_two, c).start()
        share(2, r.output, c).start()
        behind(c, sums[1])
        share(1, r.grad_two, c).wait_recv()

        @pl.when(c == CHUNKS - 1)
        def _():
            scatter_down.fill(r.grad_two[...], r.active[...])
            scatter_down.start(*order)

        at = chunk_rows(c)
        r.tmp[...] = matmul_low(r.grad_two[at], r.full_down[...].reshape(width, feed))

        def curve(i):
            to = pl.ds(pl.multiple_of(c * size + i * step, step), step)
            value = r.tmp[pl.ds(pl.multiple_of(i * step, step), step)] * r.slope[to].astype(WIDE)
            r.grad_lift[to] = value.astype(LOW)
            r.acc[6] += fold(value)

        loop(size // step, curve)
        sums[1].offer(c, against(r.grad_lift[at], r.full_up[...].reshape(width, feed)).astype(LOW))

    loop(CHUNKS, feed_back)
    sums[1].pair_up(CHUNKS - 1)

    ups_next = list(range(2, lines)) + [0]
    r.mix_grad[...] = jnp.zeros_like(r.mix_grad)
    r.kland_grad[...] = jnp.zeros_like(r.kland_grad)

    def mix_back(c):
        def piece(i):
            at = pl.ds(pl.multiple_of(c * size + core * half + i, step), step)
            kept = pl.ds(pl.multiple_of(c * half + i, step), step)
            normed = r.norm_one[kept]
            grad = r.wide_grad[kept] + sums[1].total(c, pl.ds(i, step))
            back = norm_back(grad * gain_one, normed, r.inv_one[kept])
            r.wide_grad[kept] = back
            r.grad_one[at] = back.astype(LOW)
            r.acc[3] += fold(grad * normed)
            r.acc[4] += fold(grad)
            r.acc[5] += fold(back)

        @pl.when(c == 1)
        def _():
            scatter_down.forward(order[0])
            scatter_up.fill(r.hidden[...], r.grad_lift[...])

        if lines > 2:

            @pl.when(c == 2)
            def _():
                scatter_down.forward(order[1])

        @pl.when(c == CHUNKS - 1)
        def _():
            scatter_up.start(1)

        sums[1].arrived(c)
        pieces(piece)
        share(3, r.grad_one, c).start()
        share(3, r.grad_one, c).wait_recv()
        at = chunk_rows(c)
        grad = against(r.grad_one[at], r.out_turned[0]).astype(LOW)
        r.grad_ext[pl.ds(pl.multiple_of(REACH + c * size, REACH), size)] = grad
        weights = r.weights_f[at]
        weighted = weights * against(grad, r.mixing_heads[...])
        scores = []
        for k in range(heads):
            own = slice(k * two, (k + 1) * two)
            scores.append(weighted[:, own] - weights[:, own] * jnp.sum(weighted[:, own], axis=1, keepdims=True))
        scores = jnp.concatenate(scores, axis=1).astype(LOW)
        r.grad_query[at] = matmul_low(scores, r.key_heads[...]) * scale
        r.mix_grad[...] += across(weights.astype(LOW), grad)
        r.kland_grad[...] += across(scores, r.queries[at])

    loop(CHUNKS, mix_back)
    mix_grad = own_heads(r.mix_grad[...], two, near)
    kland_grad = own_heads(r.kland_grad[...], two, near) * scale
    each = LAND // count
    r.mix_out[...] = mix_grad[0:LAND].reshape(count, each, near)
    mix_sum.start()
    for copy in rims[1]:
        copy.start()

    def convolve_back(b):
        at = pl.ds(pl.multiple_of(b * BLOCK, BLOCK), BLOCK)
        r.conv[at] = convolve(r.band_back, window(r.grad_ext, b))

    scatter_out.fill_dense(r.grad_one[...], r.mixed[...])
    scatter_out.start()
    loop(blocks // 2 - 1, lambda b: convolve_back(b + 1))
    mix_sum.add()
    if order[2:-1]:
        scatter_down.forward(*order[2:-1])
    scatter_up.start(*ups_next[:1])
    loop(blocks // 2 - 1, lambda b: convolve_back(b + blocks // 2))
    for copy in rims[1]:
        copy.wait_recv()
    loop(2, lambda b: convolve_back(b * (blocks - 1)))

    mix_sum.finish()
    mix_grads = [r.mix_sums[...].reshape(LAND, near), mix_grad[LAND:two]]
    stats = r.kernel_v[...].reshape(LAND, PAD)
    mid_totals = wide_heads(stats, near)[:, :near]
    divisors = [mid_totals, edge_totals[:, :near]]
    inverse_grads = []
    for i, (k, g) in enumerate(pairs):
        inverse_grads.append(
            exact(mix_grads[g] * masks[k][:, :near], kernel_of(g)[:, :near], (1, 1))
        )
    shrink = [
        jnp.exp(r.max_b[k * two : k * two + LAND] - stats[:, near + heads + k : near + heads + k + 1])
        for k in range(heads)
    ]
    for g in range(2):
        grad = jnp.zeros((LAND, near), WIDE)
        for i, (k, own) in enumerate(pairs):
            if own == g:
                grad = grad + exact(r.inverse[i], mix_grads[g], (0, 0)) * masks[k][:, :near]
        grad = grad / divisors[g]
        lost = grad * kernel_of(g)[:, :near]
        for k in range(heads):
            at = slice(k * two + g * LAND, k * two + (g + 1) * LAND)
            factor = shrink[k] if g == 0 else 1.0
            r.numer_heads[at] = (grad * factor * masks[k][:, :near]).astype(LOW)
            r.total_grad[at] = -jnp.sum(lost * masks[k][:, :near], axis=1, keepdims=True) * factor

    def back_b(c):
        at = chunk_rows(c)
        values = r.value_ext[pl.ds(pl.multiple_of(REACH + c * size, REACH), size), 0:near]
        grad = against(r.numer_heads[...], values) + r.total_grad[...]
        r.scores_b[:, at] = (r.weights_b[:, at] * grad).astype(LOW)

    loop(CHUNKS, back_b)
    qland_grad = own_heads(matmul_low(r.scores_b[...], r.keys[...]), two, near) * scale
    r.land_out[:, :, 0:near] = qland_grad[0:LAND].reshape(count, each, near)
    r.land_out[:, :, near:] = kland_grad[0:LAND].reshape(count, each, near)
    land_sum.start()
    for k in range(7):
        r.vectors[k : k + 1] = jnp.sum(r.acc[k], axis=0, keepdims=True)
    lanes = r.vector_out.shape[2]
    for d in range(count):
        r.vector_out[d] = r.vectors[:, d * lanes : (d + 1) * lanes] if d * lanes < width else jnp.zeros((8, lanes), WIDE)
    vector_total.start()
    if ups_next[1:]:
        scatter_up.start(*ups_next[1:])
    scatter_up.forward(1)

    def values_back(c):
        at = chunk_rows(c)
        values = across(r.weights_b[:, at].astype(LOW), r.numer_heads[...]) + r.conv[at]
        r.near_grads[at, 2 * near : 3 * near] = values.astype(LOW)
        return jnp.sum(values, axis=0, keepdims=True)

    value_bias = lax.fori_loop(
        0, CHUNKS, lambda c, total: total + values_back(c), jnp.zeros((1, near), WIDE)
    )
    scatter_v.fill_dense(r.inputs[...], r.near_grads[:, 2 * near : 3 * near])
    scatter_v.start()

    def input_terms(c):
        at = chunk_rows(c)
        r.weights_f[at, 0:near] = across(r.scores_b[:, at], r.query_heads[...]) * scale
        r.near_grads[at, 0:near] = r.grad_query[at].astype(LOW)
        r.near_grads[at, near : 2 * near] = r.weights_f[at, 0:near].astype(LOW)
        terms = against(r.near_grads[at], r.w_near[:, :, 0 : 3 * near].reshape(width, 3 * near))
        sums[2].offer(c, terms.astype(LOW))

    input_terms(0)
    input_terms(1)
    sums[2].pair_up(0)
    land_sum.add()
    vector_total.add()
    sums[2].pair_up(1)
    if lines > 2:
        scatter_up.forward(2)

    def invert_back(i, carry):
        it = PINV_STEPS - 1 - i
        grads, kernel_grads = carry
        many = range(len(pairs))
        both = lambda ref: (ref[0], ref[1])
        wides = [thrice(halves(grads[p]), both(r.uppers[it, p])) for p in many]
        product_grads = [
            thrice(
                both(r.lowers[it, p]),
                halves(jnp.concatenate([w[:, LAND:two], w[:, two:], grads[p]], axis=0)),
            )
            for p, w in enumerate(wides)
        ]
        parts = [halves(grad) for grad in product_grads]
        kernel_grads = [
            old + thrice(part, both(r.lowers[it, p, :, :, 0:LAND]))
            for p, (old, part) in enumerate(zip(kernel_grads, parts))
        ]
        grads = [wides[p][:, 0:LAND] + thrice(both(r.turned_kernel[p]), parts[p]) for p in many]
        return tuple(grads), tuple(kernel_grads)

    zeros = tuple(jnp.zeros((LAND, LAND), WIDE) for _ in pairs)
    grads, kernel_grads = lax.fori_loop(0, PINV_STEPS, invert_back, (tuple(inverse_grads), zeros))
    scatter_out.forward()
    input_terms(2)
    vector_total.finish()
    for d in range(width // lanes):
        r.vector_sum[0, :, d * lanes : (d + 1) * lanes] = r.vector_sums[d]
    vector_core.start()

    qland_a = [jnp.zeros((LAND, near), WIDE)] * 2
    kland_a = [jnp.zeros((LAND, near), WIDE)] * 2
    for i, (k, g) in enumerate(pairs):
        kernel = r.land_kernel[i]
        turned = grads[i].T
        squares = jnp.sum(kernel * kernel)
        grad = kernel_grads[i] + turned / squares - kernel * (2.0 * jnp.sum(turned * kernel) / (squares * squares))
        grad = kernel * (grad - jnp.sum(kernel * grad, axis=1, keepdims=True)) * scale
        mask = masks[k][:, :near]
        qland_a[g] = qland_a[g] + exact(grad, r.key_land[group(g)].astype(WIDE)) * mask
        kland_a[g] = kland_a[g] + exact(grad, r.query_land[group(g)].astype(WIDE), (0, 0)) * mask


    sums[2].pair_up(2)
    if lines > 3:
        scatter_up.forward(*range(3, lines))
    land_sum.finish()
    land_total = r.land_sums[...].reshape(LAND, 2 * near)
    pick = (iota((LAND, LAND), 1) == iota((LAND, LAND), 0) + first_slot).astype(WIDE)

    def slot_grads(mid, edge):
        return jnp.concatenate([exact(pick, mid * mid_scale), edge * edge_scale], axis=0)

    def parted(both):
        high = both.astype(LOW)
        return jnp.concatenate([high, (both - high.astype(WIDE)).astype(LOW)], axis=0)

    slot_q = slot_grads(qland_a[0] + land_total[:, 0:near], qland_a[1] + qland_grad[LAND:two])
    slot_k = slot_grads(kland_a[0] + land_total[:, near:], kland_a[1] + kland_grad[LAND:two])
    r.slot_q[...] = parted(slot_q)
    r.slot_k[...] = parted(slot_k)
    r.slot_both[:, 0:near] = r.slot_q[0:two]
    r.slot_both[:, near:] = r.slot_k[0:two]
    slot_terms = against(r.slot_both[...], r.w_near[:, :, 0 : 2 * near].reshape(width, 2 * near))
    correction.offer(0, slot_terms.astype(LOW))
    input_terms(3)
    correction.pair_up(0)

    def add_slots(c):
        at = chunk_rows(c)
        member = jnp.concatenate([r.member[at]] * 2, axis=1)
        queries = r.grad_query[at] + matmul_low(member, r.slot_q[...])
        keys = r.weights_f[at, 0:near] + matmul_low(member, r.slot_k[...])
        r.near_grads[at, 0:near] = queries.astype(LOW)
        r.near_grads[at, near : 2 * near] = keys.astype(LOW)
        return jnp.sum(queries, axis=0, keepdims=True)

    query_bias = lax.fori_loop(
        0, CHUNKS, lambda c, total: total + add_slots(c), jnp.zeros((1, near), WIDE)
    )
    sums[2].pair_up(3)
    scatter_qk.fill(r.inputs[...], r.near_grads[:, 0 : 2 * near])
    scatter_qk.start()
    scatter_v.forward()

    r.tap_grad[...] = jnp.zeros_like(r.tap_grad)

    def tap_products(b):
        own = r.grad_ext[pl.ds(pl.multiple_of(b * BLOCK + REACH, REACH), BLOCK), :]
        own = jnp.concatenate([own * m for m in masks_low], axis=0)
        r.tap_grad[:, 0:SPAN] += against(own, window(r.value_ext, b)[:, :near])

    loop(blocks, tap_products)
    token = lax.rem(iota((heads * BLOCK, 128), 0), BLOCK)
    slanted = r.tap_grad[...]
    for bit in range(6):
        moved = pltpu.roll(slanted, 128 - (1 << bit), 1)
        slanted = jnp.where(lax.rem(token // (1 << bit), 2) == 1, moved, slanted)
    for k in range(heads):
        r.small_part[s, 2 + k : 3 + k, 0:128] = jnp.sum(
            slanted[k * BLOCK : (k + 1) * BLOCK], axis=0, keepdims=True
        )
    r.small_part[s, 0:1, 0:near] = query_bias
    r.small_part[s, 1:2, 0:near] = value_bias
    small_spread.start()

    def settle_output(c):
        share(2, r.output, c).wait_recv()

    loop(CHUNKS, settle_output)
    store_output.start()
    r.grad_w_down[...] = scatter_down.finish()
    store_down.start()
    r.grad_w_up[...] = scatter_up.finish()
    store_up.start()
    r.grad_w_out[...] = undense(scatter_out.finish())
    store_out.start()
    r.grad_near[2] = undense(scatter_v.finish())
    scatter_qk.forward()
    here = pl.ds(pl.multiple_of(core * LAND, LAND), LAND)
    share_slots = remote(
        r.corr_all.at[here], r.corr_all.at[here], r.corr_s.at[0], r.corr_r.at[0], core_of_chip()
    )
    correction.arrived(0)
    r.corr_all[here] = correction.total(0, pl.ds(0, LAND)).astype(LOW)
    share_slots.start()
    share_slots.wait_recv()

    def store_inputs(c):
        at = chunk_rows(c)
        return pltpu.make_async_copy(r.cotangent.at[at], r.grad_inputs_hbm.at[at], r.chunk_sems.at[c])

    def inputs_done(c):
        sums[2].arrived(c)
        slots = matmul_low(r.member[my_rows(c)], r.corr_all[...])
        kept = r.wide_grad[pl.ds(pl.multiple_of(c * half, half), half)]
        r.cotangent[my_rows(c)] = (kept + sums[2].total(c, pl.ds(0, half)) + slots).astype(LOW)
        share(4, r.cotangent, c).start()

        @pl.when(c > 0)
        def _():
            share(4, r.cotangent, c - 1).wait_recv()
            store_inputs(c - 1).start()

    loop(CHUNKS, inputs_done)
    near_total = scatter_qk.finish()
    for k in range(2):
        r.grad_near[k] = near_total[:, k * near : (k + 1) * near]
    store_near.start()
    vector_core.wait_recv()
    r.vectors[0:6] = r.vector_sum[0, 0:6] + r.vector_sum[1, 0:6]
    r.vectors[6:8] = r.vector_sum[0, 6:8]
    small_spread.finish()
    r.smalls[...] = functools.reduce(jnp.add, [r.small_part[d] for d in range(count)])

    share(4, r.cotangent, CHUNKS - 1).wait_recv()
    store_inputs(CHUNKS - 1).start()

    def settle(c):
        sums[2].core_copy(c).wait_send()
        sums[2].x_copy(c).wait_send()
        store_inputs(c).wait()
        for copy in mixed_copies(c):
            copy.wait_send()
        for k, ref in enumerate((r.hidden, r.grad_two, r.output, r.grad_one, r.cotangent)):
            share(k, ref, c).wait_send()

    loop(CHUNKS, settle)
    vector_core.wait_send()
    correction.core_copy(0).wait_send()
    correction.x_copy(0).wait_send()
    share_slots.wait_send()
    for copy in stores:
        copy.wait()
    for copy in rims[0] + rims[1] + out_copies:
        copy.wait_send()
    for group_of in gathers + scatters + spreads:
        group_of.close()


def hand_out(
    output, grad_inputs, grad_out, grad_up, grad_down, grad_near, vectors, smalls,
    to_output, to_inputs, to_query, to_key, to_value, to_out, to_up, to_down,
    bias_query, bias_value, bias_out, bias_up, bias_down, gain_one, bias_one, gain_two, bias_two, taps,
    hold, hold_near, hold_feed, hold_vectors, hold_smalls, sems, more, few_sems,
):
    parts = hold.shape[1]
    rows = output.shape[0] // parts
    copy = pltpu.make_async_copy
    first, second = [], []
    for j in range(parts):
        for k, (ref, to) in enumerate(((output, to_output), (grad_inputs, to_inputs))):
            at = pl.ds(j * rows, rows)
            first.append(copy(ref.at[at], hold.at[k, j], sems.at[k, j, 0]))
            second.append(copy(hold.at[k, j], to.at[at], sems.at[k, j, 1]))
    for k, (ref, held, to) in enumerate(
        (
            (grad_near.at[0], hold_near.at[0], to_query),
            (grad_near.at[1], hold_near.at[1], to_key),
            (grad_near.at[2], hold_near.at[2], to_value),
            (grad_out, hold_near.at[3], to_out),
            (grad_up, hold_feed.at[0], to_up),
            (grad_down, hold_feed.at[1], to_down),
        )
    ):
        first.append(copy(ref, held, more.at[k, 0]))
        second.append(copy(held, to, more.at[k, 1]))
    few = [copy(vectors, hold_vectors, few_sems.at[0]), copy(smalls, hold_smalls, few_sems.at[1])]
    for one in few + first:
        one.start()
    for one in few:
        one.wait()
    for k, ref in enumerate((gain_two, bias_two, bias_down, gain_one, bias_one, bias_out, bias_up)):
        ref[...] = hold_vectors[k : k + 1].reshape(ref.shape)
    for k, ref in enumerate((bias_query, bias_value)):
        ref[...] = hold_smalls[k : k + 1, 0 : ref.shape[0]].reshape(ref.shape)
    taps[...] = hold_smalls[2 : 2 + taps.shape[0], 0:KERNEL]
    for arriving, leaving in zip(first, second):
        arriving.wait()
        leaving.start()
    for one in second:
        one.wait()


def fused_body(
    inputs, cotangent, item_lengths, w_query, w_key, w_value, w_out, w_up, w_down, bias_query, bias_value,
    bias_out, bias_up, bias_down, gain_one, bias_one, gain_two, bias_two, conv_taps,
):
    count = lax.axis_size("seq")
    rows, width = inputs.shape
    near, feed, heads = w_query.shape[1], w_up.shape[1], conv_taps.shape[0]
    size, part, lines = rows // CHUNKS, width // count, count // 2
    half, two = size // 2, 2 * LAND
    share = 128 * -(-width // 128 // count)
    low = lambda *shape: pltpu.VMEM(shape, LOW)
    wide = lambda *shape: pltpu.VMEM(shape, WIDE)
    sem = lambda *shape: pltpu.SemaphoreType.DMA(shape)
    vmem, smem = pl.BlockSpec(memory_space=pltpu.VMEM), pl.BlockSpec(memory_space=pltpu.SMEM)
    operands = dict(
        lengths=item_lengths, conv_taps=conv_taps,
        inputs_hbm=inputs, cotangent_hbm=cotangent,
        w_up=w_up, w_down=w_down,
        w_query_hbm=w_query, w_key_hbm=w_key, w_value_hbm=w_value, w_out_hbm=w_out,
        bias_query_hbm=bias_query, bias_value_hbm=bias_value,
        bias_out_hbm=bias_out, bias_up_hbm=bias_up, bias_down_hbm=bias_down,
        gain_one_hbm=gain_one, bias_one_hbm=bias_one, gain_two_hbm=gain_two, bias_two_hbm=bias_two,
    )
    outs = dict(
        output_hbm=((rows, width), LOW), grad_inputs_hbm=((rows, width), LOW),
        grad_w_out_hbm=((part, near), WIDE), grad_w_up_hbm=((part, feed), WIDE), grad_w_down_hbm=((part, feed), WIDE),
        grad_near_hbm=((3, part, near), WIDE), vectors=((8, width), WIDE), smalls=((8, PAD), WIDE),
    )
    line = lambda length: pltpu.VMEM((length,), WIDE)
    scratch = dict(
        w_query=low(part, near), w_key=low(part, near), w_value=low(part, near), w_out=low(part, near),
        bias_query=line(near), bias_value=line(near), bias_out=line(width), bias_up=line(feed), bias_down=line(width),
        gain_one=line(width), bias_one=line(width), gain_two=line(width), bias_two=line(width),
        shard_sems=sem(4), vector_sems=sem(9),
        inputs=low(rows, width), cotangent=low(rows, width), output=low(rows, width),
        grad_w_out=wide(part, near), grad_w_up=wide(part, feed), grad_w_down=wide(part, feed),
        grad_near=wide(3, part, near), io=sem(8),
        packed=low(part, 4 * near), w_near=low(count, part, 4 * near), out_turned=low(4, near, width),
        mixed_out=low(CHUNKS, 2, 3 * half // 2, 128), mixed_in=low(3, CHUNKS, 3 * half // 2, 128),
        full_up=low(count, part, feed), full_down=low(count, part, feed),
        member=low(rows, two), band=low(heads * BLOCK, 2 * SPAN), band_back=low(heads * BLOCK, 2 * SPAN),
        queries=low(rows, near), keys=low(rows, near), value_ext=low(rows + 2 * REACH, PAD),
        land_part=low(count, 3 * BORDER, 128), query_land=low(two, near), key_land=low(two, near),
        query_heads=low(heads * two, near), key_heads=low(heads * two, near),
        weights_b=wide(heads * two, rows),
        max_b=wide(heads * two, 1), total_b=wide(heads * two, 1),
        numer_out=wide(count, LAND // count, PAD), numer_in=wide(count, LAND // count, PAD),
        kernel_v=wide(count, LAND // count, PAD), kernel_edge=wide(LAND, PAD),
        land_kernel=wide(2 * heads, LAND, LAND), inverse=wide(2 * heads, LAND, LAND),
        befores=wide(PINV_STEPS, 2 * heads, LAND, LAND), products=wide(PINV_STEPS, 2 * heads, LAND, LAND),
        uppers=low(PINV_STEPS, 2 * heads, 2, LAND, 3 * LAND), lowers=low(PINV_STEPS, 2 * heads, 2, LAND, 3 * LAND),
        turned_kernel=low(2 * heads, 2, LAND, LAND),
        weights_f=wide(rows, heads * two), conv=wide(rows, near),
        mixing=low(two, near), mixing_heads=low(heads * two, near), mixed=low(rows, near),
        terms=low(CHUNKS, size, width), core_in=low(CHUNKS, half, width),
        x_out=low(CHUNKS, half, width), x_in=low(2, CHUNKS, half, width),
        hidden=low(rows, width), active=low(rows, feed), slope=low(rows, feed),
        grad_two=low(rows, width), grad_lift=low(rows, feed), grad_one=low(rows, width),
        norm_one=wide(rows // 2, width), inv_one=wide(rows // 2, 1), wide_grad=wide(rows // 2, width),
        tmp=wide(size, feed), acc=wide(7, 8, width),
        grad_ext=low(rows + 2 * REACH, near), grad_query=wide(rows, near),
        mix_grad=wide(heads * two, near), kland_grad=wide(heads * two, near),
        mix_out=wide(count, LAND // count, near), mix_in=wide(count, LAND // count, near),
        mix_sums=wide(count, LAND // count, near), land_out=wide(count, LAND // count, 2 * near),
        land_in=wide(count, LAND // count, 2 * near), land_sums=wide(count, LAND // count, 2 * near),
        vector_out=wide(count, 8, share), vector_in=wide(count, 8, share), vector_sums=wide(count, 8, share),
        tap_grad=wide(heads * BLOCK, 128), numer_heads=low(heads * two, near), total_grad=wide(heads * two, 1),
        scores_b=low(heads * two, rows), near_grads=low(rows, 3 * near),
        slot_q=low(2 * two, near), slot_k=low(2 * two, near), slot_both=low(two, 2 * near),
        vector_sum=wide(2, 8, width), small_part=wide(count, 8, PAD),
    )
    tall = 3 * part // 2
    for_out, for_up, for_down, for_qk, for_v = (
        (low(count, *of), low(lines, *of), low(lines - 1, *of), low(lines - 1, *of))
        for of in ((tall, 128), (part, feed), (part, feed), (part, 2 * near), (tall, 128))
    )
    scratch.update(
        t_out=for_out[0], yb_out=for_out[1], pr_out=for_out[2], zb_out=for_out[3],
        t_up=for_up[0], yb_up=for_up[1], pr_up=for_up[2], zb_up=for_up[3],
        t_down=for_down[0], yb_down=for_down[1], pr_down=for_down[2], zb_down=for_down[3],
        t_qk=for_qk[0], yb_qk=for_qk[1], pr_qk=for_qk[2], zb_qk=for_qk[3],
        t_v=for_v[0], yb_v=for_v[1], pr_v=for_v[2], zb_v=for_v[3],
        corr_terms=low(1, two, width), corr_core=low(1, LAND, width), corr_out=low(1, LAND, width),
        corr_in=low(1, 1, LAND, width), corr_sems=sem(1, 4, 1), corr_all=low(two, width),
        corr_s=sem(1), corr_r=sem(1),
        g_own=sem(8), g_zs=sem(8, lines - 1), g_zr=sem(8, lines - 1), g_ys=sem(8, lines), g_yr=sem(8, lines),
        s_ys=sem(5, lines), s_yr=sem(5, lines), s_zs=sem(5, lines - 1), s_zr=sem(5, lines - 1),
        e_s=sem(10, count - 1), e_r=sem(10, count - 1), h_sems=sem(3, 4, CHUNKS), w_s=sem(3), w_r=sem(3), m_s=sem(3, CHUNKS), m_r=sem(3, CHUNKS),
        rim_s=sem(2, 2), rim_r=sem(2, 2), share_s=sem(5, CHUNKS), share_r=sem(5, CHUNKS),
        core_s=sem(1), core_r=sem(1), chunk_sems=sem(CHUNKS),
    )
    any_place = pl.BlockSpec(memory_space=pltpu.HBM)
    results = pl.pallas_call(
        functools.partial(layer_kernel, count, list(operands) + list(outs) + list(scratch)),
        out_shape=tuple(jax.ShapeDtypeStruct(*out) for out in outs.values()),
        in_specs=[smem, smem] + [any_place] * (len(operands) - 2),
        out_specs=(any_place,) * 6 + (vmem, vmem),
        scratch_shapes=list(scratch.values()),
        compiler_params=pltpu.CompilerParams(
            collective_id=1, has_side_effects=True, vmem_limit_bytes=63 * 2**20
        ),
    )(*operands.values())
    vector = lambda length: jax.ShapeDtypeStruct((length,), WIDE)
    block = lambda lanes: jax.ShapeDtypeStruct((part, lanes), WIDE)
    whole = jax.ShapeDtypeStruct((rows, width), LOW)
    return pl.pallas_call(
        hand_out,
        out_shape=(
            whole, whole, block(near), block(near), block(near), block(near), block(feed), block(feed),
            vector(near), vector(near), vector(width), vector(feed), vector(width),
            vector(width), vector(width), vector(width), vector(width),
            jax.ShapeDtypeStruct((heads, KERNEL), WIDE),
        ),
        in_specs=[any_place] * 8,
        out_specs=(any_place,) * 8 + (vmem,) * 10,
        scratch_shapes=[
            low(2, CHUNKS, size, width), wide(4, part, near), wide(2, part, feed), wide(8, width), wide(8, PAD),
            sem(2, CHUNKS, 2), sem(6, 2), sem(2),
        ],
    )(*results)


def plain_body(
    inputs,
    cotangent,
    item_lengths,
    w_query,
    w_key,
    w_value,
    w_out,
    w_up,
    w_down,
    bias_query,
    bias_value,
    bias_out,
    bias_up,
    bias_down,
    gain_one,
    bias_one,
    gain_two,
    bias_two,
    conv_taps,
):
    low_type = jnp.bfloat16
    tok_rows = inputs.shape[0]
    heads_here = conv_taps.shape[0]
    width_here = heads_here * HEAD_DIM
    slots = ITEMS * LAND
    reach = (KERNEL - 1) // 2
    score_scale = HEAD_DIM ** (-0.5)
    pref = jnp.float32
    first_row = lax.axis_index("seq") * tok_rows
    positions = first_row + jnp.arange(tok_rows, dtype=jnp.int32)
    item_id, land_slot = locate(item_lengths, positions)
    rim_item = locate(
        item_lengths, first_row - reach + jnp.arange(tok_rows + 2 * reach, dtype=jnp.int32)
    )[0]
    slot_item = jnp.arange(slots, dtype=jnp.int32) // LAND
    member = land_slot[:, None] == jnp.arange(slots, dtype=jnp.int32)[None, :]
    member_low = member.astype(low_type)
    counts = jnp.repeat((item_lengths // LAND).astype(jnp.float32), LAND)
    same_f = item_id[:, None] == slot_item[None, :]
    same_b = same_f.T
    tap_cols = jnp.repeat(conv_taps, HEAD_DIM, axis=0)
    full_query, full_key, full_value, full_out, full_up, full_down = (
        lax.all_gather(w_query, "seq", axis=0, tiled=True),
        lax.all_gather(w_key, "seq", axis=0, tiled=True),
        lax.all_gather(w_value, "seq", axis=0, tiled=True),
        lax.all_gather(w_out, "seq", axis=0, tiled=True),
        lax.all_gather(w_up, "seq", axis=0, tiled=True),
        lax.all_gather(w_down, "seq", axis=0, tiled=True),
    )
    queries = (matmul_low(inputs, full_query) + bias_query).astype(low_type)
    key_rows = matmul_low(inputs, full_key).astype(low_type)
    value_rows = (matmul_low(inputs, full_value) + bias_value).astype(low_type)
    query_sums, key_sums = lax.psum(
        (across(member_low, queries), across(member_low, key_rows)), "seq"
    )
    query_land = (
        (query_sums / counts[:, None]).astype(low_type).reshape(slots, heads_here, HEAD_DIM)
    )
    key_land = (key_sums / counts[:, None]).astype(low_type).reshape(slots, heads_here, HEAD_DIM)
    query_heads = queries.reshape(tok_rows, heads_here, HEAD_DIM)
    key_heads = key_rows.reshape(tok_rows, heads_here, HEAD_DIM)
    value_heads = value_rows.reshape(tok_rows, heads_here, HEAD_DIM)
    scores_b = (
        jnp.einsum("lhd,thd->hlt", query_land, key_heads, preferred_element_type=pref) * score_scale
    )
    scores_b = jnp.where(same_b[None], scores_b, MASKED)
    maxima_b = lax.pmax(jnp.max(scores_b, axis=2), "seq")
    weights_b = jnp.exp(scores_b - maxima_b[:, :, None])
    weights_b_low = weights_b.astype(low_type)
    numer_sum, totals_b = lax.psum(
        (
            jnp.einsum("hlt,thd->lhd", weights_b_low, value_heads, preferred_element_type=pref),
            jnp.sum(weights_b, axis=2),
        ),
        "seq",
    )
    totals_cols = totals_b.T[:, :, None]
    kernel_v = numer_sum / totals_cols
    land_q = query_land.reshape(ITEMS, LAND, heads_here, HEAD_DIM)
    land_k = key_land.reshape(ITEMS, LAND, heads_here, HEAD_DIM)
    land_kernel = jax.nn.softmax(
        jnp.einsum("ilhd,imhd->ihlm", land_q, land_k, preferred_element_type=pref) * score_scale,
        axis=-1,
    )
    inverse, inverse_back = jax.vjp(pseudo_inverse, land_kernel)
    kernel_items = kernel_v.reshape(ITEMS, LAND, heads_here, HEAD_DIM)
    mixing = jnp.einsum("ihlm,imhd->ilhd", inverse, kernel_items, precision=PRECISE)
    mixing = mixing.astype(low_type).reshape(slots, heads_here, HEAD_DIM)
    scores_f = (
        jnp.einsum("thd,lhd->htl", query_heads, key_land, preferred_element_type=pref) * score_scale
    )
    weights_f = jax.nn.softmax(jnp.where(same_f[None], scores_f, MASKED), axis=-1)
    weights_f_low = weights_f.astype(low_type)
    attended = jnp.einsum("htl,lhd->thd", weights_f_low, mixing, preferred_element_type=pref)
    attended = attended.reshape(tok_rows, width_here)
    value_rim = extended(value_rows, (("seq", 0),), reach)
    conv_sum = jnp.zeros((tok_rows, width_here), jnp.float32)
    for offset in range(KERNEL):
        in_item = (rim_item[offset : offset + tok_rows] == item_id)[:, None]
        conv_sum = conv_sum + jnp.where(
            in_item,
            value_rim[offset : offset + tok_rows].astype(jnp.float32)
            * tap_cols[:, offset][None, :],
            0.0,
        )
    mixed_rows = (attended + conv_sum).astype(low_type)
    attention_sum = lax.psum(against(mixed_rows, full_out).astype(jnp.bfloat16), "head").astype(
        jnp.float32
    )
    pre_one = inputs.astype(jnp.float32) + attention_sum + bias_out
    norm_one, inv_one = normalize(pre_one)
    hidden = norm_one * gain_one + bias_one
    hidden_low = hidden.astype(low_type)
    lifted = matmul_low(hidden_low, full_up) + bias_up
    active, gelu_back = jax.vjp(gelu_tanh, lifted)
    active_low = active.astype(low_type)
    feed_terms = against(active_low, full_down)
    feed_sum = lax.psum(feed_terms.astype(jnp.bfloat16), "head").astype(jnp.float32)
    grad_output = cotangent.astype(jnp.float32)
    pre_two = hidden + feed_sum + bias_down
    norm_two, inv_two = normalize(pre_two)
    out_rows = (norm_two * gain_two + bias_two).astype(low_type)
    grad_gain_two = jnp.sum(grad_output * norm_two, axis=0)
    grad_bias_two = jnp.sum(grad_output, axis=0)
    grad_two = norm_back(grad_output * gain_two, norm_two, inv_two)
    grad_bias_down = jnp.sum(grad_two, axis=0)
    grad_two_low = grad_two.astype(low_type)
    output, grad_two_full = (out_rows, grad_two_low)
    grad_down = across(grad_two_full, active_low)
    (grad_lift,) = gelu_back(matmul_low(grad_two_full, full_down))
    grad_bias_up = jnp.sum(grad_lift, axis=0)
    grad_lift_low = grad_lift.astype(low_type)
    grad_up = across(hidden_low, grad_lift_low)
    up_terms = against(grad_lift_low, full_up)
    grad_hidden = grad_two + lax.psum(up_terms.astype(jnp.bfloat16), "head").astype(jnp.float32)
    grad_gain_one = jnp.sum(grad_hidden * norm_one, axis=0)
    grad_bias_one = jnp.sum(grad_hidden, axis=0)
    grad_one = norm_back(grad_hidden * gain_one, norm_one, inv_one)
    grad_bias_out = jnp.sum(grad_one, axis=0)
    grad_one_low = grad_one.astype(low_type)
    grad_outw = across(grad_one_low, mixed_rows)
    grad_mixed = matmul_low(grad_one_low, full_out).astype(low_type)
    grad_mixed_wide = grad_mixed.astype(jnp.float32)
    grad_heads = grad_mixed.reshape(tok_rows, heads_here, HEAD_DIM)
    grad_rim = extended(grad_mixed, (("seq", 0),), reach)
    grad_conv_v = jnp.zeros((tok_rows, width_here), jnp.float32)
    tap_terms = []
    for offset in range(KERNEL):
        in_item = (rim_item[offset : offset + tok_rows] == item_id)[:, None]
        neighbour = jnp.where(
            in_item, value_rim[offset : offset + tok_rows].astype(jnp.float32), 0.0
        )
        tap_terms.append(
            jnp.sum(
                (grad_mixed_wide * neighbour).reshape(tok_rows, heads_here, HEAD_DIM), axis=(0, 2)
            )
        )
        mirror = 2 * reach - offset
        mirror_item = (rim_item[mirror : mirror + tok_rows] == item_id)[:, None]
        grad_conv_v = grad_conv_v + jnp.where(
            mirror_item,
            grad_rim[mirror : mirror + tok_rows].astype(jnp.float32) * tap_cols[:, offset][None, :],
            0.0,
        )
    grad_taps = jnp.stack(tap_terms, axis=1)
    grad_weights_f = jnp.einsum("thd,lhd->htl", grad_heads, mixing, preferred_element_type=pref)
    grad_mix_part = jnp.einsum(
        "htl,thd->lhd", weights_f_low, grad_heads, preferred_element_type=pref
    )
    grad_scores_f = weights_f * (
        grad_weights_f - jnp.sum(weights_f * grad_weights_f, axis=2, keepdims=True)
    )
    grad_scores_f = grad_scores_f.astype(low_type)
    grad_query_f = (
        jnp.einsum("htl,lhd->thd", grad_scores_f, key_land, preferred_element_type=pref)
        * score_scale
    )
    grad_kland_part = (
        jnp.einsum("htl,thd->lhd", grad_scores_f, query_heads, preferred_element_type=pref)
        * score_scale
    )
    grad_mixing, grad_kland_f = lax.psum((grad_mix_part, grad_kland_part), "seq")
    grad_mix_items = grad_mixing.reshape(ITEMS, LAND, heads_here, HEAD_DIM)
    grad_inverse = jnp.einsum("ilhd,imhd->ihlm", grad_mix_items, kernel_items, precision=PRECISE)
    grad_kernel_v = jnp.einsum("ihlm,ilhd->imhd", inverse, grad_mix_items, precision=PRECISE)
    grad_kernel_v = grad_kernel_v.reshape(slots, heads_here, HEAD_DIM)
    (grad_land_kernel,) = inverse_back(grad_inverse)
    grad_scores_a = land_kernel * (
        grad_land_kernel - jnp.sum(land_kernel * grad_land_kernel, axis=-1, keepdims=True)
    )
    grad_scores_a = grad_scores_a * score_scale
    grad_qland_a = jnp.einsum(
        "ihlm,imhd->ilhd", grad_scores_a, land_k.astype(jnp.float32), precision=PRECISE
    )
    grad_kland_a = jnp.einsum(
        "ihlm,ilhd->imhd", grad_scores_a, land_q.astype(jnp.float32), precision=PRECISE
    )
    grad_numer = (grad_kernel_v / totals_cols).astype(low_type)
    grad_totals = -jnp.sum(grad_kernel_v * kernel_v, axis=2) / totals_b.T
    grad_weights_b = jnp.einsum(
        "lhd,thd->hlt", grad_numer, value_heads, preferred_element_type=pref
    )
    grad_weights_b = grad_weights_b + grad_totals.T[:, :, None]
    grad_scores_b = (weights_b * grad_weights_b).astype(low_type)
    grad_qland_part = (
        jnp.einsum("hlt,thd->lhd", grad_scores_b, key_heads, preferred_element_type=pref)
        * score_scale
    )
    grad_key_b = (
        jnp.einsum("hlt,lhd->thd", grad_scores_b, query_land, preferred_element_type=pref)
        * score_scale
    )
    grad_value_b = jnp.einsum(
        "hlt,lhd->thd", weights_b_low, grad_numer, preferred_element_type=pref
    )
    grad_query_rows = grad_query_f.reshape(tok_rows, width_here)
    grad_values = grad_value_b.reshape(tok_rows, width_here) + grad_conv_v
    (
        grad_qland_b,
        grad_gain_one,
        grad_bias_one,
        grad_gain_two,
        grad_bias_two,
        grad_bias_out,
        grad_bias_down,
        grad_bias_up,
        grad_taps,
        query_f_total,
        grad_bias_value,
    ) = lax.psum(
        (
            grad_qland_part,
            grad_gain_one,
            grad_bias_one,
            grad_gain_two,
            grad_bias_two,
            grad_bias_out,
            grad_bias_down,
            grad_bias_up,
            grad_taps,
            jnp.sum(grad_query_rows, axis=0),
            jnp.sum(grad_values, axis=0),
        ),
        "seq",
    )
    grad_qland = grad_qland_a.reshape(slots, width_here) + grad_qland_b.reshape(slots, width_here)
    grad_kland = grad_kland_a.reshape(slots, width_here) + grad_kland_f.reshape(slots, width_here)
    member_wide = member.astype(jnp.float32)
    grad_queries = grad_query_rows + jnp.dot(
        member_wide, grad_qland / counts[:, None], precision=PRECISE
    )
    grad_keys = grad_key_b.reshape(tok_rows, width_here) + jnp.dot(
        member_wide, grad_kland / counts[:, None], precision=PRECISE
    )
    grad_bias_query = query_f_total + jnp.sum(grad_qland, axis=0)
    queries_low = grad_queries.astype(low_type)
    keys_low = grad_keys.astype(low_type)
    values_low = grad_values.astype(low_type)
    grad_queryw = across(inputs, queries_low)
    grad_keyw = across(inputs, keys_low)
    grad_valuew = across(inputs, values_low)
    input_terms = (
        against(queries_low, full_query)
        + against(keys_low, full_key)
        + against(values_low, full_value)
    )
    grad_inputs = (
        grad_one + lax.psum(input_terms.astype(jnp.bfloat16), "head").astype(jnp.float32)
    ).astype(low_type)
    query_shard, key_shard, value_shard, out_shard, grad_up_shard, grad_down_shard = side_by_side(
        (
            grad_queryw.astype(jnp.bfloat16),
            grad_keyw.astype(jnp.bfloat16),
            grad_valuew.astype(jnp.bfloat16),
            grad_outw.astype(jnp.bfloat16),
            grad_up.astype(jnp.bfloat16),
            grad_down.astype(jnp.bfloat16),
        ),
        "seq",
        0,
        1,
    )
    return (
        output,
        grad_inputs,
        query_shard,
        key_shard,
        value_shard,
        out_shard,
        grad_up_shard,
        grad_down_shard,
        grad_bias_query,
        grad_bias_value,
        grad_bias_out,
        grad_bias_up,
        grad_bias_down,
        grad_gain_one,
        grad_bias_one,
        grad_gain_two,
        grad_bias_two,
        grad_taps,
    )


def solution(mesh):
    seq, head = mesh.shape["seq"], mesh.shape["head"]
    fits = head == 4 and seq == 8
    return jax.shard_map(
        fused_body if fits else plain_body,
        mesh=mesh,
        in_specs=(
            P("seq", None),
            P("seq", None),
            P(),
            P("seq", "head"),
            P("seq", "head"),
            P("seq", "head"),
            P("seq", "head"),
            P("seq", "head"),
            P("seq", "head"),
            P("head"),
            P("head"),
            P(),
            P("head"),
            P(),
            P(),
            P(),
            P(),
            P(),
            P("head", None),
        ),
        out_specs=(
            P("seq", None),
            P("seq", None),
            P("seq", "head"),
            P("seq", "head"),
            P("seq", "head"),
            P("seq", "head"),
            P("seq", "head"),
            P("seq", "head"),
            P("head"),
            P("head"),
            P(),
            P("head"),
            P(),
            P(),
            P(),
            P(),
            P(),
            P("head", None),
        ),
        check_vma=False,
    )
```
